768 devices in a mesh: tile: 12 (over z), group: 64 (over y, x, core).
Axes of the slice: x: 4, y: 8, z: 12, core: 2. Of those that a mesh axis runs over, the one named last changes fastest.
Arguments:
- pressure_head: float32 [96, 1024, 128], P('tile', 'group'), may hold values from -2.1 to -0.018, as said below
- old_head: float32 [96, 1024, 128], P('tile', 'group'), may hold values from -3 to -1.5
- soil_type: int32 [96, 1024, 128], P('tile', 'group'), may hold values from 0 to 11
- conduct_sat: float32 [12], replicated, may hold values from 0.1 to 2
- alpha_param: float32 [12], replicated, may hold values from 0.5 to 3
- shape_param: float32 [12], replicated, may hold values from 1.3 to 2.8
- water_span: float32 [12], replicated, may hold values from 0.25 to 0.5
Outputs:
- update: float32 [96, 1024, 128], P('tile', 'group')
- remainder: float32 [96, 1024, 128], P('tile', 'group')
The draws below stay inside these ranges and needn't reach their ends.
Inputs may be any that keep to these rules, and one draw needn't show every extreme that they name: `pressure_head`: the head is negative in every cell.
All inputs are finite; a program needn't handle non-finite values.
Results may differ from the reference program's by a relative error of at most 0.0003.
Values sent between devices are 32-bit elements; how exact they have to be, the bound alone decides.
No kernel may reach another device: no remote copies, remote signals or barrier semaphores. Data moves between devices by JAX's collectives and lax.ppermute only.
A program may use at most 128 MiB of HBM per device.

```python
import math
import jax
import jax.numpy as jnp
from jax import lax

NZ = 128
LEVELS = 4
COARSE_SWEEPS = 4
CYCLES = 2
SOILS = 12
NX = 96
NY = 1024


def draw_pressure_head(key, part):
    key = jax.random.fold_in(key, 11)
    across = jnp.arange(NY, dtype=jnp.float32) / float(NY - 1)
    depth = jnp.exp(jnp.log(0.03) + (jnp.log(1.5) - jnp.log(0.03)) * across)
    rough = jax.random.uniform(key, (NX, NY, NZ), jnp.float32, 0.6, 1.4)
    return -(depth[None, :, None] * rough)


def plant(entries, rng, smallest, high):
    place = [jax.random.randint(jax.random.fold_in(rng, axis), (), 0, length) for axis, length in enumerate(entries.shape)]
    widest = entries.shape.index(max(entries.shape))
    next_to = place[:widest] + [(place[widest] + 1) % entries.shape[widest]] + place[widest + 1:]
    return entries.at[tuple(place)].set(smallest).at[tuple(next_to)].set(high)


def levels(own_key, extent, cuts, smallest, largest):
    def one(position, blocks):
        steps = jax.random.uniform(jax.random.fold_in(jax.random.fold_in(own_key, 6), position), (blocks,), jnp.float32, smallest / len(cuts), largest / len(cuts))
        return jnp.repeat(jnp.exp(steps), extent[position] // blocks).reshape((-1,) + (1,) * (len(extent) - position - 1))

    factor_of = one(*cuts[0])
    for cut in cuts[1:]:
        factor_of = factor_of * one(*cut)
    return factor_of


def setup_inputs(seed: int = 0) -> dict:
    splits = jax.random.split(jax.random.key(seed), 8)
    return {
        "pressure_head": draw_pressure_head(jax.random.fold_in(splits[7], 71), 0),
        "old_head": jnp.clip(-3.0 + 1.5 * jax.random.uniform(splits[1], (NX, NY, NZ), jnp.float32) ** levels(splits[1], (NX, NY, NZ), ((0, 12), (1, 64)), -0.2, 0.2), -3.0, -1.5),
        "soil_type": plant(jax.random.randint(splits[2], (NX, NY, NZ), 0, SOILS), jax.random.fold_in(splits[2], 1), 0, SOILS - 1).astype(jnp.int32),
        "conduct_sat": jnp.clip(jnp.exp(jax.random.uniform(splits[3], (SOILS,), jnp.float32, math.log(0.1), math.log(2.0))), 0.1, 2.0),
        "alpha_param": jnp.clip(jnp.exp(jax.random.uniform(splits[4], (SOILS,), jnp.float32, math.log(0.5), math.log(3.0))), 0.5, 3.0),
        "shape_param": jnp.clip(jax.random.uniform(splits[5], (SOILS,), jnp.float32, 1.3, 2.8), 1.3, 2.8),
        "water_span": jnp.clip(jax.random.uniform(splits[6], (SOILS,), jnp.float32, 0.25, 0.5), 0.25, 0.5),
    }


OMEGA = 2.0 / 3.0
STORAGE = 0.01

def hydraulics(head_vals, conduct, alpha_cells, shape_cells, spread_cells):
    shape_m = 1.0 - 1.0 / shape_cells
    power = jnp.exp(shape_cells * jnp.log(alpha_cells * -head_vals))
    saturation = jnp.exp(-shape_m * jnp.log1p(power))
    fraction = power / (1.0 + power)
    factor = 1.0 - jnp.exp(shape_m * jnp.log(fraction))
    conductivity = conduct * jnp.sqrt(saturation) * factor * factor
    capacity = spread_cells * shape_m * shape_cells * power / -head_vals * saturation / (1.0 + power)
    return (saturation, conductivity, capacity)

def harmonic(first, second):
    return 2.0 * first * second / (first + second)

def assemble(padded_head, padded_cond, pressure_head, old_head, saturation, old_saturation, spread_cells, capacity):
    center = padded_cond[1:-1, 1:-1, 1:-1]
    x_low = harmonic(center, padded_cond[:-2, 1:-1, 1:-1])
    x_high = harmonic(center, padded_cond[2:, 1:-1, 1:-1])
    y_low = harmonic(center, padded_cond[1:-1, :-2, 1:-1])
    y_high = harmonic(center, padded_cond[1:-1, 2:, 1:-1])
    z_low = harmonic(center, padded_cond[1:-1, 1:-1, :-2])
    z_high = harmonic(center, padded_cond[1:-1, 1:-1, 2:])
    flux = x_low * (pressure_head - padded_head[:-2, 1:-1, 1:-1]) + x_high * (pressure_head - padded_head[2:, 1:-1, 1:-1])
    flux = flux + y_low * (pressure_head - padded_head[1:-1, :-2, 1:-1]) + y_high * (pressure_head - padded_head[1:-1, 2:, 1:-1])
    flux = flux + z_low * (pressure_head - padded_head[1:-1, 1:-1, :-2] + 1.0) + z_high * (pressure_head - padded_head[1:-1, 1:-1, 2:] - 1.0)
    misfit = spread_cells * (saturation - old_saturation) + STORAGE * (pressure_head - old_head) + flux
    band_set = jnp.stack([capacity + STORAGE, x_low, x_high, y_low, y_high, z_low, z_high])
    return (-misfit, band_set)

def diagonal_of(band_set):
    return band_set[0] + band_set[1] + band_set[2] + band_set[3] + band_set[4] + band_set[5] + band_set[6]

def apply_operator(band_set, diagonal, padded):
    center = padded[1:-1, 1:-1, :]
    vertical = jnp.pad(center, ((0, 0), (0, 0), (1, 1)))
    beside = band_set[1] * padded[:-2, 1:-1, :] + band_set[2] * padded[2:, 1:-1, :]
    beside = beside + band_set[3] * padded[1:-1, :-2, :] + band_set[4] * padded[1:-1, 2:, :]
    beside = beside + band_set[5] * vertical[:, :, :-2] + band_set[6] * vertical[:, :, 2:]
    return diagonal * center - beside

def coarsen_bands(band_set):
    seven, size_x, size_y, size_z = band_set.shape
    split = band_set.reshape(seven, size_x // 2, 2, size_y // 2, 2, size_z // 2, 2)
    storage = lax.optimization_barrier(jnp.sum(split[0], axis=(1, 3, 5)))
    x_low = lax.optimization_barrier(jnp.sum(split[1][:, 0], axis=(2, 4)))
    x_high = lax.optimization_barrier(jnp.sum(split[2][:, 1], axis=(2, 4)))
    y_low = lax.optimization_barrier(jnp.sum(split[3][:, :, :, 0], axis=(1, 4)))
    y_high = lax.optimization_barrier(jnp.sum(split[4][:, :, :, 1], axis=(1, 4)))
    z_low = lax.optimization_barrier(jnp.sum(split[5][:, :, :, :, :, 0], axis=(1, 3)))
    z_high = lax.optimization_barrier(jnp.sum(split[6][:, :, :, :, :, 1], axis=(1, 3)))
    return jnp.stack([storage, x_low, x_high, y_low, y_high, z_low, z_high])

def restrict(values):
    size_x, size_y, size_z = values.shape
    return lax.optimization_barrier(jnp.sum(values.reshape(size_x // 2, 2, size_y // 2, 2, size_z // 2, 2), axis=(1, 3, 5)))

def prolong(values):
    return jnp.repeat(jnp.repeat(jnp.repeat(values, 2, axis=0), 2, axis=1), 2, axis=2)

def pad_sides(values):
    return jnp.pad(values, ((1, 1), (1, 1), (0, 0)))

def line_start(band_set, diagonal, remain):
    inner = diagonal - band_set[3] - band_set[4]
    line_value = lax.optimization_barrier(jnp.sum(remain, axis=1, keepdims=True)) / lax.optimization_barrier(jnp.sum(inner, axis=1, keepdims=True))
    return jnp.broadcast_to(line_value, remain.shape)

def descend(level_at, remain, band_sets, diagonals):
    band_set = band_sets[level_at]
    diagonal = diagonals[level_at]
    if level_at == len(band_sets) - 1:
        update = line_start(band_set, diagonal, remain)
        for sweep_no in range(COARSE_SWEEPS):
            update = update + OMEGA * (remain - apply_operator(band_set, diagonal, pad_sides(update))) / diagonal
        return update
    update = OMEGA * remain / diagonal
    update = update + OMEGA * (remain - apply_operator(band_set, diagonal, pad_sides(update))) / diagonal
    defect = remain - apply_operator(band_set, diagonal, pad_sides(update))
    coarse = descend(level_at + 1, restrict(defect), band_sets, diagonals)
    update = update + prolong(coarse)
    update = update + OMEGA * (remain - apply_operator(band_set, diagonal, pad_sides(update))) / diagonal
    return update

def reference(pressure_head, old_head, soil_type, conduct_sat, alpha_param, shape_param, water_span):
    conduct = jnp.take(conduct_sat, soil_type)
    alpha_cells = jnp.take(alpha_param, soil_type)
    shape_cells = jnp.take(shape_param, soil_type)
    spread_cells = jnp.take(water_span, soil_type)
    saturation, conductivity, capacity = hydraulics(pressure_head, conduct, alpha_cells, shape_cells, spread_cells)
    old_saturation = hydraulics(old_head, conduct, alpha_cells, shape_cells, spread_cells)[0]
    padded_head = jnp.pad(pressure_head, 1)
    padded_cond = jnp.pad(conductivity, 1)
    rhs, band_set = assemble(padded_head, padded_cond, pressure_head, old_head, saturation, old_saturation, spread_cells, capacity)
    band_sets = [band_set]
    for level_at in range(1, LEVELS):
        band_sets.append(coarsen_bands(band_sets[-1]))
    diagonals = [diagonal_of(entry) for entry in band_sets]
    update = descend(0, rhs, band_sets, diagonals)
    for turn_no in range(CYCLES - 1):
        remain = rhs - apply_operator(band_sets[0], diagonals[0], pad_sides(update))
        update = update + descend(0, remain, band_sets, diagonals)
    remainder = rhs - apply_operator(band_sets[0], diagonals[0], pad_sides(update))
    return (update, remainder)
```

```python
import functools

import jax
import jax.numpy as jnp
from jax import lax
from jax.experimental import pallas as pl
from jax.experimental.pallas import tpu as pltpu
from jax.sharding import PartitionSpec as P

OMEGA = 2.0 / 3.0
STORAGE = 0.01
COARSE_SWEEPS = 4
SOILS = 12

BX, BY, NZ = 8, 16, 128
WX, WY = 24, 32
PX = WX + 2
L1X = WX // 2
F32 = jnp.float32


def iota(shape, dim):
    return lax.broadcasted_iota(jnp.int32, shape, dim)


def turn(v, step, axis):
    size = v.shape[axis]
    return pltpu.roll(v, step % size, axis)


def bit_of(v, step, axis):
    return (iota(v.shape, axis) // step) % 2 == 0


def pair_sum(v, step, axis):
    return v + jnp.where(bit_of(v, step, axis), turn(v, -step, axis), turn(v, step, axis))


def pair_low(v, step, axis):
    return jnp.where(bit_of(v, step, axis), v, turn(v, step, axis))


def x_low(v):
    return jnp.concatenate([v[:1], v[:-1]], axis=0)


def x_high(v):
    return jnp.concatenate([v[1:], jnp.zeros_like(v[:1])], axis=0)


def x_pair(v):
    return jnp.sum(v.reshape((v.shape[0] // 2, 2) + v.shape[1:]), axis=1)


def x_even(v):
    return v.reshape((v.shape[0] // 2, 2) + v.shape[1:])[:, 0]


def x_repeat(v):
    size = v.shape[0]
    wide = jnp.broadcast_to(v[:, None], (size, 2) + v.shape[1:])
    return wide.reshape((2 * size,) + v.shape[1:])


def operate(v, storage, wx, wy, wz, sy, sz):
    fx = wx * (v - x_low(v))
    fy = wy * (v - turn(v, sy, 1))
    fz = wz * (v - turn(v, sz, 2))
    flux = (fx - x_high(fx)) + (fy - turn(fy, -sy, 1)) + (fz - turn(fz, -sz, 2))
    return storage * v + flux


def relax_factor(storage, wx, wy, wz, sy, sz):
    diagonal = storage + wx + x_high(wx) + wy + turn(wy, -sy, 1) + wz + turn(wz, -sz, 2)
    return jnp.where(diagonal > 0.0, OMEGA / diagonal, 0.0)


def restrict(v, sy, sz):
    return pair_sum(pair_sum(x_pair(v), sy, 1), sz, 2)


def coarsen(storage, wx, wy, wz, sy, sz):
    return (
        restrict(storage, sy, sz),
        pair_sum(pair_sum(x_even(wx), sy, 1), sz, 2),
        pair_low(pair_sum(x_pair(wy), sz, 2), sy, 1),
        pair_low(pair_sum(x_pair(wz), sy, 1), sz, 2),
    )


def operate_rows(v_ref, s_ref, wx_ref, wy_ref, wz_ref, at, size):
    v = v_ref[pl.ds(at, size)]
    wx = wx_ref[pl.ds(at, size)]
    fy = wy_ref[pl.ds(at, size)] * (v - turn(v, 1, 1))
    fz = wz_ref[pl.ds(at, size)] * (v - turn(v, 1, 2))
    flux = wx * (v - v_ref[pl.ds(at - 1, size)])
    flux = flux - wx_ref[pl.ds(at + 1, size)] * (v_ref[pl.ds(at + 1, size)] - v)
    flux = flux + (fy - turn(fy, -1, 1)) + (fz - turn(fz, -1, 2))
    return v, s_ref[pl.ds(at, size)] * v + flux


def inside_grid(at, size):
    shape = (size, WY, NZ)
    gx = BX * lax.axis_index("tile") - (WX - BX) // 2 + (at - 1) + iota(shape, 0)
    gy = BY * lax.axis_index("group") - (WY - BY) // 2 + iota(shape, 1)
    return (
        (gx >= 0)
        & (gx < BX * lax.axis_size("tile"))
        & (gy >= 0)
        & (gy < BY * lax.axis_size("group"))
    )


def blank_ends(ref):
    ref[0] = jnp.zeros((WY, NZ), F32)
    ref[PX - 1] = jnp.zeros((WY, NZ), F32)


def pack_level2(v):
    sub, lane = iota(v.shape, 1), iota(v.shape, 2)
    chosen = (sub >= 8) & (sub < 24) & (sub % 4 == 0) & ((sub - 8) // 4 == lane % 4)
    return jnp.sum(jnp.where(chosen, v, 0.0), axis=1)


def send_level2(msg_ref, fields):
    rows = [pack_level2(v[2:4]) for v in fields]
    spare = msg_ref.shape[1] - 2 * len(rows)
    rows.append(jnp.zeros((spare, NZ), F32))
    whole = jnp.concatenate(rows, axis=0)
    for peer in range(msg_ref.shape[0]):
        msg_ref[peer] = whole


def descend_top(r_ref, e1_ref, e2_ref, s_ref, wx_ref, wy_ref, wz_ref, di_ref, r1_ref, each_pair):
    def second(i, carry):
        at = 1 + 2 * i
        v, av = operate_rows(e1_ref, s_ref, wx_ref, wy_ref, wz_ref, at, 2)
        e2_ref[pl.ds(at, 2)] = v + di_ref[pl.ds(at, 2)] * (r_ref[pl.ds(at, 2)] - av)
        return carry

    lax.fori_loop(0, WX // 2, second, 0)

    def third(i, carry):
        at = 1 + 2 * i
        _, av = operate_rows(e2_ref, s_ref, wx_ref, wy_ref, wz_ref, at, 2)
        r1_ref[pl.ds(i, 1)] = restrict(r_ref[pl.ds(at, 2)] - av, 1, 1)
        each_pair(i, at)
        return carry

    lax.fori_loop(0, WX // 2, third, 0)


def descend_second(r1, s1, wx1, wy1, wz1, di1):
    first = r1 * di1
    second = first + di1 * (r1 - operate(first, s1, wx1, wy1, wz1, 2, 2))
    defect = r1 - operate(second, s1, wx1, wy1, wz1, 2, 2)
    return second, restrict(defect, 2, 2)


def assemble_kernel(
    core, ylow, yhigh, ks_ref, alpha_ref, shape_ref, span_ref,
    r_ref, s_ref, di_ref, wx_ref, wy_ref, wz_ref, e2_ref,
    r1_ref, s1_ref, di1_ref, wx1_ref, wy1_ref, wz1_ref, e21_ref, msg_ref,
    h_ref, k_ref, m_ref, e1_ref,
):
    def window(field, at):
        row = pl.ds(at - 1, 1)
        return jnp.concatenate([ylow[field, row], core[field, row], yhigh[field, row]], axis=1)

    for ref in (h_ref, k_ref, s_ref, wx_ref, wy_ref, wz_ref, di_ref, r_ref, e1_ref, e2_ref):
        blank_ends(ref)

    def soils(i, carry):
        at = 1 + i
        inside = inside_grid(at, 1)
        head = jnp.where(inside, window(0, at), -1.0)
        old = jnp.where(inside, window(1, at), -1.0)
        soil = window(2, at)
        ks = jnp.full(soil.shape, ks_ref[0])
        alpha = jnp.full(soil.shape, alpha_ref[0])
        shape_n = jnp.full(soil.shape, shape_ref[0])
        span = jnp.full(soil.shape, span_ref[0])
        for kind in range(1, SOILS):
            hit = soil == float(kind)
            ks = jnp.where(hit, ks_ref[kind], ks)
            alpha = jnp.where(hit, alpha_ref[kind], alpha)
            shape_n = jnp.where(hit, shape_ref[kind], shape_n)
            span = jnp.where(hit, span_ref[kind], span)
        shape_m = 1.0 - 1.0 / shape_n
        power = jnp.exp(shape_n * jnp.log(alpha * -head))
        old_power = jnp.exp(shape_n * jnp.log(alpha * -old))
        saturation = jnp.exp(-shape_m * jnp.log1p(power))
        old_saturation = jnp.exp(-shape_m * jnp.log1p(old_power))
        portion = 1.0 / (1.0 + power)
        factor = 1.0 - jnp.exp(shape_m * jnp.log(power / (1.0 + power)))
        conductivity = ks * jnp.sqrt(saturation) * factor * factor
        capacity = span * shape_m * shape_n * power / -head * saturation * portion
        row = pl.ds(at, 1)
        h_ref[row] = head
        k_ref[row] = jnp.where(inside, conductivity, 0.0)
        s_ref[row] = capacity + STORAGE
        m_ref[row] = span * (saturation - old_saturation) + STORAGE * (head - old)
        return carry

    lax.fori_loop(0, WX, soils, 0)

    def harmonic(a, b):
        total = a + b
        return jnp.where(total > 0.0, 2.0 * a * b / total, 0.0)

    def faces(i, carry):
        at = 1 + 2 * i
        k = k_ref[pl.ds(at, 2)]
        wx_ref[pl.ds(at, 2)] = harmonic(k, k_ref[pl.ds(at - 1, 2)])
        wy_ref[pl.ds(at, 2)] = harmonic(k, turn(k, 1, 1))
        wz = harmonic(k, turn(k, 1, 2))
        wz_ref[pl.ds(at, 2)] = jnp.where(iota(wz.shape, 2) == 0, 0.0, wz)
        return carry

    lax.fori_loop(0, WX // 2, faces, 0)

    def right_side(i, carry):
        at = 1 + 2 * i
        rows = pl.ds(at, 2)
        h, wx, wy, wz = h_ref[rows], wx_ref[rows], wy_ref[rows], wz_ref[rows]
        wx_up = wx_ref[pl.ds(at + 1, 2)]
        fy = wy * (h - turn(h, 1, 1))
        fz = wz * (h - turn(h, 1, 2) + 1.0)
        flux = wx * (h - h_ref[pl.ds(at - 1, 2)]) - wx_up * (h_ref[pl.ds(at + 1, 2)] - h)
        flux = flux + (fy - turn(fy, -1, 1)) + (fz - turn(fz, -1, 2))
        rhs = jnp.where(inside_grid(at, 2), -(m_ref[rows] + flux), 0.0)
        diagonal = s_ref[rows] + wx + wx_up + wy + turn(wy, -1, 1) + wz + turn(wz, -1, 2)
        di = OMEGA / diagonal
        r_ref[rows] = rhs
        di_ref[rows] = di
        e1_ref[rows] = rhs * di
        return carry

    lax.fori_loop(0, WX // 2, right_side, 0)

    def bands(i, at):
        rows = pl.ds(at, 2)
        s1, wx1, wy1, wz1 = coarsen(s_ref[rows], wx_ref[rows], wy_ref[rows], wz_ref[rows], 1, 1)
        row = pl.ds(i, 1)
        s1_ref[row], wx1_ref[row], wy1_ref[row], wz1_ref[row] = s1, wx1, wy1, wz1

    descend_top(r_ref, e1_ref, e2_ref, s_ref, wx_ref, wy_ref, wz_ref, di_ref, r1_ref, bands)

    s1, wx1, wy1, wz1 = s1_ref[...], wx1_ref[...], wy1_ref[...], wz1_ref[...]
    di1 = relax_factor(s1, wx1, wy1, wz1, 2, 2)
    di1_ref[...] = di1
    e21, r2 = descend_second(r1_ref[...], s1, wx1, wy1, wz1, di1)
    e21_ref[...] = e21
    send_level2(msg_ref, (r2,) + coarsen(s1, wx1, wy1, wz1, 2, 2))


def again_kernel(
    core, ylow, yhigh, rhs_ref, s_ref, di_ref, wx_ref, wy_ref, wz_ref,
    s1_ref, di1_ref, wx1_ref, wy1_ref, wz1_ref,
    u_ref, r_ref, e2_ref, r1_ref, e21_ref, msg_ref, pre_ref, e1_ref,
):
    for ref in (pre_ref, u_ref, r_ref, e1_ref, e2_ref):
        blank_ends(ref)
    pre_ref[1 : PX - 1, 0:8, :] = ylow[...]
    pre_ref[1 : PX - 1, 8:24, :] = core[...]
    pre_ref[1 : PX - 1, 24:32, :] = yhigh[...]

    def post(i, carry):
        at = 1 + 2 * i
        rows = pl.ds(at, 2)
        v, av = operate_rows(pre_ref, s_ref, wx_ref, wy_ref, wz_ref, at, 2)
        u_ref[rows] = v + di_ref[rows] * (rhs_ref[rows] - av)
        return carry

    lax.fori_loop(0, WX // 2, post, 0)

    def remain(i, carry):
        at = 1 + 2 * i
        rows = pl.ds(at, 2)
        _, av = operate_rows(u_ref, s_ref, wx_ref, wy_ref, wz_ref, at, 2)
        left = rhs_ref[rows] - av
        r_ref[rows] = left
        e1_ref[rows] = left * di_ref[rows]
        return carry

    lax.fori_loop(0, WX // 2, remain, 0)
    descend_top(
        r_ref, e1_ref, e2_ref, s_ref, wx_ref, wy_ref, wz_ref, di_ref, r1_ref, lambda i, at: None
    )
    e21, r2 = descend_second(
        r1_ref[...], s1_ref[...], wx1_ref[...], wy1_ref[...], wz1_ref[...], di1_ref[...]
    )
    e21_ref[...] = e21
    send_level2(msg_ref, (r2,))


def finish_kernel(
    core, ylow, yhigh, rhs_ref, s_ref, di_ref, wx_ref, wy_ref, wz_ref, u_ref, r_ref,
    out_ref, left_ref, pre_ref, v_ref,
):
    blank_ends(pre_ref)
    pre_ref[1 : PX - 1, 0:8, :] = ylow[...]
    pre_ref[1 : PX - 1, 8:24, :] = core[...]
    pre_ref[1 : PX - 1, 24:32, :] = yhigh[...]

    def post(i, carry):
        at = 7 + 2 * i
        rows = pl.ds(at, 2)
        v, av = operate_rows(pre_ref, s_ref, wx_ref, wy_ref, wz_ref, at, 2)
        v_ref[rows] = u_ref[rows] + v + di_ref[rows] * (r_ref[rows] - av)
        return carry

    lax.fori_loop(0, BX // 2 + 2, post, 0)

    def remain(i, carry):
        at = 9 + 2 * i
        rows = pl.ds(at, 2)
        v, av = operate_rows(v_ref, s_ref, wx_ref, wy_ref, wz_ref, at, 2)
        left = rhs_ref[rows] - av
        out_ref[pl.ds(2 * i, 2)] = v[:, 8:24]
        left_ref[pl.ds(2 * i, 2)] = left[:, 8:24]
        return carry

    lax.fori_loop(0, BX // 2, remain, 0)


def unpack_level2(field, own, low, high):
    tiles = own.shape[0]
    shape = (tiles, 16, NZ)
    sub, lane = iota(shape, 1), iota(shape, 2)
    halves = []
    for half in range(2):
        at = 2 * field + half

        def spread(ref, at=at):
            return jnp.broadcast_to(ref[:, at : at + 1, :], shape)

        v = jnp.where(sub < 4, spread(low), jnp.where(sub < 8, spread(own), spread(high)))
        v = jnp.where((lane % 4 == sub % 4) & (sub < 12), v, 0.0)
        halves.append(pair_sum(pair_sum(v, 1, 2), 2, 2))
    return jnp.stack(halves, axis=1).reshape((2 * tiles, 16, NZ))


def pack_level3(v):
    sub, lane = iota((16, NZ), 0), iota((16, NZ), 1)
    rows = []
    for j in range(v.shape[0] // 4):
        total = jnp.zeros((16, NZ), F32)
        for q in range(4):
            chosen = ((sub == 4) & (lane % 8 == 2 * q)) | ((sub == 6) & (lane % 8 == 2 * q + 1))
            total = total + jnp.where(chosen, v[4 * j + q], 0.0)
        rows.append(jnp.sum(total, axis=0, keepdims=True))
    return rows


def send_level3(msg_ref, fields):
    rows = [row for v in fields for row in pack_level3(v)]
    rows.append(jnp.zeros((msg_ref.shape[1] - len(rows), NZ), F32))
    whole = jnp.concatenate(rows, axis=0)
    for peer in range(msg_ref.shape[0]):
        msg_ref[peer] = whole


def descend_third(r2, s2, wx2, wy2, wz2, di2):
    first = r2 * di2
    second = first + di2 * (r2 - operate(first, s2, wx2, wy2, wz2, 1, 4))
    return second, restrict(r2 - operate(second, s2, wx2, wy2, wz2, 1, 4), 1, 4)


def third_kernel(
    own, low, high, r2_ref, s2_ref, di2_ref, wx2_ref, wy2_ref, wz2_ref, e22_ref, msg_ref
):
    r2, s2, wx2, wy2, wz2 = (unpack_level2(f, own, low, high) for f in range(5))
    di2 = relax_factor(s2, wx2, wy2, wz2, 1, 4)
    r2_ref[...], s2_ref[...], di2_ref[...] = r2, s2, di2
    wx2_ref[...], wy2_ref[...], wz2_ref[...] = wx2, wy2, wz2
    e22, r3 = descend_third(r2, s2, wx2, wy2, wz2, di2)
    e22_ref[...] = e22
    send_level3(msg_ref, (r3,) + coarsen(s2, wx2, wy2, wz2, 1, 4))


def third_again_kernel(
    own, low, high, s2_ref, di2_ref, wx2_ref, wy2_ref, wz2_ref, r2_ref, e22_ref, msg_ref
):
    r2 = unpack_level2(0, own, low, high)
    r2_ref[...] = r2
    e22, r3 = descend_third(
        r2, s2_ref[...], wx2_ref[...], wy2_ref[...], wz2_ref[...], di2_ref[...]
    )
    e22_ref[...] = e22
    send_level3(msg_ref, (r3,))


def third_x_low(v):
    inner = iota(v.shape, 2) % 8 >= 2
    return jnp.where(inner, turn(v, 2, 2), turn(x_low(v), -6, 2))


def third_x_high(v):
    inner = iota(v.shape, 2) % 8 < 6
    return jnp.where(inner, turn(v, -2, 2), turn(x_high(v), 6, 2))


def third_y_low(v):
    return jnp.where(iota(v.shape, 2) % 2 == 1, turn(v, 1, 2), turn(turn(v, 1, 1), -1, 2))


def third_y_high(v):
    return jnp.where(iota(v.shape, 2) % 2 == 0, turn(v, -1, 2), turn(turn(v, -1, 1), 1, 2))


def solve_third(r3, s3, wx3, wy3, wz3):
    inner = s3 + wx3 + third_x_high(wx3) + wz3 + turn(wz3, -8, 2)
    di = OMEGA / (inner + wy3 + third_y_high(wy3))
    above = jnp.sum(r3, axis=1, keepdims=True)
    below = jnp.sum(inner, axis=1, keepdims=True)
    line = pair_sum(jnp.broadcast_to(above, r3.shape), 1, 2)
    line = line / pair_sum(jnp.broadcast_to(below, r3.shape), 1, 2)
    v = line
    for _ in range(COARSE_SWEEPS):
        fx = wx3 * (v - third_x_low(v))
        fy = wy3 * (v - third_y_low(v))
        fz = wz3 * (v - turn(v, 8, 2))
        flux = (fx - third_x_high(fx)) + (fy - third_y_high(fy)) + (fz - turn(fz, -8, 2))
        v = v + di * (r3 - (s3 * v + flux))
    return v


def spread_third(v):
    group = lax.axis_index("group")
    dev = iota(v.shape, 1)
    near = [
        jnp.sum(jnp.where(dev == group + off, v, 0.0), axis=1, keepdims=True) for off in (-1, 0, 1)
    ]
    shape = (v.shape[0], 16, NZ)
    sub, lane = iota(shape, 1), iota(shape, 2)
    low, own, high = (jnp.broadcast_to(part, shape) for part in near)
    rows = jnp.where(sub < 4, low, jnp.where(sub < 8, own, high))
    parts = []
    for q in range(4):
        chosen = (lane % 8 == 2 * q + (sub % 4) // 2) & (sub < 12)
        parts.append(jnp.where(chosen, rows, 0.0))
    wide = jnp.stack(parts, axis=1).reshape((4 * v.shape[0], 16, NZ))
    return pair_sum(pair_sum(pair_sum(wide, 1, 2), 2, 2), 4, 2)


def near_tiles(v):
    tile = lax.axis_index("tile")
    parts = []
    for off in (-1, 0, 1):
        total = jnp.zeros((2,) + v.shape[1:], F32)
        for t in range(v.shape[0] // 2):
            total = total + jnp.where(tile + off == t, v[2 * t : 2 * t + 2], 0.0)
        parts.append(total)
    return jnp.concatenate(parts, axis=0)


def widen_y(v):
    shape = (v.shape[0], 8, NZ)
    sub = iota(shape, 1)
    parts = []
    for at in (2, 4, 6, 8):
        first = jnp.broadcast_to(v[:, at : at + 1], shape)
        second = jnp.broadcast_to(v[:, at + 1 : at + 2], shape)
        parts.append(jnp.where(sub < 4, first, second))
    return jnp.concatenate(parts, axis=1)


def climb_kernel(
    r3_ref, bands3_ref, r2_ref, s2_ref, di2_ref, wx2_ref, wy2_ref, wz2_ref, e22_ref,
    r1_ref, s1_ref, di1_ref, wx1_ref, wy1_ref, wz1_ref, e21_ref, e2_ref, pre_ref,
    *, groups, thirds, r3_rows, band_rows,
):
    def field(ref, f, rows):
        parts = [ref[pl.ds(thirds * f + j, groups, stride=rows), :] for j in range(thirds)]
        return jnp.stack(parts, axis=0)

    r3 = field(r3_ref, 0, r3_rows)
    s3, wx3, wy3, wz3 = (field(bands3_ref, f, band_rows) for f in range(1, 5))
    corr3 = solve_third(r3, s3, wx3, wy3, wz3)
    v = e22_ref[...] + x_repeat(spread_third(corr3))
    v = v + di2_ref[...] * (
        r2_ref[...]
        - operate(v, s2_ref[...], wx2_ref[...], wy2_ref[...], wz2_ref[...], 1, 4)
    )
    corr2 = widen_y(near_tiles(v))
    v = e21_ref[...] + x_repeat(corr2)
    v = v + di1_ref[...] * (
        r1_ref[...]
        - operate(v, s1_ref[...], wx1_ref[...], wy1_ref[...], wz1_ref[...], 2, 2)
    )
    own = x_repeat(v[4:8])
    pre_ref[...] = e2_ref[9:17, 8:24, :] + own[:, 8:24, :]


def call(body, outs, operands, scratch=(), smem=()):
    vmem = pl.BlockSpec(memory_space=pltpu.VMEM)
    return pl.pallas_call(
        body,
        out_shape=[jax.ShapeDtypeStruct(shape, F32) for shape in outs],
        in_specs=[
            pl.BlockSpec(memory_space=pltpu.SMEM) if i in smem else vmem
            for i in range(len(operands))
        ],
        out_specs=[vmem] * len(outs),
        scratch_shapes=[pltpu.VMEM(shape, F32) for shape in scratch],
        compiler_params=pltpu.CompilerParams(vmem_limit_bytes=48 * 1024 * 1024),
    )(*operands)


def beside(to_low, to_high, axis):
    ends = lax.axis_size(axis) - 1
    from_low = lax.ppermute(to_high, axis, [(i, i + 1) for i in range(ends)])
    from_high = lax.ppermute(to_low, axis, [(i + 1, i) for i in range(ends)])
    return from_low, from_high


def surround(cells, dim):
    low, high = beside(cells, cells, "tile")
    core = jnp.concatenate([low, cells, high], axis=dim)
    ydim = dim + 1
    first = lax.slice_in_dim(core, 0, 8, axis=ydim)
    last = lax.slice_in_dim(core, BY - 8, BY, axis=ydim)
    ylow, yhigh = beside(first, last, "group")
    return core, ylow, yhigh


def everyone(blocks, axis):
    return lax.all_to_all(blocks, axis, 0, 0, tiled=True)


def shards(pressure_head, old_head, soil_type, conduct_sat, alpha_param, shape_param, water_span):
    tiles, groups = lax.axis_size("tile"), lax.axis_size("group")
    thirds = tiles // 4
    top, one, two = (PX, WY, NZ), (L1X, WY, NZ), (2 * tiles, 16, NZ)
    band_rows, r3_rows = -(-5 * thirds // 8) * 8, -(-thirds // 8) * 8

    raw = jnp.stack([pressure_head, old_head, soil_type.astype(F32)])
    core, ylow, yhigh = surround(raw, 1)
    rhs, s0, di0, wx0, wy0, wz0, e2, r1, s1, di1, wx1, wy1, wz1, e21, msg = call(
        assemble_kernel,
        [top] * 7 + [one] * 7 + [(tiles, 16, NZ)],
        [core, ylow, yhigh, conduct_sat, alpha_param, shape_param, water_span],
        [top] * 4,
        smem=(3, 4, 5, 6),
    )
    bands0 = [s0, di0, wx0, wy0, wz0]
    bands1 = [s1, di1, wx1, wy1, wz1]

    own = everyone(msg, "tile")
    low, high = beside(own, own, "group")
    r2, s2, di2, wx2, wy2, wz2, e22, msg = call(
        third_kernel, [two] * 7 + [(groups, band_rows, NZ)], [own, low, high]
    )
    bands2 = [s2, di2, wx2, wy2, wz2]
    bands3 = everyone(msg, "group").reshape(groups * band_rows, NZ)
    climb = functools.partial(climb_kernel, groups=groups, thirds=thirds, band_rows=band_rows)
    (pre,) = call(
        functools.partial(climb, r3_rows=band_rows),
        [(BX, BY, NZ)],
        [bands3, bands3, r2, *bands2, e22, r1, *bands1, e21, e2],
    )

    core, ylow, yhigh = surround(pre, 0)
    u, rem, e2, r1, e21, msg = call(
        again_kernel,
        [top] * 3 + [one] * 2 + [(tiles, 8, NZ)],
        [core, ylow, yhigh, rhs, *bands0, *bands1],
        [top] * 2,
    )
    own = everyone(msg, "tile")
    low, high = beside(own, own, "group")
    r2, e22, msg = call(
        third_again_kernel, [two] * 2 + [(groups, r3_rows, NZ)], [own, low, high, *bands2]
    )
    r3 = everyone(msg, "group").reshape(groups * r3_rows, NZ)
    (pre,) = call(
        functools.partial(climb, r3_rows=r3_rows),
        [(BX, BY, NZ)],
        [r3, bands3, r2, *bands2, e22, r1, *bands1, e21, e2],
    )

    core, ylow, yhigh = surround(pre, 0)
    update, remainder = call(
        finish_kernel,
        [(BX, BY, NZ)] * 2,
        [core, ylow, yhigh, rhs, *bands0, u, rem],
        [top] * 2,
    )
    return update, remainder


def solution(mesh):
    spec = P("tile", "group", None)
    return jax.shard_map(
        shards,
        mesh=mesh,
        in_specs=(spec, spec, spec, P(), P(), P(), P()),
        out_specs=(spec, spec),
        check_vma=False,
    )
```

```python
import functools

import jax
import jax.numpy as jnp
from jax import lax
from jax.experimental import pallas as pl
from jax.experimental.pallas import tpu as pltpu
from jax.sharding import PartitionSpec as P

OMEGA = 2.0 / 3.0
STORAGE = 0.01
COARSE_SWEEPS = 4
SOILS = 12

BX, BY, NZ = 8, 16, 128
WX, WY = 24, 32
PX = WX + 2
L1X = WX // 2
F32 = jnp.float32


def iota(shape, dim):
    return lax.broadcasted_iota(jnp.int32, shape, dim)


def turn(v, step, axis):
    size = v.shape[axis]
    return pltpu.roll(v, step % size, axis)


def bit_of(v, step, axis):
    return (iota(v.shape, axis) // step) % 2 == 0


def pair_sum(v, step, axis):
    return v + jnp.where(bit_of(v, step, axis), turn(v, -step, axis), turn(v, step, axis))


def pair_low(v, step, axis):
    return jnp.where(bit_of(v, step, axis), v, turn(v, step, axis))


def x_low(v):
    return jnp.concatenate([v[:1], v[:-1]], axis=0)


def x_high(v):
    return jnp.concatenate([v[1:], jnp.zeros_like(v[:1])], axis=0)


def x_pair(v):
    return jnp.sum(v.reshape((v.shape[0] // 2, 2) + v.shape[1:]), axis=1)


def x_even(v):
    return v.reshape((v.shape[0] // 2, 2) + v.shape[1:])[:, 0]


def x_repeat(v):
    size = v.shape[0]
    wide = jnp.broadcast_to(v[:, None], (size, 2) + v.shape[1:])
    return wide.reshape((2 * size,) + v.shape[1:])


def operate(v, storage, wx, wy, wz, sy, sz):
    fx = wx * (v - x_low(v))
    fy = wy * (v - turn(v, sy, 1))
    fz = wz * (v - turn(v, sz, 2))
    flux = (fx - x_high(fx)) + (fy - turn(fy, -sy, 1)) + (fz - turn(fz, -sz, 2))
    return storage * v + flux


def relax_factor(storage, wx, wy, wz, sy, sz):
    diagonal = storage + wx + x_high(wx) + wy + turn(wy, -sy, 1) + wz + turn(wz, -sz, 2)
    return jnp.where(diagonal > 0.0, OMEGA / diagonal, 0.0)


def restrict(v, sy, sz):
    return pair_sum(pair_sum(x_pair(v), sy, 1), sz, 2)


def coarsen(storage, wx, wy, wz, sy, sz):
    return (
        restrict(storage, sy, sz),
        pair_sum(pair_sum(x_even(wx), sy, 1), sz, 2),
        pair_low(pair_sum(x_pair(wy), sz, 2), sy, 1),
        pair_low(pair_sum(x_pair(wz), sy, 1), sz, 2),
    )


def operate_rows(v_ref, s_ref, wx_ref, wy_ref, wz_ref, at, size):
    v = v_ref[pl.ds(at, size)]
    wx = wx_ref[pl.ds(at, size)]
    fy = wy_ref[pl.ds(at, size)] * (v - turn(v, 1, 1))
    fz = wz_ref[pl.ds(at, size)] * (v - turn(v, 1, 2))
    flux = wx * (v - v_ref[pl.ds(at - 1, size)])
    flux = flux - wx_ref[pl.ds(at + 1, size)] * (v_ref[pl.ds(at + 1, size)] - v)
    flux = flux + (fy - turn(fy, -1, 1)) + (fz - turn(fz, -1, 2))
    return v, s_ref[pl.ds(at, size)] * v + flux


def inside_grid(at, size):
    shape = (size, WY, NZ)
    gx = BX * lax.axis_index("tile") - (WX - BX) // 2 + (at - 1) + iota(shape, 0)
    gy = BY * lax.axis_index("group") - (WY - BY) // 2 + iota(shape, 1)
    return (
        (gx >= 0)
        & (gx < BX * lax.axis_size("tile"))
        & (gy >= 0)
        & (gy < BY * lax.axis_size("group"))
    )


def blank_ends(ref):
    ref[0] = jnp.zeros((WY, NZ), F32)
    ref[PX - 1] = jnp.zeros((WY, NZ), F32)


def blank_level1(ref, size):
    ref[0:size] = jnp.zeros((size, WY, NZ), F32)
    ref[L1X - size :] = jnp.zeros((size, WY, NZ), F32)


def pack_level2(v):
    sub, lane = iota(v.shape, 1), iota(v.shape, 2)
    chosen = (sub >= 8) & (sub < 24) & (sub % 4 == 0) & ((sub - 8) // 4 == lane % 4)
    return jnp.sum(jnp.where(chosen, v, 0.0), axis=1)


def send(msg_ref, rows):
    rows = list(rows)
    parts, height = msg_ref.shape[1:3]
    spare = parts * height - sum(row.shape[0] for row in rows)
    if spare:
        rows.append(jnp.zeros((spare, NZ), F32))
    whole = jnp.concatenate(rows, axis=0)
    for part in range(parts):
        piece = whole[part * height : (part + 1) * height]
        for peer in range(msg_ref.shape[0]):
            msg_ref[peer, part] = piece


def pack_bands3(fields):
    sub, lane = iota((1, WY, NZ), 1), iota((1, WY, NZ), 2)
    total = jnp.zeros((1, WY, NZ), F32)
    for f, v in enumerate(fields):
        chosen = ((sub == 8) & (lane % 8 == 2 * f)) | ((sub == 16) & (lane % 8 == 2 * f + 1))
        total = total + jnp.where(chosen, v, 0.0)
    return jnp.sum(total, axis=1)


def pack_ring1(v):
    sub, lane = iota((2, WY, NZ), 1), iota((2, WY, NZ), 2)
    rows = v[5:7]
    parts = []
    for k in range(4):
        chosen = ((sub == 8 + 4 * k) & (lane % 2 == 0)) | ((sub == 10 + 4 * k) & (lane % 2 == 1))
        parts.append(jnp.sum(jnp.where(chosen, rows, 0.0), axis=1, keepdims=True))
    return jnp.concatenate([part[x] for x in range(2) for part in parts], axis=0)


def pack_edge1(v):
    sub, lane = iota((6, WY, NZ), 1), iota((6, WY, NZ), 2)
    chosen = ((sub == 20) & (lane % 2 == 0)) | ((sub == 10) & (lane % 2 == 1))
    return jnp.sum(jnp.where(chosen, v[3:9], 0.0), axis=1)


def descend_top(r_ref, e1_ref, e2_ref, s_ref, wx_ref, wy_ref, wz_ref, di_ref, r1_ref):
    def second(i, carry):
        at = 1 + 2 * i
        v, av = operate_rows(e1_ref, s_ref, wx_ref, wy_ref, wz_ref, at, 2)
        e2_ref[pl.ds(at, 2)] = v + di_ref[pl.ds(at, 2)] * (r_ref[pl.ds(at, 2)] - av)
        return carry

    lax.fori_loop(1, WX // 2 - 1, second, 0)

    def third(i, carry):
        at = 1 + 2 * i
        _, av = operate_rows(e2_ref, s_ref, wx_ref, wy_ref, wz_ref, at, 2)
        r1_ref[pl.ds(i, 1)] = restrict(r_ref[pl.ds(at, 2)] - av, 1, 1)
        return carry

    lax.fori_loop(2, WX // 2 - 2, third, 0)


def descend_second(r1, s1, wx1, wy1, wz1, di1):
    first = r1 * di1
    second = first + di1 * (r1 - operate(first, s1, wx1, wy1, wz1, 2, 2))
    defect = r1 - operate(second, s1, wx1, wy1, wz1, 2, 2)
    return second, restrict(defect, 2, 2)


def assemble_kernel(
    core, ylow, yhigh, ks_ref, alpha_ref, shape_ref, span_ref,
    r_ref, s_ref, di_ref, wx_ref, wy_ref, wz_ref, e2_ref,
    r1_ref, s1_ref, di1_ref, wx1_ref, wy1_ref, wz1_ref, e21_ref, msg_ref,
    h_ref, k_ref, m_ref, e1_ref,
):
    def window(field, at):
        row = pl.ds(at - 1, 1)
        return jnp.concatenate([ylow[field, row], core[field, row], yhigh[field, row]], axis=1)

    for ref in (h_ref, k_ref, s_ref, wx_ref, wy_ref, wz_ref, di_ref, r_ref, e1_ref, e2_ref):
        blank_ends(ref)

    def soils(i, carry):
        at = 1 + i
        inside = inside_grid(at, 1)
        head = jnp.where(inside, window(0, at), -1.0)
        old = jnp.where(inside, window(1, at), -1.0)
        soil = window(2, at)
        ks = jnp.full(soil.shape, ks_ref[0])
        alpha = jnp.full(soil.shape, alpha_ref[0])
        shape_n = jnp.full(soil.shape, shape_ref[0])
        span = jnp.full(soil.shape, span_ref[0])
        for kind in range(1, SOILS):
            hit = soil == float(kind)
            ks = jnp.where(hit, ks_ref[kind], ks)
            alpha = jnp.where(hit, alpha_ref[kind], alpha)
            shape_n = jnp.where(hit, shape_ref[kind], shape_n)
            span = jnp.where(hit, span_ref[kind], span)
        shape_m = 1.0 - 1.0 / shape_n
        power = jnp.exp(shape_n * jnp.log(alpha * -head))
        old_power = jnp.exp(shape_n * jnp.log(alpha * -old))
        saturation = jnp.exp(-shape_m * jnp.log1p(power))
        old_saturation = jnp.exp(-shape_m * jnp.log1p(old_power))
        portion = 1.0 / (1.0 + power)
        factor = 1.0 - jnp.exp(shape_m * jnp.log(power / (1.0 + power)))
        conductivity = ks * jnp.sqrt(saturation) * factor * factor
        capacity = span * shape_m * shape_n * power / -head * saturation * portion
        row = pl.ds(at, 1)
        h_ref[row] = head
        k_ref[row] = jnp.where(inside, conductivity, 0.0)
        s_ref[row] = capacity + STORAGE
        m_ref[row] = span * (saturation - old_saturation) + STORAGE * (head - old)
        return carry

    lax.fori_loop(0, WX, soils, 0)

    def harmonic(a, b):
        total = a + b
        return jnp.where(total > 0.0, 2.0 * a * b / total, 0.0)

    def faces(i, carry):
        at = 1 + 2 * i
        k = k_ref[pl.ds(at, 2)]
        wx_ref[pl.ds(at, 2)] = harmonic(k, k_ref[pl.ds(at - 1, 2)])
        wy_ref[pl.ds(at, 2)] = harmonic(k, turn(k, 1, 1))
        wz = harmonic(k, turn(k, 1, 2))
        wz_ref[pl.ds(at, 2)] = jnp.where(iota(wz.shape, 2) == 0, 0.0, wz)
        return carry

    lax.fori_loop(0, WX // 2, faces, 0)

    def right_side(i, carry):
        at = 1 + 2 * i
        rows = pl.ds(at, 2)
        h, wx, wy, wz = h_ref[rows], wx_ref[rows], wy_ref[rows], wz_ref[rows]
        wx_up = wx_ref[pl.ds(at + 1, 2)]
        fy = wy * (h - turn(h, 1, 1))
        fz = wz * (h - turn(h, 1, 2) + 1.0)
        flux = wx * (h - h_ref[pl.ds(at - 1, 2)]) - wx_up * (h_ref[pl.ds(at + 1, 2)] - h)
        flux = flux + (fy - turn(fy, -1, 1)) + (fz - turn(fz, -1, 2))
        rhs = jnp.where(inside_grid(at, 2), -(m_ref[rows] + flux), 0.0)
        diagonal = s_ref[rows] + wx + wx_up + wy + turn(wy, -1, 1) + wz + turn(wz, -1, 2)
        di = OMEGA / diagonal
        r_ref[rows] = rhs
        di_ref[rows] = di
        e1_ref[rows] = rhs * di
        return carry

    lax.fori_loop(0, WX // 2, right_side, 0)

    def bands(i, carry):
        rows = pl.ds(1 + 2 * i, 2)
        s1, wx1, wy1, wz1 = coarsen(s_ref[rows], wx_ref[rows], wy_ref[rows], wz_ref[rows], 1, 1)
        row = pl.ds(i, 1)
        s1_ref[row], wx1_ref[row], wy1_ref[row], wz1_ref[row] = s1, wx1, wy1, wz1
        return carry

    lax.fori_loop(1, WX // 2 - 1, bands, 0)
    for ref in (s1_ref, wx1_ref, wy1_ref, wz1_ref):
        blank_level1(ref, 1)
    blank_level1(r1_ref, 2)
    descend_top(r_ref, e1_ref, e2_ref, s_ref, wx_ref, wy_ref, wz_ref, di_ref, r1_ref)

    s1, wx1, wy1, wz1 = s1_ref[...], wx1_ref[...], wy1_ref[...], wz1_ref[...]
    di1 = relax_factor(s1, wx1, wy1, wz1, 2, 2)
    di1_ref[...] = di1
    e21, r2 = descend_second(r1_ref[...], s1, wx1, wy1, wz1, di1)
    e21_ref[...] = e21
    bands2 = coarsen(s1, wx1, wy1, wz1, 2, 2)
    bands3 = coarsen(*(v[2:4] for v in bands2), 4, 4)
    rows = [pack_level2(v[2:4]) for v in (r2,) + bands2]
    send(msg_ref, rows + [pack_bands3(bands3)])


def again_kernel(
    core, ylow, yhigh, rhs_ref, s_ref, di_ref, wx_ref, wy_ref, wz_ref,
    s1_ref, di1_ref, wx1_ref, wy1_ref, wz1_ref,
    u_ref, r_ref, e2_ref, r1_ref, e21_ref, msg_ref, edge_ref, pre_ref, e1_ref,
):
    for ref in (pre_ref, u_ref, r_ref, e1_ref, e2_ref):
        blank_ends(ref)
    pre_ref[1 : PX - 1, 0:8, :] = ylow[...]
    pre_ref[1 : PX - 1, 8:24, :] = core[...]
    pre_ref[1 : PX - 1, 24:32, :] = yhigh[...]

    def post(i, carry):
        at = 1 + 2 * i
        rows = pl.ds(at, 2)
        v, av = operate_rows(pre_ref, s_ref, wx_ref, wy_ref, wz_ref, at, 2)
        u_ref[rows] = v + di_ref[rows] * (rhs_ref[rows] - av)
        return carry

    lax.fori_loop(0, WX // 2, post, 0)

    def remain(i, carry):
        at = 1 + 2 * i
        rows = pl.ds(at, 2)
        _, av = operate_rows(u_ref, s_ref, wx_ref, wy_ref, wz_ref, at, 2)
        left = rhs_ref[rows] - av
        r_ref[rows] = left
        e1_ref[rows] = left * di_ref[rows]
        return carry

    lax.fori_loop(1, WX // 2 - 1, remain, 0)
    descend_top(r_ref, e1_ref, e2_ref, s_ref, wx_ref, wy_ref, wz_ref, di_ref, r1_ref)
    blank_level1(r1_ref, 2)
    e21, r2 = descend_second(
        r1_ref[...], s1_ref[...], wx1_ref[...], wy1_ref[...], wz1_ref[...], di1_ref[...]
    )
    e21_ref[...] = e21
    send(msg_ref, [pack_level2(r2[2:4]), pack_ring1(e21)])
    send(edge_ref, [pack_edge1(e21)])


def unpack_level2(field, own, low, high):
    tiles = lax.axis_size("tile")
    shape = (tiles, 16, NZ)
    sub, lane = iota(shape, 1), iota(shape, 2)
    halves = []
    for half in range(2):

        def spread(ref, half=half):
            return jnp.broadcast_to(ref[0:tiles, field, half : half + 1, :], shape)

        v = jnp.where(sub < 4, spread(low), jnp.where(sub < 8, spread(own), spread(high)))
        v = jnp.where((lane % 4 == sub % 4) & (sub < 12), v, 0.0)
        halves.append(pair_sum(pair_sum(v, 1, 2), 2, 2))
    return jnp.stack(halves, axis=1).reshape((2 * tiles, 16, NZ))


def pack_level3(v):
    sub, lane = iota((16, NZ), 0), iota((16, NZ), 1)
    rows = []
    for j in range(v.shape[0] // 4):
        total = jnp.zeros((16, NZ), F32)
        for q in range(4):
            chosen = ((sub == 4) & (lane % 8 == 2 * q)) | ((sub == 6) & (lane % 8 == 2 * q + 1))
            total = total + jnp.where(chosen, v[4 * j + q], 0.0)
        rows.append(jnp.sum(total, axis=0, keepdims=True))
    return rows


def descend_third(r2, s2, wx2, wy2, wz2, di2):
    first = r2 * di2
    second = first + di2 * (r2 - operate(first, s2, wx2, wy2, wz2, 1, 4))
    return second, restrict(r2 - operate(second, s2, wx2, wy2, wz2, 1, 4), 1, 4)


def third_kernel(
    own, low, high, r2_ref, s2_ref, di2_ref, wx2_ref, wy2_ref, wz2_ref, e22_ref, msg_ref
):
    r2, s2, wx2, wy2, wz2 = (unpack_level2(f, own, low, high) for f in range(5))
    di2 = relax_factor(s2, wx2, wy2, wz2, 1, 4)
    r2_ref[...], s2_ref[...], di2_ref[...] = r2, s2, di2
    wx2_ref[...], wy2_ref[...], wz2_ref[...] = wx2, wy2, wz2
    e22, r3 = descend_third(r2, s2, wx2, wy2, wz2, di2)
    e22_ref[...] = e22
    s3, wx3, _, wz3 = coarsen(s2, wx2, wy2, wz2, 1, 4)
    inner = s3 + wx3 + x_high(wx3) + wz3 + turn(wz3, -8, 2)
    send(msg_ref, pack_level3(r3) + pack_level3(inner))


def third_again_kernel(
    own, low, high, s2_ref, di2_ref, wx2_ref, wy2_ref, wz2_ref, r2_ref, e22_ref, msg_ref
):
    r2 = unpack_level2(0, own, low, high)
    r2_ref[...] = r2
    e22, r3 = descend_third(
        r2, s2_ref[...], wx2_ref[...], wy2_ref[...], wz2_ref[...], di2_ref[...]
    )
    e22_ref[...] = e22
    send(msg_ref, pack_level3(r3))


def third_masks(shape):
    sub, lane = iota(shape, 1), iota(shape, 2)
    return sub // 4, (sub % 4) // 2, lane % 8


def octuple(v):
    return pair_sum(pair_sum(pair_sum(v, 1, 2), 2, 2), 4, 2)


def unpack_bands3(sources):
    shape = (sources[0].shape[0], 24, NZ)
    dev, half, slot = third_masks(shape)
    rows = jnp.broadcast_to(sources[0], shape)
    for d in range(1, 5):
        rows = jnp.where(dev == d, jnp.broadcast_to(sources[d], shape), rows)
    rows = jnp.where(dev < 5, rows, 0.0)
    return [octuple(jnp.where(slot == 2 * f + half, rows, 0.0)) for f in range(4)]


def unpack_r3(v):
    group = lax.axis_index("group")
    at = iota(v.shape, 1)
    shape = (v.shape[0], 24, NZ)
    dev, half, slot = third_masks(shape)
    rows = jnp.zeros(shape, F32)
    for d in range(5):
        near = jnp.sum(jnp.where(at == group + (d - 2), v, 0.0), axis=1, keepdims=True)
        rows = jnp.where(dev == d, jnp.broadcast_to(near, shape), rows)
    parts = [jnp.where(slot == 2 * q + half, rows, 0.0) for q in range(4)]
    return octuple(jnp.stack(parts, axis=1).reshape((4 * v.shape[0], 24, NZ)))


def line_sums(v):
    total = jnp.sum(v, axis=1, keepdims=True)
    lane = iota(total.shape, 2) % 8
    parts = [jnp.where(lane // 2 == q, total, 0.0) for q in range(4)]
    return octuple(jnp.stack(parts, axis=1).reshape((4 * v.shape[0], 1, NZ)))


def solve_third(r3, line, s3, di3, wx3, wy3, wz3):
    v = jnp.broadcast_to(line, r3.shape)
    for _ in range(COARSE_SWEEPS):
        v = v + di3 * (r3 - operate(v, s3, wx3, wy3, wz3, 2, 8))
    return turn(v, -4, 1)[:, 0:16]


def near_tiles(v):
    tile = lax.axis_index("tile")
    parts = []
    for off in (-1, 0, 1):
        total = jnp.zeros((2,) + v.shape[1:], F32)
        for t in range(v.shape[0] // 2):
            total = total + jnp.where(tile + off == t, v[2 * t : 2 * t + 2], 0.0)
        parts.append(total)
    return jnp.concatenate(parts, axis=0)


def widen_y(v):
    shape = (v.shape[0], 8, NZ)
    sub = iota(shape, 1)
    parts = []
    for at in (2, 4, 6, 8):
        first = jnp.broadcast_to(v[:, at : at + 1], shape)
        second = jnp.broadcast_to(v[:, at + 1 : at + 2], shape)
        parts.append(jnp.where(sub < 4, first, second))
    return jnp.concatenate(parts, axis=1)


def climb_to_second(corr3, r2_ref, s2_ref, di2_ref, wx2_ref, wy2_ref, wz2_ref, e22_ref):
    v = e22_ref[...] + x_repeat(corr3)
    v = v + di2_ref[...] * (
        r2_ref[...]
        - operate(v, s2_ref[...], wx2_ref[...], wy2_ref[...], wz2_ref[...], 1, 4)
    )
    return x_repeat(widen_y(near_tiles(v)))


def climb_to_first(v, r1_ref, s1_ref, di1_ref, wx1_ref, wy1_ref, wz1_ref):
    return v + di1_ref[...] * (
        r1_ref[...]
        - operate(v, s1_ref[...], wx1_ref[...], wy1_ref[...], wz1_ref[...], 2, 2)
    )


def strided(ref, first, thirds, groups, rows):
    parts = [ref[pl.ds(first + j, groups, stride=rows), :] for j in range(thirds)]
    return jnp.stack(parts, axis=0)


def climb_kernel(
    far_low, low, own, high, far_high, third_ref,
    r2_ref, s2_ref, di2_ref, wx2_ref, wy2_ref, wz2_ref, e22_ref,
    r1_ref, s1_ref, di1_ref, wx1_ref, wy1_ref, wz1_ref, e21_ref, e2_ref,
    pre_ref, below_ref, s3_ref, di3_ref, wx3_ref, wy3_ref, wz3_ref,
    *, groups, thirds, rows,
):
    sources = [far_low[:, 0:1, :]]
    sources += [ref[:, 5, 0:1, :] for ref in (low, own, high)]
    sources += [far_high[:, 0:1, :]]
    s3, wx3, wy3, wz3 = unpack_bands3(sources)
    di3 = relax_factor(s3, wx3, wy3, wz3, 2, 8)
    s3_ref[...], di3_ref[...], wx3_ref[...], wy3_ref[...], wz3_ref[...] = s3, di3, wx3, wy3, wz3
    r3 = strided(third_ref, 0, thirds, groups, rows)
    below = line_sums(strided(third_ref, thirds, thirds, groups, rows))
    below_ref[...] = below
    corr3 = solve_third(unpack_r3(r3), line_sums(r3) / below, s3, di3, wx3, wy3, wz3)
    corr2 = climb_to_second(corr3, r2_ref, s2_ref, di2_ref, wx2_ref, wy2_ref, wz2_ref, e22_ref)
    v = climb_to_first(
        e21_ref[...] + corr2, r1_ref, s1_ref, di1_ref, wx1_ref, wy1_ref, wz1_ref
    )
    own1 = x_repeat(v[4:8])
    pre_ref[...] = e2_ref[9:17, 8:24, :] + own1[:, 8:24, :]


def tile_rows(ref, off, at):
    tile = lax.axis_index("tile")
    total = jnp.zeros((2, NZ), F32)
    for t in range(lax.axis_size("tile")):
        total = total + jnp.where(tile + off == t, ref[t, at], 0.0)
    return total


def ring_row(own, low, high, off, first):
    pairs = [tile_rows(own, off, first), tile_rows(own, off, first + 1)]
    packed = [tile_rows(low, off, first + 1)[1:2]]
    packed += [pair[k : k + 1] for pair in pairs for k in range(2)]
    packed += [tile_rows(high, off, first)[0:1]]
    return spread_pairs([row[None] for row in packed], 1)


def spread_pairs(packed, height):
    shape = (height, WY, NZ)
    sub, lane = iota(shape, 1), iota(shape, 2)
    rows = jnp.zeros(shape, F32)
    for k, row in enumerate(packed):
        rows = jnp.where(sub // 4 == k + 1, jnp.broadcast_to(row, shape), rows)
    return pair_sum(jnp.where(lane % 2 == (sub // 2) % 2, rows, 0.0), 1, 2)


def last_climb_kernel(
    third_ref, below_ref, s3_ref, di3_ref, wx3_ref, wy3_ref, wz3_ref,
    low, own, high,
    r2_ref, s2_ref, di2_ref, wx2_ref, wy2_ref, wz2_ref, e22_ref,
    r1_ref, s1_ref, di1_ref, wx1_ref, wy1_ref, wz1_ref, e21_ref,
    e2_ref, rhs_ref, s_ref, di_ref, wx_ref, wy_ref, wz_ref, u_ref, r_ref,
    out_ref, left_ref, pre_ref, v_ref,
    *, groups, thirds, rows,
):
    r3 = strided(third_ref, 0, thirds, groups, rows)
    corr3 = solve_third(
        unpack_r3(r3), line_sums(r3) / below_ref[...],
        s3_ref[...], di3_ref[...], wx3_ref[...], wy3_ref[...], wz3_ref[...],
    )
    corr2 = climb_to_second(corr3, r2_ref, s2_ref, di2_ref, wx2_ref, wy2_ref, wz2_ref, e22_ref)
    tiles = lax.axis_size("tile")
    middle = e21_ref[3:9]
    sub = iota(middle.shape, 1)
    edge_low = jnp.concatenate([low[tiles, k] for k in range(3)], axis=0)[:, None]
    edge_high = jnp.concatenate([high[tiles, k] for k in range(3)], axis=0)[:, None]
    nothing = jnp.zeros_like(edge_low)
    edges = spread_pairs([edge_low] + [nothing] * 4 + [edge_high], 6)
    kept = (sub >= 6) & (sub < 26)
    middle = jnp.where(kept, middle, edges)
    blank = jnp.zeros((2, WY, NZ), F32)
    first, last = ring_row(own, low, high, -1, 3), ring_row(own, low, high, 1, 1)
    e21 = jnp.concatenate([blank, first, middle, last, blank], axis=0)
    v = climb_to_first(e21 + corr2, r1_ref, s1_ref, di1_ref, wx1_ref, wy1_ref, wz1_ref)
    pre_ref[7:19] = e2_ref[7:19] + x_repeat(v[3:9])

    def post(i, carry):
        at = 8 + 2 * i
        here = pl.ds(at, 2)
        v, av = operate_rows(pre_ref, s_ref, wx_ref, wy_ref, wz_ref, at, 2)
        v_ref[here] = u_ref[here] + v + di_ref[here] * (r_ref[here] - av)
        return carry

    lax.fori_loop(0, BX // 2 + 1, post, 0)

    def remain(i, carry):
        at = 9 + 2 * i
        v, av = operate_rows(v_ref, s_ref, wx_ref, wy_ref, wz_ref, at, 2)
        left = rhs_ref[pl.ds(at, 2)] - av
        out_ref[pl.ds(2 * i, 2)] = v[:, 8:24]
        left_ref[pl.ds(2 * i, 2)] = left[:, 8:24]
        return carry

    lax.fori_loop(0, BX // 2, remain, 0)


def call(body, outs, operands, scratch=(), smem=()):
    vmem = pl.BlockSpec(memory_space=pltpu.VMEM)
    return pl.pallas_call(
        body,
        out_shape=[jax.ShapeDtypeStruct(shape, F32) for shape in outs],
        in_specs=[
            pl.BlockSpec(memory_space=pltpu.SMEM) if i in smem else vmem
            for i in range(len(operands))
        ],
        out_specs=[vmem] * len(outs),
        scratch_shapes=[pltpu.VMEM(shape, F32) for shape in scratch],
        compiler_params=pltpu.CompilerParams(vmem_limit_bytes=48 * 1024 * 1024),
    )(*operands)


def beside(to_low, to_high, axis, step=1):
    ends = lax.axis_size(axis) - step
    from_low = lax.ppermute(to_high, axis, [(i, i + step) for i in range(ends)])
    from_high = lax.ppermute(to_low, axis, [(i + step, i) for i in range(ends)])
    return from_low, from_high


def surround(cells, dim):
    low, high = beside(cells, cells, "tile")
    core = jnp.concatenate([low, cells, high], axis=dim)
    ydim = dim + 1
    first = lax.slice_in_dim(core, 0, 8, axis=ydim)
    last = lax.slice_in_dim(core, BY - 8, BY, axis=ydim)
    ylow, yhigh = beside(first, last, "group")
    return core, ylow, yhigh


def everyone(blocks, axis):
    return lax.all_to_all(blocks, axis, 0, 0, tiled=True)


def shards(pressure_head, old_head, soil_type, conduct_sat, alpha_param, shape_param, water_span):
    tiles, groups = lax.axis_size("tile"), lax.axis_size("group")
    thirds = tiles // 4
    top, one, two = (PX, WY, NZ), (L1X, WY, NZ), (2 * tiles, 16, NZ)
    three, line = (tiles, 24, NZ), (tiles, 1, NZ)
    rows_once, rows_again = 2 * thirds, -(-thirds // 2) * 2

    raw = jnp.stack([pressure_head, old_head, soil_type.astype(F32)])
    core, ylow, yhigh = surround(raw, 1)
    rhs, s0, di0, wx0, wy0, wz0, e2, r1, s1, di1, wx1, wy1, wz1, e21, msg = call(
        assemble_kernel,
        [top] * 7 + [one] * 7 + [(tiles, 6, 2, NZ)],
        [core, ylow, yhigh, conduct_sat, alpha_param, shape_param, water_span],
        [top] * 4,
        smem=(3, 4, 5, 6),
    )
    bands0 = [s0, di0, wx0, wy0, wz0]
    bands1 = [s1, di1, wx1, wy1, wz1]

    own = everyone(msg, "tile")
    low, high = beside(own, own, "group")
    far_low, far_high = beside(own[:, 5], own[:, 5], "group", 2)
    r2, s2, di2, wx2, wy2, wz2, e22, msg = call(
        third_kernel, [two] * 7 + [(groups, thirds, 2, NZ)], [own, low, high]
    )
    bands2 = [s2, di2, wx2, wy2, wz2]
    third = everyone(msg, "group").reshape(groups * rows_once, NZ)
    pre, below, *bands3 = call(
        functools.partial(climb_kernel, groups=groups, thirds=thirds, rows=rows_once),
        [(BX, BY, NZ), line] + [three] * 5,
        [far_low, low, own, high, far_high, third, r2, *bands2, e22, r1, *bands1, e21, e2],
    )

    core, ylow, yhigh = surround(pre, 0)
    u, rem, e2, r1, e21, msg, edge = call(
        again_kernel,
        [top] * 3 + [one] * 2 + [(tiles, 5, 2, NZ), (1, 5, 2, NZ)],
        [core, ylow, yhigh, rhs, *bands0, *bands1],
        [top] * 2,
    )
    own = jnp.concatenate([everyone(msg, "tile"), edge], axis=0)
    low, high = beside(own, own, "group")
    r2, e22, msg = call(
        third_again_kernel,
        [two] * 2 + [(groups, rows_again // 2, 2, NZ)],
        [own, low, high, *bands2],
    )
    third = everyone(msg, "group").reshape(groups * rows_again, NZ)
    update, remainder = call(
        functools.partial(last_climb_kernel, groups=groups, thirds=thirds, rows=rows_again),
        [(BX, BY, NZ)] * 2,
        [third, below, *bands3, low, own, high, r2, *bands2, e22, r1, *bands1, e21]
        + [e2, rhs, *bands0, u, rem],
        [top] * 2,
    )
    return update, remainder


def solution(mesh):
    spec = P("tile", "group", None)
    return jax.shard_map(
        shards,
        mesh=mesh,
        in_specs=(spec, spec, spec, P(), P(), P(), P()),
        out_specs=(spec, spec),
        check_vma=False,
    )
```

```python
import functools

import jax
import jax.numpy as jnp
from jax import lax
from jax.experimental import pallas as pl
from jax.experimental.pallas import tpu as pltpu
from jax.sharding import PartitionSpec as P

OMEGA = 2.0 / 3.0
STORAGE = 0.01
COARSE_SWEEPS = 4
SOILS = 12

BX, BY, NZ = 8, 16, 128
WX, WY = 24, 32
PX = WX + 2
L1X = WX // 2
F32 = jnp.float32


def iota(shape, dim):
    return lax.broadcasted_iota(jnp.int32, shape, dim)


def turn(v, step, axis):
    size = v.shape[axis]
    return pltpu.roll(v, step % size, axis)


def bit_of(v, step, axis):
    return (iota(v.shape, axis) // step) % 2 == 0


def pair_sum(v, step, axis):
    return v + jnp.where(bit_of(v, step, axis), turn(v, -step, axis), turn(v, step, axis))


def pair_low(v, step, axis):
    return jnp.where(bit_of(v, step, axis), v, turn(v, step, axis))


def x_low(v):
    return jnp.concatenate([v[:1], v[:-1]], axis=0)


def x_high(v):
    return jnp.concatenate([v[1:], jnp.zeros_like(v[:1])], axis=0)


def x_pair(v):
    return jnp.sum(v.reshape((v.shape[0] // 2, 2) + v.shape[1:]), axis=1)


def x_even(v):
    return v.reshape((v.shape[0] // 2, 2) + v.shape[1:])[:, 0]


def x_repeat(v):
    size = v.shape[0]
    wide = jnp.broadcast_to(v[:, None], (size, 2) + v.shape[1:])
    return wide.reshape((2 * size,) + v.shape[1:])


def operate(v, storage, wx, wy, wz, sy, sz):
    fx = wx * (v - x_low(v))
    fy = wy * (v - turn(v, sy, 1))
    fz = wz * (v - turn(v, sz, 2))
    flux = (fx - x_high(fx)) + (fy - turn(fy, -sy, 1)) + (fz - turn(fz, -sz, 2))
    return storage * v + flux


def relax_factor(storage, wx, wy, wz, sy, sz):
    diagonal = storage + wx + x_high(wx) + wy + turn(wy, -sy, 1) + wz + turn(wz, -sz, 2)
    return jnp.where(diagonal > 0.0, OMEGA / diagonal, 0.0)


def restrict(v, sy, sz):
    return pair_sum(pair_sum(x_pair(v), sy, 1), sz, 2)


def coarsen(storage, wx, wy, wz, sy, sz):
    return (
        restrict(storage, sy, sz),
        pair_sum(pair_sum(x_even(wx), sy, 1), sz, 2),
        pair_low(pair_sum(x_pair(wy), sz, 2), sy, 1),
        pair_low(pair_sum(x_pair(wz), sy, 1), sz, 2),
    )


def operate_rows(v_ref, s_ref, wx_ref, wy_ref, wz_ref, at, size):
    v = v_ref[pl.ds(at, size)]
    wx = wx_ref[pl.ds(at, size)]
    fy = wy_ref[pl.ds(at, size)] * (v - turn(v, 1, 1))
    fz = wz_ref[pl.ds(at, size)] * (v - turn(v, 1, 2))
    flux = wx * (v - v_ref[pl.ds(at - 1, size)])
    flux = flux - wx_ref[pl.ds(at + 1, size)] * (v_ref[pl.ds(at + 1, size)] - v)
    flux = flux + (fy - turn(fy, -1, 1)) + (fz - turn(fz, -1, 2))
    return v, s_ref[pl.ds(at, size)] * v + flux


def blank_ends(ref):
    ref[0] = jnp.zeros((WY, NZ), F32)
    ref[PX - 1] = jnp.zeros((WY, NZ), F32)


def blank_level1(ref, size):
    ref[0:size] = jnp.zeros((size, WY, NZ), F32)
    ref[L1X - size :] = jnp.zeros((size, WY, NZ), F32)


def pack_level2(v):
    sub, lane = iota(v.shape, 1), iota(v.shape, 2)
    chosen = (sub >= 8) & (sub < 24) & (sub % 4 == 0) & ((sub - 8) // 4 == lane % 4)
    return jnp.sum(jnp.where(chosen, v, 0.0), axis=1)


def send(msg_ref, rows):
    rows = list(rows)
    parts, height = msg_ref.shape[1:3]
    spare = parts * height - sum(row.shape[0] for row in rows)
    if spare:
        rows.append(jnp.zeros((spare, NZ), F32))
    whole = jnp.concatenate(rows, axis=0)
    for part in range(parts):
        piece = whole[part * height : (part + 1) * height]
        for peer in range(msg_ref.shape[0]):
            msg_ref[peer, part] = piece


def pack_bands3(fields):
    sub, lane = iota((1, WY, NZ), 1), iota((1, WY, NZ), 2)
    total = jnp.zeros((1, WY, NZ), F32)
    for f, v in enumerate(fields):
        chosen = ((sub == 8) & (lane % 8 == 2 * f)) | ((sub == 16) & (lane % 8 == 2 * f + 1))
        total = total + jnp.where(chosen, v, 0.0)
    return jnp.sum(total, axis=1)


def pack_ring1(v):
    sub, lane = iota((2, WY, NZ), 1), iota((2, WY, NZ), 2)
    rows = v[5:7]
    parts = []
    for k in range(4):
        chosen = ((sub == 8 + 4 * k) & (lane % 2 == 0)) | ((sub == 10 + 4 * k) & (lane % 2 == 1))
        parts.append(jnp.sum(jnp.where(chosen, rows, 0.0), axis=1, keepdims=True))
    return jnp.concatenate([part[x] for x in range(2) for part in parts], axis=0)


def pack_edge1(v):
    sub, lane = iota((6, WY, NZ), 1), iota((6, WY, NZ), 2)
    chosen = ((sub == 20) & (lane % 2 == 0)) | ((sub == 10) & (lane % 2 == 1))
    return jnp.sum(jnp.where(chosen, v[3:9], 0.0), axis=1)


def descend_top(r_ref, e1_ref, e2_ref, s_ref, wx_ref, wy_ref, wz_ref, di_ref, r1_ref):
    def second(i, carry):
        at = 1 + 2 * i
        v, av = operate_rows(e1_ref, s_ref, wx_ref, wy_ref, wz_ref, at, 2)
        e2_ref[pl.ds(at, 2)] = v + di_ref[pl.ds(at, 2)] * (r_ref[pl.ds(at, 2)] - av)
        return carry

    lax.fori_loop(1, WX // 2 - 1, second, 0, unroll=2)

    def third(i, carry):
        at = 1 + 2 * i
        _, av = operate_rows(e2_ref, s_ref, wx_ref, wy_ref, wz_ref, at, 2)
        r1_ref[pl.ds(i, 1)] = restrict(r_ref[pl.ds(at, 2)] - av, 1, 1)
        return carry

    lax.fori_loop(2, WX // 2 - 2, third, 0, unroll=2)


def descend_second(r1, s1, wx1, wy1, wz1, di1):
    first = r1 * di1
    second = first + di1 * (r1 - operate(first, s1, wx1, wy1, wz1, 2, 2))
    defect = r1 - operate(second, s1, wx1, wy1, wz1, 2, 2)
    return second, restrict(defect, 2, 2)


def soil_kernel(head_ref, old_ref, soil_ref, ks_ref, alpha_ref, shape_ref, span_ref, out_ref):
    def cells(i, carry):
        row = pl.ds(i, 1)
        head, old, soil = head_ref[row], old_ref[row], soil_ref[row]
        ks = jnp.full(soil.shape, ks_ref[0])
        alpha = jnp.full(soil.shape, alpha_ref[0])
        shape_n = jnp.full(soil.shape, shape_ref[0])
        span = jnp.full(soil.shape, span_ref[0])
        for kind in range(1, SOILS):
            hit = soil == kind
            ks = jnp.where(hit, ks_ref[kind], ks)
            alpha = jnp.where(hit, alpha_ref[kind], alpha)
            shape_n = jnp.where(hit, shape_ref[kind], shape_n)
            span = jnp.where(hit, span_ref[kind], span)
        shape_m = 1.0 - 1.0 / shape_n
        power = jnp.exp(shape_n * jnp.log(alpha * -head))
        old_power = jnp.exp(shape_n * jnp.log(alpha * -old))
        saturation = jnp.exp(-shape_m * jnp.log1p(power))
        old_saturation = jnp.exp(-shape_m * jnp.log1p(old_power))
        portion = 1.0 / (1.0 + power)
        factor = 1.0 - jnp.exp(shape_m * jnp.log(power / (1.0 + power)))
        capacity = span * shape_m * shape_n * power / -head * saturation * portion
        out_ref[0, row] = head
        out_ref[1, row] = ks * jnp.sqrt(saturation) * factor * factor
        out_ref[2, row] = capacity + STORAGE
        out_ref[3, row] = span * (saturation - old_saturation) + STORAGE * (head - old)
        return carry

    lax.fori_loop(0, BX, cells, 0, unroll=2)


def fill_window(ref, core, ylow, yhigh):
    ref[1 : PX - 1, 0:8, :] = ylow
    ref[1 : PX - 1, 8:24, :] = core
    ref[1 : PX - 1, 24:32, :] = yhigh


def assemble_kernel(
    core, ylow, yhigh,
    r_ref, s_ref, di_ref, wx_ref, wy_ref, wz_ref, e2_ref,
    r1_ref, s1_ref, di1_ref, wx1_ref, wy1_ref, wz1_ref, e21_ref, msg_ref,
    h_ref, k_ref, m_ref, e1_ref,
):
    for ref in (h_ref, k_ref, s_ref, wx_ref, wy_ref, wz_ref, di_ref, r_ref, e1_ref, e2_ref):
        blank_ends(ref)
    for f, ref in enumerate((h_ref, k_ref, s_ref, m_ref)):
        fill_window(ref, core[f], ylow[f], yhigh[f])

    def harmonic(a, b):
        total = a + b
        return jnp.where(total > 0.0, 2.0 * a * b / total, 0.0)

    def faces(i, carry):
        at = 1 + 2 * i
        k = k_ref[pl.ds(at, 2)]
        wx_ref[pl.ds(at, 2)] = harmonic(k, k_ref[pl.ds(at - 1, 2)])
        wy_ref[pl.ds(at, 2)] = harmonic(k, turn(k, 1, 1))
        wz = harmonic(k, turn(k, 1, 2))
        wz_ref[pl.ds(at, 2)] = jnp.where(iota(wz.shape, 2) == 0, 0.0, wz)
        return carry

    lax.fori_loop(0, WX // 2, faces, 0, unroll=2)

    def right_side(i, carry):
        at = 1 + 2 * i
        rows = pl.ds(at, 2)
        h, wx, wy, wz = h_ref[rows], wx_ref[rows], wy_ref[rows], wz_ref[rows]
        wx_up = wx_ref[pl.ds(at + 1, 2)]
        fy = wy * (h - turn(h, 1, 1))
        fz = wz * (h - turn(h, 1, 2) + 1.0)
        flux = wx * (h - h_ref[pl.ds(at - 1, 2)]) - wx_up * (h_ref[pl.ds(at + 1, 2)] - h)
        flux = flux + (fy - turn(fy, -1, 1)) + (fz - turn(fz, -1, 2))
        rhs = -(m_ref[rows] + flux)
        diagonal = s_ref[rows] + wx + wx_up + wy + turn(wy, -1, 1) + wz + turn(wz, -1, 2)
        di = jnp.where(diagonal > 0.0, OMEGA / diagonal, 0.0)
        r_ref[rows] = rhs
        di_ref[rows] = di
        e1_ref[rows] = rhs * di
        return carry

    lax.fori_loop(0, WX // 2, right_side, 0, unroll=2)

    def bands(i, carry):
        rows = pl.ds(1 + 2 * i, 2)
        s1, wx1, wy1, wz1 = coarsen(s_ref[rows], wx_ref[rows], wy_ref[rows], wz_ref[rows], 1, 1)
        row = pl.ds(i, 1)
        s1_ref[row], wx1_ref[row], wy1_ref[row], wz1_ref[row] = s1, wx1, wy1, wz1
        return carry

    lax.fori_loop(1, WX // 2 - 1, bands, 0, unroll=2)
    for ref in (s1_ref, wx1_ref, wy1_ref, wz1_ref):
        blank_level1(ref, 1)
    blank_level1(r1_ref, 2)
    descend_top(r_ref, e1_ref, e2_ref, s_ref, wx_ref, wy_ref, wz_ref, di_ref, r1_ref)

    s1, wx1, wy1, wz1 = s1_ref[...], wx1_ref[...], wy1_ref[...], wz1_ref[...]
    di1 = relax_factor(s1, wx1, wy1, wz1, 2, 2)
    di1_ref[...] = di1
    e21, r2 = descend_second(r1_ref[...], s1, wx1, wy1, wz1, di1)
    e21_ref[...] = e21
    bands2 = coarsen(s1, wx1, wy1, wz1, 2, 2)
    bands3 = coarsen(*(v[2:4] for v in bands2), 4, 4)
    rows = [pack_level2(v[2:4]) for v in (r2,) + bands2]
    send(msg_ref, rows + [pack_bands3(bands3)])


def again_kernel(
    core, ylow, yhigh, rhs_ref, s_ref, di_ref, wx_ref, wy_ref, wz_ref,
    s1_ref, di1_ref, wx1_ref, wy1_ref, wz1_ref,
    u_ref, r_ref, e2_ref, r1_ref, e21_ref, msg_ref, edge_ref, pre_ref, e1_ref,
):
    for ref in (pre_ref, u_ref, r_ref, e1_ref, e2_ref):
        blank_ends(ref)
    fill_window(pre_ref, core[...], ylow[...], yhigh[...])

    def post(i, carry):
        at = 1 + 2 * i
        rows = pl.ds(at, 2)
        v, av = operate_rows(pre_ref, s_ref, wx_ref, wy_ref, wz_ref, at, 2)
        u_ref[rows] = v + di_ref[rows] * (rhs_ref[rows] - av)
        return carry

    lax.fori_loop(0, WX // 2, post, 0, unroll=2)

    def remain(i, carry):
        at = 1 + 2 * i
        rows = pl.ds(at, 2)
        _, av = operate_rows(u_ref, s_ref, wx_ref, wy_ref, wz_ref, at, 2)
        left = rhs_ref[rows] - av
        r_ref[rows] = left
        e1_ref[rows] = left * di_ref[rows]
        return carry

    lax.fori_loop(1, WX // 2 - 1, remain, 0, unroll=2)
    descend_top(r_ref, e1_ref, e2_ref, s_ref, wx_ref, wy_ref, wz_ref, di_ref, r1_ref)
    blank_level1(r1_ref, 2)
    e21, r2 = descend_second(
        r1_ref[...], s1_ref[...], wx1_ref[...], wy1_ref[...], wz1_ref[...], di1_ref[...]
    )
    e21_ref[...] = e21
    send(msg_ref, [pack_level2(r2[2:4]), pack_ring1(e21)])
    send(edge_ref, [pack_edge1(e21)])


def unpack_level2(field, own, low, high):
    tiles = lax.axis_size("tile")
    shape = (tiles, 16, NZ)
    sub, lane = iota(shape, 1), iota(shape, 2)
    halves = []
    for half in range(2):

        def spread(ref, half=half):
            return jnp.broadcast_to(ref[0:tiles, field, half : half + 1, :], shape)

        v = jnp.where(sub < 4, spread(low), jnp.where(sub < 8, spread(own), spread(high)))
        v = jnp.where((lane % 4 == sub % 4) & (sub < 12), v, 0.0)
        halves.append(pair_sum(pair_sum(v, 1, 2), 2, 2))
    return jnp.stack(halves, axis=1).reshape((2 * tiles, 16, NZ))


def pack_level3(v):
    sub, lane = iota((16, NZ), 0), iota((16, NZ), 1)
    rows = []
    for j in range(v.shape[0] // 4):
        total = jnp.zeros((16, NZ), F32)
        for q in range(4):
            chosen = ((sub == 4) & (lane % 8 == 2 * q)) | ((sub == 6) & (lane % 8 == 2 * q + 1))
            total = total + jnp.where(chosen, v[4 * j + q], 0.0)
        rows.append(jnp.sum(total, axis=0, keepdims=True))
    return rows


def descend_third(r2, s2, wx2, wy2, wz2, di2):
    first = r2 * di2
    second = first + di2 * (r2 - operate(first, s2, wx2, wy2, wz2, 1, 4))
    return second, restrict(r2 - operate(second, s2, wx2, wy2, wz2, 1, 4), 1, 4)


def third_kernel(
    far_low, low, own, high, far_high,
    r2_ref, s2_ref, di2_ref, wx2_ref, wy2_ref, wz2_ref, e22_ref,
    s3_ref, di3_ref, wx3_ref, wy3_ref, wz3_ref, msg_ref,
):
    sources = [far_low[:, 0:1, :]]
    sources += [ref[:, 5, 0:1, :] for ref in (low, own, high)]
    sources += [far_high[:, 0:1, :]]
    s3, wx3, wy3, wz3 = unpack_bands3(sources)
    s3_ref[...], wx3_ref[...], wy3_ref[...], wz3_ref[...] = s3, wx3, wy3, wz3
    di3_ref[...] = relax_factor(s3, wx3, wy3, wz3, 2, 8)
    r2, s2, wx2, wy2, wz2 = (unpack_level2(f, own, low, high) for f in range(5))
    di2 = relax_factor(s2, wx2, wy2, wz2, 1, 4)
    r2_ref[...], s2_ref[...], di2_ref[...] = r2, s2, di2
    wx2_ref[...], wy2_ref[...], wz2_ref[...] = wx2, wy2, wz2
    e22, r3 = descend_third(r2, s2, wx2, wy2, wz2, di2)
    e22_ref[...] = e22
    s3, wx3, _, wz3 = coarsen(s2, wx2, wy2, wz2, 1, 4)
    inner = s3 + wx3 + x_high(wx3) + wz3 + turn(wz3, -8, 2)
    send(msg_ref, pack_level3(r3) + pack_level3(inner))


def third_again_kernel(
    own, low, high, s2_ref, di2_ref, wx2_ref, wy2_ref, wz2_ref, r2_ref, e22_ref, msg_ref
):
    r2 = unpack_level2(0, own, low, high)
    r2_ref[...] = r2
    e22, r3 = descend_third(
        r2, s2_ref[...], wx2_ref[...], wy2_ref[...], wz2_ref[...], di2_ref[...]
    )
    e22_ref[...] = e22
    send(msg_ref, pack_level3(r3))


def third_masks(shape):
    sub, lane = iota(shape, 1), iota(shape, 2)
    return sub // 4, (sub % 4) // 2, lane % 8


def octuple(v):
    return pair_sum(pair_sum(pair_sum(v, 1, 2), 2, 2), 4, 2)


def unpack_bands3(sources):
    shape = (sources[0].shape[0], 24, NZ)
    dev, half, slot = third_masks(shape)
    rows = jnp.broadcast_to(sources[0], shape)
    for d in range(1, 5):
        rows = jnp.where(dev == d, jnp.broadcast_to(sources[d], shape), rows)
    rows = jnp.where(dev < 5, rows, 0.0)
    return [octuple(jnp.where(slot == 2 * f + half, rows, 0.0)) for f in range(4)]


def unpack_r3(v):
    group = lax.axis_index("group")
    at = iota(v.shape, 1)
    shape = (v.shape[0], 24, NZ)
    dev, half, slot = third_masks(shape)
    rows = jnp.zeros(shape, F32)
    for d in range(5):
        near = jnp.sum(jnp.where(at == group + (d - 2), v, 0.0), axis=1, keepdims=True)
        rows = jnp.where(dev == d, jnp.broadcast_to(near, shape), rows)
    parts = [jnp.where(slot == 2 * q + half, rows, 0.0) for q in range(4)]
    return octuple(jnp.stack(parts, axis=1).reshape((4 * v.shape[0], 24, NZ)))


def line_sums(v):
    total = jnp.sum(v, axis=1, keepdims=True)
    lane = iota(total.shape, 2) % 8
    parts = [jnp.where(lane // 2 == q, total, 0.0) for q in range(4)]
    return octuple(jnp.stack(parts, axis=1).reshape((4 * v.shape[0], 1, NZ)))


def solve_third(r3, line, s3, di3, wx3, wy3, wz3):
    v = jnp.broadcast_to(line, r3.shape)
    for _ in range(COARSE_SWEEPS):
        v = v + di3 * (r3 - operate(v, s3, wx3, wy3, wz3, 2, 8))
    return turn(v, -4, 1)[:, 0:16]


def near_tiles(v):
    tile = lax.axis_index("tile")
    parts = []
    for off in (-1, 0, 1):
        total = jnp.zeros((2,) + v.shape[1:], F32)
        for t in range(v.shape[0] // 2):
            total = total + jnp.where(tile + off == t, v[2 * t : 2 * t + 2], 0.0)
        parts.append(total)
    return jnp.concatenate(parts, axis=0)


def widen_y(v):
    shape = (v.shape[0], 8, NZ)
    sub = iota(shape, 1)
    parts = []
    for at in (2, 4, 6, 8):
        first = jnp.broadcast_to(v[:, at : at + 1], shape)
        second = jnp.broadcast_to(v[:, at + 1 : at + 2], shape)
        parts.append(jnp.where(sub < 4, first, second))
    return jnp.concatenate(parts, axis=1)


def climb_to_second(corr3, r2_ref, s2_ref, di2_ref, wx2_ref, wy2_ref, wz2_ref, e22_ref):
    v = e22_ref[...] + x_repeat(corr3)
    v = v + di2_ref[...] * (
        r2_ref[...]
        - operate(v, s2_ref[...], wx2_ref[...], wy2_ref[...], wz2_ref[...], 1, 4)
    )
    return x_repeat(widen_y(near_tiles(v)))


def climb_to_first(v, r1_ref, s1_ref, di1_ref, wx1_ref, wy1_ref, wz1_ref):
    return v + di1_ref[...] * (
        r1_ref[...]
        - operate(v, s1_ref[...], wx1_ref[...], wy1_ref[...], wz1_ref[...], 2, 2)
    )


def strided(ref, first, thirds, groups, rows):
    parts = [ref[pl.ds(first + j, groups, stride=rows), :] for j in range(thirds)]
    return jnp.stack(parts, axis=0)


def climb_kernel(
    third_ref, s3_ref, di3_ref, wx3_ref, wy3_ref, wz3_ref,
    r2_ref, s2_ref, di2_ref, wx2_ref, wy2_ref, wz2_ref, e22_ref,
    r1_ref, s1_ref, di1_ref, wx1_ref, wy1_ref, wz1_ref, e21_ref, e2_ref,
    pre_ref, below_ref,
    *, groups, thirds, rows,
):
    r3 = strided(third_ref, 0, thirds, groups, rows)
    below = line_sums(strided(third_ref, thirds, thirds, groups, rows))
    below_ref[...] = below
    corr3 = solve_third(
        unpack_r3(r3), line_sums(r3) / below,
        s3_ref[...], di3_ref[...], wx3_ref[...], wy3_ref[...], wz3_ref[...],
    )
    corr2 = climb_to_second(corr3, r2_ref, s2_ref, di2_ref, wx2_ref, wy2_ref, wz2_ref, e22_ref)
    v = climb_to_first(
        e21_ref[...] + corr2, r1_ref, s1_ref, di1_ref, wx1_ref, wy1_ref, wz1_ref
    )
    own1 = x_repeat(v[4:8])
    pre_ref[...] = e2_ref[9:17, 8:24, :] + own1[:, 8:24, :]


def tile_rows(ref, off, at):
    tile = lax.axis_index("tile")
    total = jnp.zeros((2, NZ), F32)
    for t in range(lax.axis_size("tile")):
        total = total + jnp.where(tile + off == t, ref[t, at], 0.0)
    return total


def ring_row(own, low, high, off, first):
    pairs = [tile_rows(own, off, first), tile_rows(own, off, first + 1)]
    packed = [tile_rows(low, off, first + 1)[1:2]]
    packed += [pair[k : k + 1] for pair in pairs for k in range(2)]
    packed += [tile_rows(high, off, first)[0:1]]
    return spread_pairs([row[None] for row in packed], 1)


def spread_pairs(packed, height):
    shape = (height, WY, NZ)
    sub, lane = iota(shape, 1), iota(shape, 2)
    rows = jnp.zeros(shape, F32)
    for k, row in enumerate(packed):
        rows = jnp.where(sub // 4 == k + 1, jnp.broadcast_to(row, shape), rows)
    return pair_sum(jnp.where(lane % 2 == (sub // 2) % 2, rows, 0.0), 1, 2)


def last_climb_kernel(
    third_ref, below_ref, s3_ref, di3_ref, wx3_ref, wy3_ref, wz3_ref,
    low, own, high,
    r2_ref, s2_ref, di2_ref, wx2_ref, wy2_ref, wz2_ref, e22_ref,
    r1_ref, s1_ref, di1_ref, wx1_ref, wy1_ref, wz1_ref, e21_ref,
    e2_ref, rhs_ref, s_ref, di_ref, wx_ref, wy_ref, wz_ref, u_ref, r_ref,
    out_ref, left_ref, pre_ref, v_ref,
    *, groups, thirds, rows,
):
    r3 = strided(third_ref, 0, thirds, groups, rows)
    corr3 = solve_third(
        unpack_r3(r3), line_sums(r3) / below_ref[...],
        s3_ref[...], di3_ref[...], wx3_ref[...], wy3_ref[...], wz3_ref[...],
    )
    corr2 = climb_to_second(corr3, r2_ref, s2_ref, di2_ref, wx2_ref, wy2_ref, wz2_ref, e22_ref)
    tiles = lax.axis_size("tile")
    middle = e21_ref[3:9]
    sub = iota(middle.shape, 1)
    edge_low = jnp.concatenate([low[tiles, k] for k in range(3)], axis=0)[:, None]
    edge_high = jnp.concatenate([high[tiles, k] for k in range(3)], axis=0)[:, None]
    nothing = jnp.zeros_like(edge_low)
    edges = spread_pairs([edge_low] + [nothing] * 4 + [edge_high], 6)
    kept = (sub >= 6) & (sub < 26)
    middle = jnp.where(kept, middle, edges)
    blank = jnp.zeros((2, WY, NZ), F32)
    first, last = ring_row(own, low, high, -1, 3), ring_row(own, low, high, 1, 1)
    e21 = jnp.concatenate([blank, first, middle, last, blank], axis=0)
    v = climb_to_first(e21 + corr2, r1_ref, s1_ref, di1_ref, wx1_ref, wy1_ref, wz1_ref)
    pre_ref[7:19] = e2_ref[7:19] + x_repeat(v[3:9])

    def post(i, carry):
        at = 8 + 2 * i
        here = pl.ds(at, 2)
        v, av = operate_rows(pre_ref, s_ref, wx_ref, wy_ref, wz_ref, at, 2)
        v_ref[here] = u_ref[here] + v + di_ref[here] * (r_ref[here] - av)
        return carry

    lax.fori_loop(0, BX // 2 + 1, post, 0, unroll=True)

    def remain(i, carry):
        at = 9 + 2 * i
        v, av = operate_rows(v_ref, s_ref, wx_ref, wy_ref, wz_ref, at, 2)
        left = rhs_ref[pl.ds(at, 2)] - av
        out_ref[pl.ds(2 * i, 2)] = v[:, 8:24]
        left_ref[pl.ds(2 * i, 2)] = left[:, 8:24]
        return carry

    lax.fori_loop(0, BX // 2, remain, 0, unroll=True)


def call(body, outs, operands, scratch=(), smem=()):
    vmem = pl.BlockSpec(memory_space=pltpu.VMEM)
    return pl.pallas_call(
        body,
        out_shape=[jax.ShapeDtypeStruct(shape, F32) for shape in outs],
        in_specs=[
            pl.BlockSpec(memory_space=pltpu.SMEM) if i in smem else vmem
            for i in range(len(operands))
        ],
        out_specs=[vmem] * len(outs),
        scratch_shapes=[pltpu.VMEM(shape, F32) for shape in scratch],
        compiler_params=pltpu.CompilerParams(vmem_limit_bytes=16 * 1024 * 1024),
    )(*operands)


def beside(to_low, to_high, axis, step=1):
    ends = lax.axis_size(axis) - step
    from_low = lax.ppermute(to_high, axis, [(i, i + step) for i in range(ends)])
    from_high = lax.ppermute(to_low, axis, [(i + step, i) for i in range(ends)])
    return from_low, from_high


def surround(cells, dim):
    low, high = beside(cells, cells, "tile")
    core = jnp.concatenate([low, cells, high], axis=dim)
    ydim = dim + 1
    first = lax.slice_in_dim(core, 0, 8, axis=ydim)
    last = lax.slice_in_dim(core, BY - 8, BY, axis=ydim)
    ylow, yhigh = beside(first, last, "group")
    return core, ylow, yhigh


def everyone(blocks, axis):
    return lax.all_to_all(blocks, axis, 0, 0, tiled=True)


def shards(pressure_head, old_head, soil_type, conduct_sat, alpha_param, shape_param, water_span):
    tiles, groups = lax.axis_size("tile"), lax.axis_size("group")
    thirds = tiles // 4
    top, one, two = (PX, WY, NZ), (L1X, WY, NZ), (2 * tiles, 16, NZ)
    three, line = (tiles, 24, NZ), (tiles, 1, NZ)
    rows_once, rows_again = 2 * thirds, thirds

    (fields,) = call(
        soil_kernel,
        [(4, BX, BY, NZ)],
        [pressure_head, old_head, soil_type, conduct_sat, alpha_param, shape_param, water_span],
        smem=(3, 4, 5, 6),
    )
    core, ylow, yhigh = surround(fields, 1)
    rhs, s0, di0, wx0, wy0, wz0, e2, r1, s1, di1, wx1, wy1, wz1, e21, msg = call(
        assemble_kernel,
        [top] * 7 + [one] * 7 + [(tiles, 6, 2, NZ)],
        [core, ylow, yhigh],
        [top] * 4,
    )
    bands0 = [s0, di0, wx0, wy0, wz0]
    bands1 = [s1, di1, wx1, wy1, wz1]

    own = everyone(msg, "tile")
    low, high = beside(own, own, "group")
    far_low, far_high = beside(own[:, 5], own[:, 5], "group", 2)
    r2, s2, di2, wx2, wy2, wz2, e22, s3, di3, wx3, wy3, wz3, msg = call(
        third_kernel,
        [two] * 7 + [three] * 5 + [(groups, thirds, 2, NZ)],
        [far_low, low, own, high, far_high],
    )
    bands3 = [s3, di3, wx3, wy3, wz3]
    bands2 = [s2, di2, wx2, wy2, wz2]
    third = everyone(msg, "group").reshape(groups * rows_once, NZ)
    pre, below = call(
        functools.partial(climb_kernel, groups=groups, thirds=thirds, rows=rows_once),
        [(BX, BY, NZ), line],
        [third, *bands3, r2, *bands2, e22, r1, *bands1, e21, e2],
    )

    core, ylow, yhigh = surround(pre, 0)
    u, rem, e2, r1, e21, msg, edge = call(
        again_kernel,
        [top] * 3 + [one] * 2 + [(tiles, 5, 2, NZ), (1, 5, 2, NZ)],
        [core, ylow, yhigh, rhs, *bands0, *bands1],
        [top] * 2,
    )
    own = jnp.concatenate([everyone(msg, "tile"), edge], axis=0)
    low, high = beside(own, own, "group")
    r2, e22, msg = call(
        third_again_kernel,
        [two] * 2 + [(groups, rows_again, 1, NZ)],
        [own, low, high, *bands2],
    )
    third = everyone(msg, "group").reshape(groups * rows_again, NZ)
    update, remainder = call(
        functools.partial(last_climb_kernel, groups=groups, thirds=thirds, rows=rows_again),
        [(BX, BY, NZ)] * 2,
        [third, below, *bands3, low, own, high, r2, *bands2, e22, r1, *bands1, e21]
        + [e2, rhs, *bands0, u, rem],
        [top] * 2,
    )
    return update, remainder


def solution(mesh):
    spec = P("tile", "group", None)
    return jax.shard_map(
        shards,
        mesh=mesh,
        in_specs=(spec, spec, spec, P(), P(), P(), P()),
        out_specs=(spec, spec),
        check_vma=False,
    )
```

```python
import functools

import jax
import jax.numpy as jnp
from jax import lax
from jax.experimental import pallas as pl
from jax.experimental.pallas import tpu as pltpu
from jax.sharding import PartitionSpec as P

OMEGA = 2.0 / 3.0
STORAGE = 0.01
COARSE_SWEEPS = 4
SOILS = 12

BX, BY, NZ = 8, 16, 128
WX, WY = 24, 32
PX = WX + 2
L1X = WX // 2
F32 = jnp.float32


def iota(shape, dim):
    return lax.broadcasted_iota(jnp.int32, shape, dim)


def turn(v, step, axis):
    size = v.shape[axis]
    return pltpu.roll(v, step % size, axis)


def bit_of(v, step, axis):
    return (iota(v.shape, axis) // step) % 2 == 0


def pair_sum(v, step, axis):
    return v + jnp.where(bit_of(v, step, axis), turn(v, -step, axis), turn(v, step, axis))


def pair_low(v, step, axis):
    return jnp.where(bit_of(v, step, axis), v, turn(v, step, axis))


def x_low(v):
    return jnp.concatenate([v[:1], v[:-1]], axis=0)


def x_high(v):
    return jnp.concatenate([v[1:], jnp.zeros_like(v[:1])], axis=0)


def x_pair(v):
    return jnp.sum(v.reshape((v.shape[0] // 2, 2) + v.shape[1:]), axis=1)


def x_even(v):
    return v.reshape((v.shape[0] // 2, 2) + v.shape[1:])[:, 0]


def x_repeat(v):
    size = v.shape[0]
    wide = jnp.broadcast_to(v[:, None], (size, 2) + v.shape[1:])
    return wide.reshape((2 * size,) + v.shape[1:])


def operate(v, storage, wx, wy, wz, sy, sz):
    fx = wx * (v - x_low(v))
    fy = wy * (v - turn(v, sy, 1))
    fz = wz * (v - turn(v, sz, 2))
    flux = (fx - x_high(fx)) + (fy - turn(fy, -sy, 1)) + (fz - turn(fz, -sz, 2))
    return storage * v + flux


def relax_factor(storage, wx, wy, wz, sy, sz):
    diagonal = storage + wx + x_high(wx) + wy + turn(wy, -sy, 1) + wz + turn(wz, -sz, 2)
    return jnp.where(diagonal > 0.0, OMEGA / diagonal, 0.0)


def restrict(v, sy, sz):
    return pair_sum(pair_sum(x_pair(v), sy, 1), sz, 2)


def coarsen(storage, wx, wy, wz, sy, sz):
    return (
        restrict(storage, sy, sz),
        pair_sum(pair_sum(x_even(wx), sy, 1), sz, 2),
        pair_low(pair_sum(x_pair(wy), sz, 2), sy, 1),
        pair_low(pair_sum(x_pair(wz), sy, 1), sz, 2),
    )


def operate_rows(v_ref, s_ref, wx_ref, wy_ref, wz_ref, at, size):
    v = v_ref[pl.ds(at, size)]
    wx = wx_ref[pl.ds(at, size)]
    fy = wy_ref[pl.ds(at, size)] * (v - turn(v, 1, 1))
    fz = wz_ref[pl.ds(at, size)] * (v - turn(v, 1, 2))
    flux = wx * (v - v_ref[pl.ds(at - 1, size)])
    flux = flux - wx_ref[pl.ds(at + 1, size)] * (v_ref[pl.ds(at + 1, size)] - v)
    flux = flux + (fy - turn(fy, -1, 1)) + (fz - turn(fz, -1, 2))
    return v, s_ref[pl.ds(at, size)] * v + flux


def blank_ends(ref):
    ref[0] = jnp.zeros((WY, NZ), F32)
    ref[PX - 1] = jnp.zeros((WY, NZ), F32)


def blank_level1(ref, size):
    ref[0:size] = jnp.zeros((size, WY, NZ), F32)
    ref[L1X - size :] = jnp.zeros((size, WY, NZ), F32)


def pack_level2(v):
    sub, lane = iota(v.shape, 1), iota(v.shape, 2)
    chosen = (sub >= 8) & (sub < 24) & (sub % 4 == 0) & ((sub - 8) // 4 == lane % 4)
    return jnp.sum(jnp.where(chosen, v, 0.0), axis=1)


def send(msg_ref, rows):
    rows = list(rows)
    parts, height = msg_ref.shape[1:3]
    spare = parts * height - sum(row.shape[0] for row in rows)
    if spare:
        rows.append(jnp.zeros((spare, NZ), F32))
    whole = jnp.concatenate(rows, axis=0)
    for part in range(parts):
        piece = whole[part * height : (part + 1) * height]
        for peer in range(msg_ref.shape[0]):
            msg_ref[peer, part] = piece


def pack_bands3(fields):
    sub, lane = iota((1, WY, NZ), 1), iota((1, WY, NZ), 2)
    total = jnp.zeros((1, WY, NZ), F32)
    for f, v in enumerate(fields):
        chosen = ((sub == 8) & (lane % 8 == 2 * f)) | ((sub == 16) & (lane % 8 == 2 * f + 1))
        total = total + jnp.where(chosen, v, 0.0)
    return jnp.sum(total, axis=1)


def pack_ring1(v):
    sub, lane = iota((2, WY, NZ), 1), iota((2, WY, NZ), 2)
    rows = v[5:7]
    parts = []
    for k in range(4):
        chosen = ((sub == 8 + 4 * k) & (lane % 2 == 0)) | ((sub == 10 + 4 * k) & (lane % 2 == 1))
        parts.append(jnp.sum(jnp.where(chosen, rows, 0.0), axis=1, keepdims=True))
    return jnp.concatenate([part[x] for x in range(2) for part in parts], axis=0)


def pack_edge1(v):
    sub, lane = iota((6, WY, NZ), 1), iota((6, WY, NZ), 2)
    chosen = ((sub == 20) & (lane % 2 == 0)) | ((sub == 10) & (lane % 2 == 1))
    return jnp.sum(jnp.where(chosen, v[3:9], 0.0), axis=1)


def descend_top(r_ref, e1_ref, e2_ref, s_ref, wx_ref, wy_ref, wz_ref, di_ref, r1_ref):
    def second(i, carry):
        at = 1 + 2 * i
        v, av = operate_rows(e1_ref, s_ref, wx_ref, wy_ref, wz_ref, at, 2)
        e2_ref[pl.ds(at, 2)] = v + di_ref[pl.ds(at, 2)] * (r_ref[pl.ds(at, 2)] - av)
        return carry

    lax.fori_loop(1, WX // 2 - 1, second, 0, unroll=5)

    def third(i, carry):
        at = 1 + 2 * i
        _, av = operate_rows(e2_ref, s_ref, wx_ref, wy_ref, wz_ref, at, 2)
        r1_ref[pl.ds(i, 1)] = restrict(r_ref[pl.ds(at, 2)] - av, 1, 1)
        return carry

    lax.fori_loop(2, WX // 2 - 2, third, 0, unroll=4)


def descend_second(r1, s1, wx1, wy1, wz1, di1):
    first = r1 * di1
    second = first + di1 * (r1 - operate(first, s1, wx1, wy1, wz1, 2, 2))
    defect = r1 - operate(second, s1, wx1, wy1, wz1, 2, 2)
    return second, restrict(defect, 2, 2)


def soil_kernel(
    head_in, old_in, soil_in, ks_in, alpha_in, shape_in, span_in, out_ref,
    head_ref, old_ref, soil_ref, ks_ref, alpha_ref, shape_ref, span_ref, sems,
):
    given = (ks_in, alpha_in, shape_in, span_in, head_in, old_in, soil_in)
    held = (ks_ref, alpha_ref, shape_ref, span_ref, head_ref, old_ref, soil_ref)
    copies = [
        pltpu.make_async_copy(src, dst, sems.at[i])
        for i, (src, dst) in enumerate(zip(given, held, strict=True))
    ]
    for copy in copies:
        copy.start()
    for copy in copies:
        copy.wait()

    def cells(i, carry):
        row = pl.ds(i, 1)
        head, old, soil = head_ref[row], old_ref[row], soil_ref[row]
        ks = jnp.full(soil.shape, ks_ref[0])
        alpha = jnp.full(soil.shape, alpha_ref[0])
        shape_n = jnp.full(soil.shape, shape_ref[0])
        span = jnp.full(soil.shape, span_ref[0])
        for kind in range(1, SOILS):
            hit = soil == kind
            ks = jnp.where(hit, ks_ref[kind], ks)
            alpha = jnp.where(hit, alpha_ref[kind], alpha)
            shape_n = jnp.where(hit, shape_ref[kind], shape_n)
            span = jnp.where(hit, span_ref[kind], span)
        shape_m = 1.0 - 1.0 / shape_n
        power = jnp.exp(shape_n * jnp.log(alpha * -head))
        old_power = jnp.exp(shape_n * jnp.log(alpha * -old))
        saturation = jnp.exp(-shape_m * jnp.log1p(power))
        old_saturation = jnp.exp(-shape_m * jnp.log1p(old_power))
        portion = 1.0 / (1.0 + power)
        factor = 1.0 - jnp.exp(shape_m * jnp.log(power / (1.0 + power)))
        capacity = span * shape_m * shape_n * power / -head * saturation * portion
        out_ref[0, row] = head
        out_ref[1, row] = ks * jnp.sqrt(saturation) * factor * factor
        out_ref[2, row] = capacity + STORAGE
        out_ref[3, row] = span * (saturation - old_saturation) + STORAGE * (head - old)
        return carry

    lax.fori_loop(0, BX, cells, 0, unroll=2)


def fill_window(ref, core, ylow, yhigh):
    ref[1 : PX - 1, 0:8, :] = ylow
    ref[1 : PX - 1, 8:24, :] = core
    ref[1 : PX - 1, 24:32, :] = yhigh


def assemble_kernel(
    core, ylow, yhigh,
    r_ref, s_ref, di_ref, wx_ref, wy_ref, wz_ref, e2_ref,
    r1_ref, s1_ref, di1_ref, wx1_ref, wy1_ref, wz1_ref, e21_ref, msg_ref,
    h_ref, k_ref, m_ref, e1_ref,
):
    for ref in (h_ref, k_ref, s_ref, wx_ref, wy_ref, wz_ref, di_ref, r_ref, e1_ref, e2_ref):
        blank_ends(ref)
    for f, ref in enumerate((h_ref, k_ref, s_ref, m_ref)):
        fill_window(ref, core[f], ylow[f], yhigh[f])

    def harmonic(a, b):
        total = a + b
        return jnp.where(total > 0.0, 2.0 * a * b / total, 0.0)

    def faces(i, carry):
        at = 1 + 2 * i
        k = k_ref[pl.ds(at, 2)]
        wx_ref[pl.ds(at, 2)] = harmonic(k, k_ref[pl.ds(at - 1, 2)])
        wy_ref[pl.ds(at, 2)] = harmonic(k, turn(k, 1, 1))
        wz = harmonic(k, turn(k, 1, 2))
        wz_ref[pl.ds(at, 2)] = jnp.where(iota(wz.shape, 2) == 0, 0.0, wz)
        return carry

    lax.fori_loop(0, WX // 2, faces, 0, unroll=4)

    def right_side(i, carry):
        at = 1 + 2 * i
        rows = pl.ds(at, 2)
        h, wx, wy, wz = h_ref[rows], wx_ref[rows], wy_ref[rows], wz_ref[rows]
        wx_up = wx_ref[pl.ds(at + 1, 2)]
        fy = wy * (h - turn(h, 1, 1))
        fz = wz * (h - turn(h, 1, 2) + 1.0)
        flux = wx * (h - h_ref[pl.ds(at - 1, 2)]) - wx_up * (h_ref[pl.ds(at + 1, 2)] - h)
        flux = flux + (fy - turn(fy, -1, 1)) + (fz - turn(fz, -1, 2))
        rhs = -(m_ref[rows] + flux)
        diagonal = s_ref[rows] + wx + wx_up + wy + turn(wy, -1, 1) + wz + turn(wz, -1, 2)
        di = jnp.where(diagonal > 0.0, OMEGA / diagonal, 0.0)
        r_ref[rows] = rhs
        di_ref[rows] = di
        e1_ref[rows] = rhs * di
        return carry

    lax.fori_loop(0, WX // 2, right_side, 0, unroll=4)

    def bands(i, carry):
        rows = pl.ds(1 + 2 * i, 2)
        s1, wx1, wy1, wz1 = coarsen(s_ref[rows], wx_ref[rows], wy_ref[rows], wz_ref[rows], 1, 1)
        row = pl.ds(i, 1)
        s1_ref[row], wx1_ref[row], wy1_ref[row], wz1_ref[row] = s1, wx1, wy1, wz1
        return carry

    lax.fori_loop(1, WX // 2 - 1, bands, 0, unroll=5)
    for ref in (s1_ref, wx1_ref, wy1_ref, wz1_ref):
        blank_level1(ref, 1)
    blank_level1(r1_ref, 2)
    descend_top(r_ref, e1_ref, e2_ref, s_ref, wx_ref, wy_ref, wz_ref, di_ref, r1_ref)

    s1, wx1, wy1, wz1 = s1_ref[...], wx1_ref[...], wy1_ref[...], wz1_ref[...]
    di1 = relax_factor(s1, wx1, wy1, wz1, 2, 2)
    di1_ref[...] = di1
    e21, r2 = descend_second(r1_ref[...], s1, wx1, wy1, wz1, di1)
    e21_ref[...] = e21
    bands2 = coarsen(s1, wx1, wy1, wz1, 2, 2)
    bands3 = coarsen(*(v[2:4] for v in bands2), 4, 4)
    rows = [pack_level2(v[2:4]) for v in (r2,) + bands2]
    send(msg_ref, rows + [pack_bands3(bands3)])


def again_kernel(
    core, ylow, yhigh, rhs_ref, s_ref, di_ref, wx_ref, wy_ref, wz_ref,
    s1_ref, di1_ref, wx1_ref, wy1_ref, wz1_ref,
    u_ref, r_ref, e2_ref, r1_ref, e21_ref, msg_ref, edge_ref, pre_ref, e1_ref,
):
    for ref in (pre_ref, u_ref, r_ref, e1_ref, e2_ref):
        blank_ends(ref)
    fill_window(pre_ref, core[...], ylow[...], yhigh[...])

    def post(i, carry):
        at = 1 + 2 * i
        rows = pl.ds(at, 2)
        v, av = operate_rows(pre_ref, s_ref, wx_ref, wy_ref, wz_ref, at, 2)
        u_ref[rows] = v + di_ref[rows] * (rhs_ref[rows] - av)
        return carry

    lax.fori_loop(0, WX // 2, post, 0, unroll=4)

    def remain(i, carry):
        at = 1 + 2 * i
        rows = pl.ds(at, 2)
        _, av = operate_rows(u_ref, s_ref, wx_ref, wy_ref, wz_ref, at, 2)
        left = rhs_ref[rows] - av
        r_ref[rows] = left
        e1_ref[rows] = left * di_ref[rows]
        return carry

    lax.fori_loop(1, WX // 2 - 1, remain, 0, unroll=5)
    descend_top(r_ref, e1_ref, e2_ref, s_ref, wx_ref, wy_ref, wz_ref, di_ref, r1_ref)
    blank_level1(r1_ref, 2)
    e21, r2 = descend_second(
        r1_ref[...], s1_ref[...], wx1_ref[...], wy1_ref[...], wz1_ref[...], di1_ref[...]
    )
    e21_ref[...] = e21
    send(msg_ref, [pack_level2(r2[2:4]), pack_ring1(e21)])
    send(edge_ref, [pack_edge1(e21)])


def message_rows(ref):
    tiles = lax.axis_size("tile")
    return lambda field, half: ref[0:tiles, field, half : half + 1, :]


def pair_rows(refs):
    even = lax.axis_index("group") % 2 == 0

    def pick(ref, core):
        return lambda field, half: ref[:, core, field, half : half + 1, :]

    six = [pick(ref, core) for ref in refs for core in range(2)]

    def choose(first, second):
        return lambda field, half: jnp.where(even, first(field, half), second(field, half))

    return [choose(six[i], six[i + 1]) for i in range(5)]


def unpack_level2(field, own, low, high):
    tiles = lax.axis_size("tile")
    shape = (tiles, 16, NZ)
    sub, lane = iota(shape, 1), iota(shape, 2)
    halves = []
    for half in range(2):

        def spread(pick, half=half):
            return jnp.broadcast_to(pick(field, half), shape)

        v = jnp.where(sub < 4, spread(low), jnp.where(sub < 8, spread(own), spread(high)))
        v = jnp.where((lane % 4 == sub % 4) & (sub < 12), v, 0.0)
        halves.append(pair_sum(pair_sum(v, 1, 2), 2, 2))
    return jnp.stack(halves, axis=1).reshape((2 * tiles, 16, NZ))


def pack_level3(v):
    sub, lane = iota((16, NZ), 0), iota((16, NZ), 1)
    rows = []
    for j in range(v.shape[0] // 4):
        total = jnp.zeros((16, NZ), F32)
        for q in range(4):
            chosen = ((sub == 4) & (lane % 8 == 2 * q)) | ((sub == 6) & (lane % 8 == 2 * q + 1))
            total = total + jnp.where(chosen, v[4 * j + q], 0.0)
        rows.append(jnp.sum(total, axis=0, keepdims=True))
    return rows


def pack_sums3(v):
    v = v + turn(v, -2, 1)
    sub, lane = iota((16, NZ), 0), iota((16, NZ), 1)
    rows = []
    for first in range(0, v.shape[0], 8):
        total = jnp.zeros((16, NZ), F32)
        for q in range(min(8, v.shape[0] - first)):
            total = total + jnp.where((sub == 4) & (lane % 8 == q), v[first + q], 0.0)
        rows.append(jnp.sum(total, axis=0, keepdims=True))
    return rows


def descend_third(r2, s2, wx2, wy2, wz2, di2):
    first = r2 * di2
    second = first + di2 * (r2 - operate(first, s2, wx2, wy2, wz2, 1, 4))
    return second, restrict(r2 - operate(second, s2, wx2, wy2, wz2, 1, 4), 1, 4)


def third_kernel(
    before, here, after,
    r2_ref, s2_ref, di2_ref, wx2_ref, wy2_ref, wz2_ref, e22_ref,
    s3_ref, di3_ref, wx3_ref, wy3_ref, wz3_ref, msg_ref,
):
    near = pair_rows((before, here, after))
    _, low, own, high, _ = near
    sources = [rows(5, 0) for rows in near]
    s3, wx3, wy3, wz3 = unpack_bands3(sources)
    s3_ref[...], wx3_ref[...], wy3_ref[...], wz3_ref[...] = s3, wx3, wy3, wz3
    di3_ref[...] = relax_factor(s3, wx3, wy3, wz3, 2, 8)
    r2, s2, wx2, wy2, wz2 = (unpack_level2(f, own, low, high) for f in range(5))
    di2 = relax_factor(s2, wx2, wy2, wz2, 1, 4)
    r2_ref[...], s2_ref[...], di2_ref[...] = r2, s2, di2
    wx2_ref[...], wy2_ref[...], wz2_ref[...] = wx2, wy2, wz2
    e22, r3 = descend_third(r2, s2, wx2, wy2, wz2, di2)
    e22_ref[...] = e22
    s3, wx3, _, wz3 = coarsen(s2, wx2, wy2, wz2, 1, 4)
    inner = s3 + wx3 + x_high(wx3) + wz3 + turn(wz3, -8, 2)
    send(msg_ref, pack_level3(r3) + pack_sums3(inner))


def third_again_kernel(
    own, low, high, s2_ref, di2_ref, wx2_ref, wy2_ref, wz2_ref, r2_ref, e22_ref, msg_ref
):
    r2 = unpack_level2(0, message_rows(own), message_rows(low), message_rows(high))
    r2_ref[...] = r2
    e22, r3 = descend_third(
        r2, s2_ref[...], wx2_ref[...], wy2_ref[...], wz2_ref[...], di2_ref[...]
    )
    e22_ref[...] = e22
    send(msg_ref, pack_level3(r3))


def third_masks(shape):
    sub, lane = iota(shape, 1), iota(shape, 2)
    return sub // 4, (sub % 4) // 2, lane % 8


def octuple(v):
    return pair_sum(pair_sum(pair_sum(v, 1, 2), 2, 2), 4, 2)


def unpack_bands3(sources):
    shape = (sources[0].shape[0], 24, NZ)
    dev, half, slot = third_masks(shape)
    rows = jnp.broadcast_to(sources[0], shape)
    for d in range(1, 5):
        rows = jnp.where(dev == d, jnp.broadcast_to(sources[d], shape), rows)
    rows = jnp.where(dev < 5, rows, 0.0)
    return [octuple(jnp.where(slot == 2 * f + half, rows, 0.0)) for f in range(4)]


def unpack_r3(v):
    group = lax.axis_index("group")
    at = iota(v.shape, 1)
    shape = (v.shape[0], 24, NZ)
    dev, half, slot = third_masks(shape)
    rows = jnp.zeros(shape, F32)
    for d in range(5):
        near = jnp.sum(jnp.where(at == group + (d - 2), v, 0.0), axis=1, keepdims=True)
        rows = jnp.where(dev == d, jnp.broadcast_to(near, shape), rows)
    parts = [jnp.where(slot == 2 * q + half, rows, 0.0) for q in range(4)]
    return octuple(jnp.stack(parts, axis=1).reshape((4 * v.shape[0], 24, NZ)))


def line_sums(v, held):
    total = jnp.sum(v, axis=1, keepdims=True)
    lane = iota(total.shape, 2) % 8
    parts = [jnp.where(lane * held // 8 == q, total, 0.0) for q in range(held)]
    wide = jnp.stack(parts, axis=1).reshape((held * v.shape[0], 1, NZ))
    return octuple(wide[: lax.axis_size("tile")])


def solve_third(r3, line, s3, di3, wx3, wy3, wz3):
    v = jnp.broadcast_to(line, r3.shape)
    for _ in range(COARSE_SWEEPS):
        v = v + di3 * (r3 - operate(v, s3, wx3, wy3, wz3, 2, 8))
    return turn(v, -4, 1)[:, 0:16]


def near_tiles(v):
    tile = lax.axis_index("tile")
    parts = []
    for off in (-1, 0, 1):
        total = jnp.zeros((2,) + v.shape[1:], F32)
        for t in range(v.shape[0] // 2):
            total = total + jnp.where(tile + off == t, v[2 * t : 2 * t + 2], 0.0)
        parts.append(total)
    return jnp.concatenate(parts, axis=0)


def widen_y(v):
    shape = (v.shape[0], 8, NZ)
    sub = iota(shape, 1)
    parts = []
    for at in (2, 4, 6, 8):
        first = jnp.broadcast_to(v[:, at : at + 1], shape)
        second = jnp.broadcast_to(v[:, at + 1 : at + 2], shape)
        parts.append(jnp.where(sub < 4, first, second))
    return jnp.concatenate(parts, axis=1)


def climb_to_second(corr3, r2_ref, s2_ref, di2_ref, wx2_ref, wy2_ref, wz2_ref, e22_ref):
    v = e22_ref[...] + x_repeat(corr3)
    v = v + di2_ref[...] * (
        r2_ref[...]
        - operate(v, s2_ref[...], wx2_ref[...], wy2_ref[...], wz2_ref[...], 1, 4)
    )
    return x_repeat(widen_y(near_tiles(v)))


def climb_to_first(v, r1_ref, s1_ref, di1_ref, wx1_ref, wy1_ref, wz1_ref):
    return v + di1_ref[...] * (
        r1_ref[...]
        - operate(v, s1_ref[...], wx1_ref[...], wy1_ref[...], wz1_ref[...], 2, 2)
    )


def strided(ref, first, thirds, groups, rows):
    parts = [ref[pl.ds(first + j, groups, stride=rows), :] for j in range(thirds)]
    return jnp.stack(parts, axis=0)


def climb_kernel(
    third_ref, s3_ref, di3_ref, wx3_ref, wy3_ref, wz3_ref,
    r2_ref, s2_ref, di2_ref, wx2_ref, wy2_ref, wz2_ref, e22_ref,
    r1_ref, s1_ref, di1_ref, wx1_ref, wy1_ref, wz1_ref, e21_ref, e2_ref,
    pre_ref, below_ref,
    *, groups, thirds, rows,
):
    r3 = strided(third_ref, 0, thirds, groups, rows)
    below = line_sums(strided(third_ref, thirds, rows - thirds, groups, rows), 8)
    below_ref[...] = below
    corr3 = solve_third(
        unpack_r3(r3), line_sums(r3, 4) / below,
        s3_ref[...], di3_ref[...], wx3_ref[...], wy3_ref[...], wz3_ref[...],
    )
    corr2 = climb_to_second(corr3, r2_ref, s2_ref, di2_ref, wx2_ref, wy2_ref, wz2_ref, e22_ref)
    v = climb_to_first(
        e21_ref[...] + corr2, r1_ref, s1_ref, di1_ref, wx1_ref, wy1_ref, wz1_ref
    )
    own1 = x_repeat(v[4:8])
    pre_ref[...] = e2_ref[9:17, 8:24, :] + own1[:, 8:24, :]


def tile_rows(ref, off, at):
    tile = lax.axis_index("tile")
    total = jnp.zeros((2, NZ), F32)
    for t in range(lax.axis_size("tile")):
        total = total + jnp.where(tile + off == t, ref[t, at], 0.0)
    return total


def ring_row(own, low, high, off, first):
    pairs = [tile_rows(own, off, first), tile_rows(own, off, first + 1)]
    packed = [tile_rows(low, off, first + 1)[1:2]]
    packed += [pair[k : k + 1] for pair in pairs for k in range(2)]
    packed += [tile_rows(high, off, first)[0:1]]
    return spread_pairs([row[None] for row in packed], 1)


def spread_pairs(packed, height):
    shape = (height, WY, NZ)
    sub, lane = iota(shape, 1), iota(shape, 2)
    rows = jnp.zeros(shape, F32)
    for k, row in enumerate(packed):
        rows = jnp.where(sub // 4 == k + 1, jnp.broadcast_to(row, shape), rows)
    return pair_sum(jnp.where(lane % 2 == (sub // 2) % 2, rows, 0.0), 1, 2)


def last_climb_kernel(
    third_ref, below_ref, s3_ref, di3_ref, wx3_ref, wy3_ref, wz3_ref,
    low, own, high,
    r2_ref, s2_ref, di2_ref, wx2_ref, wy2_ref, wz2_ref, e22_ref,
    r1_ref, s1_ref, di1_ref, wx1_ref, wy1_ref, wz1_ref, e21_ref,
    e2_ref, rhs_ref, s_ref, di_ref, wx_ref, wy_ref, wz_ref, u_ref, r_ref,
    out_ref, left_ref, pre_ref, v_ref,
    *, groups, thirds, rows,
):
    r3 = strided(third_ref, 0, thirds, groups, rows)
    corr3 = solve_third(
        unpack_r3(r3), line_sums(r3, 4) / below_ref[...],
        s3_ref[...], di3_ref[...], wx3_ref[...], wy3_ref[...], wz3_ref[...],
    )
    corr2 = climb_to_second(corr3, r2_ref, s2_ref, di2_ref, wx2_ref, wy2_ref, wz2_ref, e22_ref)
    tiles = lax.axis_size("tile")
    middle = e21_ref[3:9]
    sub = iota(middle.shape, 1)
    edge_low = jnp.concatenate([low[tiles, k] for k in range(3)], axis=0)[:, None]
    edge_high = jnp.concatenate([high[tiles, k] for k in range(3)], axis=0)[:, None]
    nothing = jnp.zeros_like(edge_low)
    edges = spread_pairs([edge_low] + [nothing] * 4 + [edge_high], 6)
    kept = (sub >= 6) & (sub < 26)
    middle = jnp.where(kept, middle, edges)
    blank = jnp.zeros((2, WY, NZ), F32)
    first, last = ring_row(own, low, high, -1, 3), ring_row(own, low, high, 1, 1)
    e21 = jnp.concatenate([blank, first, middle, last, blank], axis=0)
    v = climb_to_first(e21 + corr2, r1_ref, s1_ref, di1_ref, wx1_ref, wy1_ref, wz1_ref)
    pre_ref[7:19] = e2_ref[7:19] + x_repeat(v[3:9])

    def post(i, carry):
        at = 8 + 2 * i
        here = pl.ds(at, 2)
        v, av = operate_rows(pre_ref, s_ref, wx_ref, wy_ref, wz_ref, at, 2)
        v_ref[here] = u_ref[here] + v + di_ref[here] * (r_ref[here] - av)
        return carry

    lax.fori_loop(0, BX // 2 + 1, post, 0, unroll=True)

    def remain(i, carry):
        at = 9 + 2 * i
        v, av = operate_rows(v_ref, s_ref, wx_ref, wy_ref, wz_ref, at, 2)
        left = rhs_ref[pl.ds(at, 2)] - av
        out_ref[pl.ds(2 * i, 2)] = v[:, 8:24]
        left_ref[pl.ds(2 * i, 2)] = left[:, 8:24]
        return carry

    lax.fori_loop(0, BX // 2, remain, 0, unroll=True)


def call(body, outs, operands, scratch=()):
    vmem = pl.BlockSpec(memory_space=pltpu.VMEM)
    return pl.pallas_call(
        body,
        out_shape=[jax.ShapeDtypeStruct(shape, F32) for shape in outs],
        in_specs=[vmem] * len(operands),
        out_specs=[vmem] * len(outs),
        scratch_shapes=[pltpu.VMEM(shape, F32) for shape in scratch],
        compiler_params=pltpu.CompilerParams(vmem_limit_bytes=16 * 1024 * 1024),
    )(*operands)


def beside(to_low, to_high, axis, step=1):
    ends = lax.axis_size(axis) - step
    from_low = lax.ppermute(to_high, axis, [(i, i + step) for i in range(ends)])
    from_high = lax.ppermute(to_low, axis, [(i + step, i) for i in range(ends)])
    return from_low, from_high


def surround(cells, dim):
    low, high = beside(cells, cells, "tile")
    core = jnp.concatenate([low, cells, high], axis=dim)
    ydim = dim + 1
    first = lax.slice_in_dim(core, 0, 8, axis=ydim)
    last = lax.slice_in_dim(core, BY - 8, BY, axis=ydim)
    ylow, yhigh = beside(first, last, "group")
    return core, ylow, yhigh


def everyone(blocks, axis):
    return lax.all_to_all(blocks, axis, 0, 0, tiled=True)


def pairs_of_tiles(block):
    tiles, groups = lax.axis_size("tile"), lax.axis_size("group")
    members = [
        [t * groups + 2 * pair + core for t in range(tiles) for core in range(2)]
        for pair in range(groups // 2)
    ]
    given = lax.all_to_all(
        block, ("tile", "group"), 0, 0, axis_index_groups=members, tiled=True
    )
    return given.reshape((tiles, 2) + block.shape[1:])


def shards(pressure_head, old_head, soil_type, conduct_sat, alpha_param, shape_param, water_span):
    tiles, groups = lax.axis_size("tile"), lax.axis_size("group")
    thirds = tiles // 4
    top, one, two = (PX, WY, NZ), (L1X, WY, NZ), (2 * tiles, 16, NZ)
    three, line = (tiles, 24, NZ), (tiles, 1, NZ)
    rows_once, rows_again = thirds + -(-tiles // 8), thirds

    fields = pl.pallas_call(
        soil_kernel,
        out_shape=jax.ShapeDtypeStruct((4, BX, BY, NZ), F32),
        in_specs=[pl.BlockSpec(memory_space=pltpu.HBM)] * 7,
        out_specs=pl.BlockSpec(memory_space=pltpu.VMEM),
        scratch_shapes=[
            pltpu.VMEM((BX, BY, NZ), F32),
            pltpu.VMEM((BX, BY, NZ), F32),
            pltpu.VMEM((BX, BY, NZ), jnp.int32),
            *[pltpu.SMEM((SOILS,), F32) for _ in range(4)],
            pltpu.SemaphoreType.DMA((7,)),
        ],
    )(pressure_head, old_head, soil_type, conduct_sat, alpha_param, shape_param, water_span)
    core, ylow, yhigh = surround(fields, 1)
    rhs, s0, di0, wx0, wy0, wz0, e2, r1, s1, di1, wx1, wy1, wz1, e21, msg = call(
        assemble_kernel,
        [top] * 7 + [one] * 7 + [(2 * tiles, 6, 2, NZ)],
        [core, ylow, yhigh],
        [top] * 4,
    )
    bands0 = [s0, di0, wx0, wy0, wz0]
    bands1 = [s1, di1, wx1, wy1, wz1]

    here = pairs_of_tiles(msg)
    before, after = beside(here, here, "group", 2)
    r2, s2, di2, wx2, wy2, wz2, e22, s3, di3, wx3, wy3, wz3, msg = call(
        third_kernel,
        [two] * 7 + [three] * 5 + [(groups, rows_once, 1, NZ)],
        [before, here, after],
    )
    bands3 = [s3, di3, wx3, wy3, wz3]
    bands2 = [s2, di2, wx2, wy2, wz2]
    third = everyone(msg, "group").reshape(groups * rows_once, NZ)
    pre, below = call(
        functools.partial(climb_kernel, groups=groups, thirds=thirds, rows=rows_once),
        [(BX, BY, NZ), line],
        [third, *bands3, r2, *bands2, e22, r1, *bands1, e21, e2],
    )

    core, ylow, yhigh = surround(pre, 0)
    u, rem, e2, r1, e21, msg, edge = call(
        again_kernel,
        [top] * 3 + [one] * 2 + [(tiles, 5, 2, NZ), (1, 5, 2, NZ)],
        [core, ylow, yhigh, rhs, *bands0, *bands1],
        [top] * 2,
    )
    own = jnp.concatenate([everyone(msg, "tile"), edge], axis=0)
    low, high = beside(own, own, "group")
    r2, e22, msg = call(
        third_again_kernel,
        [two] * 2 + [(groups, rows_again, 1, NZ)],
        [own, low, high, *bands2],
    )
    third = everyone(msg, "group").reshape(groups * rows_again, NZ)
    update, remainder = call(
        functools.partial(last_climb_kernel, groups=groups, thirds=thirds, rows=rows_again),
        [(BX, BY, NZ)] * 2,
        [third, below, *bands3, low, own, high, r2, *bands2, e22, r1, *bands1, e21]
        + [e2, rhs, *bands0, u, rem],
        [top] * 2,
    )
    return update, remainder


def solution(mesh):
    spec = P("tile", "group", None)
    return jax.shard_map(
        shards,
        mesh=mesh,
        in_specs=(spec, spec, spec, P(), P(), P(), P()),
        out_specs=(spec, spec),
        check_vma=False,
    )
```

```python
import functools
import math

import jax
import jax.numpy as jnp
from jax import lax
from jax.experimental import pallas as pl
from jax.experimental.pallas import tpu as pltpu
from jax.sharding import PartitionSpec as P

OMEGA = 2.0 / 3.0
STORAGE = 0.01
COARSE_SWEEPS = 4
SOILS = 12

BX, BY, NZ = 8, 16, 128
WX, WY = 24, 32
PX = WX + 2
L1X = WX // 2
F32 = jnp.float32


def iota(shape, dim):
    return lax.broadcasted_iota(jnp.int32, shape, dim)


def turn(v, step, axis):
    size = v.shape[axis]
    return pltpu.roll(v, step % size, axis)


def bit_of(v, step, axis):
    return (iota(v.shape, axis) // step) % 2 == 0


def pair_sum(v, step, axis):
    return v + jnp.where(bit_of(v, step, axis), turn(v, -step, axis), turn(v, step, axis))


def pair_low(v, step, axis):
    return jnp.where(bit_of(v, step, axis), v, turn(v, step, axis))


def x_low(v):
    return jnp.concatenate([v[:1], v[:-1]], axis=0)


def x_high(v):
    return jnp.concatenate([v[1:], jnp.zeros_like(v[:1])], axis=0)


def x_pair(v):
    return jnp.sum(v.reshape((v.shape[0] // 2, 2) + v.shape[1:]), axis=1)


def x_even(v):
    return v.reshape((v.shape[0] // 2, 2) + v.shape[1:])[:, 0]


def x_repeat(v):
    size = v.shape[0]
    wide = jnp.broadcast_to(v[:, None], (size, 2) + v.shape[1:])
    return wide.reshape((2 * size,) + v.shape[1:])


def operate(v, storage, wx, wy, wz, sy, sz):
    fx = wx * (v - x_low(v))
    fy = wy * (v - turn(v, sy, 1))
    fz = wz * (v - turn(v, sz, 2))
    flux = (fx - x_high(fx)) + (fy - turn(fy, -sy, 1)) + (fz - turn(fz, -sz, 2))
    return storage * v + flux


def relax_factor(storage, wx, wy, wz, sy, sz):
    diagonal = storage + wx + x_high(wx) + wy + turn(wy, -sy, 1) + wz + turn(wz, -sz, 2)
    return jnp.where(diagonal > 0.0, OMEGA / diagonal, 0.0)


def restrict(v, sy, sz):
    return pair_sum(pair_sum(x_pair(v), sy, 1), sz, 2)


def coarsen(storage, wx, wy, wz, sy, sz):
    return (
        restrict(storage, sy, sz),
        pair_sum(pair_sum(x_even(wx), sy, 1), sz, 2),
        pair_low(pair_sum(x_pair(wy), sz, 2), sy, 1),
        pair_low(pair_sum(x_pair(wz), sy, 1), sz, 2),
    )


def operate_rows(v_ref, s_ref, wx_ref, wy_ref, wz_ref, at, size):
    v = v_ref[pl.ds(at, size)]
    wx = wx_ref[pl.ds(at, size)]
    fy = wy_ref[pl.ds(at, size)] * (v - turn(v, 1, 1))
    fz = wz_ref[pl.ds(at, size)] * (v - turn(v, 1, 2))
    flux = wx * (v - v_ref[pl.ds(at - 1, size)])
    flux = flux - wx_ref[pl.ds(at + 1, size)] * (v_ref[pl.ds(at + 1, size)] - v)
    flux = flux + (fy - turn(fy, -1, 1)) + (fz - turn(fz, -1, 2))
    return v, s_ref[pl.ds(at, size)] * v + flux


def blank_ends(ref):
    ref[0] = jnp.zeros((WY, NZ), F32)
    ref[PX - 1] = jnp.zeros((WY, NZ), F32)


def blank_level1(ref, size):
    ref[0:size] = jnp.zeros((size, WY, NZ), F32)
    ref[L1X - size :] = jnp.zeros((size, WY, NZ), F32)


def pack_level2(v):
    sub, lane = iota(v.shape, 1), iota(v.shape, 2)
    chosen = (sub >= 8) & (sub < 24) & (sub % 4 == 0) & ((sub - 8) // 4 == lane % 4)
    return jnp.sum(jnp.where(chosen, v, 0.0), axis=1)


def send(msg_ref, rows):
    rows = list(rows)
    parts, height = msg_ref.shape[1:3]
    spare = parts * height - sum(row.shape[0] for row in rows)
    if spare:
        rows.append(jnp.zeros((spare, NZ), F32))
    whole = jnp.concatenate(rows, axis=0)
    for part in range(parts):
        piece = whole[part * height : (part + 1) * height]
        for peer in range(msg_ref.shape[0]):
            msg_ref[peer, part] = piece


def pack_bands3(fields):
    sub, lane = iota((1, WY, NZ), 1), iota((1, WY, NZ), 2)
    total = jnp.zeros((1, WY, NZ), F32)
    for f, v in enumerate(fields):
        chosen = ((sub == 8) & (lane % 8 == 2 * f)) | ((sub == 16) & (lane % 8 == 2 * f + 1))
        total = total + jnp.where(chosen, v, 0.0)
    return jnp.sum(total, axis=1)


def pack_ring1(v):
    sub, lane = iota((2, WY, NZ), 1), iota((2, WY, NZ), 2)
    rows = v[5:7]
    parts = []
    for k in range(4):
        chosen = ((sub == 8 + 4 * k) & (lane % 2 == 0)) | ((sub == 10 + 4 * k) & (lane % 2 == 1))
        parts.append(jnp.sum(jnp.where(chosen, rows, 0.0), axis=1, keepdims=True))
    return jnp.concatenate([part[x] for x in range(2) for part in parts], axis=0)


def pack_edge1(v):
    sub, lane = iota((6, WY, NZ), 1), iota((6, WY, NZ), 2)
    chosen = ((sub == 20) & (lane % 2 == 0)) | ((sub == 10) & (lane % 2 == 1))
    return jnp.sum(jnp.where(chosen, v[3:9], 0.0), axis=1)


def descend_top(r_ref, e1_ref, e2_ref, s_ref, wx_ref, wy_ref, wz_ref, di_ref, r1_ref):
    def second(i, carry):
        at = 1 + 2 * i
        v, av = operate_rows(e1_ref, s_ref, wx_ref, wy_ref, wz_ref, at, 2)
        e2_ref[pl.ds(at, 2)] = v + di_ref[pl.ds(at, 2)] * (r_ref[pl.ds(at, 2)] - av)
        return carry

    lax.fori_loop(1, WX // 2 - 1, second, 0, unroll=5)

    def third(i, carry):
        at = 1 + 2 * i
        _, av = operate_rows(e2_ref, s_ref, wx_ref, wy_ref, wz_ref, at, 2)
        r1_ref[pl.ds(i, 1)] = restrict(r_ref[pl.ds(at, 2)] - av, 1, 1)
        return carry

    lax.fori_loop(2, WX // 2 - 2, third, 0, unroll=4)


def descend_second(r1, s1, wx1, wy1, wz1, di1):
    first = r1 * di1
    second = first + di1 * (r1 - operate(first, s1, wx1, wy1, wz1, 2, 2))
    defect = r1 - operate(second, s1, wx1, wy1, wz1, 2, 2)
    return second, restrict(defect, 2, 2)


def soil_kernel(
    head_in, old_in, soil_in, ks_in, alpha_in, shape_in, span_in, out_ref,
    head_ref, old_ref, soil_ref, ks_ref, alpha_ref, shape_ref, span_ref, sems,
):
    given = (ks_in, alpha_in, shape_in, span_in, head_in, old_in, soil_in)
    held = (ks_ref, alpha_ref, shape_ref, span_ref, head_ref, old_ref, soil_ref)
    copies = [
        pltpu.make_async_copy(src, dst, sems.at[i])
        for i, (src, dst) in enumerate(zip(given, held, strict=True))
    ]
    for copy in copies:
        copy.start()
    for copy in copies:
        copy.wait()

    def cells(i, carry):
        row = pl.ds(i, 1)
        head, old, soil = head_ref[row], old_ref[row], soil_ref[row]
        ks = jnp.full(soil.shape, ks_ref[0])
        alpha = jnp.full(soil.shape, alpha_ref[0])
        shape_n = jnp.full(soil.shape, shape_ref[0])
        span = jnp.full(soil.shape, span_ref[0])
        for kind in range(1, SOILS):
            hit = soil == kind
            ks = jnp.where(hit, ks_ref[kind], ks)
            alpha = jnp.where(hit, alpha_ref[kind], alpha)
            shape_n = jnp.where(hit, shape_ref[kind], shape_n)
            span = jnp.where(hit, span_ref[kind], span)
        shape_m = 1.0 - 1.0 / shape_n
        power = jnp.exp(shape_n * jnp.log(alpha * -head))
        old_power = jnp.exp(shape_n * jnp.log(alpha * -old))
        saturation = jnp.exp(-shape_m * jnp.log1p(power))
        old_saturation = jnp.exp(-shape_m * jnp.log1p(old_power))
        portion = 1.0 / (1.0 + power)
        factor = 1.0 - jnp.exp(shape_m * jnp.log(power / (1.0 + power)))
        capacity = span * shape_m * shape_n * power / -head * saturation * portion
        out_ref[0, row] = head
        out_ref[1, row] = ks * jnp.sqrt(saturation) * factor * factor
        out_ref[2, row] = capacity + STORAGE
        out_ref[3, row] = span * (saturation - old_saturation) + STORAGE * (head - old)
        return carry

    lax.fori_loop(0, BX, cells, 0, unroll=2)


def fill_window(ref, xlow, own, xhigh, ylow, yhigh):
    ref[1 : 1 + BX, 8:24, :] = xlow
    ref[1 + BX : 1 + 2 * BX, 8:24, :] = own
    ref[1 + 2 * BX : 1 + 3 * BX, 8:24, :] = xhigh
    ref[1 : PX - 1, 0:8, :] = ylow
    ref[1 : PX - 1, 24:32, :] = yhigh


def assemble_kernel(
    xlow, own, xhigh, ylow, yhigh,
    r_ref, s_ref, di_ref, wx_ref, wy_ref, wz_ref, e2_ref,
    r1_ref, s1_ref, di1_ref, wx1_ref, wy1_ref, wz1_ref, e21_ref, msg_ref,
    h_ref, k_ref, m_ref, e1_ref,
):
    for ref in (h_ref, k_ref, s_ref, wx_ref, wy_ref, wz_ref, di_ref, r_ref, e1_ref, e2_ref):
        blank_ends(ref)
    for f, ref in enumerate((h_ref, k_ref, s_ref, m_ref)):
        fill_window(ref, xlow[f], own[f], xhigh[f], ylow[f], yhigh[f])

    def harmonic(a, b):
        total = a + b
        return jnp.where(total > 0.0, 2.0 * a * b / total, 0.0)

    def faces(i, carry):
        at = 1 + 2 * i
        k = k_ref[pl.ds(at, 2)]
        wx_ref[pl.ds(at, 2)] = harmonic(k, k_ref[pl.ds(at - 1, 2)])
        wy_ref[pl.ds(at, 2)] = harmonic(k, turn(k, 1, 1))
        wz = harmonic(k, turn(k, 1, 2))
        wz_ref[pl.ds(at, 2)] = jnp.where(iota(wz.shape, 2) == 0, 0.0, wz)
        return carry

    lax.fori_loop(0, WX // 2, faces, 0, unroll=4)

    def right_side(i, carry):
        at = 1 + 2 * i
        rows = pl.ds(at, 2)
        h, wx, wy, wz = h_ref[rows], wx_ref[rows], wy_ref[rows], wz_ref[rows]
        wx_up = wx_ref[pl.ds(at + 1, 2)]
        fy = wy * (h - turn(h, 1, 1))
        fz = wz * (h - turn(h, 1, 2) + 1.0)
        flux = wx * (h - h_ref[pl.ds(at - 1, 2)]) - wx_up * (h_ref[pl.ds(at + 1, 2)] - h)
        flux = flux + (fy - turn(fy, -1, 1)) + (fz - turn(fz, -1, 2))
        rhs = -(m_ref[rows] + flux)
        diagonal = s_ref[rows] + wx + wx_up + wy + turn(wy, -1, 1) + wz + turn(wz, -1, 2)
        di = jnp.where(diagonal > 0.0, OMEGA / diagonal, 0.0)
        r_ref[rows] = rhs
        di_ref[rows] = di
        e1_ref[rows] = rhs * di
        return carry

    lax.fori_loop(0, WX // 2, right_side, 0, unroll=4)

    def bands(i, carry):
        rows = pl.ds(1 + 2 * i, 2)
        s1, wx1, wy1, wz1 = coarsen(s_ref[rows], wx_ref[rows], wy_ref[rows], wz_ref[rows], 1, 1)
        row = pl.ds(i, 1)
        s1_ref[row], wx1_ref[row], wy1_ref[row], wz1_ref[row] = s1, wx1, wy1, wz1
        return carry

    lax.fori_loop(1, WX // 2 - 1, bands, 0, unroll=5)
    for ref in (s1_ref, wx1_ref, wy1_ref, wz1_ref):
        blank_level1(ref, 1)
    blank_level1(r1_ref, 2)
    descend_top(r_ref, e1_ref, e2_ref, s_ref, wx_ref, wy_ref, wz_ref, di_ref, r1_ref)

    s1, wx1, wy1, wz1 = s1_ref[...], wx1_ref[...], wy1_ref[...], wz1_ref[...]
    di1 = relax_factor(s1, wx1, wy1, wz1, 2, 2)
    di1_ref[...] = di1
    e21, r2 = descend_second(r1_ref[...], s1, wx1, wy1, wz1, di1)
    e21_ref[...] = e21
    bands2 = coarsen(s1, wx1, wy1, wz1, 2, 2)
    bands3 = coarsen(*(v[2:4] for v in bands2), 4, 4)
    rows = [pack_level2(v[2:4]) for v in (r2,) + bands2]
    send(msg_ref, rows + [pack_bands3(bands3)])


def again_kernel(
    xlow, own, xhigh, ylow, yhigh, rhs_ref, s_ref, di_ref, wx_ref, wy_ref, wz_ref,
    s1_ref, di1_ref, wx1_ref, wy1_ref, wz1_ref,
    u_ref, r_ref, e2_ref, r1_ref, e21_ref, msg_ref, edge_ref, pre_ref, e1_ref,
):
    for ref in (pre_ref, u_ref, r_ref, e1_ref, e2_ref):
        blank_ends(ref)
    fill_window(pre_ref, xlow[...], own[...], xhigh[...], ylow[...], yhigh[...])

    def post(i, carry):
        at = 1 + 2 * i
        rows = pl.ds(at, 2)
        v, av = operate_rows(pre_ref, s_ref, wx_ref, wy_ref, wz_ref, at, 2)
        u_ref[rows] = v + di_ref[rows] * (rhs_ref[rows] - av)
        return carry

    lax.fori_loop(0, WX // 2, post, 0, unroll=4)

    def remain(i, carry):
        at = 1 + 2 * i
        rows = pl.ds(at, 2)
        _, av = operate_rows(u_ref, s_ref, wx_ref, wy_ref, wz_ref, at, 2)
        left = rhs_ref[rows] - av
        r_ref[rows] = left
        e1_ref[rows] = left * di_ref[rows]
        return carry

    lax.fori_loop(1, WX // 2 - 1, remain, 0, unroll=5)
    descend_top(r_ref, e1_ref, e2_ref, s_ref, wx_ref, wy_ref, wz_ref, di_ref, r1_ref)
    blank_level1(r1_ref, 2)
    e21, r2 = descend_second(
        r1_ref[...], s1_ref[...], wx1_ref[...], wy1_ref[...], wz1_ref[...], di1_ref[...]
    )
    e21_ref[...] = e21
    send(msg_ref, [pack_level2(r2[2:4]), pack_ring1(e21)])
    send(edge_ref, [pack_edge1(e21)])


def message_rows(ref):
    tiles = lax.axis_size("tile")
    return lambda field, half: ref[0:tiles, field, half : half + 1, :]


def pair_rows(here, before, after):
    even = lax.axis_index("group") % 2 == 0

    def choose(first, second):
        return lambda field, half: jnp.where(even, first(field, half), second(field, half))

    one, two = message_rows(here.at[:, 0]), message_rows(here.at[:, 1])
    return choose(message_rows(before), one), choose(one, two), choose(two, message_rows(after))


def band_rows3(here, before, after):
    even = lax.axis_index("group") % 2 == 0
    six = [ref[:, 5, half : half + 1, :] for ref in (before,) for half in range(2)]
    six += [here[:, core, 5, 0:1, :] for core in range(2)]
    six += [after[:, 5, half : half + 1, :] for half in range(2)]
    return [jnp.where(even, six[i], six[i + 1]) for i in range(5)]


def unpack_level2(field, own, low, high):
    tiles = lax.axis_size("tile")
    shape = (tiles, 16, NZ)
    sub, lane = iota(shape, 1), iota(shape, 2)
    halves = []
    for half in range(2):

        def spread(pick, half=half):
            return jnp.broadcast_to(pick(field, half), shape)

        v = jnp.where(sub < 4, spread(low), jnp.where(sub < 8, spread(own), spread(high)))
        v = jnp.where((lane % 4 == sub % 4) & (sub < 12), v, 0.0)
        halves.append(pair_sum(pair_sum(v, 1, 2), 2, 2))
    return jnp.stack(halves, axis=1).reshape((2 * tiles, 16, NZ))


def pack_level3(v):
    sub, lane = iota((16, NZ), 0), iota((16, NZ), 1)
    rows = []
    for j in range(v.shape[0] // 4):
        total = jnp.zeros((16, NZ), F32)
        for q in range(4):
            chosen = ((sub == 4) & (lane % 8 == 2 * q)) | ((sub == 6) & (lane % 8 == 2 * q + 1))
            total = total + jnp.where(chosen, v[4 * j + q], 0.0)
        rows.append(jnp.sum(total, axis=0, keepdims=True))
    return rows


def pack_sums3(v):
    v = v + turn(v, -2, 1)
    sub, lane = iota((16, NZ), 0), iota((16, NZ), 1)
    rows = []
    for first in range(0, v.shape[0], 8):
        total = jnp.zeros((16, NZ), F32)
        for q in range(min(8, v.shape[0] - first)):
            total = total + jnp.where((sub == 4) & (lane % 8 == q), v[first + q], 0.0)
        rows.append(jnp.sum(total, axis=0, keepdims=True))
    return rows


def descend_third(r2, s2, wx2, wy2, wz2, di2):
    first = r2 * di2
    second = first + di2 * (r2 - operate(first, s2, wx2, wy2, wz2, 1, 4))
    return second, restrict(r2 - operate(second, s2, wx2, wy2, wz2, 1, 4), 1, 4)


def sides_kernel(here, low_ref, high_ref):
    low_ref[:, 0:5], high_ref[:, 0:5] = here[:, 0, 0:5], here[:, 1, 0:5]
    for core in range(2):
        rows = here[:, core, 5, 0:1, :]
        low_ref[:, 5, core : core + 1, :] = rows
        high_ref[:, 5, core : core + 1, :] = rows


def bands3_kernel(before, here, after, s3_ref, di3_ref, wx3_ref, wy3_ref, wz3_ref):
    s3, wx3, wy3, wz3 = unpack_bands3(band_rows3(here, before, after))
    s3_ref[...], wx3_ref[...], wy3_ref[...], wz3_ref[...] = s3, wx3, wy3, wz3
    di3_ref[...] = relax_factor(s3, wx3, wy3, wz3, 2, 8)


def third_kernel(
    before, here, after,
    r2_ref, s2_ref, di2_ref, wx2_ref, wy2_ref, wz2_ref, e22_ref, msg_ref,
):
    low, own, high = pair_rows(here, before, after)
    r2, s2, wx2, wy2, wz2 = (unpack_level2(f, own, low, high) for f in range(5))
    di2 = relax_factor(s2, wx2, wy2, wz2, 1, 4)
    r2_ref[...], s2_ref[...], di2_ref[...] = r2, s2, di2
    wx2_ref[...], wy2_ref[...], wz2_ref[...] = wx2, wy2, wz2
    e22, r3 = descend_third(r2, s2, wx2, wy2, wz2, di2)
    e22_ref[...] = e22
    s3, wx3, _, wz3 = coarsen(s2, wx2, wy2, wz2, 1, 4)
    inner = s3 + wx3 + x_high(wx3) + wz3 + turn(wz3, -8, 2)
    send(msg_ref, pack_level3(r3) + pack_sums3(inner))


def third_again_kernel(
    own, low, high, s2_ref, di2_ref, wx2_ref, wy2_ref, wz2_ref, r2_ref, e22_ref, msg_ref
):
    r2 = unpack_level2(0, message_rows(own), message_rows(low), message_rows(high))
    r2_ref[...] = r2
    e22, r3 = descend_third(
        r2, s2_ref[...], wx2_ref[...], wy2_ref[...], wz2_ref[...], di2_ref[...]
    )
    e22_ref[...] = e22
    send(msg_ref, pack_level3(r3))


def third_masks(shape):
    sub, lane = iota(shape, 1), iota(shape, 2)
    return sub // 4, (sub % 4) // 2, lane % 8


def octuple(v):
    return pair_sum(pair_sum(pair_sum(v, 1, 2), 2, 2), 4, 2)


def unpack_bands3(sources):
    shape = (sources[0].shape[0], 24, NZ)
    dev, half, slot = third_masks(shape)
    rows = jnp.broadcast_to(sources[0], shape)
    for d in range(1, 5):
        rows = jnp.where(dev == d, jnp.broadcast_to(sources[d], shape), rows)
    rows = jnp.where(dev < 5, rows, 0.0)
    return [octuple(jnp.where(slot == 2 * f + half, rows, 0.0)) for f in range(4)]


def unpack_r3(v):
    group = lax.axis_index("group")
    at = iota(v.shape, 1)
    shape = (v.shape[0], 24, NZ)
    dev, half, slot = third_masks(shape)
    rows = jnp.zeros(shape, F32)
    for d in range(5):
        near = jnp.sum(jnp.where(at == group + (d - 2), v, 0.0), axis=1, keepdims=True)
        rows = jnp.where(dev == d, jnp.broadcast_to(near, shape), rows)
    parts = [jnp.where(slot == 2 * q + half, rows, 0.0) for q in range(4)]
    return octuple(jnp.stack(parts, axis=1).reshape((4 * v.shape[0], 24, NZ)))


def line_sums(v, held):
    total = jnp.sum(v, axis=1, keepdims=True)
    lane = iota(total.shape, 2) % 8
    parts = [jnp.where(lane * held // 8 == q, total, 0.0) for q in range(held)]
    wide = jnp.stack(parts, axis=1).reshape((held * v.shape[0], 1, NZ))
    return octuple(wide[: lax.axis_size("tile")])


def solve_third(r3, line, s3, di3, wx3, wy3, wz3):
    v = jnp.broadcast_to(line, r3.shape)
    for _ in range(COARSE_SWEEPS):
        v = v + di3 * (r3 - operate(v, s3, wx3, wy3, wz3, 2, 8))
    return turn(v, -4, 1)[:, 0:16]


def near_tiles(v):
    tile = lax.axis_index("tile")
    parts = []
    for off in (-1, 0, 1):
        total = jnp.zeros((2,) + v.shape[1:], F32)
        for t in range(v.shape[0] // 2):
            total = total + jnp.where(tile + off == t, v[2 * t : 2 * t + 2], 0.0)
        parts.append(total)
    return jnp.concatenate(parts, axis=0)


def widen_y(v):
    shape = (v.shape[0], 8, NZ)
    sub = iota(shape, 1)
    parts = []
    for at in (2, 4, 6, 8):
        first = jnp.broadcast_to(v[:, at : at + 1], shape)
        second = jnp.broadcast_to(v[:, at + 1 : at + 2], shape)
        parts.append(jnp.where(sub < 4, first, second))
    return jnp.concatenate(parts, axis=1)


def climb_to_second(corr3, r2_ref, s2_ref, di2_ref, wx2_ref, wy2_ref, wz2_ref, e22_ref):
    v = e22_ref[...] + x_repeat(corr3)
    v = v + di2_ref[...] * (
        r2_ref[...]
        - operate(v, s2_ref[...], wx2_ref[...], wy2_ref[...], wz2_ref[...], 1, 4)
    )
    return x_repeat(widen_y(near_tiles(v)))


def climb_to_first(v, r1_ref, s1_ref, di1_ref, wx1_ref, wy1_ref, wz1_ref):
    return v + di1_ref[...] * (
        r1_ref[...]
        - operate(v, s1_ref[...], wx1_ref[...], wy1_ref[...], wz1_ref[...], 2, 2)
    )


def strided(ref, first, thirds, groups, rows):
    parts = [ref[pl.ds(first + j, groups, stride=rows), :] for j in range(thirds)]
    return jnp.stack(parts, axis=0)


def climb_kernel(
    third_ref, s3_ref, di3_ref, wx3_ref, wy3_ref, wz3_ref,
    r2_ref, s2_ref, di2_ref, wx2_ref, wy2_ref, wz2_ref, e22_ref,
    r1_ref, s1_ref, di1_ref, wx1_ref, wy1_ref, wz1_ref, e21_ref, e2_ref,
    pre_ref, below_ref,
    *, groups, thirds, rows,
):
    r3 = strided(third_ref, 0, thirds, groups, rows)
    below = line_sums(strided(third_ref, thirds, rows - thirds, groups, rows), 8)
    below_ref[...] = below
    corr3 = solve_third(
        unpack_r3(r3), line_sums(r3, 4) / below,
        s3_ref[...], di3_ref[...], wx3_ref[...], wy3_ref[...], wz3_ref[...],
    )
    corr2 = climb_to_second(corr3, r2_ref, s2_ref, di2_ref, wx2_ref, wy2_ref, wz2_ref, e22_ref)
    v = climb_to_first(
        e21_ref[...] + corr2, r1_ref, s1_ref, di1_ref, wx1_ref, wy1_ref, wz1_ref
    )
    own1 = x_repeat(v[4:8])
    pre_ref[...] = e2_ref[9:17, 8:24, :] + own1[:, 8:24, :]


def tile_rows(ref, off, at):
    tile = lax.axis_index("tile")
    total = jnp.zeros((2, NZ), F32)
    for t in range(lax.axis_size("tile")):
        total = total + jnp.where(tile + off == t, ref[t, at], 0.0)
    return total


def ring_row(own, low, high, off, first):
    pairs = [tile_rows(own, off, first), tile_rows(own, off, first + 1)]
    packed = [tile_rows(low, off, first + 1)[1:2]]
    packed += [pair[k : k + 1] for pair in pairs for k in range(2)]
    packed += [tile_rows(high, off, first)[0:1]]
    return spread_pairs([row[None] for row in packed], 1)


def spread_pairs(packed, height):
    shape = (height, WY, NZ)
    sub, lane = iota(shape, 1), iota(shape, 2)
    rows = jnp.zeros(shape, F32)
    for k, row in enumerate(packed):
        rows = jnp.where(sub // 4 == k + 1, jnp.broadcast_to(row, shape), rows)
    return pair_sum(jnp.where(lane % 2 == (sub // 2) % 2, rows, 0.0), 1, 2)


def last_climb_kernel(
    third_ref, below_ref, s3_ref, di3_ref, wx3_ref, wy3_ref, wz3_ref,
    low, own, high,
    r2_ref, s2_ref, di2_ref, wx2_ref, wy2_ref, wz2_ref, e22_ref,
    r1_ref, s1_ref, di1_ref, wx1_ref, wy1_ref, wz1_ref, e21_ref,
    e2_ref, rhs_ref, s_ref, di_ref, wx_ref, wy_ref, wz_ref, u_ref, r_ref,
    out_ref, left_ref, pre_ref, v_ref,
    *, groups, thirds, rows,
):
    r3 = strided(third_ref, 0, thirds, groups, rows)
    corr3 = solve_third(
        unpack_r3(r3), line_sums(r3, 4) / below_ref[...],
        s3_ref[...], di3_ref[...], wx3_ref[...], wy3_ref[...], wz3_ref[...],
    )
    corr2 = climb_to_second(corr3, r2_ref, s2_ref, di2_ref, wx2_ref, wy2_ref, wz2_ref, e22_ref)
    tiles = lax.axis_size("tile")
    middle = e21_ref[3:9]
    sub = iota(middle.shape, 1)
    edge_low = jnp.concatenate([low[tiles, k] for k in range(3)], axis=0)[:, None]
    edge_high = jnp.concatenate([high[tiles, k] for k in range(3)], axis=0)[:, None]
    nothing = jnp.zeros_like(edge_low)
    edges = spread_pairs([edge_low] + [nothing] * 4 + [edge_high], 6)
    kept = (sub >= 6) & (sub < 26)
    middle = jnp.where(kept, middle, edges)
    blank = jnp.zeros((2, WY, NZ), F32)
    first, last = ring_row(own, low, high, -1, 3), ring_row(own, low, high, 1, 1)
    e21 = jnp.concatenate([blank, first, middle, last, blank], axis=0)
    v = climb_to_first(e21 + corr2, r1_ref, s1_ref, di1_ref, wx1_ref, wy1_ref, wz1_ref)
    pre_ref[7:19] = e2_ref[7:19] + x_repeat(v[3:9])

    def post(i, carry):
        at = 8 + 2 * i
        here = pl.ds(at, 2)
        v, av = operate_rows(pre_ref, s_ref, wx_ref, wy_ref, wz_ref, at, 2)
        v_ref[here] = u_ref[here] + v + di_ref[here] * (r_ref[here] - av)
        return carry

    lax.fori_loop(0, BX // 2 + 1, post, 0, unroll=True)

    def remain(i, carry):
        at = 9 + 2 * i
        v, av = operate_rows(v_ref, s_ref, wx_ref, wy_ref, wz_ref, at, 2)
        left = rhs_ref[pl.ds(at, 2)] - av
        out_ref[pl.ds(2 * i, 2)] = v[:, 8:24]
        left_ref[pl.ds(2 * i, 2)] = left[:, 8:24]
        return carry

    lax.fori_loop(0, BX // 2, remain, 0, unroll=True)


def call(body, outs, operands, scratch=()):
    cells = sum(math.prod(shape) for shape in outs)
    vmem = pl.BlockSpec(memory_space=pltpu.VMEM)
    return pl.pallas_call(
        body,
        out_shape=[jax.ShapeDtypeStruct(shape, F32) for shape in outs],
        in_specs=[vmem] * len(operands),
        out_specs=[vmem] * len(outs),
        scratch_shapes=[pltpu.VMEM(shape, F32) for shape in scratch],
        compiler_params=pltpu.CompilerParams(vmem_limit_bytes=16 * 1024 * 1024),
        cost_estimate=pl.CostEstimate(
            flops=20 * cells, bytes_accessed=8 * cells, transcendentals=0
        ),
    )(*operands)


def beside(to_low, to_high, axis, step=1):
    ends = lax.axis_size(axis) - step
    from_low = lax.ppermute(to_high, axis, [(i, i + step) for i in range(ends)])
    from_high = lax.ppermute(to_low, axis, [(i + step, i) for i in range(ends)])
    return from_low, from_high


def surround(cells, dim):
    low, high = beside(cells, cells, "tile")
    ydim = dim + 1

    def part(first):
        pieces = [lax.slice_in_dim(v, first, first + 8, axis=ydim) for v in (low, cells, high)]
        return jnp.concatenate(pieces, axis=dim)

    ylow, yhigh = beside(part(0), part(BY - 8), "group")
    return low, cells, high, ylow, yhigh


def everyone(blocks, axis):
    return lax.all_to_all(blocks, axis, 0, 0, tiled=True)


def pairs_of_tiles(block):
    tiles, groups = lax.axis_size("tile"), lax.axis_size("group")
    members = [
        [t * groups + 2 * pair + core for t in range(tiles) for core in range(2)]
        for pair in range(groups // 2)
    ]
    given = lax.all_to_all(
        block, ("tile", "group"), 0, 0, axis_index_groups=members, tiled=True
    )
    return given.reshape((tiles, 2) + block.shape[1:])


def shards(pressure_head, old_head, soil_type, conduct_sat, alpha_param, shape_param, water_span):
    tiles, groups = lax.axis_size("tile"), lax.axis_size("group")
    thirds = tiles // 4
    top, one, two = (PX, WY, NZ), (L1X, WY, NZ), (2 * tiles, 16, NZ)
    three, line = (tiles, 24, NZ), (tiles, 1, NZ)
    rows_once, rows_again = thirds + -(-tiles // 8), thirds

    fields = pl.pallas_call(
        soil_kernel,
        out_shape=jax.ShapeDtypeStruct((4, BX, BY, NZ), F32),
        in_specs=[pl.BlockSpec(memory_space=pltpu.HBM)] * 7,
        out_specs=pl.BlockSpec(memory_space=pltpu.VMEM),
        scratch_shapes=[
            pltpu.VMEM((BX, BY, NZ), F32),
            pltpu.VMEM((BX, BY, NZ), F32),
            pltpu.VMEM((BX, BY, NZ), jnp.int32),
            *[pltpu.SMEM((SOILS,), F32) for _ in range(4)],
            pltpu.SemaphoreType.DMA((7,)),
        ],
    )(pressure_head, old_head, soil_type, conduct_sat, alpha_param, shape_param, water_span)
    around = surround(fields, 1)
    rhs, s0, di0, wx0, wy0, wz0, e2, r1, s1, di1, wx1, wy1, wz1, e21, msg = call(
        assemble_kernel,
        [top] * 7 + [one] * 7 + [(2 * tiles, 6, 2, NZ)],
        list(around),
        [top] * 4,
    )
    bands0 = [s0, di0, wx0, wy0, wz0]
    bands1 = [s1, di1, wx1, wy1, wz1]

    here = pairs_of_tiles(msg)
    to_low, to_high = call(sides_kernel, [(tiles, 6, 2, NZ)] * 2, [here])
    before, after = beside(to_low, to_high, "group", 2)
    r2, s2, di2, wx2, wy2, wz2, e22, msg = call(
        third_kernel,
        [two] * 7 + [(groups, rows_once, 1, NZ)],
        [before, here, after],
    )
    bands3 = call(bands3_kernel, [three] * 5, [before, here, after])
    bands2 = [s2, di2, wx2, wy2, wz2]
    third = everyone(msg, "group").reshape(groups * rows_once, NZ)
    pre, below = call(
        functools.partial(climb_kernel, groups=groups, thirds=thirds, rows=rows_once),
        [(BX, BY, NZ), line],
        [third, *bands3, r2, *bands2, e22, r1, *bands1, e21, e2],
    )

    around = surround(pre, 0)
    u, rem, e2, r1, e21, msg, edge = call(
        again_kernel,
        [top] * 3 + [one] * 2 + [(tiles, 5, 2, NZ), (1, 5, 2, NZ)],
        [*around, rhs, *bands0, *bands1],
        [top] * 2,
    )
    own = jnp.concatenate([everyone(msg, "tile"), edge], axis=0)
    low, high = beside(own, own, "group")
    r2, e22, msg = call(
        third_again_kernel,
        [two] * 2 + [(groups, rows_again, 1, NZ)],
        [own, low, high, *bands2],
    )
    third = everyone(msg, "group").reshape(groups * rows_again, NZ)
    update, remainder = call(
        functools.partial(last_climb_kernel, groups=groups, thirds=thirds, rows=rows_again),
        [(BX, BY, NZ)] * 2,
        [third, below, *bands3, low, own, high, r2, *bands2, e22, r1, *bands1, e21]
        + [e2, rhs, *bands0, u, rem],
        [top] * 2,
    )
    return update, remainder


def solution(mesh):
    spec = P("tile", "group", None)
    return jax.shard_map(
        shards,
        mesh=mesh,
        in_specs=(spec, spec, spec, P(), P(), P(), P()),
        out_specs=(spec, spec),
        check_vma=False,
    )
```

```python
import functools
import math

import jax
import jax.numpy as jnp
from jax import lax
from jax.experimental import pallas as pl
from jax.experimental.pallas import tpu as pltpu
from jax.sharding import PartitionSpec as P

OMEGA = 2.0 / 3.0
STORAGE = 0.01
COARSE_SWEEPS = 4
SOILS = 12

BX, BY, NZ = 8, 16, 128
WX, WY = 24, 32
PX = WX + 2
L1X = WX // 2
F32 = jnp.float32


def iota(shape, dim):
    return lax.broadcasted_iota(jnp.int32, shape, dim)


def turn(v, step, axis):
    size = v.shape[axis]
    return pltpu.roll(v, step % size, axis)


def bit_of(v, step, axis):
    return (iota(v.shape, axis) // step) % 2 == 0


def pair_sum(v, step, axis):
    return v + jnp.where(bit_of(v, step, axis), turn(v, -step, axis), turn(v, step, axis))


def pair_low(v, step, axis):
    return jnp.where(bit_of(v, step, axis), v, turn(v, step, axis))


def x_low(v):
    return jnp.concatenate([v[:1], v[:-1]], axis=0)


def x_high(v):
    return jnp.concatenate([v[1:], jnp.zeros_like(v[:1])], axis=0)


def x_pair(v):
    return jnp.sum(v.reshape((v.shape[0] // 2, 2) + v.shape[1:]), axis=1)


def x_even(v):
    return v.reshape((v.shape[0] // 2, 2) + v.shape[1:])[:, 0]


def x_repeat(v):
    size = v.shape[0]
    wide = jnp.broadcast_to(v[:, None], (size, 2) + v.shape[1:])
    return wide.reshape((2 * size,) + v.shape[1:])


def operate(v, storage, wx, wy, wz, sy, sz):
    fx = wx * (v - x_low(v))
    fy = wy * (v - turn(v, sy, 1))
    fz = wz * (v - turn(v, sz, 2))
    flux = (fx - x_high(fx)) + (fy - turn(fy, -sy, 1)) + (fz - turn(fz, -sz, 2))
    return storage * v + flux


def relax_factor(storage, wx, wy, wz, sy, sz):
    diagonal = storage + wx + x_high(wx) + wy + turn(wy, -sy, 1) + wz + turn(wz, -sz, 2)
    return jnp.where(diagonal > 0.0, OMEGA / diagonal, 0.0)


def restrict(v, sy, sz):
    return pair_sum(pair_sum(x_pair(v), sy, 1), sz, 2)


def coarsen(storage, wx, wy, wz, sy, sz):
    return (
        restrict(storage, sy, sz),
        pair_sum(pair_sum(x_even(wx), sy, 1), sz, 2),
        pair_low(pair_sum(x_pair(wy), sz, 2), sy, 1),
        pair_low(pair_sum(x_pair(wz), sy, 1), sz, 2),
    )


def operate_rows(v_ref, s_ref, wx_ref, wy_ref, wz_ref, at, size):
    v = v_ref[pl.ds(at, size)]
    wx = wx_ref[pl.ds(at, size)]
    fy = wy_ref[pl.ds(at, size)] * (v - turn(v, 1, 1))
    fz = wz_ref[pl.ds(at, size)] * (v - turn(v, 1, 2))
    flux = wx * (v - v_ref[pl.ds(at - 1, size)])
    flux = flux - wx_ref[pl.ds(at + 1, size)] * (v_ref[pl.ds(at + 1, size)] - v)
    flux = flux + (fy - turn(fy, -1, 1)) + (fz - turn(fz, -1, 2))
    return v, s_ref[pl.ds(at, size)] * v + flux


def blank_ends(ref):
    ref[0] = jnp.zeros((WY, NZ), F32)
    ref[PX - 1] = jnp.zeros((WY, NZ), F32)


def blank_level1(ref, size):
    ref[0:size] = jnp.zeros((size, WY, NZ), F32)
    ref[L1X - size :] = jnp.zeros((size, WY, NZ), F32)


def pack_level2(v):
    sub, lane = iota(v.shape, 1), iota(v.shape, 2)
    chosen = (sub >= 8) & (sub < 24) & (sub % 4 == 0) & ((sub - 8) // 4 == lane % 4)
    return jnp.sum(jnp.where(chosen, v, 0.0), axis=1)


def send(msg_ref, rows):
    rows = list(rows)
    parts, height = msg_ref.shape[1:3]
    spare = parts * height - sum(row.shape[0] for row in rows)
    if spare:
        rows.append(jnp.zeros((spare, NZ), F32))
    whole = jnp.concatenate(rows, axis=0)
    for part in range(parts):
        piece = whole[part * height : (part + 1) * height]
        for peer in range(msg_ref.shape[0]):
            msg_ref[peer, part] = piece


def pack_bands3(fields):
    sub, lane = iota((1, WY, NZ), 1), iota((1, WY, NZ), 2)
    total = jnp.zeros((1, WY, NZ), F32)
    for f, v in enumerate(fields):
        chosen = ((sub == 8) & (lane % 8 == 2 * f)) | ((sub == 16) & (lane % 8 == 2 * f + 1))
        total = total + jnp.where(chosen, v, 0.0)
    return jnp.sum(total, axis=1)


def pack_ring1(v):
    sub, lane = iota((2, WY, NZ), 1), iota((2, WY, NZ), 2)
    rows = v[5:7]
    parts = []
    for k in range(4):
        chosen = ((sub == 8 + 4 * k) & (lane % 2 == 0)) | ((sub == 10 + 4 * k) & (lane % 2 == 1))
        parts.append(jnp.sum(jnp.where(chosen, rows, 0.0), axis=1, keepdims=True))
    return jnp.concatenate([part[x] for x in range(2) for part in parts], axis=0)


def pack_edge1(v):
    sub, lane = iota((6, WY, NZ), 1), iota((6, WY, NZ), 2)
    chosen = ((sub == 20) & (lane % 2 == 0)) | ((sub == 10) & (lane % 2 == 1))
    return jnp.sum(jnp.where(chosen, v[3:9], 0.0), axis=1)


def descend_top(r_ref, e1_ref, e2_ref, s_ref, wx_ref, wy_ref, wz_ref, di_ref, r1_ref):
    def second(i, carry):
        at = 1 + 2 * i
        v, av = operate_rows(e1_ref, s_ref, wx_ref, wy_ref, wz_ref, at, 2)
        e2_ref[pl.ds(at, 2)] = v + di_ref[pl.ds(at, 2)] * (r_ref[pl.ds(at, 2)] - av)
        return carry

    lax.fori_loop(1, WX // 2 - 1, second, 0, unroll=5)

    def third(i, carry):
        at = 1 + 2 * i
        _, av = operate_rows(e2_ref, s_ref, wx_ref, wy_ref, wz_ref, at, 2)
        r1_ref[pl.ds(i, 1)] = restrict(r_ref[pl.ds(at, 2)] - av, 1, 1)
        return carry

    lax.fori_loop(2, WX // 2 - 2, third, 0, unroll=4)


def descend_second(r1, s1, wx1, wy1, wz1, di1):
    first = r1 * di1
    second = first + di1 * (r1 - operate(first, s1, wx1, wy1, wz1, 2, 2))
    defect = r1 - operate(second, s1, wx1, wy1, wz1, 2, 2)
    return second, restrict(defect, 2, 2)


def soil_kernel(
    head_in, old_in, soil_in, ks_in, alpha_in, shape_in, span_in, out_ref,
    head_ref, old_ref, soil_ref, ks_ref, alpha_ref, shape_ref, span_ref, sems,
):
    given = (ks_in, alpha_in, shape_in, span_in, head_in, old_in, soil_in)
    held = (ks_ref, alpha_ref, shape_ref, span_ref, head_ref, old_ref, soil_ref)
    copies = [
        pltpu.make_async_copy(src, dst, sems.at[i])
        for i, (src, dst) in enumerate(zip(given, held, strict=True))
    ]
    for copy in copies:
        copy.start()
    for copy in copies:
        copy.wait()

    def cells(i, carry):
        row = pl.ds(i, 1)
        head, old, soil = head_ref[row], old_ref[row], soil_ref[row]
        ks = jnp.full(soil.shape, ks_ref[0])
        alpha = jnp.full(soil.shape, alpha_ref[0])
        shape_n = jnp.full(soil.shape, shape_ref[0])
        span = jnp.full(soil.shape, span_ref[0])
        for kind in range(1, SOILS):
            hit = soil == kind
            ks = jnp.where(hit, ks_ref[kind], ks)
            alpha = jnp.where(hit, alpha_ref[kind], alpha)
            shape_n = jnp.where(hit, shape_ref[kind], shape_n)
            span = jnp.where(hit, span_ref[kind], span)
        shape_m = 1.0 - 1.0 / shape_n
        power = jnp.exp(shape_n * jnp.log(alpha * -head))
        old_power = jnp.exp(shape_n * jnp.log(alpha * -old))
        saturation = jnp.exp(-shape_m * jnp.log1p(power))
        old_saturation = jnp.exp(-shape_m * jnp.log1p(old_power))
        portion = 1.0 / (1.0 + power)
        factor = 1.0 - jnp.exp(shape_m * jnp.log(power / (1.0 + power)))
        capacity = span * shape_m * shape_n * power / -head * saturation * portion
        out_ref[0, row] = head
        out_ref[1, row] = ks * jnp.sqrt(saturation) * factor * factor
        out_ref[2, row] = capacity + STORAGE
        out_ref[3, row] = span * (saturation - old_saturation) + STORAGE * (head - old)
        return carry

    lax.fori_loop(0, BX, cells, 0, unroll=2)


def fill_window(ref, xlow, own, xhigh, ylow, yhigh):
    ref[1 : 1 + BX, 8:24, :] = xlow
    ref[1 + BX : 1 + 2 * BX, 8:24, :] = own
    ref[1 + 2 * BX : 1 + 3 * BX, 8:24, :] = xhigh
    ref[1 : PX - 1, 0:8, :] = ylow
    ref[1 : PX - 1, 24:32, :] = yhigh


def assemble_kernel(
    xlow, own, xhigh, ylow, yhigh,
    r_ref, s_ref, di_ref, wx_ref, wy_ref, wz_ref, e2_ref,
    r1_ref, s1_ref, di1_ref, wx1_ref, wy1_ref, wz1_ref, e21_ref, msg_ref,
    h_ref, k_ref, m_ref, e1_ref,
):
    for ref in (h_ref, k_ref, s_ref, wx_ref, wy_ref, wz_ref, di_ref, r_ref, e1_ref, e2_ref):
        blank_ends(ref)
    for f, ref in enumerate((h_ref, k_ref, s_ref, m_ref)):
        fill_window(ref, xlow[f], own[f], xhigh[f], ylow[f], yhigh[f])

    def harmonic(a, b):
        total = a + b
        return jnp.where(total > 0.0, 2.0 * a * b / total, 0.0)

    def faces(i, carry):
        at = 1 + 2 * i
        k = k_ref[pl.ds(at, 2)]
        wx_ref[pl.ds(at, 2)] = harmonic(k, k_ref[pl.ds(at - 1, 2)])
        wy_ref[pl.ds(at, 2)] = harmonic(k, turn(k, 1, 1))
        wz = harmonic(k, turn(k, 1, 2))
        wz_ref[pl.ds(at, 2)] = jnp.where(iota(wz.shape, 2) == 0, 0.0, wz)
        return carry

    lax.fori_loop(0, WX // 2, faces, 0, unroll=4)

    def right_side(i, carry):
        at = 1 + 2 * i
        rows = pl.ds(at, 2)
        h, wx, wy, wz = h_ref[rows], wx_ref[rows], wy_ref[rows], wz_ref[rows]
        wx_up = wx_ref[pl.ds(at + 1, 2)]
        fy = wy * (h - turn(h, 1, 1))
        fz = wz * (h - turn(h, 1, 2) + 1.0)
        flux = wx * (h - h_ref[pl.ds(at - 1, 2)]) - wx_up * (h_ref[pl.ds(at + 1, 2)] - h)
        flux = flux + (fy - turn(fy, -1, 1)) + (fz - turn(fz, -1, 2))
        rhs = -(m_ref[rows] + flux)
        diagonal = s_ref[rows] + wx + wx_up + wy + turn(wy, -1, 1) + wz + turn(wz, -1, 2)
        di = jnp.where(diagonal > 0.0, OMEGA / diagonal, 0.0)
        r_ref[rows] = rhs
        di_ref[rows] = di
        e1_ref[rows] = rhs * di
        return carry

    lax.fori_loop(0, WX // 2, right_side, 0, unroll=4)

    def bands(i, carry):
        rows = pl.ds(1 + 2 * i, 2)
        s1, wx1, wy1, wz1 = coarsen(s_ref[rows], wx_ref[rows], wy_ref[rows], wz_ref[rows], 1, 1)
        row = pl.ds(i, 1)
        s1_ref[row], wx1_ref[row], wy1_ref[row], wz1_ref[row] = s1, wx1, wy1, wz1
        return carry

    lax.fori_loop(1, WX // 2 - 1, bands, 0, unroll=5)
    for ref in (s1_ref, wx1_ref, wy1_ref, wz1_ref):
        blank_level1(ref, 1)
    blank_level1(r1_ref, 2)
    descend_top(r_ref, e1_ref, e2_ref, s_ref, wx_ref, wy_ref, wz_ref, di_ref, r1_ref)

    s1, wx1, wy1, wz1 = s1_ref[...], wx1_ref[...], wy1_ref[...], wz1_ref[...]
    di1 = relax_factor(s1, wx1, wy1, wz1, 2, 2)
    di1_ref[...] = di1
    e21, r2 = descend_second(r1_ref[...], s1, wx1, wy1, wz1, di1)
    e21_ref[...] = e21
    bands2 = coarsen(s1, wx1, wy1, wz1, 2, 2)
    bands3 = coarsen(*(v[2:4] for v in bands2), 4, 4)
    rows = [pack_level2(v[2:4]) for v in (r2,) + bands2]
    send(msg_ref, rows + [pack_bands3(bands3)])


def again_kernel(
    xlow, own, xhigh, ylow, yhigh, rhs_ref, s_ref, di_ref, wx_ref, wy_ref, wz_ref,
    s1_ref, di1_ref, wx1_ref, wy1_ref, wz1_ref,
    u_ref, r_ref, e2_ref, r1_ref, e21_ref, msg_ref, edge_ref, pre_ref, e1_ref,
):
    for ref in (pre_ref, u_ref, r_ref, e1_ref, e2_ref):
        blank_ends(ref)
    fill_window(pre_ref, xlow[...], own[...], xhigh[...], ylow[...], yhigh[...])

    def post(i, carry):
        at = 1 + 2 * i
        rows = pl.ds(at, 2)
        v, av = operate_rows(pre_ref, s_ref, wx_ref, wy_ref, wz_ref, at, 2)
        u_ref[rows] = v + di_ref[rows] * (rhs_ref[rows] - av)
        return carry

    lax.fori_loop(0, WX // 2, post, 0, unroll=4)

    def remain(i, carry):
        at = 1 + 2 * i
        rows = pl.ds(at, 2)
        _, av = operate_rows(u_ref, s_ref, wx_ref, wy_ref, wz_ref, at, 2)
        left = rhs_ref[rows] - av
        r_ref[rows] = left
        e1_ref[rows] = left * di_ref[rows]
        return carry

    lax.fori_loop(1, WX // 2 - 1, remain, 0, unroll=5)
    descend_top(r_ref, e1_ref, e2_ref, s_ref, wx_ref, wy_ref, wz_ref, di_ref, r1_ref)
    blank_level1(r1_ref, 2)
    e21, r2 = descend_second(
        r1_ref[...], s1_ref[...], wx1_ref[...], wy1_ref[...], wz1_ref[...], di1_ref[...]
    )
    e21_ref[...] = e21
    send(msg_ref, [pack_level2(r2[2:4]), pack_ring1(e21)])
    send(edge_ref, [pack_edge1(e21)])


def message_rows(ref):
    tiles = lax.axis_size("tile")
    return lambda field, half: ref[0:tiles, field, half : half + 1, :]


def pair_rows(here, before, after):
    even = lax.axis_index("group") % 2 == 0

    def choose(first, second):
        return lambda field, half: jnp.where(even, first(field, half), second(field, half))

    one, two = message_rows(here.at[:, 0]), message_rows(here.at[:, 1])
    return choose(message_rows(before), one), choose(one, two), choose(two, message_rows(after))


def band_rows3(here, before, after):
    even = lax.axis_index("group") % 2 == 0
    six = [ref[:, 5, half : half + 1, :] for ref in (before,) for half in range(2)]
    six += [here[:, core, 5, 0:1, :] for core in range(2)]
    six += [after[:, 5, half : half + 1, :] for half in range(2)]
    return [jnp.where(even, six[i], six[i + 1]) for i in range(5)]


def unpack_level2(field, own, low, high):
    tiles = lax.axis_size("tile")
    shape = (tiles, 16, NZ)
    sub, lane = iota(shape, 1), iota(shape, 2)
    halves = []
    for half in range(2):

        def spread(pick, half=half):
            return jnp.broadcast_to(pick(field, half), shape)

        v = jnp.where(sub < 4, spread(low), jnp.where(sub < 8, spread(own), spread(high)))
        v = jnp.where((lane % 4 == sub % 4) & (sub < 12), v, 0.0)
        halves.append(pair_sum(pair_sum(v, 1, 2), 2, 2))
    return jnp.stack(halves, axis=1).reshape((2 * tiles, 16, NZ))


def pack_level3(v):
    sub, lane = iota((16, NZ), 0), iota((16, NZ), 1)
    rows = []
    for j in range(v.shape[0] // 4):
        total = jnp.zeros((16, NZ), F32)
        for q in range(4):
            chosen = ((sub == 4) & (lane % 8 == 2 * q)) | ((sub == 6) & (lane % 8 == 2 * q + 1))
            total = total + jnp.where(chosen, v[4 * j + q], 0.0)
        rows.append(jnp.sum(total, axis=0, keepdims=True))
    return rows


def pack_sums3(v):
    v = v + turn(v, -2, 1)
    sub, lane = iota((16, NZ), 0), iota((16, NZ), 1)
    rows = []
    for first in range(0, v.shape[0], 8):
        total = jnp.zeros((16, NZ), F32)
        for q in range(min(8, v.shape[0] - first)):
            total = total + jnp.where((sub == 4) & (lane % 8 == q), v[first + q], 0.0)
        rows.append(jnp.sum(total, axis=0, keepdims=True))
    return rows


def descend_third(r2, s2, wx2, wy2, wz2, di2):
    first = r2 * di2
    second = first + di2 * (r2 - operate(first, s2, wx2, wy2, wz2, 1, 4))
    return second, restrict(r2 - operate(second, s2, wx2, wy2, wz2, 1, 4), 1, 4)


def sides_kernel(here, low_ref, high_ref):
    low_ref[:, 0:5], high_ref[:, 0:5] = here[:, 0, 0:5], here[:, 1, 0:5]
    for core in range(2):
        rows = here[:, core, 5, 0:1, :]
        low_ref[:, 5, core : core + 1, :] = rows
        high_ref[:, 5, core : core + 1, :] = rows


def third_kernel(
    before, here, after,
    r2_ref, s2_ref, di2_ref, wx2_ref, wy2_ref, wz2_ref, e22_ref,
    s3_ref, di3_ref, wx3_ref, wy3_ref, wz3_ref, msg_ref,
):
    s3, wx3, wy3, wz3 = unpack_bands3(band_rows3(here, before, after))
    s3_ref[...], wx3_ref[...], wy3_ref[...], wz3_ref[...] = s3, wx3, wy3, wz3
    di3_ref[...] = relax_factor(s3, wx3, wy3, wz3, 2, 8)
    low, own, high = pair_rows(here, before, after)
    r2, s2, wx2, wy2, wz2 = (unpack_level2(f, own, low, high) for f in range(5))
    di2 = relax_factor(s2, wx2, wy2, wz2, 1, 4)
    r2_ref[...], s2_ref[...], di2_ref[...] = r2, s2, di2
    wx2_ref[...], wy2_ref[...], wz2_ref[...] = wx2, wy2, wz2
    e22, r3 = descend_third(r2, s2, wx2, wy2, wz2, di2)
    e22_ref[...] = e22
    s3, wx3, _, wz3 = coarsen(s2, wx2, wy2, wz2, 1, 4)
    inner = s3 + wx3 + x_high(wx3) + wz3 + turn(wz3, -8, 2)
    send(msg_ref, pack_level3(r3) + pack_sums3(inner))


def third_again_kernel(
    own, low, high, s2_ref, di2_ref, wx2_ref, wy2_ref, wz2_ref, r2_ref, e22_ref, msg_ref
):
    r2 = unpack_level2(0, message_rows(own), message_rows(low), message_rows(high))
    r2_ref[...] = r2
    e22, r3 = descend_third(
        r2, s2_ref[...], wx2_ref[...], wy2_ref[...], wz2_ref[...], di2_ref[...]
    )
    e22_ref[...] = e22
    send(msg_ref, pack_level3(r3))


def third_masks(shape):
    sub, lane = iota(shape, 1), iota(shape, 2)
    return sub // 4, (sub % 4) // 2, lane % 8


def octuple(v):
    return pair_sum(pair_sum(pair_sum(v, 1, 2), 2, 2), 4, 2)


def unpack_bands3(sources):
    shape = (sources[0].shape[0], 24, NZ)
    dev, half, slot = third_masks(shape)
    rows = jnp.broadcast_to(sources[0], shape)
    for d in range(1, 5):
        rows = jnp.where(dev == d, jnp.broadcast_to(sources[d], shape), rows)
    rows = jnp.where(dev < 5, rows, 0.0)
    return [octuple(jnp.where(slot == 2 * f + half, rows, 0.0)) for f in range(4)]


def unpack_r3(v):
    group = lax.axis_index("group")
    at = iota(v.shape, 1)
    shape = (v.shape[0], 24, NZ)
    dev, half, slot = third_masks(shape)
    rows = jnp.zeros(shape, F32)
    for d in range(5):
        near = jnp.sum(jnp.where(at == group + (d - 2), v, 0.0), axis=1, keepdims=True)
        rows = jnp.where(dev == d, jnp.broadcast_to(near, shape), rows)
    parts = [jnp.where(slot == 2 * q + half, rows, 0.0) for q in range(4)]
    return octuple(jnp.stack(parts, axis=1).reshape((4 * v.shape[0], 24, NZ)))


def line_sums(v, held):
    total = jnp.sum(v, axis=1, keepdims=True)
    lane = iota(total.shape, 2) % 8
    parts = [jnp.where(lane * held // 8 == q, total, 0.0) for q in range(held)]
    wide = jnp.stack(parts, axis=1).reshape((held * v.shape[0], 1, NZ))
    return octuple(wide[: lax.axis_size("tile")])


def solve_third(r3, line, s3, di3, wx3, wy3, wz3):
    v = jnp.broadcast_to(line, r3.shape)
    for _ in range(COARSE_SWEEPS):
        v = v + di3 * (r3 - operate(v, s3, wx3, wy3, wz3, 2, 8))
    return turn(v, -4, 1)[:, 0:16]


def near_tiles(v):
    tile = lax.axis_index("tile")
    parts = []
    for off in (-1, 0, 1):
        total = jnp.zeros((2,) + v.shape[1:], F32)
        for t in range(v.shape[0] // 2):
            total = total + jnp.where(tile + off == t, v[2 * t : 2 * t + 2], 0.0)
        parts.append(total)
    return jnp.concatenate(parts, axis=0)


def widen_y(v):
    shape = (v.shape[0], 8, NZ)
    sub = iota(shape, 1)
    parts = []
    for at in (2, 4, 6, 8):
        first = jnp.broadcast_to(v[:, at : at + 1], shape)
        second = jnp.broadcast_to(v[:, at + 1 : at + 2], shape)
        parts.append(jnp.where(sub < 4, first, second))
    return jnp.concatenate(parts, axis=1)


def climb_to_second(corr3, r2_ref, s2_ref, di2_ref, wx2_ref, wy2_ref, wz2_ref, e22_ref):
    v = e22_ref[...] + x_repeat(corr3)
    v = v + di2_ref[...] * (
        r2_ref[...]
        - operate(v, s2_ref[...], wx2_ref[...], wy2_ref[...], wz2_ref[...], 1, 4)
    )
    return x_repeat(widen_y(near_tiles(v)))


def climb_to_first(v, r1_ref, s1_ref, di1_ref, wx1_ref, wy1_ref, wz1_ref):
    return v + di1_ref[...] * (
        r1_ref[...]
        - operate(v, s1_ref[...], wx1_ref[...], wy1_ref[...], wz1_ref[...], 2, 2)
    )


def strided(ref, first, thirds, groups, rows):
    parts = [ref[pl.ds(first + j, groups, stride=rows), :] for j in range(thirds)]
    return jnp.stack(parts, axis=0)


def climb_kernel(
    third_ref, s3_ref, di3_ref, wx3_ref, wy3_ref, wz3_ref,
    r2_ref, s2_ref, di2_ref, wx2_ref, wy2_ref, wz2_ref, e22_ref,
    r1_ref, s1_ref, di1_ref, wx1_ref, wy1_ref, wz1_ref, e21_ref, e2_ref,
    pre_ref, below_ref,
    *, groups, thirds, rows,
):
    r3 = strided(third_ref, 0, thirds, groups, rows)
    below = line_sums(strided(third_ref, thirds, rows - thirds, groups, rows), 8)
    below_ref[...] = below
    corr3 = solve_third(
        unpack_r3(r3), line_sums(r3, 4) / below,
        s3_ref[...], di3_ref[...], wx3_ref[...], wy3_ref[...], wz3_ref[...],
    )
    corr2 = climb_to_second(corr3, r2_ref, s2_ref, di2_ref, wx2_ref, wy2_ref, wz2_ref, e22_ref)
    v = climb_to_first(
        e21_ref[...] + corr2, r1_ref, s1_ref, di1_ref, wx1_ref, wy1_ref, wz1_ref
    )
    own1 = x_repeat(v[4:8])
    pre_ref[...] = e2_ref[9:17, 8:24, :] + own1[:, 8:24, :]


def tile_rows(ref, off, at):
    tile = lax.axis_index("tile")
    total = jnp.zeros((2, NZ), F32)
    for t in range(lax.axis_size("tile")):
        total = total + jnp.where(tile + off == t, ref[t, at], 0.0)
    return total


def ring_row(own, low, high, off, first):
    pairs = [tile_rows(own, off, first), tile_rows(own, off, first + 1)]
    packed = [tile_rows(low, off, first + 1)[1:2]]
    packed += [pair[k : k + 1] for pair in pairs for k in range(2)]
    packed += [tile_rows(high, off, first)[0:1]]
    return spread_pairs([row[None] for row in packed], 1)


def spread_pairs(packed, height):
    shape = (height, WY, NZ)
    sub, lane = iota(shape, 1), iota(shape, 2)
    rows = jnp.zeros(shape, F32)
    for k, row in enumerate(packed):
        rows = jnp.where(sub // 4 == k + 1, jnp.broadcast_to(row, shape), rows)
    return pair_sum(jnp.where(lane % 2 == (sub // 2) % 2, rows, 0.0), 1, 2)


def last_climb_kernel(
    third_ref, below_ref, s3_ref, di3_ref, wx3_ref, wy3_ref, wz3_ref,
    low, own, high,
    r2_ref, s2_ref, di2_ref, wx2_ref, wy2_ref, wz2_ref, e22_ref,
    r1_ref, s1_ref, di1_ref, wx1_ref, wy1_ref, wz1_ref, e21_ref,
    e2_ref, rhs_ref, s_ref, di_ref, wx_ref, wy_ref, wz_ref, u_ref, r_ref,
    out_ref, left_ref, pre_ref, v_ref,
    *, groups, thirds, rows,
):
    r3 = strided(third_ref, 0, thirds, groups, rows)
    corr3 = solve_third(
        unpack_r3(r3), line_sums(r3, 4) / below_ref[...],
        s3_ref[...], di3_ref[...], wx3_ref[...], wy3_ref[...], wz3_ref[...],
    )
    corr2 = climb_to_second(corr3, r2_ref, s2_ref, di2_ref, wx2_ref, wy2_ref, wz2_ref, e22_ref)
    tiles = lax.axis_size("tile")
    middle = e21_ref[3:9]
    sub = iota(middle.shape, 1)
    edge_low = jnp.concatenate([low[tiles, k] for k in range(3)], axis=0)[:, None]
    edge_high = jnp.concatenate([high[tiles, k] for k in range(3)], axis=0)[:, None]
    nothing = jnp.zeros_like(edge_low)
    edges = spread_pairs([edge_low] + [nothing] * 4 + [edge_high], 6)
    kept = (sub >= 6) & (sub < 26)
    middle = jnp.where(kept, middle, edges)
    blank = jnp.zeros((2, WY, NZ), F32)
    first, last = ring_row(own, low, high, -1, 3), ring_row(own, low, high, 1, 1)
    e21 = jnp.concatenate([blank, first, middle, last, blank], axis=0)
    v = climb_to_first(e21 + corr2, r1_ref, s1_ref, di1_ref, wx1_ref, wy1_ref, wz1_ref)
    pre_ref[7:19] = e2_ref[7:19] + x_repeat(v[3:9])

    def post(i, carry):
        at = 8 + 2 * i
        here = pl.ds(at, 2)
        v, av = operate_rows(pre_ref, s_ref, wx_ref, wy_ref, wz_ref, at, 2)
        v_ref[here] = u_ref[here] + v + di_ref[here] * (r_ref[here] - av)
        return carry

    lax.fori_loop(0, BX // 2 + 1, post, 0, unroll=True)

    def remain(i, carry):
        at = 9 + 2 * i
        v, av = operate_rows(v_ref, s_ref, wx_ref, wy_ref, wz_ref, at, 2)
        left = rhs_ref[pl.ds(at, 2)] - av
        out_ref[pl.ds(2 * i, 2)] = v[:, 8:24]
        left_ref[pl.ds(2 * i, 2)] = left[:, 8:24]
        return carry

    lax.fori_loop(0, BX // 2, remain, 0, unroll=True)


def call(body, outs, operands, scratch=()):
    cells = sum(math.prod(shape) for shape in outs)
    vmem = pl.BlockSpec(memory_space=pltpu.VMEM)
    return pl.pallas_call(
        body,
        out_shape=[jax.ShapeDtypeStruct(shape, F32) for shape in outs],
        in_specs=[vmem] * len(operands),
        out_specs=[vmem] * len(outs),
        scratch_shapes=[pltpu.VMEM(shape, F32) for shape in scratch],
        compiler_params=pltpu.CompilerParams(vmem_limit_bytes=16 * 1024 * 1024),
        cost_estimate=pl.CostEstimate(
            flops=20 * cells, bytes_accessed=8 * cells, transcendentals=0
        ),
    )(*operands)


def beside(to_low, to_high, axis, step=1):
    ends = lax.axis_size(axis) - step
    from_low = lax.ppermute(to_high, axis, [(i, i + step) for i in range(ends)])
    from_high = lax.ppermute(to_low, axis, [(i + step, i) for i in range(ends)])
    return from_low, from_high


def surround(cells, dim):
    low, high = beside(cells, cells, "tile")
    ydim = dim + 1

    def part(first):
        pieces = [lax.slice_in_dim(v, first, first + 8, axis=ydim) for v in (low, cells, high)]
        return jnp.concatenate(pieces, axis=dim)

    ylow, yhigh = beside(part(0), part(BY - 8), "group")
    return low, cells, high, ylow, yhigh


def everyone(blocks, axis):
    return lax.all_to_all(blocks, axis, 0, 0, tiled=True)


def pairs_of_tiles(block):
    tiles, groups = lax.axis_size("tile"), lax.axis_size("group")
    members = [
        [t * groups + 2 * pair + core for t in range(tiles) for core in range(2)]
        for pair in range(groups // 2)
    ]
    given = lax.all_to_all(
        block, ("tile", "group"), 0, 0, axis_index_groups=members, tiled=True
    )
    return given.reshape((tiles, 2) + block.shape[1:])


def shards(pressure_head, old_head, soil_type, conduct_sat, alpha_param, shape_param, water_span):
    tiles, groups = lax.axis_size("tile"), lax.axis_size("group")
    thirds = tiles // 4
    top, one, two = (PX, WY, NZ), (L1X, WY, NZ), (2 * tiles, 16, NZ)
    three, line = (tiles, 24, NZ), (tiles, 1, NZ)
    rows_once, rows_again = thirds + -(-tiles // 8), thirds

    fields = pl.pallas_call(
        soil_kernel,
        out_shape=jax.ShapeDtypeStruct((4, BX, BY, NZ), F32),
        in_specs=[pl.BlockSpec(memory_space=pltpu.HBM)] * 7,
        out_specs=pl.BlockSpec(memory_space=pltpu.VMEM),
        scratch_shapes=[
            pltpu.VMEM((BX, BY, NZ), F32),
            pltpu.VMEM((BX, BY, NZ), F32),
            pltpu.VMEM((BX, BY, NZ), jnp.int32),
            *[pltpu.SMEM((SOILS,), F32) for _ in range(4)],
            pltpu.SemaphoreType.DMA((7,)),
        ],
    )(pressure_head, old_head, soil_type, conduct_sat, alpha_param, shape_param, water_span)
    around = surround(fields, 1)
    rhs, s0, di0, wx0, wy0, wz0, e2, r1, s1, di1, wx1, wy1, wz1, e21, msg = call(
        assemble_kernel,
        [top] * 7 + [one] * 7 + [(2 * tiles, 6, 2, NZ)],
        list(around),
        [top] * 4,
    )
    bands0 = [s0, di0, wx0, wy0, wz0]
    bands1 = [s1, di1, wx1, wy1, wz1]

    here = pairs_of_tiles(msg)
    to_low, to_high = call(sides_kernel, [(tiles, 6, 2, NZ)] * 2, [here])
    before, after = beside(to_low, to_high, "group", 2)
    r2, s2, di2, wx2, wy2, wz2, e22, *bands3, msg = call(
        third_kernel,
        [two] * 7 + [three] * 5 + [(groups, rows_once, 1, NZ)],
        [before, here, after],
    )
    bands2 = [s2, di2, wx2, wy2, wz2]
    third = everyone(msg, "group").reshape(groups * rows_once, NZ)
    pre, below = call(
        functools.partial(climb_kernel, groups=groups, thirds=thirds, rows=rows_once),
        [(BX, BY, NZ), line],
        [third, *bands3, r2, *bands2, e22, r1, *bands1, e21, e2],
    )

    around = surround(pre, 0)
    u, rem, e2, r1, e21, msg, edge = call(
        again_kernel,
        [top] * 3 + [one] * 2 + [(tiles, 5, 2, NZ), (1, 5, 2, NZ)],
        [*around, rhs, *bands0, *bands1],
        [top] * 2,
    )
    own = jnp.concatenate([everyone(msg, "tile"), edge], axis=0)
    low, high = beside(own, own, "group")
    r2, e22, msg = call(
        third_again_kernel,
        [two] * 2 + [(groups, rows_again, 1, NZ)],
        [own, low, high, *bands2],
    )
    third = everyone(msg, "group").reshape(groups * rows_again, NZ)
    update, remainder = call(
        functools.partial(last_climb_kernel, groups=groups, thirds=thirds, rows=rows_again),
        [(BX, BY, NZ)] * 2,
        [third, below, *bands3, low, own, high, r2, *bands2, e22, r1, *bands1, e21]
        + [e2, rhs, *bands0, u, rem],
        [top] * 2,
    )
    return update, remainder


def solution(mesh):
    spec = P("tile", "group", None)
    return jax.shard_map(
        shards,
        mesh=mesh,
        in_specs=(spec, spec, spec, P(), P(), P(), P()),
        out_specs=(spec, spec),
        check_vma=False,
    )
```

```python
import functools
import math

import jax
import jax.numpy as jnp
from jax import lax
from jax.experimental import pallas as pl
from jax.experimental.pallas import tpu as pltpu
from jax.sharding import PartitionSpec as P

OMEGA = 2.0 / 3.0
STORAGE = 0.01
COARSE_SWEEPS = 4
SOILS = 12

BX, BY, NZ = 8, 16, 128
WX, WY = 24, 32
PX = WX + 2
L1X = WX // 2
F32 = jnp.float32


def iota(shape, dim):
    return lax.broadcasted_iota(jnp.int32, shape, dim)


def turn(v, step, axis):
    size = v.shape[axis]
    return pltpu.roll(v, step % size, axis)


def bit_of(v, step, axis):
    return (iota(v.shape, axis) // step) % 2 == 0


def pair_sum(v, step, axis):
    return v + jnp.where(bit_of(v, step, axis), turn(v, -step, axis), turn(v, step, axis))


def pair_low(v, step, axis):
    return jnp.where(bit_of(v, step, axis), v, turn(v, step, axis))


def x_low(v):
    return jnp.concatenate([v[:1], v[:-1]], axis=0)


def x_high(v):
    return jnp.concatenate([v[1:], jnp.zeros_like(v[:1])], axis=0)


def x_pair(v):
    return jnp.sum(v.reshape((v.shape[0] // 2, 2) + v.shape[1:]), axis=1)


def x_even(v):
    return v.reshape((v.shape[0] // 2, 2) + v.shape[1:])[:, 0]


def x_repeat(v):
    size = v.shape[0]
    wide = jnp.broadcast_to(v[:, None], (size, 2) + v.shape[1:])
    return wide.reshape((2 * size,) + v.shape[1:])


def operate(v, storage, wx, wy, wz, sy, sz):
    fx = wx * (v - x_low(v))
    fy = wy * (v - turn(v, sy, 1))
    fz = wz * (v - turn(v, sz, 2))
    flux = (fx - x_high(fx)) + (fy - turn(fy, -sy, 1)) + (fz - turn(fz, -sz, 2))
    return storage * v + flux


def relax_factor(storage, wx, wy, wz, sy, sz):
    diagonal = storage + wx + x_high(wx) + wy + turn(wy, -sy, 1) + wz + turn(wz, -sz, 2)
    return jnp.where(diagonal > 0.0, OMEGA / diagonal, 0.0)


def restrict(v, sy, sz):
    return pair_sum(pair_sum(x_pair(v), sy, 1), sz, 2)


def coarsen(storage, wx, wy, wz, sy, sz):
    return (
        restrict(storage, sy, sz),
        pair_sum(pair_sum(x_even(wx), sy, 1), sz, 2),
        pair_low(pair_sum(x_pair(wy), sz, 2), sy, 1),
        pair_low(pair_sum(x_pair(wz), sy, 1), sz, 2),
    )


def operate_rows(v_ref, s_ref, wx_ref, wy_ref, wz_ref, at, size):
    v = v_ref[pl.ds(at, size)]
    wx = wx_ref[pl.ds(at, size)]
    fy = wy_ref[pl.ds(at, size)] * (v - turn(v, 1, 1))
    fz = wz_ref[pl.ds(at, size)] * (v - turn(v, 1, 2))
    flux = wx * (v - v_ref[pl.ds(at - 1, size)])
    flux = flux - wx_ref[pl.ds(at + 1, size)] * (v_ref[pl.ds(at + 1, size)] - v)
    flux = flux + (fy - turn(fy, -1, 1)) + (fz - turn(fz, -1, 2))
    return v, s_ref[pl.ds(at, size)] * v + flux


def blank_ends(ref):
    ref[0] = jnp.zeros((WY, NZ), F32)
    ref[PX - 1] = jnp.zeros((WY, NZ), F32)


def blank_level1(ref, size):
    ref[0:size] = jnp.zeros((size, WY, NZ), F32)
    ref[L1X - size :] = jnp.zeros((size, WY, NZ), F32)


def pack_level2(v):
    sub, lane = iota(v.shape, 1), iota(v.shape, 2)
    chosen = (sub >= 8) & (sub < 24) & (sub % 4 == 0) & ((sub - 8) // 4 == lane % 4)
    return jnp.sum(jnp.where(chosen, v, 0.0), axis=1)


def send(msg_ref, rows):
    rows = list(rows)
    parts, height = msg_ref.shape[1:3]
    spare = parts * height - sum(row.shape[0] for row in rows)
    if spare:
        rows.append(jnp.zeros((spare, NZ), F32))
    whole = jnp.concatenate(rows, axis=0)
    for part in range(parts):
        piece = whole[part * height : (part + 1) * height]
        for peer in range(msg_ref.shape[0]):
            msg_ref[peer, part] = piece


def pack_bands3(fields):
    sub, lane = iota((1, WY, NZ), 1), iota((1, WY, NZ), 2)
    total = jnp.zeros((1, WY, NZ), F32)
    for f, v in enumerate(fields):
        chosen = ((sub == 8) & (lane % 8 == 2 * f)) | ((sub == 16) & (lane % 8 == 2 * f + 1))
        total = total + jnp.where(chosen, v, 0.0)
    return jnp.sum(total, axis=1)


def pack_ring1(v):
    sub, lane = iota((2, WY, NZ), 1), iota((2, WY, NZ), 2)
    rows = v[5:7]
    parts = []
    for k in range(4):
        chosen = ((sub == 8 + 4 * k) & (lane % 2 == 0)) | ((sub == 10 + 4 * k) & (lane % 2 == 1))
        parts.append(jnp.sum(jnp.where(chosen, rows, 0.0), axis=1, keepdims=True))
    return [jnp.concatenate([part[x] for part in parts], axis=0) for x in range(2)]


def pack_edge1(v):
    sub, lane = iota((6, WY, NZ), 1), iota((6, WY, NZ), 2)
    chosen = ((sub == 20) & (lane % 2 == 0)) | ((sub == 10) & (lane % 2 == 1))
    return jnp.sum(jnp.where(chosen, v[3:9], 0.0), axis=1)


def descend_top(r_ref, e1_ref, e2_ref, s_ref, wx_ref, wy_ref, wz_ref, di_ref, r1_ref):
    def second(i, carry):
        at = 1 + 2 * i
        v, av = operate_rows(e1_ref, s_ref, wx_ref, wy_ref, wz_ref, at, 2)
        e2_ref[pl.ds(at, 2)] = v + di_ref[pl.ds(at, 2)] * (r_ref[pl.ds(at, 2)] - av)
        return carry

    lax.fori_loop(1, WX // 2 - 1, second, 0, unroll=5)

    def third(i, carry):
        at = 1 + 2 * i
        _, av = operate_rows(e2_ref, s_ref, wx_ref, wy_ref, wz_ref, at, 2)
        r1_ref[pl.ds(i, 1)] = restrict(r_ref[pl.ds(at, 2)] - av, 1, 1)
        return carry

    lax.fori_loop(2, WX // 2 - 2, third, 0, unroll=4)


def descend_second(r1, s1, wx1, wy1, wz1, di1):
    first = r1 * di1
    second = first + di1 * (r1 - operate(first, s1, wx1, wy1, wz1, 2, 2))
    defect = r1 - operate(second, s1, wx1, wy1, wz1, 2, 2)
    return second, restrict(defect, 2, 2)


def soil_kernel(
    head_in, old_in, soil_in, ks_in, alpha_in, shape_in, span_in, out_ref,
    head_ref, old_ref, soil_ref, ks_ref, alpha_ref, shape_ref, span_ref, sems,
):
    given = (ks_in, alpha_in, shape_in, span_in, head_in, old_in, soil_in)
    held = (ks_ref, alpha_ref, shape_ref, span_ref, head_ref, old_ref, soil_ref)
    copies = [
        pltpu.make_async_copy(src, dst, sems.at[i])
        for i, (src, dst) in enumerate(zip(given, held, strict=True))
    ]
    for copy in copies:
        copy.start()
    for copy in copies:
        copy.wait()

    def cells(i, carry):
        row = pl.ds(i, 1)
        head, old, soil = head_ref[row], old_ref[row], soil_ref[row]
        ks = jnp.full(soil.shape, ks_ref[0])
        alpha = jnp.full(soil.shape, alpha_ref[0])
        shape_n = jnp.full(soil.shape, shape_ref[0])
        span = jnp.full(soil.shape, span_ref[0])
        for kind in range(1, SOILS):
            hit = soil == kind
            ks = jnp.where(hit, ks_ref[kind], ks)
            alpha = jnp.where(hit, alpha_ref[kind], alpha)
            shape_n = jnp.where(hit, shape_ref[kind], shape_n)
            span = jnp.where(hit, span_ref[kind], span)
        shape_m = 1.0 - 1.0 / shape_n
        power = jnp.exp(shape_n * jnp.log(alpha * -head))
        old_power = jnp.exp(shape_n * jnp.log(alpha * -old))
        saturation = jnp.exp(-shape_m * jnp.log1p(power))
        old_saturation = jnp.exp(-shape_m * jnp.log1p(old_power))
        portion = 1.0 / (1.0 + power)
        factor = 1.0 - jnp.exp(shape_m * jnp.log(power / (1.0 + power)))
        capacity = span * shape_m * shape_n * power / -head * saturation * portion
        out_ref[0, row] = head
        out_ref[1, row] = ks * jnp.sqrt(saturation) * factor * factor
        out_ref[2, row] = capacity + STORAGE
        out_ref[3, row] = span * (saturation - old_saturation) + STORAGE * (head - old)
        return carry

    lax.fori_loop(0, BX, cells, 0, unroll=2)


def is_even(axis, step=1):
    return (lax.axis_index(axis) // step) % 2 == 0


def sides(first, second, axis, step=1):
    even = is_even(axis, step)
    return jnp.where(even, second, first), jnp.where(even, first, second)


def fill_window(ref, xfirst, own, xsecond, yfirst, ysecond):
    ref[1 : 1 + BX, 8:24, :], ref[1 + 2 * BX : 1 + 3 * BX, 8:24, :] = sides(xfirst, xsecond, "tile")
    ref[1 + BX : 1 + 2 * BX, 8:24, :] = own
    ylow, yhigh = sides(yfirst, ysecond, "group")
    for y, part in ((0, ylow), (24, yhigh)):
        low, high = sides(part[:BX], part[2 * BX :], "tile")
        ref[1 : 1 + BX, y : y + 8, :] = low
        ref[1 + BX : 1 + 2 * BX, y : y + 8, :] = part[BX : 2 * BX]
        ref[1 + 2 * BX : 1 + 3 * BX, y : y + 8, :] = high


def assemble_kernel(
    xfirst, own, xsecond, yfirst, ysecond,
    r_ref, s_ref, di_ref, wx_ref, wy_ref, wz_ref, e2_ref,
    r1_ref, s1_ref, di1_ref, wx1_ref, wy1_ref, wz1_ref, e21_ref, msg_ref,
    h_ref, k_ref, m_ref, e1_ref,
):
    for ref in (h_ref, k_ref, s_ref, wx_ref, wy_ref, wz_ref, di_ref, r_ref, e1_ref, e2_ref):
        blank_ends(ref)
    for f, ref in enumerate((h_ref, k_ref, s_ref, m_ref)):
        fill_window(ref, xfirst[f], own[f], xsecond[f], yfirst[f], ysecond[f])

    def harmonic(a, b):
        total = a + b
        return jnp.where(total > 0.0, 2.0 * a * b / total, 0.0)

    def faces(i, carry):
        at = 1 + 2 * i
        k = k_ref[pl.ds(at, 2)]
        wx_ref[pl.ds(at, 2)] = harmonic(k, k_ref[pl.ds(at - 1, 2)])
        wy_ref[pl.ds(at, 2)] = harmonic(k, turn(k, 1, 1))
        wz = harmonic(k, turn(k, 1, 2))
        wz_ref[pl.ds(at, 2)] = jnp.where(iota(wz.shape, 2) == 0, 0.0, wz)
        return carry

    lax.fori_loop(0, WX // 2, faces, 0, unroll=4)

    def right_side(i, carry):
        at = 1 + 2 * i
        rows = pl.ds(at, 2)
        h, wx, wy, wz = h_ref[rows], wx_ref[rows], wy_ref[rows], wz_ref[rows]
        wx_up = wx_ref[pl.ds(at + 1, 2)]
        fy = wy * (h - turn(h, 1, 1))
        fz = wz * (h - turn(h, 1, 2) + 1.0)
        flux = wx * (h - h_ref[pl.ds(at - 1, 2)]) - wx_up * (h_ref[pl.ds(at + 1, 2)] - h)
        flux = flux + (fy - turn(fy, -1, 1)) + (fz - turn(fz, -1, 2))
        rhs = -(m_ref[rows] + flux)
        diagonal = s_ref[rows] + wx + wx_up + wy + turn(wy, -1, 1) + wz + turn(wz, -1, 2)
        di = jnp.where(diagonal > 0.0, OMEGA / diagonal, 0.0)
        r_ref[rows] = rhs
        di_ref[rows] = di
        e1_ref[rows] = rhs * di
        return carry

    lax.fori_loop(0, WX // 2, right_side, 0, unroll=4)

    def bands(i, carry):
        rows = pl.ds(1 + 2 * i, 2)
        s1, wx1, wy1, wz1 = coarsen(s_ref[rows], wx_ref[rows], wy_ref[rows], wz_ref[rows], 1, 1)
        row = pl.ds(i, 1)
        s1_ref[row], wx1_ref[row], wy1_ref[row], wz1_ref[row] = s1, wx1, wy1, wz1
        return carry

    lax.fori_loop(1, WX // 2 - 1, bands, 0, unroll=5)
    for ref in (s1_ref, wx1_ref, wy1_ref, wz1_ref):
        blank_level1(ref, 1)
    blank_level1(r1_ref, 2)
    descend_top(r_ref, e1_ref, e2_ref, s_ref, wx_ref, wy_ref, wz_ref, di_ref, r1_ref)

    s1, wx1, wy1, wz1 = s1_ref[...], wx1_ref[...], wy1_ref[...], wz1_ref[...]
    di1 = relax_factor(s1, wx1, wy1, wz1, 2, 2)
    di1_ref[...] = di1
    e21, r2 = descend_second(r1_ref[...], s1, wx1, wy1, wz1, di1)
    e21_ref[...] = e21
    bands2 = coarsen(s1, wx1, wy1, wz1, 2, 2)
    bands3 = coarsen(*(v[2:4] for v in bands2), 4, 4)
    rows = [pack_level2(v[2:4]) for v in (r2,) + bands2]
    send(msg_ref, rows + [pack_bands3(bands3)])


def again_kernel(
    xfirst, own, xsecond, yfirst, ysecond, rhs_ref, s_ref, di_ref, wx_ref, wy_ref, wz_ref,
    s1_ref, di1_ref, wx1_ref, wy1_ref, wz1_ref,
    u_ref, r_ref, e2_ref, r1_ref, e21_ref, msg_ref, edge_ref, pre_ref, e1_ref,
):
    for ref in (pre_ref, u_ref, r_ref, e1_ref, e2_ref):
        blank_ends(ref)
    fill_window(pre_ref, xfirst[...], own[...], xsecond[...], yfirst[...], ysecond[...])

    def post(i, carry):
        at = 1 + 2 * i
        rows = pl.ds(at, 2)
        v, av = operate_rows(pre_ref, s_ref, wx_ref, wy_ref, wz_ref, at, 2)
        u_ref[rows] = v + di_ref[rows] * (rhs_ref[rows] - av)
        return carry

    lax.fori_loop(0, WX // 2, post, 0, unroll=4)

    def remain(i, carry):
        at = 1 + 2 * i
        rows = pl.ds(at, 2)
        _, av = operate_rows(u_ref, s_ref, wx_ref, wy_ref, wz_ref, at, 2)
        left = rhs_ref[rows] - av
        r_ref[rows] = left
        e1_ref[rows] = left * di_ref[rows]
        return carry

    lax.fori_loop(1, WX // 2 - 1, remain, 0, unroll=5)
    descend_top(r_ref, e1_ref, e2_ref, s_ref, wx_ref, wy_ref, wz_ref, di_ref, r1_ref)
    blank_level1(r1_ref, 2)
    e21, r2 = descend_second(
        r1_ref[...], s1_ref[...], wx1_ref[...], wy1_ref[...], wz1_ref[...], di1_ref[...]
    )
    e21_ref[...] = e21
    tile = lax.axis_index("tile")
    to_low, to_high = pack_ring1(e21)
    for peer in range(msg_ref.shape[0]):
        ring = jnp.where(tile > peer, to_low, to_high)
        msg_ref[peer, 0] = pack_level2(r2[2:4])
        msg_ref[peer, 1], msg_ref[peer, 2] = ring[0:2], ring[2:4]
    send(edge_ref, [pack_edge1(e21)])


def message_rows(ref):
    tiles = lax.axis_size("tile")
    return lambda field, half: ref[0:tiles, field, half : half + 1, :]


def choose(which, one, two):
    return lambda field, half: jnp.where(which, one(field, half), two(field, half))


def both_sides(first, second, step):
    even = is_even("group", step)
    one, two = message_rows(first), message_rows(second)
    return choose(even, two, one), choose(even, one, two)


def pair_rows(here, first, second):
    before, after = both_sides(first, second, 2)
    even = is_even("group")
    one, two = message_rows(here.at[:, 0]), message_rows(here.at[:, 1])
    return choose(even, before, one), choose(even, one, two), choose(even, two, after)


def band_rows3(here, first, second):
    before, after = both_sides(first, second, 2)
    even = is_even("group")
    six = [before(5, half) for half in range(2)]
    six += [here[:, core, 5, 0:1, :] for core in range(2)]
    six += [after(5, half) for half in range(2)]
    return [jnp.where(even, six[i], six[i + 1]) for i in range(5)]


def unpack_level2(field, own, low, high):
    tiles = lax.axis_size("tile")
    shape = (tiles, 16, NZ)
    sub, lane = iota(shape, 1), iota(shape, 2)
    halves = []
    for half in range(2):

        def spread(pick, half=half):
            return jnp.broadcast_to(pick(field, half), shape)

        v = jnp.where(sub < 4, spread(low), jnp.where(sub < 8, spread(own), spread(high)))
        v = jnp.where((lane % 4 == sub % 4) & (sub < 12), v, 0.0)
        halves.append(pair_sum(pair_sum(v, 1, 2), 2, 2))
    return jnp.stack(halves, axis=1).reshape((2 * tiles, 16, NZ))


def pack_level3(v):
    sub, lane = iota((16, NZ), 0), iota((16, NZ), 1)
    rows = []
    for j in range(v.shape[0] // 4):
        total = jnp.zeros((16, NZ), F32)
        for q in range(4):
            chosen = ((sub == 4) & (lane % 8 == 2 * q)) | ((sub == 6) & (lane % 8 == 2 * q + 1))
            total = total + jnp.where(chosen, v[4 * j + q], 0.0)
        rows.append(jnp.sum(total, axis=0, keepdims=True))
    return rows


def pack_sums3(v):
    v = v + turn(v, -2, 1)
    sub, lane = iota((16, NZ), 0), iota((16, NZ), 1)
    rows = []
    for first in range(0, v.shape[0], 8):
        total = jnp.zeros((16, NZ), F32)
        for q in range(min(8, v.shape[0] - first)):
            total = total + jnp.where((sub == 4) & (lane % 8 == q), v[first + q], 0.0)
        rows.append(jnp.sum(total, axis=0, keepdims=True))
    return rows


def descend_third(r2, s2, wx2, wy2, wz2, di2):
    first = r2 * di2
    second = first + di2 * (r2 - operate(first, s2, wx2, wy2, wz2, 1, 4))
    return second, restrict(r2 - operate(second, s2, wx2, wy2, wz2, 1, 4), 1, 4)


def sides_kernel(here, first_ref, second_ref):
    even = is_even("group", 2)
    low, high = here[:, 0, 0:5], here[:, 1, 0:5]
    first_ref[:, 0:5] = jnp.where(even, high, low)
    second_ref[:, 0:5] = jnp.where(even, low, high)
    for core in range(2):
        rows = here[:, core, 5, 0:1, :]
        first_ref[:, 5, core : core + 1, :] = rows
        second_ref[:, 5, core : core + 1, :] = rows


def third_kernel(
    first, here, second,
    r2_ref, s2_ref, di2_ref, wx2_ref, wy2_ref, wz2_ref, e22_ref,
    s3_ref, di3_ref, wx3_ref, wy3_ref, wz3_ref, msg_ref,
):
    s3, wx3, wy3, wz3 = unpack_bands3(band_rows3(here, first, second))
    s3_ref[...], wx3_ref[...], wy3_ref[...], wz3_ref[...] = s3, wx3, wy3, wz3
    di3_ref[...] = relax_factor(s3, wx3, wy3, wz3, 2, 8)
    low, own, high = pair_rows(here, first, second)
    r2, s2, wx2, wy2, wz2 = (unpack_level2(f, own, low, high) for f in range(5))
    di2 = relax_factor(s2, wx2, wy2, wz2, 1, 4)
    r2_ref[...], s2_ref[...], di2_ref[...] = r2, s2, di2
    wx2_ref[...], wy2_ref[...], wz2_ref[...] = wx2, wy2, wz2
    e22, r3 = descend_third(r2, s2, wx2, wy2, wz2, di2)
    e22_ref[...] = e22
    s3, wx3, _, wz3 = coarsen(s2, wx2, wy2, wz2, 1, 4)
    inner = s3 + wx3 + x_high(wx3) + wz3 + turn(wz3, -8, 2)
    send(msg_ref, pack_level3(r3) + pack_sums3(inner))


def third_again_kernel(
    own, first, second, s2_ref, di2_ref, wx2_ref, wy2_ref, wz2_ref, r2_ref, e22_ref, msg_ref
):
    r2 = unpack_level2(0, message_rows(own), *both_sides(first, second, 1))
    r2_ref[...] = r2
    e22, r3 = descend_third(
        r2, s2_ref[...], wx2_ref[...], wy2_ref[...], wz2_ref[...], di2_ref[...]
    )
    e22_ref[...] = e22
    send(msg_ref, pack_level3(r3))


def third_masks(shape):
    sub, lane = iota(shape, 1), iota(shape, 2)
    return sub // 4, (sub % 4) // 2, lane % 8


def octuple(v):
    return pair_sum(pair_sum(pair_sum(v, 1, 2), 2, 2), 4, 2)


def unpack_bands3(sources):
    shape = (sources[0].shape[0], 24, NZ)
    dev, half, slot = third_masks(shape)
    rows = jnp.broadcast_to(sources[0], shape)
    for d in range(1, 5):
        rows = jnp.where(dev == d, jnp.broadcast_to(sources[d], shape), rows)
    rows = jnp.where(dev < 5, rows, 0.0)
    return [octuple(jnp.where(slot == 2 * f + half, rows, 0.0)) for f in range(4)]


def unpack_r3(v):
    group = lax.axis_index("group")
    at = iota(v.shape, 1)
    shape = (v.shape[0], 24, NZ)
    dev, half, slot = third_masks(shape)
    rows = jnp.zeros(shape, F32)
    for d in range(5):
        near = jnp.sum(jnp.where(at == group + (d - 2), v, 0.0), axis=1, keepdims=True)
        rows = jnp.where(dev == d, jnp.broadcast_to(near, shape), rows)
    parts = [jnp.where(slot == 2 * q + half, rows, 0.0) for q in range(4)]
    return octuple(jnp.stack(parts, axis=1).reshape((4 * v.shape[0], 24, NZ)))


def line_sums(v, held):
    total = jnp.sum(v, axis=1, keepdims=True)
    lane = iota(total.shape, 2) % 8
    parts = [jnp.where(lane * held // 8 == q, total, 0.0) for q in range(held)]
    wide = jnp.stack(parts, axis=1).reshape((held * v.shape[0], 1, NZ))
    return octuple(wide[: lax.axis_size("tile")])


def solve_third(r3, line, s3, di3, wx3, wy3, wz3):
    v = jnp.broadcast_to(line, r3.shape)
    for _ in range(COARSE_SWEEPS):
        v = v + di3 * (r3 - operate(v, s3, wx3, wy3, wz3, 2, 8))
    return turn(v, -4, 1)[:, 0:16]


def near_tiles(v):
    tile = lax.axis_index("tile")
    parts = []
    for off in (-1, 0, 1):
        total = jnp.zeros((2,) + v.shape[1:], F32)
        for t in range(v.shape[0] // 2):
            total = total + jnp.where(tile + off == t, v[2 * t : 2 * t + 2], 0.0)
        parts.append(total)
    return jnp.concatenate(parts, axis=0)


def widen_y(v):
    shape = (v.shape[0], 8, NZ)
    sub = iota(shape, 1)
    parts = []
    for at in (2, 4, 6, 8):
        first = jnp.broadcast_to(v[:, at : at + 1], shape)
        second = jnp.broadcast_to(v[:, at + 1 : at + 2], shape)
        parts.append(jnp.where(sub < 4, first, second))
    return jnp.concatenate(parts, axis=1)


def climb_to_second(corr3, r2_ref, s2_ref, di2_ref, wx2_ref, wy2_ref, wz2_ref, e22_ref):
    v = e22_ref[...] + x_repeat(corr3)
    v = v + di2_ref[...] * (
        r2_ref[...]
        - operate(v, s2_ref[...], wx2_ref[...], wy2_ref[...], wz2_ref[...], 1, 4)
    )
    return x_repeat(widen_y(near_tiles(v)))


def climb_to_first(v, r1_ref, s1_ref, di1_ref, wx1_ref, wy1_ref, wz1_ref):
    return v + di1_ref[...] * (
        r1_ref[...]
        - operate(v, s1_ref[...], wx1_ref[...], wy1_ref[...], wz1_ref[...], 2, 2)
    )


def strided(ref, first, thirds, groups, rows):
    parts = [ref[pl.ds(first + j, groups, stride=rows), :] for j in range(thirds)]
    return jnp.stack(parts, axis=0)


def climb_kernel(
    third_ref, s3_ref, di3_ref, wx3_ref, wy3_ref, wz3_ref,
    r2_ref, s2_ref, di2_ref, wx2_ref, wy2_ref, wz2_ref, e22_ref,
    r1_ref, s1_ref, di1_ref, wx1_ref, wy1_ref, wz1_ref, e21_ref, e2_ref,
    pre_ref, below_ref,
    *, groups, thirds, rows,
):
    r3 = strided(third_ref, 0, thirds, groups, rows)
    below = line_sums(strided(third_ref, thirds, rows - thirds, groups, rows), 8)
    below_ref[...] = below
    corr3 = solve_third(
        unpack_r3(r3), line_sums(r3, 4) / below,
        s3_ref[...], di3_ref[...], wx3_ref[...], wy3_ref[...], wz3_ref[...],
    )
    corr2 = climb_to_second(corr3, r2_ref, s2_ref, di2_ref, wx2_ref, wy2_ref, wz2_ref, e22_ref)
    v = climb_to_first(
        e21_ref[...] + corr2, r1_ref, s1_ref, di1_ref, wx1_ref, wy1_ref, wz1_ref
    )
    own1 = x_repeat(v[4:8])
    pre_ref[...] = e2_ref[9:17, 8:24, :] + own1[:, 8:24, :]


def tile_rows(refs, even, off, at):
    tile = lax.axis_index("tile")
    total = jnp.zeros((2, NZ), F32)
    for t in range(lax.axis_size("tile")):
        rows = refs[0][t, at] if len(refs) == 1 else jnp.where(even, refs[0][t, at], refs[1][t, at])
        total = total + jnp.where(tile + off == t, rows, 0.0)
    return total


def ring_row(own, first, second, off):
    even = is_even("group")
    pairs = [tile_rows((own,), even, off, 1), tile_rows((own,), even, off, 2)]
    packed = [tile_rows((second, first), even, off, 2)[1:2]]
    packed += [pair[k : k + 1] for pair in pairs for k in range(2)]
    packed += [tile_rows((first, second), even, off, 1)[0:1]]
    return spread_pairs([row[None] for row in packed], 1)


def spread_pairs(packed, height):
    shape = (height, WY, NZ)
    sub, lane = iota(shape, 1), iota(shape, 2)
    rows = jnp.zeros(shape, F32)
    for k, row in enumerate(packed):
        rows = jnp.where(sub // 4 == k + 1, jnp.broadcast_to(row, shape), rows)
    return pair_sum(jnp.where(lane % 2 == (sub // 2) % 2, rows, 0.0), 1, 2)


def last_climb_kernel(
    third_ref, below_ref, s3_ref, di3_ref, wx3_ref, wy3_ref, wz3_ref,
    first, own, second,
    r2_ref, s2_ref, di2_ref, wx2_ref, wy2_ref, wz2_ref, e22_ref,
    r1_ref, s1_ref, di1_ref, wx1_ref, wy1_ref, wz1_ref, e21_ref,
    e2_ref, rhs_ref, s_ref, di_ref, wx_ref, wy_ref, wz_ref, u_ref, r_ref,
    out_ref, left_ref, pre_ref, v_ref,
    *, groups, thirds, rows,
):
    r3 = strided(third_ref, 0, thirds, groups, rows)
    corr3 = solve_third(
        unpack_r3(r3), line_sums(r3, 4) / below_ref[...],
        s3_ref[...], di3_ref[...], wx3_ref[...], wy3_ref[...], wz3_ref[...],
    )
    corr2 = climb_to_second(corr3, r2_ref, s2_ref, di2_ref, wx2_ref, wy2_ref, wz2_ref, e22_ref)
    tiles = lax.axis_size("tile")
    middle = e21_ref[3:9]
    sub = iota(middle.shape, 1)
    edge_first = jnp.concatenate([first[tiles, k] for k in range(3)], axis=0)[:, None]
    edge_second = jnp.concatenate([second[tiles, k] for k in range(3)], axis=0)[:, None]
    edge_low, edge_high = sides(edge_first, edge_second, "group")
    nothing = jnp.zeros_like(edge_low)
    edges = spread_pairs([edge_low] + [nothing] * 4 + [edge_high], 6)
    kept = (sub >= 6) & (sub < 26)
    middle = jnp.where(kept, middle, edges)
    blank = jnp.zeros((2, WY, NZ), F32)
    ends = [ring_row(own, first, second, off) for off in (-1, 1)]
    e21 = jnp.concatenate([blank, ends[0], middle, ends[1], blank], axis=0)
    v = climb_to_first(e21 + corr2, r1_ref, s1_ref, di1_ref, wx1_ref, wy1_ref, wz1_ref)
    pre_ref[7:19] = e2_ref[7:19] + x_repeat(v[3:9])

    def post(i, carry):
        at = 8 + 2 * i
        here = pl.ds(at, 2)
        v, av = operate_rows(pre_ref, s_ref, wx_ref, wy_ref, wz_ref, at, 2)
        v_ref[here] = u_ref[here] + v + di_ref[here] * (r_ref[here] - av)
        return carry

    lax.fori_loop(0, BX // 2 + 1, post, 0, unroll=True)

    def remain(i, carry):
        at = 9 + 2 * i
        v, av = operate_rows(v_ref, s_ref, wx_ref, wy_ref, wz_ref, at, 2)
        left = rhs_ref[pl.ds(at, 2)] - av
        out_ref[pl.ds(2 * i, 2)] = v[:, 8:24]
        left_ref[pl.ds(2 * i, 2)] = left[:, 8:24]
        return carry

    lax.fori_loop(0, BX // 2, remain, 0, unroll=True)


def call(body, outs, operands, scratch=()):
    cells = sum(math.prod(shape) for shape in outs)
    vmem = pl.BlockSpec(memory_space=pltpu.VMEM)
    return pl.pallas_call(
        body,
        out_shape=[jax.ShapeDtypeStruct(shape, F32) for shape in outs],
        in_specs=[vmem] * len(operands),
        out_specs=[vmem] * len(outs),
        scratch_shapes=[pltpu.VMEM(shape, F32) for shape in scratch],
        compiler_params=pltpu.CompilerParams(vmem_limit_bytes=16 * 1024 * 1024),
        cost_estimate=pl.CostEstimate(
            flops=20 * cells, bytes_accessed=8 * cells, transcendentals=0
        ),
    )(*operands)


def swaps(to_first, to_second, axis, step=1):
    count = lax.axis_size(axis)

    def swap(cells, odd):
        ups = [
            (i, i + step) for i in range(count - step) if (i // step) % 2 == odd
        ]
        return lax.ppermute(cells, axis, ups + [(j, i) for i, j in ups])

    return swap(to_first, 0), swap(to_second, 1)


def surround(cells, dim):
    first, second = swaps(cells, cells, "tile")
    ydim = dim + 1
    even = is_even("group")

    def halves(v):
        low = lax.slice_in_dim(v, 0, 8, axis=ydim)
        high = lax.slice_in_dim(v, BY - 8, BY, axis=ydim)
        return jnp.where(even, high, low), jnp.where(even, low, high)

    parts = [halves(v) for v in (first, cells, second)]
    to_first, to_second = (jnp.concatenate(list(v), axis=dim) for v in zip(*parts, strict=True))
    return first, cells, second, *swaps(to_first, to_second, "group")


def everyone(blocks, axis):
    return lax.all_to_all(blocks, axis, 0, 0, tiled=True)


def pairs_of_tiles(block):
    tiles, groups = lax.axis_size("tile"), lax.axis_size("group")
    members = [
        [t * groups + 2 * pair + core for t in range(tiles) for core in range(2)]
        for pair in range(groups // 2)
    ]
    given = lax.all_to_all(
        block, ("tile", "group"), 0, 0, axis_index_groups=members, tiled=True
    )
    return given.reshape((tiles, 2) + block.shape[1:])


def shards(pressure_head, old_head, soil_type, conduct_sat, alpha_param, shape_param, water_span):
    tiles, groups = lax.axis_size("tile"), lax.axis_size("group")
    thirds = tiles // 4
    top, one, two = (PX, WY, NZ), (L1X, WY, NZ), (2 * tiles, 16, NZ)
    three, line = (tiles, 24, NZ), (tiles, 1, NZ)
    rows_once, rows_again = thirds + -(-tiles // 8), thirds

    fields = pl.pallas_call(
        soil_kernel,
        out_shape=jax.ShapeDtypeStruct((4, BX, BY, NZ), F32),
        in_specs=[pl.BlockSpec(memory_space=pltpu.HBM)] * 7,
        out_specs=pl.BlockSpec(memory_space=pltpu.VMEM),
        scratch_shapes=[
            pltpu.VMEM((BX, BY, NZ), F32),
            pltpu.VMEM((BX, BY, NZ), F32),
            pltpu.VMEM((BX, BY, NZ), jnp.int32),
            *[pltpu.SMEM((SOILS,), F32) for _ in range(4)],
            pltpu.SemaphoreType.DMA((7,)),
        ],
    )(pressure_head, old_head, soil_type, conduct_sat, alpha_param, shape_param, water_span)
    around = surround(fields, 1)
    rhs, s0, di0, wx0, wy0, wz0, e2, r1, s1, di1, wx1, wy1, wz1, e21, msg = call(
        assemble_kernel,
        [top] * 7 + [one] * 7 + [(2 * tiles, 6, 2, NZ)],
        list(around),
        [top] * 4,
    )
    bands0 = [s0, di0, wx0, wy0, wz0]
    bands1 = [s1, di1, wx1, wy1, wz1]

    here = pairs_of_tiles(msg)
    to_first, to_second = call(sides_kernel, [(tiles, 6, 2, NZ)] * 2, [here])
    first, second = swaps(to_first, to_second, "group", 2)
    r2, s2, di2, wx2, wy2, wz2, e22, *bands3, msg = call(
        third_kernel,
        [two] * 7 + [three] * 5 + [(groups, rows_once, 1, NZ)],
        [first, here, second],
    )
    bands2 = [s2, di2, wx2, wy2, wz2]
    third = everyone(msg, "group").reshape(groups * rows_once, NZ)
    pre, below = call(
        functools.partial(climb_kernel, groups=groups, thirds=thirds, rows=rows_once),
        [(BX, BY, NZ), line],
        [third, *bands3, r2, *bands2, e22, r1, *bands1, e21, e2],
    )

    around = surround(pre, 0)
    u, rem, e2, r1, e21, msg, edge = call(
        again_kernel,
        [top] * 3 + [one] * 2 + [(tiles, 3, 2, NZ), (1, 3, 2, NZ)],
        [*around, rhs, *bands0, *bands1],
        [top] * 2,
    )
    own = jnp.concatenate([everyone(msg, "tile"), edge], axis=0)
    first, second = swaps(own, own, "group")
    r2, e22, msg = call(
        third_again_kernel,
        [two] * 2 + [(groups, rows_again, 1, NZ)],
        [own, first, second, *bands2],
    )
    third = everyone(msg, "group").reshape(groups * rows_again, NZ)
    update, remainder = call(
        functools.partial(last_climb_kernel, groups=groups, thirds=thirds, rows=rows_again),
        [(BX, BY, NZ)] * 2,
        [third, below, *bands3, first, own, second, r2, *bands2, e22, r1, *bands1, e21]
        + [e2, rhs, *bands0, u, rem],
        [top] * 2,
    )
    return update, remainder


def solution(mesh):
    spec = P("tile", "group", None)
    return jax.shard_map(
        shards,
        mesh=mesh,
        in_specs=(spec, spec, spec, P(), P(), P(), P()),
        out_specs=(spec, spec),
        check_vma=False,
    )
```

```python
import functools
import math

import jax
import jax.numpy as jnp
from jax import lax
from jax.experimental import pallas as pl
from jax.experimental.pallas import tpu as pltpu
from jax.sharding import PartitionSpec as P

OMEGA = 2.0 / 3.0
STORAGE = 0.01
COARSE_SWEEPS = 4
SOILS = 12

BX, BY, NZ = 8, 16, 128
WX, WY = 24, 32
PX = WX + 2
L1X = WX // 2
F32 = jnp.float32


def iota(shape, dim):
    return lax.broadcasted_iota(jnp.int32, shape, dim)


def turn(v, step, axis):
    size = v.shape[axis]
    return pltpu.roll(v, step % size, axis)


def bit_of(v, step, axis):
    return (iota(v.shape, axis) // step) % 2 == 0


def pair_sum(v, step, axis):
    return v + jnp.where(bit_of(v, step, axis), turn(v, -step, axis), turn(v, step, axis))


def pair_low(v, step, axis):
    return jnp.where(bit_of(v, step, axis), v, turn(v, step, axis))


def x_low(v):
    return jnp.concatenate([v[:1], v[:-1]], axis=0)


def x_high(v):
    return jnp.concatenate([v[1:], jnp.zeros_like(v[:1])], axis=0)


def x_pair(v):
    return jnp.sum(v.reshape((v.shape[0] // 2, 2) + v.shape[1:]), axis=1)


def x_even(v):
    return v.reshape((v.shape[0] // 2, 2) + v.shape[1:])[:, 0]


def x_repeat(v):
    size = v.shape[0]
    wide = jnp.broadcast_to(v[:, None], (size, 2) + v.shape[1:])
    return wide.reshape((2 * size,) + v.shape[1:])


def operate(v, storage, wx, wy, wz, sy, sz):
    fx = wx * (v - x_low(v))
    fy = wy * (v - turn(v, sy, 1))
    fz = wz * (v - turn(v, sz, 2))
    flux = (fx - x_high(fx)) + (fy - turn(fy, -sy, 1)) + (fz - turn(fz, -sz, 2))
    return storage * v + flux


def relax_factor(storage, wx, wy, wz, sy, sz):
    diagonal = storage + wx + x_high(wx) + wy + turn(wy, -sy, 1) + wz + turn(wz, -sz, 2)
    return jnp.where(diagonal > 0.0, OMEGA / diagonal, 0.0)


def restrict(v, sy, sz):
    return pair_sum(pair_sum(x_pair(v), sy, 1), sz, 2)


def coarsen(storage, wx, wy, wz, sy, sz):
    return (
        restrict(storage, sy, sz),
        pair_sum(pair_sum(x_even(wx), sy, 1), sz, 2),
        pair_low(pair_sum(x_pair(wy), sz, 2), sy, 1),
        pair_low(pair_sum(x_pair(wz), sy, 1), sz, 2),
    )


def operate_rows(v_ref, s_ref, wx_ref, wy_ref, wz_ref, at, size):
    v = v_ref[pl.ds(at, size)]
    wx = wx_ref[pl.ds(at, size)]
    fy = wy_ref[pl.ds(at, size)] * (v - turn(v, 1, 1))
    fz = wz_ref[pl.ds(at, size)] * (v - turn(v, 1, 2))
    flux = wx * (v - v_ref[pl.ds(at - 1, size)])
    flux = flux - wx_ref[pl.ds(at + 1, size)] * (v_ref[pl.ds(at + 1, size)] - v)
    flux = flux + (fy - turn(fy, -1, 1)) + (fz - turn(fz, -1, 2))
    return v, s_ref[pl.ds(at, size)] * v + flux


def blank_ends(ref):
    ref[0] = jnp.zeros((WY, NZ), F32)
    ref[PX - 1] = jnp.zeros((WY, NZ), F32)


def blank_level1(ref, size):
    ref[0:size] = jnp.zeros((size, WY, NZ), F32)
    ref[L1X - size :] = jnp.zeros((size, WY, NZ), F32)


def pack_level2(v):
    sub, lane = iota(v.shape, 1), iota(v.shape, 2)
    chosen = (sub >= 8) & (sub < 24) & (sub % 4 == 0) & ((sub - 8) // 4 == lane % 4)
    return jnp.sum(jnp.where(chosen, v, 0.0), axis=1)


def send(msg_ref, rows):
    rows = list(rows)
    parts, height = msg_ref.shape[1:3]
    spare = parts * height - sum(row.shape[0] for row in rows)
    if spare:
        rows.append(jnp.zeros((spare, NZ), F32))
    whole = jnp.concatenate(rows, axis=0)
    for part in range(parts):
        piece = whole[part * height : (part + 1) * height]
        for peer in range(msg_ref.shape[0]):
            msg_ref[peer, part] = piece


def pack_bands3(fields):
    sub, lane = iota((1, WY, NZ), 1), iota((1, WY, NZ), 2)
    total = jnp.zeros((1, WY, NZ), F32)
    for f, v in enumerate(fields):
        chosen = ((sub == 8) & (lane % 8 == 2 * f)) | ((sub == 16) & (lane % 8 == 2 * f + 1))
        total = total + jnp.where(chosen, v, 0.0)
    return jnp.sum(total, axis=1)


def pack_ring1(v):
    sub, lane = iota((2, WY, NZ), 1), iota((2, WY, NZ), 2)
    rows = v[5:7]
    parts = []
    for k in range(4):
        chosen = ((sub == 8 + 4 * k) & (lane % 2 == 0)) | ((sub == 10 + 4 * k) & (lane % 2 == 1))
        parts.append(jnp.sum(jnp.where(chosen, rows, 0.0), axis=1, keepdims=True))
    return [jnp.concatenate([part[x] for part in parts], axis=0) for x in range(2)]


def pack_edge1(v):
    sub, lane = iota((6, WY, NZ), 1), iota((6, WY, NZ), 2)
    chosen = ((sub == 20) & (lane % 2 == 0)) | ((sub == 10) & (lane % 2 == 1))
    return jnp.sum(jnp.where(chosen, v[3:9], 0.0), axis=1)


def descend_top(r_ref, e1_ref, e2_ref, s_ref, wx_ref, wy_ref, wz_ref, di_ref, r1_ref):
    def second(i, carry):
        at = 1 + 2 * i
        v, av = operate_rows(e1_ref, s_ref, wx_ref, wy_ref, wz_ref, at, 2)
        e2_ref[pl.ds(at, 2)] = v + di_ref[pl.ds(at, 2)] * (r_ref[pl.ds(at, 2)] - av)
        return carry

    lax.fori_loop(1, WX // 2 - 1, second, 0, unroll=5)

    def third(i, carry):
        at = 1 + 2 * i
        _, av = operate_rows(e2_ref, s_ref, wx_ref, wy_ref, wz_ref, at, 2)
        r1_ref[pl.ds(i, 1)] = restrict(r_ref[pl.ds(at, 2)] - av, 1, 1)
        return carry

    lax.fori_loop(2, WX // 2 - 2, third, 0, unroll=4)


def descend_second(r1, s1, wx1, wy1, wz1, di1):
    first = r1 * di1
    second = first + di1 * (r1 - operate(first, s1, wx1, wy1, wz1, 2, 2))
    defect = r1 - operate(second, s1, wx1, wy1, wz1, 2, 2)
    return second, restrict(defect, 2, 2)


def soil_kernel(
    head_in, old_in, soil_in, ks_in, alpha_in, shape_in, span_in, out_ref,
    head_ref, old_ref, soil_ref, ks_ref, alpha_ref, shape_ref, span_ref, sems,
):
    given = (ks_in, alpha_in, shape_in, span_in, head_in, old_in, soil_in)
    held = (ks_ref, alpha_ref, shape_ref, span_ref, head_ref, old_ref, soil_ref)
    copies = [
        pltpu.make_async_copy(src, dst, sems.at[i])
        for i, (src, dst) in enumerate(zip(given, held, strict=True))
    ]
    for copy in copies:
        copy.start()
    for copy in copies:
        copy.wait()

    def cells(i, carry):
        row = pl.ds(i, 1)
        head, old, soil = head_ref[row], old_ref[row], soil_ref[row]
        ks = jnp.full(soil.shape, ks_ref[0])
        alpha = jnp.full(soil.shape, alpha_ref[0])
        shape_n = jnp.full(soil.shape, shape_ref[0])
        span = jnp.full(soil.shape, span_ref[0])
        for kind in range(1, SOILS):
            hit = soil == kind
            ks = jnp.where(hit, ks_ref[kind], ks)
            alpha = jnp.where(hit, alpha_ref[kind], alpha)
            shape_n = jnp.where(hit, shape_ref[kind], shape_n)
            span = jnp.where(hit, span_ref[kind], span)
        shape_m = 1.0 - 1.0 / shape_n
        power = jnp.exp(shape_n * jnp.log(alpha * -head))
        old_power = jnp.exp(shape_n * jnp.log(alpha * -old))
        saturation = jnp.exp(-shape_m * jnp.log1p(power))
        old_saturation = jnp.exp(-shape_m * jnp.log1p(old_power))
        portion = 1.0 / (1.0 + power)
        factor = 1.0 - jnp.exp(shape_m * jnp.log(power / (1.0 + power)))
        capacity = span * shape_m * shape_n * power / -head * saturation * portion
        out_ref[0, row] = head
        out_ref[1, row] = ks * jnp.sqrt(saturation) * factor * factor
        out_ref[2, row] = capacity + STORAGE
        out_ref[3, row] = span * (saturation - old_saturation) + STORAGE * (head - old)
        return carry

    lax.fori_loop(0, BX, cells, 0, unroll=2)


def is_even(axis, step=1, lead=0):
    return (lax.axis_index(axis) // step) % 2 == lead


def sides(first, second, axis, lead=0):
    even = is_even(axis, 1, lead)
    return jnp.where(even, second, first), jnp.where(even, first, second)


def fill_window(ref, xfirst, own, xsecond, yfirst, ysecond):
    ref[1 : 1 + BX, 8:24, :], ref[1 + 2 * BX : 1 + 3 * BX, 8:24, :] = sides(xfirst, xsecond, "tile")
    ref[1 + BX : 1 + 2 * BX, 8:24, :] = own
    ylow, yhigh = sides(yfirst, ysecond, "group", 1)
    for y, part in ((0, ylow), (24, yhigh)):
        low, high = sides(part[:BX], part[2 * BX :], "tile")
        ref[1 : 1 + BX, y : y + 8, :] = low
        ref[1 + BX : 1 + 2 * BX, y : y + 8, :] = part[BX : 2 * BX]
        ref[1 + 2 * BX : 1 + 3 * BX, y : y + 8, :] = high


def assemble_kernel(
    xfirst, own, xsecond, yfirst, ysecond,
    r_ref, s_ref, di_ref, wx_ref, wy_ref, wz_ref, e2_ref,
    r1_ref, s1_ref, di1_ref, wx1_ref, wy1_ref, wz1_ref, e21_ref, msg_ref,
    h_ref, k_ref, m_ref, e1_ref,
):
    for ref in (h_ref, k_ref, s_ref, wx_ref, wy_ref, wz_ref, di_ref, r_ref, e1_ref, e2_ref):
        blank_ends(ref)
    for f, ref in enumerate((h_ref, k_ref, s_ref, m_ref)):
        fill_window(ref, xfirst[f], own[f], xsecond[f], yfirst[f], ysecond[f])

    def harmonic(a, b):
        total = a + b
        return jnp.where(total > 0.0, 2.0 * a * b / total, 0.0)

    def faces(i, carry):
        at = 1 + 2 * i
        k = k_ref[pl.ds(at, 2)]
        wx_ref[pl.ds(at, 2)] = harmonic(k, k_ref[pl.ds(at - 1, 2)])
        wy_ref[pl.ds(at, 2)] = harmonic(k, turn(k, 1, 1))
        wz = harmonic(k, turn(k, 1, 2))
        wz_ref[pl.ds(at, 2)] = jnp.where(iota(wz.shape, 2) == 0, 0.0, wz)
        return carry

    lax.fori_loop(0, WX // 2, faces, 0, unroll=4)

    def right_side(i, carry):
        at = 1 + 2 * i
        rows = pl.ds(at, 2)
        h, wx, wy, wz = h_ref[rows], wx_ref[rows], wy_ref[rows], wz_ref[rows]
        wx_up = wx_ref[pl.ds(at + 1, 2)]
        fy = wy * (h - turn(h, 1, 1))
        fz = wz * (h - turn(h, 1, 2) + 1.0)
        flux = wx * (h - h_ref[pl.ds(at - 1, 2)]) - wx_up * (h_ref[pl.ds(at + 1, 2)] - h)
        flux = flux + (fy - turn(fy, -1, 1)) + (fz - turn(fz, -1, 2))
        rhs = -(m_ref[rows] + flux)
        diagonal = s_ref[rows] + wx + wx_up + wy + turn(wy, -1, 1) + wz + turn(wz, -1, 2)
        di = jnp.where(diagonal > 0.0, OMEGA / diagonal, 0.0)
        r_ref[rows] = rhs
        di_ref[rows] = di
        e1_ref[rows] = rhs * di
        return carry

    lax.fori_loop(0, WX // 2, right_side, 0, unroll=4)

    def bands(i, carry):
        rows = pl.ds(1 + 2 * i, 2)
        s1, wx1, wy1, wz1 = coarsen(s_ref[rows], wx_ref[rows], wy_ref[rows], wz_ref[rows], 1, 1)
        row = pl.ds(i, 1)
        s1_ref[row], wx1_ref[row], wy1_ref[row], wz1_ref[row] = s1, wx1, wy1, wz1
        return carry

    lax.fori_loop(1, WX // 2 - 1, bands, 0, unroll=5)
    for ref in (s1_ref, wx1_ref, wy1_ref, wz1_ref):
        blank_level1(ref, 1)
    blank_level1(r1_ref, 2)
    descend_top(r_ref, e1_ref, e2_ref, s_ref, wx_ref, wy_ref, wz_ref, di_ref, r1_ref)

    s1, wx1, wy1, wz1 = s1_ref[...], wx1_ref[...], wy1_ref[...], wz1_ref[...]
    di1 = relax_factor(s1, wx1, wy1, wz1, 2, 2)
    di1_ref[...] = di1
    e21, r2 = descend_second(r1_ref[...], s1, wx1, wy1, wz1, di1)
    e21_ref[...] = e21
    bands2 = coarsen(s1, wx1, wy1, wz1, 2, 2)
    bands3 = coarsen(*(v[2:4] for v in bands2), 4, 4)
    rows = [pack_level2(v[2:4]) for v in (r2,) + bands2]
    send(msg_ref, rows + [pack_bands3(bands3)])


def again_kernel(
    xfirst, own, xsecond, yfirst, ysecond, rhs_ref, s_ref, di_ref, wx_ref, wy_ref, wz_ref,
    s1_ref, di1_ref, wx1_ref, wy1_ref, wz1_ref,
    u_ref, r_ref, e2_ref, r1_ref, e21_ref, msg_ref, edge_ref, pre_ref, e1_ref,
):
    for ref in (pre_ref, u_ref, r_ref, e1_ref, e2_ref):
        blank_ends(ref)
    fill_window(pre_ref, xfirst[...], own[...], xsecond[...], yfirst[...], ysecond[...])

    def post(i, carry):
        at = 1 + 2 * i
        rows = pl.ds(at, 2)
        v, av = operate_rows(pre_ref, s_ref, wx_ref, wy_ref, wz_ref, at, 2)
        u_ref[rows] = v + di_ref[rows] * (rhs_ref[rows] - av)
        return carry

    lax.fori_loop(0, WX // 2, post, 0, unroll=4)

    def remain(i, carry):
        at = 1 + 2 * i
        rows = pl.ds(at, 2)
        _, av = operate_rows(u_ref, s_ref, wx_ref, wy_ref, wz_ref, at, 2)
        left = rhs_ref[rows] - av
        r_ref[rows] = left
        e1_ref[rows] = left * di_ref[rows]
        return carry

    lax.fori_loop(1, WX // 2 - 1, remain, 0, unroll=5)
    descend_top(r_ref, e1_ref, e2_ref, s_ref, wx_ref, wy_ref, wz_ref, di_ref, r1_ref)
    blank_level1(r1_ref, 2)
    e21, r2 = descend_second(
        r1_ref[...], s1_ref[...], wx1_ref[...], wy1_ref[...], wz1_ref[...], di1_ref[...]
    )
    e21_ref[...] = e21
    tile = lax.axis_index("tile")
    to_low, to_high = pack_ring1(e21)
    for peer in range(msg_ref.shape[0]):
        ring = jnp.where(tile > peer, to_low, to_high)
        msg_ref[peer, 0] = pack_level2(r2[2:4])
        msg_ref[peer, 1], msg_ref[peer, 2] = ring[0:2], ring[2:4]
    send(edge_ref, [pack_edge1(e21)])


def message_rows(ref):
    tiles = lax.axis_size("tile")
    return lambda field, half: ref[0:tiles, field, half : half + 1, :]


def choose(which, one, two):
    return lambda field, half: jnp.where(which, one(field, half), two(field, half))


def both_sides(first, second, step, lead):
    even = is_even("group", step, lead)
    one, two = message_rows(first), message_rows(second)
    return choose(even, two, one), choose(even, one, two)


def pair_rows(here, first, second):
    before, after = both_sides(first, second, 2, 1)
    even = is_even("group")
    one, two = message_rows(here.at[:, 0]), message_rows(here.at[:, 1])
    return choose(even, before, one), choose(even, one, two), choose(even, two, after)


def band_rows3(here, first, second):
    before, after = both_sides(first, second, 2, 1)
    even = is_even("group")
    six = [before(5, half) for half in range(2)]
    six += [here[:, core, 5, 0:1, :] for core in range(2)]
    six += [after(5, half) for half in range(2)]
    return [jnp.where(even, six[i], six[i + 1]) for i in range(5)]


def unpack_level2(field, own, low, high):
    tiles = lax.axis_size("tile")
    shape = (tiles, 16, NZ)
    sub, lane = iota(shape, 1), iota(shape, 2)
    halves = []
    for half in range(2):

        def spread(pick, half=half):
            return jnp.broadcast_to(pick(field, half), shape)

        v = jnp.where(sub < 4, spread(low), jnp.where(sub < 8, spread(own), spread(high)))
        v = jnp.where((lane % 4 == sub % 4) & (sub < 12), v, 0.0)
        halves.append(pair_sum(pair_sum(v, 1, 2), 2, 2))
    return jnp.stack(halves, axis=1).reshape((2 * tiles, 16, NZ))


def pack_level3(v):
    sub, lane = iota((16, NZ), 0), iota((16, NZ), 1)
    rows = []
    for j in range(v.shape[0] // 4):
        total = jnp.zeros((16, NZ), F32)
        for q in range(4):
            chosen = ((sub == 4) & (lane % 8 == 2 * q)) | ((sub == 6) & (lane % 8 == 2 * q + 1))
            total = total + jnp.where(chosen, v[4 * j + q], 0.0)
        rows.append(jnp.sum(total, axis=0, keepdims=True))
    return rows


def pack_sums3(v):
    even = is_even("group")
    tiles = v.shape[0]
    start = jnp.where(even, 8, 4)
    sub, lane = iota((24, NZ), 0), iota((24, NZ), 1)
    once = (sub >= start) & (sub < start + 8) & (sub % 2 == 0)
    total = jnp.zeros((24, NZ), F32)
    for q in range(tiles // 2):
        part = jnp.where(even, v[q], v[tiles // 2 + q])
        total = total + jnp.where(once & (lane % 8 == q), part, 0.0)
    return [jnp.sum(total, axis=0, keepdims=True)]


def descend_third(r2, s2, wx2, wy2, wz2, di2):
    first = r2 * di2
    second = first + di2 * (r2 - operate(first, s2, wx2, wy2, wz2, 1, 4))
    return second, restrict(r2 - operate(second, s2, wx2, wy2, wz2, 1, 4), 1, 4)


def sides_kernel(here, first_ref, second_ref):
    even = is_even("group", 2, 1)
    low, high = here[:, 0, 0:5], here[:, 1, 0:5]
    first_ref[:, 0:5] = jnp.where(even, high, low)
    second_ref[:, 0:5] = jnp.where(even, low, high)
    for core in range(2):
        rows = here[:, core, 5, 0:1, :]
        first_ref[:, 5, core : core + 1, :] = rows
        second_ref[:, 5, core : core + 1, :] = rows


def third_kernel(
    first, here, second,
    r2_ref, s2_ref, di2_ref, wx2_ref, wy2_ref, wz2_ref, e22_ref,
    s3_ref, di3_ref, wx3_ref, wy3_ref, wz3_ref, msg_ref,
):
    s3, wx3, wy3, wz3 = unpack_bands3(band_rows3(here, first, second))
    s3_ref[...], wx3_ref[...], wy3_ref[...], wz3_ref[...] = s3, wx3, wy3, wz3
    di3_ref[...] = relax_factor(s3, wx3, wy3, wz3, 2, 8)
    inner = s3 + wx3 + x_high(wx3) + wz3 + turn(wz3, -8, 2)
    low, own, high = pair_rows(here, first, second)
    r2, s2, wx2, wy2, wz2 = (unpack_level2(f, own, low, high) for f in range(5))
    di2 = relax_factor(s2, wx2, wy2, wz2, 1, 4)
    r2_ref[...], s2_ref[...], di2_ref[...] = r2, s2, di2
    wx2_ref[...], wy2_ref[...], wz2_ref[...] = wx2, wy2, wz2
    e22, r3 = descend_third(r2, s2, wx2, wy2, wz2, di2)
    e22_ref[...] = e22
    send(msg_ref, pack_level3(r3) + pack_sums3(inner))


def third_again_kernel(
    own, first, second, s2_ref, di2_ref, wx2_ref, wy2_ref, wz2_ref, r2_ref, e22_ref, msg_ref
):
    r2 = unpack_level2(0, message_rows(own), *both_sides(first, second, 1, 0))
    r2_ref[...] = r2
    e22, r3 = descend_third(
        r2, s2_ref[...], wx2_ref[...], wy2_ref[...], wz2_ref[...], di2_ref[...]
    )
    e22_ref[...] = e22
    send(msg_ref, pack_level3(r3))


def third_masks(shape):
    sub, lane = iota(shape, 1), iota(shape, 2)
    return sub // 4, (sub % 4) // 2, lane % 8


def octuple(v):
    return pair_sum(pair_sum(pair_sum(v, 1, 2), 2, 2), 4, 2)


def unpack_bands3(sources):
    shape = (sources[0].shape[0], 24, NZ)
    dev, half, slot = third_masks(shape)
    rows = jnp.broadcast_to(sources[0], shape)
    for d in range(1, 5):
        rows = jnp.where(dev == d, jnp.broadcast_to(sources[d], shape), rows)
    rows = jnp.where(dev < 5, rows, 0.0)
    return [octuple(jnp.where(slot == 2 * f + half, rows, 0.0)) for f in range(4)]


def unpack_r3(v):
    group = lax.axis_index("group")
    at = iota(v.shape, 1)
    shape = (v.shape[0], 24, NZ)
    dev, half, slot = third_masks(shape)
    rows = jnp.zeros(shape, F32)
    for d in range(5):
        near = jnp.sum(jnp.where(at == group + (d - 2), v, 0.0), axis=1, keepdims=True)
        rows = jnp.where(dev == d, jnp.broadcast_to(near, shape), rows)
    parts = [jnp.where(slot == 2 * q + half, rows, 0.0) for q in range(4)]
    return octuple(jnp.stack(parts, axis=1).reshape((4 * v.shape[0], 24, NZ)))


def line_sums(v, held):
    total = jnp.sum(v, axis=1, keepdims=True)
    lane = iota(total.shape, 2) % 8
    parts = [jnp.where(lane * held // 8 == q, total, 0.0) for q in range(held)]
    wide = jnp.stack(parts, axis=1).reshape((held * v.shape[0], 1, NZ))
    return octuple(wide)


def solve_third(r3, line, s3, di3, wx3, wy3, wz3):
    v = jnp.broadcast_to(line, r3.shape)
    for _ in range(COARSE_SWEEPS):
        v = v + di3 * (r3 - operate(v, s3, wx3, wy3, wz3, 2, 8))
    return turn(v, -4, 1)[:, 0:16]


def near_tiles(v):
    tile = lax.axis_index("tile")
    parts = []
    for off in (-1, 0, 1):
        total = jnp.zeros((2,) + v.shape[1:], F32)
        for t in range(v.shape[0] // 2):
            total = total + jnp.where(tile + off == t, v[2 * t : 2 * t + 2], 0.0)
        parts.append(total)
    return jnp.concatenate(parts, axis=0)


def widen_y(v):
    shape = (v.shape[0], 8, NZ)
    sub = iota(shape, 1)
    parts = []
    for at in (2, 4, 6, 8):
        first = jnp.broadcast_to(v[:, at : at + 1], shape)
        second = jnp.broadcast_to(v[:, at + 1 : at + 2], shape)
        parts.append(jnp.where(sub < 4, first, second))
    return jnp.concatenate(parts, axis=1)


def climb_to_second(corr3, r2_ref, s2_ref, di2_ref, wx2_ref, wy2_ref, wz2_ref, e22_ref):
    v = e22_ref[...] + x_repeat(corr3)
    v = v + di2_ref[...] * (
        r2_ref[...]
        - operate(v, s2_ref[...], wx2_ref[...], wy2_ref[...], wz2_ref[...], 1, 4)
    )
    return x_repeat(widen_y(near_tiles(v)))


def climb_to_first(v, r1_ref, s1_ref, di1_ref, wx1_ref, wy1_ref, wz1_ref):
    return v + di1_ref[...] * (
        r1_ref[...]
        - operate(v, s1_ref[...], wx1_ref[...], wy1_ref[...], wz1_ref[...], 2, 2)
    )


def strided(ref, first, thirds, groups, rows):
    parts = [ref[pl.ds(first + j, groups, stride=rows), :] for j in range(thirds)]
    return jnp.stack(parts, axis=0)


def climb_kernel(
    third_ref, s3_ref, di3_ref, wx3_ref, wy3_ref, wz3_ref,
    r2_ref, s2_ref, di2_ref, wx2_ref, wy2_ref, wz2_ref, e22_ref,
    r1_ref, s1_ref, di1_ref, wx1_ref, wy1_ref, wz1_ref, e21_ref, e2_ref,
    pre_ref, below_ref,
    *, groups, thirds, rows,
):
    r3 = strided(third_ref, 0, thirds, groups, rows)
    tiles = lax.axis_size("tile")
    sums = strided(third_ref, thirds, 1, groups, rows)
    odd = iota(sums.shape, 1) % 2
    below = jnp.concatenate(
        [line_sums(jnp.where(odd == half, sums, 0.0), 8)[: tiles // 2] for half in range(2)], axis=0
    )
    below_ref[...] = below
    corr3 = solve_third(
        unpack_r3(r3), line_sums(r3, 4) / below,
        s3_ref[...], di3_ref[...], wx3_ref[...], wy3_ref[...], wz3_ref[...],
    )
    corr2 = climb_to_second(corr3, r2_ref, s2_ref, di2_ref, wx2_ref, wy2_ref, wz2_ref, e22_ref)
    v = climb_to_first(
        e21_ref[...] + corr2, r1_ref, s1_ref, di1_ref, wx1_ref, wy1_ref, wz1_ref
    )
    own1 = x_repeat(v[4:8])
    pre_ref[...] = e2_ref[9:17, 8:24, :] + own1[:, 8:24, :]


def tile_rows(refs, even, off, at):
    tile = lax.axis_index("tile")
    total = jnp.zeros((2, NZ), F32)
    for t in range(lax.axis_size("tile")):
        rows = refs[0][t, at] if len(refs) == 1 else jnp.where(even, refs[0][t, at], refs[1][t, at])
        total = total + jnp.where(tile + off == t, rows, 0.0)
    return total


def ring_row(own, first, second, off):
    even = is_even("group")
    pairs = [tile_rows((own,), even, off, 1), tile_rows((own,), even, off, 2)]
    packed = [tile_rows((second, first), even, off, 2)[1:2]]
    packed += [pair[k : k + 1] for pair in pairs for k in range(2)]
    packed += [tile_rows((first, second), even, off, 1)[0:1]]
    return spread_pairs([row[None] for row in packed], 1)


def spread_pairs(packed, height):
    shape = (height, WY, NZ)
    sub, lane = iota(shape, 1), iota(shape, 2)
    rows = jnp.zeros(shape, F32)
    for k, row in enumerate(packed):
        rows = jnp.where(sub // 4 == k + 1, jnp.broadcast_to(row, shape), rows)
    return pair_sum(jnp.where(lane % 2 == (sub // 2) % 2, rows, 0.0), 1, 2)


def last_climb_kernel(
    third_ref, below_ref, s3_ref, di3_ref, wx3_ref, wy3_ref, wz3_ref,
    first, own, second,
    r2_ref, s2_ref, di2_ref, wx2_ref, wy2_ref, wz2_ref, e22_ref,
    r1_ref, s1_ref, di1_ref, wx1_ref, wy1_ref, wz1_ref, e21_ref,
    e2_ref, rhs_ref, s_ref, di_ref, wx_ref, wy_ref, wz_ref, u_ref, r_ref,
    out_ref, left_ref, pre_ref, v_ref,
    *, groups, thirds, rows,
):
    r3 = strided(third_ref, 0, thirds, groups, rows)
    corr3 = solve_third(
        unpack_r3(r3), line_sums(r3, 4) / below_ref[...],
        s3_ref[...], di3_ref[...], wx3_ref[...], wy3_ref[...], wz3_ref[...],
    )
    corr2 = climb_to_second(corr3, r2_ref, s2_ref, di2_ref, wx2_ref, wy2_ref, wz2_ref, e22_ref)
    tiles = lax.axis_size("tile")
    middle = e21_ref[3:9]
    sub = iota(middle.shape, 1)
    edge_first = jnp.concatenate([first[tiles, k] for k in range(3)], axis=0)[:, None]
    edge_second = jnp.concatenate([second[tiles, k] for k in range(3)], axis=0)[:, None]
    edge_low, edge_high = sides(edge_first, edge_second, "group")
    nothing = jnp.zeros_like(edge_low)
    edges = spread_pairs([edge_low] + [nothing] * 4 + [edge_high], 6)
    kept = (sub >= 6) & (sub < 26)
    middle = jnp.where(kept, middle, edges)
    blank = jnp.zeros((2, WY, NZ), F32)
    ends = [ring_row(own, first, second, off) for off in (-1, 1)]
    e21 = jnp.concatenate([blank, ends[0], middle, ends[1], blank], axis=0)
    v = climb_to_first(e21 + corr2, r1_ref, s1_ref, di1_ref, wx1_ref, wy1_ref, wz1_ref)
    pre_ref[7:19] = e2_ref[7:19] + x_repeat(v[3:9])

    def post(i, carry):
        at = 8 + 2 * i
        here = pl.ds(at, 2)
        v, av = operate_rows(pre_ref, s_ref, wx_ref, wy_ref, wz_ref, at, 2)
        v_ref[here] = u_ref[here] + v + di_ref[here] * (r_ref[here] - av)
        return carry

    lax.fori_loop(0, BX // 2 + 1, post, 0, unroll=True)

    def remain(i, carry):
        at = 9 + 2 * i
        v, av = operate_rows(v_ref, s_ref, wx_ref, wy_ref, wz_ref, at, 2)
        left = rhs_ref[pl.ds(at, 2)] - av
        out_ref[pl.ds(2 * i, 2)] = v[:, 8:24]
        left_ref[pl.ds(2 * i, 2)] = left[:, 8:24]
        return carry

    lax.fori_loop(0, BX // 2, remain, 0, unroll=True)


def call(body, outs, operands, scratch=()):
    cells = sum(math.prod(shape) for shape in outs)
    vmem = pl.BlockSpec(memory_space=pltpu.VMEM)
    return pl.pallas_call(
        body,
        out_shape=[jax.ShapeDtypeStruct(shape, F32) for shape in outs],
        in_specs=[vmem] * len(operands),
        out_specs=[vmem] * len(outs),
        scratch_shapes=[pltpu.VMEM(shape, F32) for shape in scratch],
        compiler_params=pltpu.CompilerParams(vmem_limit_bytes=16 * 1024 * 1024),
        cost_estimate=pl.CostEstimate(
            flops=20 * cells, bytes_accessed=8 * cells, transcendentals=0
        ),
    )(*operands)


def swaps(to_first, to_second, axis, step=1, lead=0):
    count = lax.axis_size(axis)

    def swap(cells, odd):
        ups = [
            (i, i + step) for i in range(count - step) if (i // step) % 2 == odd
        ]
        return lax.ppermute(cells, axis, ups + [(j, i) for i, j in ups])

    return swap(to_first, lead), swap(to_second, 1 - lead)


def surround(cells, dim):
    first, second = swaps(cells, cells, "tile")
    ydim = dim + 1
    even = is_even("group", 1, 1)

    def halves(v):
        low = lax.slice_in_dim(v, 0, 8, axis=ydim)
        high = lax.slice_in_dim(v, BY - 8, BY, axis=ydim)
        return jnp.where(even, high, low), jnp.where(even, low, high)

    parts = [halves(v) for v in (first, cells, second)]
    to_first, to_second = (jnp.concatenate(list(v), axis=dim) for v in zip(*parts, strict=True))
    return first, cells, second, *swaps(to_first, to_second, "group", 1, 1)


def everyone(blocks, axis):
    return lax.all_to_all(blocks, axis, 0, 0, tiled=True)


def pairs_of_tiles(block):
    tiles, groups = lax.axis_size("tile"), lax.axis_size("group")
    members = [
        [t * groups + 2 * pair + core for t in range(tiles) for core in range(2)]
        for pair in range(groups // 2)
    ]
    given = lax.all_to_all(
        block, ("tile", "group"), 0, 0, axis_index_groups=members, tiled=True
    )
    return given.reshape((tiles, 2) + block.shape[1:])


def shards(pressure_head, old_head, soil_type, conduct_sat, alpha_param, shape_param, water_span):
    tiles, groups = lax.axis_size("tile"), lax.axis_size("group")
    thirds = tiles // 4
    top, one, two = (PX, WY, NZ), (L1X, WY, NZ), (2 * tiles, 16, NZ)
    three, line = (tiles, 24, NZ), (tiles, 1, NZ)
    rows_once, rows_again = thirds + 1, thirds

    fields = pl.pallas_call(
        soil_kernel,
        out_shape=jax.ShapeDtypeStruct((4, BX, BY, NZ), F32),
        in_specs=[pl.BlockSpec(memory_space=pltpu.HBM)] * 7,
        out_specs=pl.BlockSpec(memory_space=pltpu.VMEM),
        scratch_shapes=[
            pltpu.VMEM((BX, BY, NZ), F32),
            pltpu.VMEM((BX, BY, NZ), F32),
            pltpu.VMEM((BX, BY, NZ), jnp.int32),
            *[pltpu.SMEM((SOILS,), F32) for _ in range(4)],
            pltpu.SemaphoreType.DMA((7,)),
        ],
    )(pressure_head, old_head, soil_type, conduct_sat, alpha_param, shape_param, water_span)
    around = surround(fields, 1)
    rhs, s0, di0, wx0, wy0, wz0, e2, r1, s1, di1, wx1, wy1, wz1, e21, msg = call(
        assemble_kernel,
        [top] * 7 + [one] * 7 + [(2 * tiles, 6, 2, NZ)],
        list(around),
        [top] * 4,
    )
    bands0 = [s0, di0, wx0, wy0, wz0]
    bands1 = [s1, di1, wx1, wy1, wz1]

    here = pairs_of_tiles(msg)
    to_first, to_second = call(sides_kernel, [(tiles, 6, 2, NZ)] * 2, [here])
    first, second = swaps(to_first, to_second, "group", 2, 1)
    r2, s2, di2, wx2, wy2, wz2, e22, *bands3, msg = call(
        third_kernel,
        [two] * 7 + [three] * 5 + [(groups, rows_once, 1, NZ)],
        [first, here, second],
    )
    bands2 = [s2, di2, wx2, wy2, wz2]
    third = everyone(msg, "group").reshape(groups * rows_once, NZ)
    pre, below = call(
        functools.partial(climb_kernel, groups=groups, thirds=thirds, rows=rows_once),
        [(BX, BY, NZ), line],
        [third, *bands3, r2, *bands2, e22, r1, *bands1, e21, e2],
    )

    around = surround(pre, 0)
    u, rem, e2, r1, e21, msg, edge = call(
        again_kernel,
        [top] * 3 + [one] * 2 + [(tiles, 3, 2, NZ), (1, 3, 2, NZ)],
        [*around, rhs, *bands0, *bands1],
        [top] * 2,
    )
    own = jnp.concatenate([everyone(msg, "tile"), edge], axis=0)
    first, second = swaps(own, own, "group")
    r2, e22, msg = call(
        third_again_kernel,
        [two] * 2 + [(groups, rows_again, 1, NZ)],
        [own, first, second, *bands2],
    )
    third = everyone(msg, "group").reshape(groups * rows_again, NZ)
    update, remainder = call(
        functools.partial(last_climb_kernel, groups=groups, thirds=thirds, rows=rows_again),
        [(BX, BY, NZ)] * 2,
        [third, below, *bands3, first, own, second, r2, *bands2, e22, r1, *bands1, e21]
        + [e2, rhs, *bands0, u, rem],
        [top] * 2,
    )
    return update, remainder


def solution(mesh):
    spec = P("tile", "group", None)
    return jax.shard_map(
        shards,
        mesh=mesh,
        in_specs=(spec, spec, spec, P(), P(), P(), P()),
        out_specs=(spec, spec),
        check_vma=False,
    )
```

```python
import functools
import math

import jax
import jax.numpy as jnp
from jax import lax
from jax.experimental import pallas as pl
from jax.experimental.pallas import tpu as pltpu
from jax.sharding import PartitionSpec as P

OMEGA = 2.0 / 3.0
STORAGE = 0.01
COARSE_SWEEPS = 4
SOILS = 12

BX, BY, NZ = 8, 16, 128
WX, WY = 24, 32
PX = WX + 2
L1X = WX // 2
F32 = jnp.float32


def iota(shape, dim):
    return lax.broadcasted_iota(jnp.int32, shape, dim)


def turn(v, step, axis):
    size = v.shape[axis]
    return pltpu.roll(v, step % size, axis)


def bit_of(v, step, axis):
    return (iota(v.shape, axis) // step) % 2 == 0


def pair_sum(v, step, axis):
    return v + jnp.where(bit_of(v, step, axis), turn(v, -step, axis), turn(v, step, axis))


def pair_low(v, step, axis):
    return jnp.where(bit_of(v, step, axis), v, turn(v, step, axis))


def x_low(v):
    return jnp.concatenate([v[:1], v[:-1]], axis=0)


def x_high(v):
    return jnp.concatenate([v[1:], jnp.zeros_like(v[:1])], axis=0)


def x_pair(v):
    return jnp.sum(v.reshape((v.shape[0] // 2, 2) + v.shape[1:]), axis=1)


def x_even(v):
    return v.reshape((v.shape[0] // 2, 2) + v.shape[1:])[:, 0]


def x_repeat(v):
    size = v.shape[0]
    wide = jnp.broadcast_to(v[:, None], (size, 2) + v.shape[1:])
    return wide.reshape((2 * size,) + v.shape[1:])


def operate(v, storage, wx, wy, wz, sy, sz):
    fx = wx * (v - x_low(v))
    fy = wy * (v - turn(v, sy, 1))
    fz = wz * (v - turn(v, sz, 2))
    flux = (fx - x_high(fx)) + (fy - turn(fy, -sy, 1)) + (fz - turn(fz, -sz, 2))
    return storage * v + flux


def relax_factor(storage, wx, wy, wz, sy, sz):
    diagonal = storage + wx + x_high(wx) + wy + turn(wy, -sy, 1) + wz + turn(wz, -sz, 2)
    return jnp.where(diagonal > 0.0, OMEGA / diagonal, 0.0)


def restrict(v, sy, sz):
    return pair_sum(pair_sum(x_pair(v), sy, 1), sz, 2)


def coarsen(storage, wx, wy, wz, sy, sz):
    return (
        restrict(storage, sy, sz),
        pair_sum(pair_sum(x_even(wx), sy, 1), sz, 2),
        pair_low(pair_sum(x_pair(wy), sz, 2), sy, 1),
        pair_low(pair_sum(x_pair(wz), sy, 1), sz, 2),
    )


def operate_rows(v_ref, s_ref, wx_ref, wy_ref, wz_ref, at, size):
    v = v_ref[pl.ds(at, size)]
    wx = wx_ref[pl.ds(at, size)]
    fy = wy_ref[pl.ds(at, size)] * (v - turn(v, 1, 1))
    fz = wz_ref[pl.ds(at, size)] * (v - turn(v, 1, 2))
    flux = wx * (v - v_ref[pl.ds(at - 1, size)])
    flux = flux - wx_ref[pl.ds(at + 1, size)] * (v_ref[pl.ds(at + 1, size)] - v)
    flux = flux + (fy - turn(fy, -1, 1)) + (fz - turn(fz, -1, 2))
    return v, s_ref[pl.ds(at, size)] * v + flux


def blank_ends(ref):
    ref[0] = jnp.zeros((WY, NZ), F32)
    ref[PX - 1] = jnp.zeros((WY, NZ), F32)


def blank_level1(ref, size):
    ref[0:size] = jnp.zeros((size, WY, NZ), F32)
    ref[L1X - size :] = jnp.zeros((size, WY, NZ), F32)


def pack_level2(v):
    sub, lane = iota(v.shape, 1), iota(v.shape, 2)
    chosen = (sub >= 8) & (sub < 24) & (sub % 4 == 0) & ((sub - 8) // 4 == lane % 4)
    return jnp.sum(jnp.where(chosen, v, 0.0), axis=1)


def send(msg_ref, rows):
    rows = list(rows)
    parts, height = msg_ref.shape[1:3]
    spare = parts * height - sum(row.shape[0] for row in rows)
    if spare:
        rows.append(jnp.zeros((spare, NZ), F32))
    whole = jnp.concatenate(rows, axis=0)
    for part in range(parts):
        piece = whole[part * height : (part + 1) * height]
        for peer in range(msg_ref.shape[0]):
            msg_ref[peer, part] = piece


def pack_bands3(fields):
    sub, lane = iota((1, WY, NZ), 1), iota((1, WY, NZ), 2)
    total = jnp.zeros((1, WY, NZ), F32)
    for f, v in enumerate(fields):
        chosen = ((sub == 8) & (lane % 8 == 2 * f)) | ((sub == 16) & (lane % 8 == 2 * f + 1))
        total = total + jnp.where(chosen, v, 0.0)
    return jnp.sum(total, axis=1)


def pack_ring1(v):
    sub, lane = iota((2, WY, NZ), 1), iota((2, WY, NZ), 2)
    rows = v[5:7]
    parts = []
    for k in range(4):
        chosen = ((sub == 8 + 4 * k) & (lane % 2 == 0)) | ((sub == 10 + 4 * k) & (lane % 2 == 1))
        parts.append(jnp.sum(jnp.where(chosen, rows, 0.0), axis=1, keepdims=True))
    return [jnp.concatenate([part[x] for part in parts], axis=0) for x in range(2)]


def pack_edge1(v):
    sub, lane = iota((6, WY, NZ), 1), iota((6, WY, NZ), 2)
    chosen = ((sub == 20) & (lane % 2 == 0)) | ((sub == 10) & (lane % 2 == 1))
    return jnp.sum(jnp.where(chosen, v[3:9], 0.0), axis=1)


def descend_top(r_ref, e1_ref, e2_ref, s_ref, wx_ref, wy_ref, wz_ref, di_ref, r1_ref):
    def second(i, carry):
        at = 1 + 2 * i
        v, av = operate_rows(e1_ref, s_ref, wx_ref, wy_ref, wz_ref, at, 2)
        e2_ref[pl.ds(at, 2)] = v + di_ref[pl.ds(at, 2)] * (r_ref[pl.ds(at, 2)] - av)
        return carry

    lax.fori_loop(1, WX // 2 - 1, second, 0, unroll=5)

    def third(i, carry):
        at = 1 + 2 * i
        _, av = operate_rows(e2_ref, s_ref, wx_ref, wy_ref, wz_ref, at, 2)
        r1_ref[pl.ds(i, 1)] = restrict(r_ref[pl.ds(at, 2)] - av, 1, 1)
        return carry

    lax.fori_loop(2, WX // 2 - 2, third, 0, unroll=4)


def descend_second(r1, s1, wx1, wy1, wz1, di1):
    first = r1 * di1
    second = first + di1 * (r1 - operate(first, s1, wx1, wy1, wz1, 2, 2))
    defect = r1 - operate(second, s1, wx1, wy1, wz1, 2, 2)
    return second, restrict(defect, 2, 2)


def soil_kernel(
    head_in, old_in, soil_in, ks_in, alpha_in, shape_in, span_in, out_ref,
    head_ref, old_ref, soil_ref, ks_ref, alpha_ref, shape_ref, span_ref, sems,
):
    given = (ks_in, alpha_in, shape_in, span_in, head_in, old_in, soil_in)
    held = (ks_ref, alpha_ref, shape_ref, span_ref, head_ref, old_ref, soil_ref)
    copies = [
        pltpu.make_async_copy(src, dst, sems.at[i])
        for i, (src, dst) in enumerate(zip(given, held, strict=True))
    ]
    for copy in copies:
        copy.start()
    for copy in copies:
        copy.wait()

    def cells(i, carry):
        row = pl.ds(i, 1)
        head, old, soil = head_ref[row], old_ref[row], soil_ref[row]
        ks = jnp.full(soil.shape, ks_ref[0])
        alpha = jnp.full(soil.shape, alpha_ref[0])
        shape_n = jnp.full(soil.shape, shape_ref[0])
        span = jnp.full(soil.shape, span_ref[0])
        for kind in range(1, SOILS):
            hit = soil == kind
            ks = jnp.where(hit, ks_ref[kind], ks)
            alpha = jnp.where(hit, alpha_ref[kind], alpha)
            shape_n = jnp.where(hit, shape_ref[kind], shape_n)
            span = jnp.where(hit, span_ref[kind], span)
        shape_m = 1.0 - 1.0 / shape_n
        power = jnp.exp(shape_n * jnp.log(alpha * -head))
        old_power = jnp.exp(shape_n * jnp.log(alpha * -old))
        saturation = jnp.exp(-shape_m * jnp.log1p(power))
        old_saturation = jnp.exp(-shape_m * jnp.log1p(old_power))
        portion = 1.0 / (1.0 + power)
        factor = 1.0 - jnp.exp(shape_m * jnp.log(power / (1.0 + power)))
        capacity = span * shape_m * shape_n * power / -head * saturation * portion
        out_ref[0, row] = head
        out_ref[1, row] = ks * jnp.sqrt(saturation) * factor * factor
        out_ref[2, row] = capacity + STORAGE
        out_ref[3, row] = span * (saturation - old_saturation) + STORAGE * (head - old)
        return carry

    lax.fori_loop(0, BX, cells, 0, unroll=2)


def is_even(axis, step=1, lead=0):
    return (lax.axis_index(axis) // step) % 2 == lead


def sides(first, second, axis, lead=0):
    even = is_even(axis, 1, lead)
    return jnp.where(even, second, first), jnp.where(even, first, second)


def fill_window(ref, xfirst, own, xsecond, yfirst, ysecond):
    ref[1 : 1 + BX, 8:24, :], ref[1 + 2 * BX : 1 + 3 * BX, 8:24, :] = sides(xfirst, xsecond, "tile")
    ref[1 + BX : 1 + 2 * BX, 8:24, :] = own
    ylow, yhigh = sides(yfirst, ysecond, "group", 1)
    for y, part in ((0, ylow), (24, yhigh)):
        low, high = sides(part[:BX], part[2 * BX :], "tile")
        ref[1 : 1 + BX, y : y + 8, :] = low
        ref[1 + BX : 1 + 2 * BX, y : y + 8, :] = part[BX : 2 * BX]
        ref[1 + 2 * BX : 1 + 3 * BX, y : y + 8, :] = high


def assemble_kernel(
    xfirst, own, xsecond, yfirst, ysecond,
    r_ref, s_ref, di_ref, wx_ref, wy_ref, wz_ref, e2_ref,
    r1_ref, s1_ref, di1_ref, wx1_ref, wy1_ref, wz1_ref, e21_ref, msg_ref,
    h_ref, k_ref, m_ref, e1_ref,
):
    for ref in (h_ref, k_ref, s_ref, wx_ref, wy_ref, wz_ref, di_ref, r_ref, e1_ref, e2_ref):
        blank_ends(ref)
    for f, ref in enumerate((h_ref, k_ref, s_ref, m_ref)):
        fill_window(ref, xfirst[f], own[f], xsecond[f], yfirst[f], ysecond[f])

    def harmonic(a, b):
        total = a + b
        return jnp.where(total > 0.0, 2.0 * a * b / total, 0.0)

    def faces(i, carry):
        at = 1 + 2 * i
        k = k_ref[pl.ds(at, 2)]
        wx_ref[pl.ds(at, 2)] = harmonic(k, k_ref[pl.ds(at - 1, 2)])
        wy_ref[pl.ds(at, 2)] = harmonic(k, turn(k, 1, 1))
        wz = harmonic(k, turn(k, 1, 2))
        wz_ref[pl.ds(at, 2)] = jnp.where(iota(wz.shape, 2) == 0, 0.0, wz)
        return carry

    lax.fori_loop(0, WX // 2, faces, 0, unroll=4)

    def right_side(i, carry):
        at = 1 + 2 * i
        rows = pl.ds(at, 2)
        h, wx, wy, wz = h_ref[rows], wx_ref[rows], wy_ref[rows], wz_ref[rows]
        wx_up = wx_ref[pl.ds(at + 1, 2)]
        fy = wy * (h - turn(h, 1, 1))
        fz = wz * (h - turn(h, 1, 2) + 1.0)
        flux = wx * (h - h_ref[pl.ds(at - 1, 2)]) - wx_up * (h_ref[pl.ds(at + 1, 2)] - h)
        flux = flux + (fy - turn(fy, -1, 1)) + (fz - turn(fz, -1, 2))
        rhs = -(m_ref[rows] + flux)
        diagonal = s_ref[rows] + wx + wx_up + wy + turn(wy, -1, 1) + wz + turn(wz, -1, 2)
        di = jnp.where(diagonal > 0.0, OMEGA / diagonal, 0.0)
        r_ref[rows] = rhs
        di_ref[rows] = di
        e1_ref[rows] = rhs * di
        return carry

    lax.fori_loop(0, WX // 2, right_side, 0, unroll=4)

    def bands(i, carry):
        rows = pl.ds(1 + 2 * i, 2)
        s1, wx1, wy1, wz1 = coarsen(s_ref[rows], wx_ref[rows], wy_ref[rows], wz_ref[rows], 1, 1)
        row = pl.ds(i, 1)
        s1_ref[row], wx1_ref[row], wy1_ref[row], wz1_ref[row] = s1, wx1, wy1, wz1
        return carry

    lax.fori_loop(1, WX // 2 - 1, bands, 0, unroll=5)
    for ref in (s1_ref, wx1_ref, wy1_ref, wz1_ref):
        blank_level1(ref, 1)
    blank_level1(r1_ref, 2)
    descend_top(r_ref, e1_ref, e2_ref, s_ref, wx_ref, wy_ref, wz_ref, di_ref, r1_ref)

    s1, wx1, wy1, wz1 = s1_ref[...], wx1_ref[...], wy1_ref[...], wz1_ref[...]
    di1 = relax_factor(s1, wx1, wy1, wz1, 2, 2)
    di1_ref[...] = di1
    e21, r2 = descend_second(r1_ref[...], s1, wx1, wy1, wz1, di1)
    e21_ref[...] = e21
    bands2 = coarsen(s1, wx1, wy1, wz1, 2, 2)
    bands3 = coarsen(*(v[2:4] for v in bands2), 4, 4)
    rows = [pack_level2(v[2:4]) for v in (r2,) + bands2]
    send(msg_ref, rows + [pack_bands3(bands3)])


def again_kernel(
    xfirst, own, xsecond, yfirst, ysecond, rhs_ref, s_ref, di_ref, wx_ref, wy_ref, wz_ref,
    s1_ref, di1_ref, wx1_ref, wy1_ref, wz1_ref,
    u_ref, r_ref, e2_ref, r1_ref, e21_ref, msg_ref, edge_ref, pre_ref, e1_ref,
):
    for ref in (pre_ref, u_ref, r_ref, e1_ref, e2_ref):
        blank_ends(ref)
    fill_window(pre_ref, xfirst[...], own[...], xsecond[...], yfirst[...], ysecond[...])

    def post(i, carry):
        at = 1 + 2 * i
        rows = pl.ds(at, 2)
        v, av = operate_rows(pre_ref, s_ref, wx_ref, wy_ref, wz_ref, at, 2)
        u_ref[rows] = v + di_ref[rows] * (rhs_ref[rows] - av)
        return carry

    lax.fori_loop(0, WX // 2, post, 0, unroll=4)

    def remain(i, carry):
        at = 1 + 2 * i
        rows = pl.ds(at, 2)
        _, av = operate_rows(u_ref, s_ref, wx_ref, wy_ref, wz_ref, at, 2)
        left = rhs_ref[rows] - av
        r_ref[rows] = left
        e1_ref[rows] = left * di_ref[rows]
        return carry

    lax.fori_loop(1, WX // 2 - 1, remain, 0, unroll=5)
    descend_top(r_ref, e1_ref, e2_ref, s_ref, wx_ref, wy_ref, wz_ref, di_ref, r1_ref)
    blank_level1(r1_ref, 2)
    e21, r2 = descend_second(
        r1_ref[...], s1_ref[...], wx1_ref[...], wy1_ref[...], wz1_ref[...], di1_ref[...]
    )
    e21_ref[...] = e21
    tile = lax.axis_index("tile")
    to_low, to_high = pack_ring1(e21)
    for peer in range(msg_ref.shape[0]):
        ring = jnp.where(tile > peer, to_low, to_high)
        msg_ref[peer, 0] = pack_level2(r2[2:4])
        msg_ref[peer, 1], msg_ref[peer, 2] = ring[0:2], ring[2:4]
    send(edge_ref, [pack_edge1(e21)])


def message_rows(ref):
    tiles = lax.axis_size("tile")
    return lambda field, half: ref[0:tiles, field, half : half + 1, :]


def choose(which, one, two):
    return lambda field, half: jnp.where(which, one(field, half), two(field, half))


def both_sides(first, second, step, lead):
    even = is_even("group", step, lead)
    one, two = message_rows(first), message_rows(second)
    return choose(even, two, one), choose(even, one, two)


def pair_rows(here, first, second):
    before, after = both_sides(first, second, 2, 1)
    even = is_even("group")
    one, two = message_rows(here.at[:, 0]), message_rows(here.at[:, 1])
    return choose(even, before, one), choose(even, one, two), choose(even, two, after)


def band_rows3(here, first, second):
    before, after = both_sides(first, second, 2, 1)
    even = is_even("group")
    six = [before(5, half) for half in range(2)]
    six += [here[:, core, 5, 0:1, :] for core in range(2)]
    six += [after(5, half) for half in range(2)]
    return [jnp.where(even, six[i], six[i + 1]) for i in range(5)]


def unpack_level2(field, own, low, high):
    tiles = lax.axis_size("tile")
    shape = (tiles, 16, NZ)
    sub, lane = iota(shape, 1), iota(shape, 2)
    halves = []
    for half in range(2):

        def spread(pick, half=half):
            return jnp.broadcast_to(pick(field, half), shape)

        v = jnp.where(sub < 4, spread(low), jnp.where(sub < 8, spread(own), spread(high)))
        v = jnp.where((lane % 4 == sub % 4) & (sub < 12), v, 0.0)
        halves.append(pair_sum(pair_sum(v, 1, 2), 2, 2))
    return jnp.stack(halves, axis=1).reshape((2 * tiles, 16, NZ))


def pack_level3(v):
    sub, lane = iota((16, NZ), 0), iota((16, NZ), 1)
    rows = []
    for j in range(v.shape[0] // 4):
        total = jnp.zeros((16, NZ), F32)
        for q in range(4):
            chosen = ((sub == 4) & (lane % 8 == 2 * q)) | ((sub == 6) & (lane % 8 == 2 * q + 1))
            total = total + jnp.where(chosen, v[4 * j + q], 0.0)
        rows.append(jnp.sum(total, axis=0, keepdims=True))
    return rows


def pack_sums3(v):
    even = is_even("group")
    tiles = v.shape[0]
    start = jnp.where(even, 8, 4)
    sub, lane = iota((24, NZ), 0), iota((24, NZ), 1)
    once = (sub >= start) & (sub < start + 8) & (sub % 2 == 0)
    total = jnp.zeros((24, NZ), F32)
    for q in range(tiles // 2):
        part = jnp.where(even, v[q], v[tiles // 2 + q])
        total = total + jnp.where(once & (lane % 8 == q), part, 0.0)
    return [jnp.sum(total, axis=0, keepdims=True)]


def descend_third(r2, s2, wx2, wy2, wz2, di2):
    first = r2 * di2
    second = first + di2 * (r2 - operate(first, s2, wx2, wy2, wz2, 1, 4))
    return second, restrict(r2 - operate(second, s2, wx2, wy2, wz2, 1, 4), 1, 4)


def sides_kernel(here, first_ref, second_ref):
    even = is_even("group", 2, 1)
    low, high = here[:, 0, 0:5], here[:, 1, 0:5]
    first_ref[:, 0:5] = jnp.where(even, high, low)
    second_ref[:, 0:5] = jnp.where(even, low, high)
    for core in range(2):
        rows = here[:, core, 5, 0:1, :]
        first_ref[:, 5, core : core + 1, :] = rows
        second_ref[:, 5, core : core + 1, :] = rows


def third_kernel(
    first, here, second,
    r2_ref, s2_ref, di2_ref, wx2_ref, wy2_ref, wz2_ref, e22_ref,
    s3_ref, di3_ref, wx3_ref, wy3_ref, wz3_ref, msg_ref,
):
    s3, wx3, wy3, wz3 = unpack_bands3(band_rows3(here, first, second))
    s3_ref[...], wx3_ref[...], wy3_ref[...], wz3_ref[...] = s3, wx3, wy3, wz3
    di3_ref[...] = relax_factor(s3, wx3, wy3, wz3, 2, 8)
    inner = s3 + wx3 + x_high(wx3) + wz3 + turn(wz3, -8, 2)
    low, own, high = pair_rows(here, first, second)
    r2, s2, wx2, wy2, wz2 = (unpack_level2(f, own, low, high) for f in range(5))
    di2 = relax_factor(s2, wx2, wy2, wz2, 1, 4)
    r2_ref[...], s2_ref[...], di2_ref[...] = r2, s2, di2
    wx2_ref[...], wy2_ref[...], wz2_ref[...] = wx2, wy2, wz2
    e22, r3 = descend_third(r2, s2, wx2, wy2, wz2, di2)
    e22_ref[...] = e22
    send(msg_ref, pack_level3(r3) + pack_sums3(inner))


def third_again_kernel(
    own, first, second, s2_ref, di2_ref, wx2_ref, wy2_ref, wz2_ref, r2_ref, e22_ref, msg_ref
):
    r2 = unpack_level2(0, message_rows(own), *both_sides(first, second, 1, 0))
    r2_ref[...] = r2
    e22, r3 = descend_third(
        r2, s2_ref[...], wx2_ref[...], wy2_ref[...], wz2_ref[...], di2_ref[...]
    )
    e22_ref[...] = e22
    send(msg_ref, pack_level3(r3))


def third_masks(shape):
    sub, lane = iota(shape, 1), iota(shape, 2)
    return sub // 4, (sub % 4) // 2, lane % 8


def octuple(v):
    return pair_sum(pair_sum(pair_sum(v, 1, 2), 2, 2), 4, 2)


def unpack_bands3(sources):
    shape = (sources[0].shape[0], 24, NZ)
    dev, half, slot = third_masks(shape)
    rows = jnp.broadcast_to(sources[0], shape)
    for d in range(1, 5):
        rows = jnp.where(dev == d, jnp.broadcast_to(sources[d], shape), rows)
    rows = jnp.where(dev < 5, rows, 0.0)
    return [octuple(jnp.where(slot == 2 * f + half, rows, 0.0)) for f in range(4)]


def unpack_r3(v):
    group = lax.axis_index("group")
    at = iota(v.shape, 1)
    shape = (v.shape[0], 24, NZ)
    dev, half, slot = third_masks(shape)
    rows = jnp.zeros(shape, F32)
    for d in range(5):
        near = jnp.sum(jnp.where(at == group + (d - 2), v, 0.0), axis=1, keepdims=True)
        rows = jnp.where(dev == d, jnp.broadcast_to(near, shape), rows)
    parts = [jnp.where(slot == 2 * q + half, rows, 0.0) for q in range(4)]
    return octuple(jnp.stack(parts, axis=1).reshape((4 * v.shape[0], 24, NZ)))


def line_sums(v, held):
    total = jnp.sum(v, axis=1, keepdims=True)
    lane = iota(total.shape, 2) % 8
    parts = [jnp.where(lane * held // 8 == q, total, 0.0) for q in range(held)]
    wide = jnp.stack(parts, axis=1).reshape((held * v.shape[0], 1, NZ))
    return octuple(wide)


def solve_third(r3, line, s3, di3, wx3, wy3, wz3):
    v = jnp.broadcast_to(line, r3.shape)
    for _ in range(COARSE_SWEEPS):
        v = v + di3 * (r3 - operate(v, s3, wx3, wy3, wz3, 2, 8))
    return turn(v, -4, 1)[:, 0:16]


def widen_y(v):
    shape = (v.shape[0], 8, NZ)
    sub = iota(shape, 1)
    parts = []
    for at in (2, 4, 6, 8):
        first = jnp.broadcast_to(v[:, at : at + 1], shape)
        second = jnp.broadcast_to(v[:, at + 1 : at + 2], shape)
        parts.append(jnp.where(sub < 4, first, second))
    return jnp.concatenate(parts, axis=1)


def climb_to_second(
    corr3, r2_ref, s2_ref, di2_ref, wx2_ref, wy2_ref, wz2_ref, e22_ref, corr3_ref, corr2_ref
):
    tile, tiles = lax.axis_index("tile"), lax.axis_size("tile")
    start = jnp.clip(tile - 2, 0, tiles - 4)
    corr3_ref[...] = corr3
    rows = pl.ds(2 * start, 8)
    v = e22_ref[rows] + x_repeat(corr3_ref[pl.ds(start, 4)])
    v = v + di2_ref[rows] * (
        r2_ref[rows]
        - operate(v, s2_ref[rows], wx2_ref[rows], wy2_ref[rows], wz2_ref[rows], 1, 4)
    )
    corr2_ref[0:4] = jnp.zeros((4, 16, NZ), F32)
    corr2_ref[4:12] = v
    corr2_ref[12:16] = jnp.zeros((4, 16, NZ), F32)
    near = corr2_ref[pl.ds(2 * (tile - start) + 2, 6)]
    return x_repeat(widen_y(near))


def climb_to_first(v, r1_ref, s1_ref, di1_ref, wx1_ref, wy1_ref, wz1_ref):
    rows = slice(2, 10)
    v = v[rows]
    return v + di1_ref[rows] * (
        r1_ref[rows]
        - operate(v, s1_ref[rows], wx1_ref[rows], wy1_ref[rows], wz1_ref[rows], 2, 2)
    )


def strided(ref, first, thirds, groups, rows):
    parts = [ref[pl.ds(first + j, groups, stride=rows), :] for j in range(thirds)]
    return jnp.stack(parts, axis=0)


def climb_kernel(
    third_ref, s3_ref, di3_ref, wx3_ref, wy3_ref, wz3_ref,
    r2_ref, s2_ref, di2_ref, wx2_ref, wy2_ref, wz2_ref, e22_ref,
    r1_ref, s1_ref, di1_ref, wx1_ref, wy1_ref, wz1_ref, e21_ref, e2_ref,
    pre_ref, below_ref, corr3_ref, corr2_ref,
    *, groups, thirds, rows,
):
    r3 = strided(third_ref, 0, thirds, groups, rows)
    tiles = lax.axis_size("tile")
    sums = strided(third_ref, thirds, 1, groups, rows)
    odd = iota(sums.shape, 1) % 2
    below = jnp.concatenate(
        [line_sums(jnp.where(odd == half, sums, 0.0), 8)[: tiles // 2] for half in range(2)], axis=0
    )
    below_ref[...] = below
    corr3 = solve_third(
        unpack_r3(r3), line_sums(r3, 4) / below,
        s3_ref[...], di3_ref[...], wx3_ref[...], wy3_ref[...], wz3_ref[...],
    )
    corr2 = climb_to_second(
        corr3, r2_ref, s2_ref, di2_ref, wx2_ref, wy2_ref, wz2_ref, e22_ref, corr3_ref, corr2_ref
    )
    v = climb_to_first(
        e21_ref[...] + corr2, r1_ref, s1_ref, di1_ref, wx1_ref, wy1_ref, wz1_ref
    )
    own1 = x_repeat(v[2:6])
    pre_ref[...] = e2_ref[9:17, 8:24, :] + own1[:, 8:24, :]


def tile_rows(refs, even, off, at):
    tile = lax.axis_index("tile")
    total = jnp.zeros((2, NZ), F32)
    for t in range(lax.axis_size("tile")):
        rows = refs[0][t, at] if len(refs) == 1 else jnp.where(even, refs[0][t, at], refs[1][t, at])
        total = total + jnp.where(tile + off == t, rows, 0.0)
    return total


def ring_row(own, first, second, off):
    even = is_even("group")
    pairs = [tile_rows((own,), even, off, 1), tile_rows((own,), even, off, 2)]
    packed = [tile_rows((second, first), even, off, 2)[1:2]]
    packed += [pair[k : k + 1] for pair in pairs for k in range(2)]
    packed += [tile_rows((first, second), even, off, 1)[0:1]]
    return spread_pairs([row[None] for row in packed], 1)


def spread_pairs(packed, height):
    shape = (height, WY, NZ)
    sub, lane = iota(shape, 1), iota(shape, 2)
    rows = jnp.zeros(shape, F32)
    for k, row in enumerate(packed):
        rows = jnp.where(sub // 4 == k + 1, jnp.broadcast_to(row, shape), rows)
    return pair_sum(jnp.where(lane % 2 == (sub // 2) % 2, rows, 0.0), 1, 2)


def last_climb_kernel(
    third_ref, below_ref, s3_ref, di3_ref, wx3_ref, wy3_ref, wz3_ref,
    first, own, second,
    r2_ref, s2_ref, di2_ref, wx2_ref, wy2_ref, wz2_ref, e22_ref,
    r1_ref, s1_ref, di1_ref, wx1_ref, wy1_ref, wz1_ref, e21_ref,
    e2_ref, rhs_ref, s_ref, di_ref, wx_ref, wy_ref, wz_ref, u_ref, r_ref,
    out_ref, left_ref, pre_ref, v_ref, corr3_ref, corr2_ref,
    *, groups, thirds, rows,
):
    r3 = strided(third_ref, 0, thirds, groups, rows)
    corr3 = solve_third(
        unpack_r3(r3), line_sums(r3, 4) / below_ref[...],
        s3_ref[...], di3_ref[...], wx3_ref[...], wy3_ref[...], wz3_ref[...],
    )
    corr2 = climb_to_second(
        corr3, r2_ref, s2_ref, di2_ref, wx2_ref, wy2_ref, wz2_ref, e22_ref, corr3_ref, corr2_ref
    )
    tiles = lax.axis_size("tile")
    middle = e21_ref[3:9]
    sub = iota(middle.shape, 1)
    edge_first = jnp.concatenate([first[tiles, k] for k in range(3)], axis=0)[:, None]
    edge_second = jnp.concatenate([second[tiles, k] for k in range(3)], axis=0)[:, None]
    edge_low, edge_high = sides(edge_first, edge_second, "group")
    nothing = jnp.zeros_like(edge_low)
    edges = spread_pairs([edge_low] + [nothing] * 4 + [edge_high], 6)
    kept = (sub >= 6) & (sub < 26)
    middle = jnp.where(kept, middle, edges)
    blank = jnp.zeros((2, WY, NZ), F32)
    ends = [ring_row(own, first, second, off) for off in (-1, 1)]
    e21 = jnp.concatenate([blank, ends[0], middle, ends[1], blank], axis=0)
    v = climb_to_first(e21 + corr2, r1_ref, s1_ref, di1_ref, wx1_ref, wy1_ref, wz1_ref)
    pre_ref[7:19] = e2_ref[7:19] + x_repeat(v[1:7])

    def post(i, carry):
        at = 8 + 2 * i
        here = pl.ds(at, 2)
        v, av = operate_rows(pre_ref, s_ref, wx_ref, wy_ref, wz_ref, at, 2)
        v_ref[here] = u_ref[here] + v + di_ref[here] * (r_ref[here] - av)
        return carry

    lax.fori_loop(0, BX // 2 + 1, post, 0, unroll=True)

    def remain(i, carry):
        at = 9 + 2 * i
        v, av = operate_rows(v_ref, s_ref, wx_ref, wy_ref, wz_ref, at, 2)
        left = rhs_ref[pl.ds(at, 2)] - av
        out_ref[pl.ds(2 * i, 2)] = v[:, 8:24]
        left_ref[pl.ds(2 * i, 2)] = left[:, 8:24]
        return carry

    lax.fori_loop(0, BX // 2, remain, 0, unroll=True)


def call(body, outs, operands, scratch=()):
    cells = sum(math.prod(shape) for shape in outs)
    vmem = pl.BlockSpec(memory_space=pltpu.VMEM)
    return pl.pallas_call(
        body,
        out_shape=[jax.ShapeDtypeStruct(shape, F32) for shape in outs],
        in_specs=[vmem] * len(operands),
        out_specs=[vmem] * len(outs),
        scratch_shapes=[pltpu.VMEM(shape, F32) for shape in scratch],
        compiler_params=pltpu.CompilerParams(vmem_limit_bytes=16 * 1024 * 1024),
        cost_estimate=pl.CostEstimate(
            flops=20 * cells, bytes_accessed=8 * cells, transcendentals=0
        ),
    )(*operands)


def swaps(to_first, to_second, axis, step=1, lead=0):
    count = lax.axis_size(axis)

    def swap(cells, odd):
        ups = [
            (i, i + step) for i in range(count - step) if (i // step) % 2 == odd
        ]
        return lax.ppermute(cells, axis, ups + [(j, i) for i, j in ups])

    return swap(to_first, lead), swap(to_second, 1 - lead)


def surround(cells, dim):
    first, second = swaps(cells, cells, "tile")
    ydim = dim + 1
    even = is_even("group", 1, 1)

    def halves(v):
        low = lax.slice_in_dim(v, 0, 8, axis=ydim)
        high = lax.slice_in_dim(v, BY - 8, BY, axis=ydim)
        return jnp.where(even, high, low), jnp.where(even, low, high)

    parts = [halves(v) for v in (first, cells, second)]
    to_first, to_second = (jnp.concatenate(list(v), axis=dim) for v in zip(*parts, strict=True))
    return first, cells, second, *swaps(to_first, to_second, "group", 1, 1)


def everyone(blocks, axis):
    return lax.all_to_all(blocks, axis, 0, 0, tiled=True)


def pairs_of_tiles(block):
    tiles, groups = lax.axis_size("tile"), lax.axis_size("group")
    members = [
        [t * groups + 2 * pair + core for t in range(tiles) for core in range(2)]
        for pair in range(groups // 2)
    ]
    given = lax.all_to_all(
        block, ("tile", "group"), 0, 0, axis_index_groups=members, tiled=True
    )
    return given.reshape((tiles, 2) + block.shape[1:])


def shards(pressure_head, old_head, soil_type, conduct_sat, alpha_param, shape_param, water_span):
    tiles, groups = lax.axis_size("tile"), lax.axis_size("group")
    thirds = tiles // 4
    top, one, two = (PX, WY, NZ), (L1X, WY, NZ), (2 * tiles, 16, NZ)
    three, line = (tiles, 24, NZ), (tiles, 1, NZ)
    rows_once, rows_again = thirds + 1, thirds

    fields = pl.pallas_call(
        soil_kernel,
        out_shape=jax.ShapeDtypeStruct((4, BX, BY, NZ), F32),
        in_specs=[pl.BlockSpec(memory_space=pltpu.HBM)] * 7,
        out_specs=pl.BlockSpec(memory_space=pltpu.VMEM),
        scratch_shapes=[
            pltpu.VMEM((BX, BY, NZ), F32),
            pltpu.VMEM((BX, BY, NZ), F32),
            pltpu.VMEM((BX, BY, NZ), jnp.int32),
            *[pltpu.SMEM((SOILS,), F32) for _ in range(4)],
            pltpu.SemaphoreType.DMA((7,)),
        ],
    )(pressure_head, old_head, soil_type, conduct_sat, alpha_param, shape_param, water_span)
    around = surround(fields, 1)
    rhs, s0, di0, wx0, wy0, wz0, e2, r1, s1, di1, wx1, wy1, wz1, e21, msg = call(
        assemble_kernel,
        [top] * 7 + [one] * 7 + [(2 * tiles, 6, 2, NZ)],
        list(around),
        [top] * 4,
    )
    bands0 = [s0, di0, wx0, wy0, wz0]
    bands1 = [s1, di1, wx1, wy1, wz1]

    here = pairs_of_tiles(msg)
    to_first, to_second = call(sides_kernel, [(tiles, 6, 2, NZ)] * 2, [here])
    first, second = swaps(to_first, to_second, "group", 2, 1)
    r2, s2, di2, wx2, wy2, wz2, e22, *bands3, msg = call(
        third_kernel,
        [two] * 7 + [three] * 5 + [(groups, rows_once, 1, NZ)],
        [first, here, second],
    )
    bands2 = [s2, di2, wx2, wy2, wz2]
    third = everyone(msg, "group").reshape(groups * rows_once, NZ)
    pre, below = call(
        functools.partial(climb_kernel, groups=groups, thirds=thirds, rows=rows_once),
        [(BX, BY, NZ), line],
        [third, *bands3, r2, *bands2, e22, r1, *bands1, e21, e2],
        [(tiles, 16, NZ), (16, 16, NZ)],
    )

    around = surround(pre, 0)
    u, rem, e2, r1, e21, msg, edge = call(
        again_kernel,
        [top] * 3 + [one] * 2 + [(tiles, 3, 2, NZ), (1, 3, 2, NZ)],
        [*around, rhs, *bands0, *bands1],
        [top] * 2,
    )
    own = jnp.concatenate([everyone(msg, "tile"), edge], axis=0)
    first, second = swaps(own, own, "group")
    r2, e22, msg = call(
        third_again_kernel,
        [two] * 2 + [(groups, rows_again, 1, NZ)],
        [own, first, second, *bands2],
    )
    third = everyone(msg, "group").reshape(groups * rows_again, NZ)
    update, remainder = call(
        functools.partial(last_climb_kernel, groups=groups, thirds=thirds, rows=rows_again),
        [(BX, BY, NZ)] * 2,
        [third, below, *bands3, first, own, second, r2, *bands2, e22, r1, *bands1, e21]
        + [e2, rhs, *bands0, u, rem],
        [top] * 2 + [(tiles, 16, NZ), (16, 16, NZ)],
    )
    return update, remainder


def solution(mesh):
    spec = P("tile", "group", None)
    return jax.shard_map(
        shards,
        mesh=mesh,
        in_specs=(spec, spec, spec, P(), P(), P(), P()),
        out_specs=(spec, spec),
        check_vma=False,
    )
```

```python
import functools
import math

import jax
import jax.numpy as jnp
from jax import lax
from jax.experimental import pallas as pl
from jax.experimental.pallas import tpu as pltpu
from jax.sharding import PartitionSpec as P

OMEGA = 2.0 / 3.0
STORAGE = 0.01
COARSE_SWEEPS = 4
SOILS = 12

BX, BY, NZ = 8, 16, 128
WX, WY = 24, 32
PX = WX + 2
L1X = WX // 2
F32 = jnp.float32


def iota(shape, dim):
    return lax.broadcasted_iota(jnp.int32, shape, dim)


def turn(v, step, axis):
    size = v.shape[axis]
    return pltpu.roll(v, step % size, axis)


def bit_of(v, step, axis):
    return (iota(v.shape, axis) // step) % 2 == 0


def pair_sum(v, step, axis):
    return v + jnp.where(bit_of(v, step, axis), turn(v, -step, axis), turn(v, step, axis))


def pair_low(v, step, axis):
    return jnp.where(bit_of(v, step, axis), v, turn(v, step, axis))


def x_low(v):
    return jnp.concatenate([v[:1], v[:-1]], axis=0)


def x_high(v):
    return jnp.concatenate([v[1:], jnp.zeros_like(v[:1])], axis=0)


def x_pair(v):
    return jnp.sum(v.reshape((v.shape[0] // 2, 2) + v.shape[1:]), axis=1)


def x_even(v):
    return v.reshape((v.shape[0] // 2, 2) + v.shape[1:])[:, 0]


def x_repeat(v):
    size = v.shape[0]
    wide = jnp.broadcast_to(v[:, None], (size, 2) + v.shape[1:])
    return wide.reshape((2 * size,) + v.shape[1:])


def operate(v, storage, wx, wy, wz, sy, sz):
    fx = wx * (v - x_low(v))
    fy = wy * (v - turn(v, sy, 1))
    fz = wz * (v - turn(v, sz, 2))
    flux = (fx - x_high(fx)) + (fy - turn(fy, -sy, 1)) + (fz - turn(fz, -sz, 2))
    return storage * v + flux


def relax_factor(storage, wx, wy, wz, sy, sz):
    diagonal = storage + wx + x_high(wx) + wy + turn(wy, -sy, 1) + wz + turn(wz, -sz, 2)
    return jnp.where(diagonal > 0.0, OMEGA / diagonal, 0.0)


def restrict(v, sy, sz):
    return pair_sum(pair_sum(x_pair(v), sy, 1), sz, 2)


def coarsen(storage, wx, wy, wz, sy, sz):
    return (
        restrict(storage, sy, sz),
        pair_sum(pair_sum(x_even(wx), sy, 1), sz, 2),
        pair_low(pair_sum(x_pair(wy), sz, 2), sy, 1),
        pair_low(pair_sum(x_pair(wz), sy, 1), sz, 2),
    )


def operate_rows(v_ref, s_ref, wx_ref, wy_ref, wz_ref, at, size):
    v = v_ref[pl.ds(at, size)]
    wx = wx_ref[pl.ds(at, size)]
    fy = wy_ref[pl.ds(at, size)] * (v - turn(v, 1, 1))
    fz = wz_ref[pl.ds(at, size)] * (v - turn(v, 1, 2))
    flux = wx * (v - v_ref[pl.ds(at - 1, size)])
    flux = flux - wx_ref[pl.ds(at + 1, size)] * (v_ref[pl.ds(at + 1, size)] - v)
    flux = flux + (fy - turn(fy, -1, 1)) + (fz - turn(fz, -1, 2))
    return v, s_ref[pl.ds(at, size)] * v + flux


def blank_ends(ref):
    ref[0] = jnp.zeros((WY, NZ), F32)
    ref[PX - 1] = jnp.zeros((WY, NZ), F32)


def blank_level1(ref, size):
    ref[0:size] = jnp.zeros((size, WY, NZ), F32)
    ref[L1X - size :] = jnp.zeros((size, WY, NZ), F32)


def pack_level2(v):
    sub, lane = iota(v.shape, 1), iota(v.shape, 2)
    chosen = (sub >= 8) & (sub < 24) & (sub % 4 == 0) & ((sub - 8) // 4 == lane % 4)
    return jnp.sum(jnp.where(chosen, v, 0.0), axis=1)


def send(msg_ref, rows):
    rows = list(rows)
    parts, height = msg_ref.shape[1:3]
    spare = parts * height - sum(row.shape[0] for row in rows)
    if spare:
        rows.append(jnp.zeros((spare, NZ), F32))
    whole = jnp.concatenate(rows, axis=0)
    for part in range(parts):
        piece = whole[part * height : (part + 1) * height]
        for peer in range(msg_ref.shape[0]):
            msg_ref[peer, part] = piece


def pack_bands3(fields):
    sub, lane = iota((1, WY, NZ), 1), iota((1, WY, NZ), 2)
    total = jnp.zeros((1, WY, NZ), F32)
    for f, v in enumerate(fields):
        chosen = ((sub == 8) & (lane % 8 == 2 * f)) | ((sub == 16) & (lane % 8 == 2 * f + 1))
        total = total + jnp.where(chosen, v, 0.0)
    return jnp.sum(total, axis=1)


def pack_ring1(v):
    sub, lane = iota((2, WY, NZ), 1), iota((2, WY, NZ), 2)
    rows = v[5:7]
    parts = []
    for k in range(4):
        chosen = ((sub == 8 + 4 * k) & (lane % 2 == 0)) | ((sub == 10 + 4 * k) & (lane % 2 == 1))
        parts.append(jnp.sum(jnp.where(chosen, rows, 0.0), axis=1, keepdims=True))
    return [jnp.concatenate([part[x] for part in parts], axis=0) for x in range(2)]


def pack_edge1(v):
    sub, lane = iota((6, WY, NZ), 1), iota((6, WY, NZ), 2)
    chosen = ((sub == 20) & (lane % 2 == 0)) | ((sub == 10) & (lane % 2 == 1))
    return jnp.sum(jnp.where(chosen, v[3:9], 0.0), axis=1)


def descend_top(r_ref, e1_ref, e2_ref, s_ref, wx_ref, wy_ref, wz_ref, di_ref, r1_ref):
    def second(i, carry):
        at = 1 + 2 * i
        v, av = operate_rows(e1_ref, s_ref, wx_ref, wy_ref, wz_ref, at, 2)
        e2_ref[pl.ds(at, 2)] = v + di_ref[pl.ds(at, 2)] * (r_ref[pl.ds(at, 2)] - av)
        return carry

    lax.fori_loop(1, WX // 2 - 1, second, 0, unroll=5)

    def third(i, carry):
        at = 1 + 2 * i
        _, av = operate_rows(e2_ref, s_ref, wx_ref, wy_ref, wz_ref, at, 2)
        r1_ref[pl.ds(i, 1)] = restrict(r_ref[pl.ds(at, 2)] - av, 1, 1)
        return carry

    lax.fori_loop(2, WX // 2 - 2, third, 0, unroll=4)


def descend_second(r1, s1, wx1, wy1, wz1, di1):
    first = r1 * di1
    second = first + di1 * (r1 - operate(first, s1, wx1, wy1, wz1, 2, 2))
    defect = r1 - operate(second, s1, wx1, wy1, wz1, 2, 2)
    return second, restrict(defect, 2, 2)


def soil_kernel(
    head_in, old_in, soil_in, ks_in, alpha_in, shape_in, span_in, out_ref,
    head_ref, old_ref, soil_ref, ks_ref, alpha_ref, shape_ref, span_ref, sems,
):
    given = (head_in, old_in, soil_in, ks_in, alpha_in, shape_in, span_in)
    held = (head_ref, old_ref, soil_ref, ks_ref, alpha_ref, shape_ref, span_ref)
    copies = [
        pltpu.make_async_copy(src, dst, sems.at[i])
        for i, (src, dst) in enumerate(zip(given, held, strict=True))
    ]
    for copy in copies:
        copy.start()
    for copy in copies:
        copy.wait()

    def cells(i, carry):
        row = pl.ds(i, 1)
        head, old, soil = head_ref[row], old_ref[row], soil_ref[row]
        ks = jnp.full(soil.shape, ks_ref[0])
        alpha = jnp.full(soil.shape, alpha_ref[0])
        shape_n = jnp.full(soil.shape, shape_ref[0])
        span = jnp.full(soil.shape, span_ref[0])
        for kind in range(1, SOILS):
            hit = soil == kind
            ks = jnp.where(hit, ks_ref[kind], ks)
            alpha = jnp.where(hit, alpha_ref[kind], alpha)
            shape_n = jnp.where(hit, shape_ref[kind], shape_n)
            span = jnp.where(hit, span_ref[kind], span)
        shape_m = 1.0 - 1.0 / shape_n
        power = jnp.exp(shape_n * jnp.log(alpha * -head))
        old_power = jnp.exp(shape_n * jnp.log(alpha * -old))
        saturation = jnp.exp(-shape_m * jnp.log1p(power))
        old_saturation = jnp.exp(-shape_m * jnp.log1p(old_power))
        portion = 1.0 / (1.0 + power)
        factor = 1.0 - jnp.exp(shape_m * jnp.log(power / (1.0 + power)))
        capacity = span * shape_m * shape_n * power / -head * saturation * portion
        out_ref[0, row] = head
        out_ref[1, row] = ks * jnp.sqrt(saturation) * factor * factor
        out_ref[2, row] = capacity + STORAGE
        out_ref[3, row] = span * (saturation - old_saturation) + STORAGE * (head - old)
        return carry

    lax.fori_loop(0, BX, cells, 0, unroll=4)


def is_even(axis, step=1, lead=0):
    return (lax.axis_index(axis) // step) % 2 == lead


def sides(first, second, axis, lead=0):
    even = is_even(axis, 1, lead)
    return jnp.where(even, second, first), jnp.where(even, first, second)


def fill_window(ref, xfirst, own, xsecond, yfirst, ysecond):
    ref[1 : 1 + BX, 8:24, :], ref[1 + 2 * BX : 1 + 3 * BX, 8:24, :] = sides(xfirst, xsecond, "tile")
    ref[1 + BX : 1 + 2 * BX, 8:24, :] = own
    ylow, yhigh = sides(yfirst, ysecond, "group", 1)
    for y, part in ((0, ylow), (24, yhigh)):
        low, high = sides(part[:BX], part[2 * BX :], "tile")
        ref[1 : 1 + BX, y : y + 8, :] = low
        ref[1 + BX : 1 + 2 * BX, y : y + 8, :] = part[BX : 2 * BX]
        ref[1 + 2 * BX : 1 + 3 * BX, y : y + 8, :] = high


def assemble_kernel(
    xfirst, own, xsecond, yfirst, ysecond,
    r_ref, s_ref, di_ref, wx_ref, wy_ref, wz_ref, e2_ref,
    r1_ref, s1_ref, di1_ref, wx1_ref, wy1_ref, wz1_ref, e21_ref, msg_ref,
    h_ref, k_ref, m_ref, e1_ref,
):
    for ref in (h_ref, k_ref, s_ref, wx_ref, wy_ref, wz_ref, di_ref, r_ref, e1_ref, e2_ref):
        blank_ends(ref)
    for f, ref in enumerate((h_ref, k_ref, s_ref, m_ref)):
        fill_window(ref, xfirst[f], own[f], xsecond[f], yfirst[f], ysecond[f])

    def harmonic(a, b):
        total = a + b
        return jnp.where(total > 0.0, 2.0 * a * b / total, 0.0)

    def faces(i, carry):
        at = 1 + 2 * i
        k = k_ref[pl.ds(at, 2)]
        wx_ref[pl.ds(at, 2)] = harmonic(k, k_ref[pl.ds(at - 1, 2)])
        wy_ref[pl.ds(at, 2)] = harmonic(k, turn(k, 1, 1))
        wz = harmonic(k, turn(k, 1, 2))
        wz_ref[pl.ds(at, 2)] = jnp.where(iota(wz.shape, 2) == 0, 0.0, wz)
        return carry

    lax.fori_loop(0, WX // 2, faces, 0, unroll=4)

    def right_side(i, carry):
        at = 1 + 2 * i
        rows = pl.ds(at, 2)
        h, wx, wy, wz = h_ref[rows], wx_ref[rows], wy_ref[rows], wz_ref[rows]
        wx_up = wx_ref[pl.ds(at + 1, 2)]
        fy = wy * (h - turn(h, 1, 1))
        fz = wz * (h - turn(h, 1, 2) + 1.0)
        flux = wx * (h - h_ref[pl.ds(at - 1, 2)]) - wx_up * (h_ref[pl.ds(at + 1, 2)] - h)
        flux = flux + (fy - turn(fy, -1, 1)) + (fz - turn(fz, -1, 2))
        rhs = -(m_ref[rows] + flux)
        diagonal = s_ref[rows] + wx + wx_up + wy + turn(wy, -1, 1) + wz + turn(wz, -1, 2)
        di = jnp.where(diagonal > 0.0, OMEGA / diagonal, 0.0)
        r_ref[rows] = rhs
        di_ref[rows] = di
        e1_ref[rows] = rhs * di
        return carry

    lax.fori_loop(0, WX // 2, right_side, 0, unroll=4)

    def bands(i, carry):
        rows = pl.ds(1 + 2 * i, 2)
        s1, wx1, wy1, wz1 = coarsen(s_ref[rows], wx_ref[rows], wy_ref[rows], wz_ref[rows], 1, 1)
        row = pl.ds(i, 1)
        s1_ref[row], wx1_ref[row], wy1_ref[row], wz1_ref[row] = s1, wx1, wy1, wz1
        return carry

    lax.fori_loop(1, WX // 2 - 1, bands, 0, unroll=5)
    for ref in (s1_ref, wx1_ref, wy1_ref, wz1_ref):
        blank_level1(ref, 1)
    blank_level1(r1_ref, 2)
    descend_top(r_ref, e1_ref, e2_ref, s_ref, wx_ref, wy_ref, wz_ref, di_ref, r1_ref)

    s1, wx1, wy1, wz1 = s1_ref[...], wx1_ref[...], wy1_ref[...], wz1_ref[...]
    di1 = relax_factor(s1, wx1, wy1, wz1, 2, 2)
    di1_ref[...] = di1
    e21, r2 = descend_second(r1_ref[...], s1, wx1, wy1, wz1, di1)
    e21_ref[...] = e21
    bands2 = coarsen(s1, wx1, wy1, wz1, 2, 2)
    bands3 = coarsen(*(v[2:4] for v in bands2), 4, 4)
    rows = [pack_level2(v[2:4]) for v in (r2,) + bands2]
    send(msg_ref, rows + [pack_bands3(bands3)])


def again_kernel(
    xfirst, own, xsecond, yfirst, ysecond, rhs_ref, s_ref, di_ref, wx_ref, wy_ref, wz_ref,
    s1_ref, di1_ref, wx1_ref, wy1_ref, wz1_ref,
    u_ref, r_ref, e2_ref, r1_ref, e21_ref, msg_ref, edge_ref, pre_ref, e1_ref,
):
    for ref in (pre_ref, u_ref, r_ref, e1_ref, e2_ref):
        blank_ends(ref)
    fill_window(pre_ref, xfirst[...], own[...], xsecond[...], yfirst[...], ysecond[...])

    def post(i, carry):
        at = 1 + 2 * i
        rows = pl.ds(at, 2)
        v, av = operate_rows(pre_ref, s_ref, wx_ref, wy_ref, wz_ref, at, 2)
        u_ref[rows] = v + di_ref[rows] * (rhs_ref[rows] - av)
        return carry

    lax.fori_loop(0, WX // 2, post, 0, unroll=4)

    def remain(i, carry):
        at = 1 + 2 * i
        rows = pl.ds(at, 2)
        _, av = operate_rows(u_ref, s_ref, wx_ref, wy_ref, wz_ref, at, 2)
        left = rhs_ref[rows] - av
        r_ref[rows] = left
        e1_ref[rows] = left * di_ref[rows]
        return carry

    lax.fori_loop(1, WX // 2 - 1, remain, 0, unroll=5)
    descend_top(r_ref, e1_ref, e2_ref, s_ref, wx_ref, wy_ref, wz_ref, di_ref, r1_ref)
    blank_level1(r1_ref, 2)
    e21, r2 = descend_second(
        r1_ref[...], s1_ref[...], wx1_ref[...], wy1_ref[...], wz1_ref[...], di1_ref[...]
    )
    e21_ref[...] = e21
    tile = lax.axis_index("tile")
    to_low, to_high = pack_ring1(e21)
    for peer in range(msg_ref.shape[0]):
        ring = jnp.where(tile > peer, to_low, to_high)
        msg_ref[peer, 0] = pack_level2(r2[2:4])
        msg_ref[peer, 1], msg_ref[peer, 2] = ring[0:2], ring[2:4]
    send(edge_ref, [pack_edge1(e21)])


def message_rows(ref):
    tiles = lax.axis_size("tile")
    return lambda field, half: ref[0:tiles, field, half : half + 1, :]


def choose(which, one, two):
    return lambda field, half: jnp.where(which, one(field, half), two(field, half))


def both_sides(first, second, step, lead):
    even = is_even("group", step, lead)
    one, two = message_rows(first), message_rows(second)
    return choose(even, two, one), choose(even, one, two)


def pair_rows(here, first, second):
    before, after = both_sides(first, second, 2, 1)
    even = is_even("group")
    one, two = message_rows(here.at[:, 0]), message_rows(here.at[:, 1])
    return choose(even, before, one), choose(even, one, two), choose(even, two, after)


def band_rows3(here, first, second):
    before, after = both_sides(first, second, 2, 1)
    even = is_even("group")
    six = [before(5, half) for half in range(2)]
    six += [here[:, core, 5, 0:1, :] for core in range(2)]
    six += [after(5, half) for half in range(2)]
    return [jnp.where(even, six[i], six[i + 1]) for i in range(5)]


def unpack_level2(field, own, low, high):
    tiles = lax.axis_size("tile")
    shape = (tiles, 16, NZ)
    sub, lane = iota(shape, 1), iota(shape, 2)
    halves = []
    for half in range(2):

        def spread(pick, half=half):
            return jnp.broadcast_to(pick(field, half), shape)

        v = jnp.where(sub < 4, spread(low), jnp.where(sub < 8, spread(own), spread(high)))
        v = jnp.where((lane % 4 == sub % 4) & (sub < 12), v, 0.0)
        halves.append(pair_sum(pair_sum(v, 1, 2), 2, 2))
    return jnp.stack(halves, axis=1).reshape((2 * tiles, 16, NZ))


def pack_level3(v):
    sub, lane = iota((16, NZ), 0), iota((16, NZ), 1)
    rows = []
    for j in range(v.shape[0] // 4):
        total = jnp.zeros((16, NZ), F32)
        for q in range(4):
            chosen = ((sub == 4) & (lane % 8 == 2 * q)) | ((sub == 6) & (lane % 8 == 2 * q + 1))
            total = total + jnp.where(chosen, v[4 * j + q], 0.0)
        rows.append(jnp.sum(total, axis=0, keepdims=True))
    return rows


def pack_sums3(v):
    even = is_even("group")
    tiles = v.shape[0]
    start = jnp.where(even, 8, 4)
    sub, lane = iota((24, NZ), 0), iota((24, NZ), 1)
    once = (sub >= start) & (sub < start + 8) & (sub % 2 == 0)
    total = jnp.zeros((24, NZ), F32)
    for q in range(tiles // 2):
        part = jnp.where(even, v[q], v[tiles // 2 + q])
        total = total + jnp.where(once & (lane % 8 == q), part, 0.0)
    return [jnp.sum(total, axis=0, keepdims=True)]


def descend_third(r2, s2, wx2, wy2, wz2, di2):
    first = r2 * di2
    second = first + di2 * (r2 - operate(first, s2, wx2, wy2, wz2, 1, 4))
    return second, restrict(r2 - operate(second, s2, wx2, wy2, wz2, 1, 4), 1, 4)


def sides_kernel(here, first_ref, second_ref):
    even = is_even("group", 2, 1)
    low, high = here[:, 0, 0:5], here[:, 1, 0:5]
    first_ref[:, 0:5] = jnp.where(even, high, low)
    second_ref[:, 0:5] = jnp.where(even, low, high)
    for core in range(2):
        rows = here[:, core, 5, 0:1, :]
        first_ref[:, 5, core : core + 1, :] = rows
        second_ref[:, 5, core : core + 1, :] = rows


def third_kernel(
    first, here, second,
    r2_ref, s2_ref, di2_ref, wx2_ref, wy2_ref, wz2_ref, e22_ref,
    s3_ref, di3_ref, wx3_ref, wy3_ref, wz3_ref, msg_ref,
):
    s3, wx3, wy3, wz3 = unpack_bands3(band_rows3(here, first, second))
    s3_ref[...], wx3_ref[...], wy3_ref[...], wz3_ref[...] = s3, wx3, wy3, wz3
    di3_ref[...] = relax_factor(s3, wx3, wy3, wz3, 2, 8)
    inner = s3 + wx3 + x_high(wx3) + wz3 + turn(wz3, -8, 2)
    low, own, high = pair_rows(here, first, second)
    r2, s2, wx2, wy2, wz2 = (unpack_level2(f, own, low, high) for f in range(5))
    di2 = relax_factor(s2, wx2, wy2, wz2, 1, 4)
    r2_ref[...], s2_ref[...], di2_ref[...] = r2, s2, di2
    wx2_ref[...], wy2_ref[...], wz2_ref[...] = wx2, wy2, wz2
    e22, r3 = descend_third(r2, s2, wx2, wy2, wz2, di2)
    e22_ref[...] = e22
    send(msg_ref, pack_level3(r3) + pack_sums3(inner))


def third_again_kernel(
    own, first, second, s2_ref, di2_ref, wx2_ref, wy2_ref, wz2_ref, r2_ref, e22_ref, msg_ref
):
    r2 = unpack_level2(0, message_rows(own), *both_sides(first, second, 1, 0))
    r2_ref[...] = r2
    e22, r3 = descend_third(
        r2, s2_ref[...], wx2_ref[...], wy2_ref[...], wz2_ref[...], di2_ref[...]
    )
    e22_ref[...] = e22
    send(msg_ref, pack_level3(r3))


def third_masks(shape):
    sub, lane = iota(shape, 1), iota(shape, 2)
    return sub // 4, (sub % 4) // 2, lane % 8


def octuple(v):
    return pair_sum(pair_sum(pair_sum(v, 1, 2), 2, 2), 4, 2)


def unpack_bands3(sources):
    shape = (sources[0].shape[0], 24, NZ)
    dev, half, slot = third_masks(shape)
    rows = jnp.broadcast_to(sources[0], shape)
    for d in range(1, 5):
        rows = jnp.where(dev == d, jnp.broadcast_to(sources[d], shape), rows)
    rows = jnp.where(dev < 5, rows, 0.0)
    return [octuple(jnp.where(slot == 2 * f + half, rows, 0.0)) for f in range(4)]


def unpack_r3(v):
    group = lax.axis_index("group")
    at = iota(v.shape, 1)
    shape = (v.shape[0], 24, NZ)
    dev, half, slot = third_masks(shape)
    rows = jnp.zeros(shape, F32)
    for d in range(5):
        near = jnp.sum(jnp.where(at == group + (d - 2), v, 0.0), axis=1, keepdims=True)
        rows = jnp.where(dev == d, jnp.broadcast_to(near, shape), rows)
    parts = [jnp.where(slot == 2 * q + half, rows, 0.0) for q in range(4)]
    return octuple(jnp.stack(parts, axis=1).reshape((4 * v.shape[0], 24, NZ)))


def line_sums(v, held):
    total = jnp.sum(v, axis=1, keepdims=True)
    lane = iota(total.shape, 2) % 8
    parts = [jnp.where(lane * held // 8 == q, total, 0.0) for q in range(held)]
    wide = jnp.stack(parts, axis=1).reshape((held * v.shape[0], 1, NZ))
    return octuple(wide)


def solve_third(r3, line, s3, di3, wx3, wy3, wz3):
    v = jnp.broadcast_to(line, r3.shape)
    for _ in range(COARSE_SWEEPS):
        v = v + di3 * (r3 - operate(v, s3, wx3, wy3, wz3, 2, 8))
    return turn(v, -4, 1)[:, 0:16]


def widen_y(v):
    shape = (v.shape[0], 8, NZ)
    sub = iota(shape, 1)
    parts = []
    for at in (2, 4, 6, 8):
        first = jnp.broadcast_to(v[:, at : at + 1], shape)
        second = jnp.broadcast_to(v[:, at + 1 : at + 2], shape)
        parts.append(jnp.where(sub < 4, first, second))
    return jnp.concatenate(parts, axis=1)


def climb_to_second(
    corr3, r2_ref, s2_ref, di2_ref, wx2_ref, wy2_ref, wz2_ref, e22_ref, corr3_ref, corr2_ref
):
    tile, tiles = lax.axis_index("tile"), lax.axis_size("tile")
    start = jnp.clip(tile - 2, 0, tiles - 4)
    corr3_ref[...] = corr3
    rows = pl.ds(2 * start, 8)
    v = e22_ref[rows] + x_repeat(corr3_ref[pl.ds(start, 4)])
    v = v + di2_ref[rows] * (
        r2_ref[rows]
        - operate(v, s2_ref[rows], wx2_ref[rows], wy2_ref[rows], wz2_ref[rows], 1, 4)
    )
    corr2_ref[0:4] = jnp.zeros((4, 16, NZ), F32)
    corr2_ref[4:12] = v
    corr2_ref[12:16] = jnp.zeros((4, 16, NZ), F32)
    near = corr2_ref[pl.ds(2 * (tile - start) + 2, 6)]
    return x_repeat(widen_y(near))


def climb_to_first(v, r1_ref, s1_ref, di1_ref, wx1_ref, wy1_ref, wz1_ref):
    rows = slice(2, 10)
    v = v[rows]
    return v + di1_ref[rows] * (
        r1_ref[rows]
        - operate(v, s1_ref[rows], wx1_ref[rows], wy1_ref[rows], wz1_ref[rows], 2, 2)
    )


def strided(ref, first, thirds, groups, rows):
    parts = [ref[pl.ds(first + j, groups, stride=rows), :] for j in range(thirds)]
    return jnp.stack(parts, axis=0)


def climb_kernel(
    third_ref, s3_ref, di3_ref, wx3_ref, wy3_ref, wz3_ref,
    r2_ref, s2_ref, di2_ref, wx2_ref, wy2_ref, wz2_ref, e22_ref,
    r1_ref, s1_ref, di1_ref, wx1_ref, wy1_ref, wz1_ref, e21_ref, e2_ref,
    pre_ref, below_ref, corr3_ref, corr2_ref, rows_ref,
    *, groups, thirds, rows,
):
    rows_ref[0 : groups * rows] = third_ref[...]
    r3 = strided(rows_ref, 0, thirds, groups, rows)
    tiles = lax.axis_size("tile")
    sums = strided(rows_ref, thirds, 1, groups, rows)
    odd = iota(sums.shape, 1) % 2
    below = jnp.concatenate(
        [line_sums(jnp.where(odd == half, sums, 0.0), 8)[: tiles // 2] for half in range(2)], axis=0
    )
    below_ref[...] = below
    corr3 = solve_third(
        unpack_r3(r3), line_sums(r3, 4) / below,
        s3_ref[...], di3_ref[...], wx3_ref[...], wy3_ref[...], wz3_ref[...],
    )
    corr2 = climb_to_second(
        corr3, r2_ref, s2_ref, di2_ref, wx2_ref, wy2_ref, wz2_ref, e22_ref, corr3_ref, corr2_ref
    )
    v = climb_to_first(
        e21_ref[...] + corr2, r1_ref, s1_ref, di1_ref, wx1_ref, wy1_ref, wz1_ref
    )
    own1 = x_repeat(v[2:6])
    pre_ref[...] = e2_ref[9:17, 8:24, :] + own1[:, 8:24, :]


def tile_rows(refs, even, off, at):
    tile = lax.axis_index("tile")
    total = jnp.zeros((2, NZ), F32)
    for t in range(lax.axis_size("tile")):
        rows = refs[0][t, at] if len(refs) == 1 else jnp.where(even, refs[0][t, at], refs[1][t, at])
        total = total + jnp.where(tile + off == t, rows, 0.0)
    return total


def ring_row(own, first, second, off):
    even = is_even("group")
    pairs = [tile_rows((own,), even, off, 1), tile_rows((own,), even, off, 2)]
    packed = [tile_rows((second, first), even, off, 2)[1:2]]
    packed += [pair[k : k + 1] for pair in pairs for k in range(2)]
    packed += [tile_rows((first, second), even, off, 1)[0:1]]
    return spread_pairs([row[None] for row in packed], 1)


def spread_pairs(packed, height):
    shape = (height, WY, NZ)
    sub, lane = iota(shape, 1), iota(shape, 2)
    rows = jnp.zeros(shape, F32)
    for k, row in enumerate(packed):
        rows = jnp.where(sub // 4 == k + 1, jnp.broadcast_to(row, shape), rows)
    return pair_sum(jnp.where(lane % 2 == (sub // 2) % 2, rows, 0.0), 1, 2)


def last_climb_kernel(
    third_ref, below_ref, s3_ref, di3_ref, wx3_ref, wy3_ref, wz3_ref,
    first, own, second,
    r2_ref, s2_ref, di2_ref, wx2_ref, wy2_ref, wz2_ref, e22_ref,
    r1_ref, s1_ref, di1_ref, wx1_ref, wy1_ref, wz1_ref, e21_ref,
    e2_ref, rhs_ref, s_ref, di_ref, wx_ref, wy_ref, wz_ref, u_ref, r_ref,
    out_ref, left_ref, pre_ref, v_ref, corr3_ref, corr2_ref, rows_ref,
    *, groups, thirds, rows,
):
    rows_ref[0 : groups * rows] = third_ref[...]
    r3 = strided(rows_ref, 0, thirds, groups, rows)
    corr3 = solve_third(
        unpack_r3(r3), line_sums(r3, 4) / below_ref[...],
        s3_ref[...], di3_ref[...], wx3_ref[...], wy3_ref[...], wz3_ref[...],
    )
    corr2 = climb_to_second(
        corr3, r2_ref, s2_ref, di2_ref, wx2_ref, wy2_ref, wz2_ref, e22_ref, corr3_ref, corr2_ref
    )
    tiles = lax.axis_size("tile")
    middle = e21_ref[3:9]
    sub = iota(middle.shape, 1)
    edge_first = jnp.concatenate([first[tiles, k] for k in range(3)], axis=0)[:, None]
    edge_second = jnp.concatenate([second[tiles, k] for k in range(3)], axis=0)[:, None]
    edge_low, edge_high = sides(edge_first, edge_second, "group")
    nothing = jnp.zeros_like(edge_low)
    edges = spread_pairs([edge_low] + [nothing] * 4 + [edge_high], 6)
    kept = (sub >= 6) & (sub < 26)
    middle = jnp.where(kept, middle, edges)
    blank = jnp.zeros((2, WY, NZ), F32)
    ends = [ring_row(own, first, second, off) for off in (-1, 1)]
    e21 = jnp.concatenate([blank, ends[0], middle, ends[1], blank], axis=0)
    v = climb_to_first(e21 + corr2, r1_ref, s1_ref, di1_ref, wx1_ref, wy1_ref, wz1_ref)
    pre_ref[7:19] = e2_ref[7:19] + x_repeat(v[1:7])

    def post(i, carry):
        at = 8 + 2 * i
        here = pl.ds(at, 2)
        v, av = operate_rows(pre_ref, s_ref, wx_ref, wy_ref, wz_ref, at, 2)
        v_ref[here] = u_ref[here] + v + di_ref[here] * (r_ref[here] - av)
        return carry

    lax.fori_loop(0, BX // 2 + 1, post, 0, unroll=True)

    def remain(i, carry):
        at = 9 + 2 * i
        v, av = operate_rows(v_ref, s_ref, wx_ref, wy_ref, wz_ref, at, 2)
        left = rhs_ref[pl.ds(at, 2)] - av
        out_ref[pl.ds(2 * i, 2)] = v[:, 8:24]
        left_ref[pl.ds(2 * i, 2)] = left[:, 8:24]
        return carry

    lax.fori_loop(0, BX // 2, remain, 0, unroll=True)


def call(body, outs, operands, scratch=()):
    cells = sum(math.prod(shape) for shape in outs)
    vmem = pl.BlockSpec(memory_space=pltpu.VMEM)
    return pl.pallas_call(
        body,
        out_shape=[jax.ShapeDtypeStruct(shape, F32) for shape in outs],
        in_specs=[vmem] * len(operands),
        out_specs=[vmem] * len(outs),
        scratch_shapes=[pltpu.VMEM(shape, F32) for shape in scratch],
        compiler_params=pltpu.CompilerParams(vmem_limit_bytes=16 * 1024 * 1024),
        cost_estimate=pl.CostEstimate(
            flops=20 * cells, bytes_accessed=8 * cells, transcendentals=0
        ),
    )(*operands)


def swaps(to_first, to_second, axis, step=1, lead=0):
    count = lax.axis_size(axis)

    def swap(cells, odd):
        ups = [
            (i, i + step) for i in range(count - step) if (i // step) % 2 == odd
        ]
        return lax.ppermute(cells, axis, ups + [(j, i) for i, j in ups])

    return swap(to_first, lead), swap(to_second, 1 - lead)


def surround(cells, dim):
    first, second = swaps(cells, cells, "tile")
    ydim = dim + 1
    even = is_even("group", 1, 1)

    def halves(v):
        low = lax.slice_in_dim(v, 0, 8, axis=ydim)
        high = lax.slice_in_dim(v, BY - 8, BY, axis=ydim)
        return jnp.where(even, high, low), jnp.where(even, low, high)

    parts = [halves(v) for v in (first, cells, second)]
    to_first, to_second = (jnp.concatenate(list(v), axis=dim) for v in zip(*parts, strict=True))
    return first, cells, second, *swaps(to_first, to_second, "group", 1, 1)


def everyone(blocks, axis):
    return lax.all_to_all(blocks, axis, 0, 0, tiled=True)


def pairs_of_tiles(block):
    tiles, groups = lax.axis_size("tile"), lax.axis_size("group")
    members = [
        [t * groups + 2 * pair + core for t in range(tiles) for core in range(2)]
        for pair in range(groups // 2)
    ]
    given = lax.all_to_all(
        block, ("tile", "group"), 0, 0, axis_index_groups=members, tiled=True
    )
    return given.reshape((tiles, 2) + block.shape[1:])


def shards(pressure_head, old_head, soil_type, conduct_sat, alpha_param, shape_param, water_span):
    tiles, groups = lax.axis_size("tile"), lax.axis_size("group")
    thirds = tiles // 4
    top, one, two = (PX, WY, NZ), (L1X, WY, NZ), (2 * tiles, 16, NZ)
    three, line = (tiles, 24, NZ), (tiles, 1, NZ)
    rows_once, rows_again = thirds + 1, thirds

    fields = pl.pallas_call(
        soil_kernel,
        out_shape=jax.ShapeDtypeStruct((4, BX, BY, NZ), F32),
        in_specs=[pl.BlockSpec(memory_space=pltpu.HBM)] * 7,
        out_specs=pl.BlockSpec(memory_space=pltpu.VMEM),
        scratch_shapes=[
            pltpu.VMEM((BX, BY, NZ), F32),
            pltpu.VMEM((BX, BY, NZ), F32),
            pltpu.VMEM((BX, BY, NZ), jnp.int32),
            *[pltpu.SMEM((SOILS,), F32) for _ in range(4)],
            pltpu.SemaphoreType.DMA((7,)),
        ],
    )(pressure_head, old_head, soil_type, conduct_sat, alpha_param, shape_param, water_span)
    around = surround(fields, 1)
    rhs, s0, di0, wx0, wy0, wz0, e2, r1, s1, di1, wx1, wy1, wz1, e21, msg = call(
        assemble_kernel,
        [top] * 7 + [one] * 7 + [(2 * tiles, 6, 2, NZ)],
        list(around),
        [top] * 4,
    )
    bands0 = [s0, di0, wx0, wy0, wz0]
    bands1 = [s1, di1, wx1, wy1, wz1]

    here = pairs_of_tiles(msg)
    to_first, to_second = call(sides_kernel, [(tiles, 6, 2, NZ)] * 2, [here])
    first, second = swaps(to_first, to_second, "group", 2, 1)
    r2, s2, di2, wx2, wy2, wz2, e22, *bands3, msg = call(
        third_kernel,
        [two] * 7 + [three] * 5 + [(groups, rows_once, 1, NZ)],
        [first, here, second],
    )
    bands2 = [s2, di2, wx2, wy2, wz2]
    third = everyone(msg, "group").reshape(groups * rows_once, NZ)
    pre, below = call(
        functools.partial(climb_kernel, groups=groups, thirds=thirds, rows=rows_once),
        [(BX, BY, NZ), line],
        [third, *bands3, r2, *bands2, e22, r1, *bands1, e21, e2],
        [(tiles, 16, NZ), (16, 16, NZ), (groups * rows_once + 8, NZ)],
    )

    around = surround(pre, 0)
    u, rem, e2, r1, e21, msg, edge = call(
        again_kernel,
        [top] * 3 + [one] * 2 + [(tiles, 3, 2, NZ), (1, 3, 2, NZ)],
        [*around, rhs, *bands0, *bands1],
        [top] * 2,
    )
    own = jnp.concatenate([everyone(msg, "tile"), edge], axis=0)
    first, second = swaps(own, own, "group")
    r2, e22, msg = call(
        third_again_kernel,
        [two] * 2 + [(groups, rows_again, 1, NZ)],
        [own, first, second, *bands2],
    )
    third = everyone(msg, "group").reshape(groups * rows_again, NZ)
    update, remainder = call(
        functools.partial(last_climb_kernel, groups=groups, thirds=thirds, rows=rows_again),
        [(BX, BY, NZ)] * 2,
        [third, below, *bands3, first, own, second, r2, *bands2, e22, r1, *bands1, e21]
        + [e2, rhs, *bands0, u, rem],
        [top] * 2 + [(tiles, 16, NZ), (16, 16, NZ), (groups * rows_again + 8, NZ)],
    )
    return update, remainder


def solution(mesh):
    spec = P("tile", "group", None)
    return jax.shard_map(
        shards,
        mesh=mesh,
        in_specs=(spec, spec, spec, P(), P(), P(), P()),
        out_specs=(spec, spec),
        check_vma=False,
    )
```

```python
import functools
import math

import jax
import jax.numpy as jnp
from jax import lax
from jax.experimental import pallas as pl
from jax.experimental.pallas import tpu as pltpu
from jax.sharding import PartitionSpec as P

OMEGA = 2.0 / 3.0
STORAGE = 0.01
COARSE_SWEEPS = 4
SOILS = 12

BX, BY, NZ = 8, 16, 128
WX, WY = 24, 32
PX = WX + 2
L1X = WX // 2
F32 = jnp.float32


def iota(shape, dim):
    return lax.broadcasted_iota(jnp.int32, shape, dim)


def turn(v, step, axis):
    size = v.shape[axis]
    return pltpu.roll(v, step % size, axis)


def bit_of(v, step, axis):
    return (iota(v.shape, axis) // step) % 2 == 0


def pair_sum(v, step, axis):
    return v + jnp.where(bit_of(v, step, axis), turn(v, -step, axis), turn(v, step, axis))


def pair_low(v, step, axis):
    return jnp.where(bit_of(v, step, axis), v, turn(v, step, axis))


def x_low(v):
    return jnp.concatenate([v[:1], v[:-1]], axis=0)


def x_high(v):
    return jnp.concatenate([v[1:], jnp.zeros_like(v[:1])], axis=0)


def x_pair(v):
    return jnp.sum(v.reshape((v.shape[0] // 2, 2) + v.shape[1:]), axis=1)


def x_even(v):
    return v.reshape((v.shape[0] // 2, 2) + v.shape[1:])[:, 0]


def x_repeat(v):
    size = v.shape[0]
    wide = jnp.broadcast_to(v[:, None], (size, 2) + v.shape[1:])
    return wide.reshape((2 * size,) + v.shape[1:])


def operate(v, storage, wx, wy, wz, sy, sz):
    fx = wx * (v - x_low(v))
    fy = wy * (v - turn(v, sy, 1))
    fz = wz * (v - turn(v, sz, 2))
    flux = (fx - x_high(fx)) + (fy - turn(fy, -sy, 1)) + (fz - turn(fz, -sz, 2))
    return storage * v + flux


def relax_factor(storage, wx, wy, wz, sy, sz):
    diagonal = storage + wx + x_high(wx) + wy + turn(wy, -sy, 1) + wz + turn(wz, -sz, 2)
    return jnp.where(diagonal > 0.0, OMEGA / diagonal, 0.0)


def restrict(v, sy, sz):
    return pair_sum(pair_sum(x_pair(v), sy, 1), sz, 2)


def coarsen(storage, wx, wy, wz, sy, sz):
    return (
        restrict(storage, sy, sz),
        pair_sum(pair_sum(x_even(wx), sy, 1), sz, 2),
        pair_low(pair_sum(x_pair(wy), sz, 2), sy, 1),
        pair_low(pair_sum(x_pair(wz), sy, 1), sz, 2),
    )


def operate_rows(v_ref, s_ref, wx_ref, wy_ref, wz_ref, at, size):
    v = v_ref[pl.ds(at, size)]
    wx = wx_ref[pl.ds(at, size)]
    fy = wy_ref[pl.ds(at, size)] * (v - turn(v, 1, 1))
    fz = wz_ref[pl.ds(at, size)] * (v - turn(v, 1, 2))
    flux = wx * (v - v_ref[pl.ds(at - 1, size)])
    flux = flux - wx_ref[pl.ds(at + 1, size)] * (v_ref[pl.ds(at + 1, size)] - v)
    flux = flux + (fy - turn(fy, -1, 1)) + (fz - turn(fz, -1, 2))
    return v, s_ref[pl.ds(at, size)] * v + flux


def blank_ends(ref):
    ref[0] = jnp.zeros((WY, NZ), F32)
    ref[PX - 1] = jnp.zeros((WY, NZ), F32)


def blank_level1(ref, size):
    ref[0:size] = jnp.zeros((size, WY, NZ), F32)
    ref[L1X - size :] = jnp.zeros((size, WY, NZ), F32)


def pack_level2(v):
    sub, lane = iota(v.shape, 1), iota(v.shape, 2)
    chosen = (sub >= 8) & (sub < 24) & (sub % 4 == 0) & ((sub - 8) // 4 == lane % 4)
    return jnp.sum(jnp.where(chosen, v, 0.0), axis=1)


def send(msg_ref, rows):
    rows = list(rows)
    parts, height = msg_ref.shape[1:3]
    spare = parts * height - sum(row.shape[0] for row in rows)
    if spare:
        rows.append(jnp.zeros((spare, NZ), F32))
    whole = jnp.concatenate(rows, axis=0)
    for part in range(parts):
        piece = whole[part * height : (part + 1) * height]
        for peer in range(msg_ref.shape[0]):
            msg_ref[peer, part] = piece


def pack_bands3(fields):
    sub, lane = iota((1, WY, NZ), 1), iota((1, WY, NZ), 2)
    total = jnp.zeros((1, WY, NZ), F32)
    for f, v in enumerate(fields):
        chosen = ((sub == 8) & (lane % 8 == 2 * f)) | ((sub == 16) & (lane % 8 == 2 * f + 1))
        total = total + jnp.where(chosen, v, 0.0)
    return jnp.sum(total, axis=1)


def pack_ring1(v):
    sub, lane = iota((2, WY, NZ), 1), iota((2, WY, NZ), 2)
    rows = v[5:7]
    parts = []
    for k in range(4):
        chosen = ((sub == 8 + 4 * k) & (lane % 2 == 0)) | ((sub == 10 + 4 * k) & (lane % 2 == 1))
        parts.append(jnp.sum(jnp.where(chosen, rows, 0.0), axis=1, keepdims=True))
    return [jnp.concatenate([part[x] for part in parts], axis=0) for x in range(2)]


def pack_edge1(v):
    sub, lane = iota((6, WY, NZ), 1), iota((6, WY, NZ), 2)
    chosen = ((sub == 20) & (lane % 2 == 0)) | ((sub == 10) & (lane % 2 == 1))
    return jnp.sum(jnp.where(chosen, v[3:9], 0.0), axis=1)


def descend_top(r_ref, e1_ref, e2_ref, s_ref, wx_ref, wy_ref, wz_ref, di_ref, r1_ref):
    def second(i, carry):
        at = 1 + 2 * i
        v, av = operate_rows(e1_ref, s_ref, wx_ref, wy_ref, wz_ref, at, 2)
        e2_ref[pl.ds(at, 2)] = v + di_ref[pl.ds(at, 2)] * (r_ref[pl.ds(at, 2)] - av)
        return carry

    lax.fori_loop(1, WX // 2 - 1, second, 0, unroll=5)

    def third(i, carry):
        at = 1 + 2 * i
        _, av = operate_rows(e2_ref, s_ref, wx_ref, wy_ref, wz_ref, at, 2)
        r1_ref[pl.ds(i, 1)] = restrict(r_ref[pl.ds(at, 2)] - av, 1, 1)
        return carry

    lax.fori_loop(2, WX // 2 - 2, third, 0, unroll=4)


def descend_second(r1, s1, wx1, wy1, wz1, di1):
    first = r1 * di1
    second = first + di1 * (r1 - operate(first, s1, wx1, wy1, wz1, 2, 2))
    defect = r1 - operate(second, s1, wx1, wy1, wz1, 2, 2)
    return second, restrict(defect, 2, 2)


def soil_kernel(
    head_in, old_in, soil_in, ks_in, alpha_in, shape_in, span_in, out_ref,
    head_ref, old_ref, soil_ref, ks_ref, alpha_ref, shape_ref, span_ref, sems,
):
    given = (head_in, old_in, soil_in, ks_in, alpha_in, shape_in, span_in)
    held = (head_ref, old_ref, soil_ref, ks_ref, alpha_ref, shape_ref, span_ref)
    copies = [
        pltpu.make_async_copy(src, dst, sems.at[i])
        for i, (src, dst) in enumerate(zip(given, held, strict=True))
    ]
    for copy in copies:
        copy.start()
    for copy in copies:
        copy.wait()

    def cells(i, carry):
        row = pl.ds(i, 1)
        head, old, soil = head_ref[row], old_ref[row], soil_ref[row]
        ks = jnp.full(soil.shape, ks_ref[0])
        alpha = jnp.full(soil.shape, alpha_ref[0])
        shape_n = jnp.full(soil.shape, shape_ref[0])
        span = jnp.full(soil.shape, span_ref[0])
        for kind in range(1, SOILS):
            hit = soil == kind
            ks = jnp.where(hit, ks_ref[kind], ks)
            alpha = jnp.where(hit, alpha_ref[kind], alpha)
            shape_n = jnp.where(hit, shape_ref[kind], shape_n)
            span = jnp.where(hit, span_ref[kind], span)
        shape_m = 1.0 - 1.0 / shape_n
        power = jnp.exp(shape_n * jnp.log(alpha * -head))
        old_power = jnp.exp(shape_n * jnp.log(alpha * -old))
        saturation = jnp.exp(-shape_m * jnp.log1p(power))
        old_saturation = jnp.exp(-shape_m * jnp.log1p(old_power))
        portion = 1.0 / (1.0 + power)
        factor = 1.0 - jnp.exp(shape_m * jnp.log(power / (1.0 + power)))
        capacity = span * shape_m * shape_n * power / -head * saturation * portion
        out_ref[0, row] = head
        out_ref[1, row] = ks * jnp.sqrt(saturation) * factor * factor
        out_ref[2, row] = capacity + STORAGE
        out_ref[3, row] = span * (saturation - old_saturation) + STORAGE * (head - old)
        return carry

    lax.fori_loop(0, BX, cells, 0, unroll=4)


def is_even(axis, step=1, lead=0):
    return (lax.axis_index(axis) // step) % 2 == lead


def sides(first, second, axis, lead=0):
    even = is_even(axis, 1, lead)
    return jnp.where(even, second, first), jnp.where(even, first, second)


def fill_window(ref, xfirst, own, xsecond, yfirst, ysecond):
    ref[1 : 1 + BX, 8:24, :], ref[1 + 2 * BX : 1 + 3 * BX, 8:24, :] = sides(xfirst, xsecond, "tile")
    ref[1 + BX : 1 + 2 * BX, 8:24, :] = own
    ylow, yhigh = sides(yfirst, ysecond, "group", 1)
    for y, part in ((0, ylow), (24, yhigh)):
        low, high = sides(part[:BX], part[2 * BX :], "tile")
        ref[1 : 1 + BX, y : y + 8, :] = low
        ref[1 + BX : 1 + 2 * BX, y : y + 8, :] = part[BX : 2 * BX]
        ref[1 + 2 * BX : 1 + 3 * BX, y : y + 8, :] = high


def assemble_kernel(
    xfirst, own, xsecond, yfirst, ysecond,
    r_ref, s_ref, di_ref, wx_ref, wy_ref, wz_ref, e2_ref,
    r1_ref, s1_ref, di1_ref, wx1_ref, wy1_ref, wz1_ref, e21_ref, msg_ref,
    h_ref, k_ref, m_ref, e1_ref,
):
    for ref in (h_ref, k_ref, s_ref, wx_ref, wy_ref, wz_ref, di_ref, r_ref, e1_ref, e2_ref):
        blank_ends(ref)
    for f, ref in enumerate((h_ref, k_ref, s_ref, m_ref)):
        fill_window(ref, xfirst[f], own[f], xsecond[f], yfirst[f], ysecond[f])

    def harmonic(a, b):
        total = a + b
        return jnp.where(total > 0.0, 2.0 * a * b / total, 0.0)

    def faces(i, carry):
        at = 1 + 2 * i
        k = k_ref[pl.ds(at, 2)]
        wx_ref[pl.ds(at, 2)] = harmonic(k, k_ref[pl.ds(at - 1, 2)])
        wy_ref[pl.ds(at, 2)] = harmonic(k, turn(k, 1, 1))
        wz = harmonic(k, turn(k, 1, 2))
        wz_ref[pl.ds(at, 2)] = jnp.where(iota(wz.shape, 2) == 0, 0.0, wz)
        return carry

    lax.fori_loop(0, WX // 2, faces, 0, unroll=4)

    def right_side(i, carry):
        at = 1 + 2 * i
        rows = pl.ds(at, 2)
        h, wx, wy, wz = h_ref[rows], wx_ref[rows], wy_ref[rows], wz_ref[rows]
        wx_up = wx_ref[pl.ds(at + 1, 2)]
        fy = wy * (h - turn(h, 1, 1))
        fz = wz * (h - turn(h, 1, 2) + 1.0)
        flux = wx * (h - h_ref[pl.ds(at - 1, 2)]) - wx_up * (h_ref[pl.ds(at + 1, 2)] - h)
        flux = flux + (fy - turn(fy, -1, 1)) + (fz - turn(fz, -1, 2))
        rhs = -(m_ref[rows] + flux)
        diagonal = s_ref[rows] + wx + wx_up + wy + turn(wy, -1, 1) + wz + turn(wz, -1, 2)
        di = jnp.where(diagonal > 0.0, OMEGA / diagonal, 0.0)
        r_ref[rows] = rhs
        di_ref[rows] = di
        e1_ref[rows] = rhs * di
        return carry

    lax.fori_loop(0, WX // 2, right_side, 0, unroll=4)

    def bands(i, carry):
        rows = pl.ds(1 + 2 * i, 2)
        s1, wx1, wy1, wz1 = coarsen(s_ref[rows], wx_ref[rows], wy_ref[rows], wz_ref[rows], 1, 1)
        row = pl.ds(i, 1)
        s1_ref[row], wx1_ref[row], wy1_ref[row], wz1_ref[row] = s1, wx1, wy1, wz1
        return carry

    lax.fori_loop(1, WX // 2 - 1, bands, 0, unroll=5)
    for ref in (s1_ref, wx1_ref, wy1_ref, wz1_ref):
        blank_level1(ref, 1)
    blank_level1(r1_ref, 2)
    descend_top(r_ref, e1_ref, e2_ref, s_ref, wx_ref, wy_ref, wz_ref, di_ref, r1_ref)

    s1, wx1, wy1, wz1 = s1_ref[...], wx1_ref[...], wy1_ref[...], wz1_ref[...]
    di1 = relax_factor(s1, wx1, wy1, wz1, 2, 2)
    di1_ref[...] = di1
    e21, r2 = descend_second(r1_ref[...], s1, wx1, wy1, wz1, di1)
    e21_ref[...] = e21
    bands2 = coarsen(s1, wx1, wy1, wz1, 2, 2)
    bands3 = coarsen(*(v[2:4] for v in bands2), 4, 4)
    rows = [pack_level2(v[2:4]) for v in (r2,) + bands2]
    send(msg_ref, rows + [pack_bands3(bands3)])


def again_kernel(
    xfirst, own, xsecond, yfirst, ysecond, rhs_ref, s_ref, di_ref, wx_ref, wy_ref, wz_ref,
    s1_ref, di1_ref, wx1_ref, wy1_ref, wz1_ref,
    u_ref, r_ref, e2_ref, r1_ref, e21_ref, msg_ref, edge_ref, pre_ref, e1_ref,
):
    for ref in (pre_ref, u_ref, r_ref, e1_ref, e2_ref):
        blank_ends(ref)
    fill_window(pre_ref, xfirst[...], own[...], xsecond[...], yfirst[...], ysecond[...])

    def post(i, carry):
        at = 1 + 2 * i
        rows = pl.ds(at, 2)
        v, av = operate_rows(pre_ref, s_ref, wx_ref, wy_ref, wz_ref, at, 2)
        u_ref[rows] = v + di_ref[rows] * (rhs_ref[rows] - av)
        return carry

    lax.fori_loop(0, WX // 2, post, 0, unroll=4)

    def remain(i, carry):
        at = 1 + 2 * i
        rows = pl.ds(at, 2)
        _, av = operate_rows(u_ref, s_ref, wx_ref, wy_ref, wz_ref, at, 2)
        left = rhs_ref[rows] - av
        r_ref[rows] = left
        e1_ref[rows] = left * di_ref[rows]
        return carry

    lax.fori_loop(1, WX // 2 - 1, remain, 0, unroll=5)
    descend_top(r_ref, e1_ref, e2_ref, s_ref, wx_ref, wy_ref, wz_ref, di_ref, r1_ref)
    blank_level1(r1_ref, 2)
    e21, r2 = descend_second(
        r1_ref[...], s1_ref[...], wx1_ref[...], wy1_ref[...], wz1_ref[...], di1_ref[...]
    )
    e21_ref[...] = e21
    tile = lax.axis_index("tile")
    to_low, to_high = pack_ring1(e21)
    for peer in range(msg_ref.shape[0]):
        ring = jnp.where(tile > peer, to_low, to_high)
        msg_ref[peer, 0] = pack_level2(r2[2:4])
        msg_ref[peer, 1], msg_ref[peer, 2] = ring[0:2], ring[2:4]
    send(edge_ref, [pack_edge1(e21)])


def message_rows(ref):
    tiles = lax.axis_size("tile")
    return lambda field, half: ref[0:tiles, field, half : half + 1, :]


def choose(which, one, two):
    return lambda field, half: jnp.where(which, one(field, half), two(field, half))


def both_sides(first, second, step, lead):
    even = is_even("group", step, lead)
    one, two = message_rows(first), message_rows(second)
    return choose(even, two, one), choose(even, one, two)


def pair_rows(here, first, second):
    before, after = both_sides(first, second, 2, 1)
    even = is_even("group")
    one, two = message_rows(here.at[:, 0]), message_rows(here.at[:, 1])
    return choose(even, before, one), choose(even, one, two), choose(even, two, after)


def band_rows3(here, first, second):
    before, after = both_sides(first, second, 2, 1)
    even = is_even("group")
    six = [before(5, half) for half in range(2)]
    six += [here[:, core, 5, 0:1, :] for core in range(2)]
    six += [after(5, half) for half in range(2)]
    return [jnp.where(even, six[i], six[i + 1]) for i in range(5)]


def unpack_level2(field, own, low, high):
    tiles = lax.axis_size("tile")
    shape = (tiles, 16, NZ)
    sub, lane = iota(shape, 1), iota(shape, 2)
    halves = []
    for half in range(2):

        def spread(pick, half=half):
            return jnp.broadcast_to(pick(field, half), shape)

        v = jnp.where(sub < 4, spread(low), jnp.where(sub < 8, spread(own), spread(high)))
        v = jnp.where((lane % 4 == sub % 4) & (sub < 12), v, 0.0)
        halves.append(pair_sum(pair_sum(v, 1, 2), 2, 2))
    return jnp.stack(halves, axis=1).reshape((2 * tiles, 16, NZ))


def pack_level3(v):
    sub, lane = iota((16, NZ), 0), iota((16, NZ), 1)
    rows = []
    for j in range(v.shape[0] // 4):
        total = jnp.zeros((16, NZ), F32)
        for q in range(4):
            chosen = ((sub == 4) & (lane % 8 == 2 * q)) | ((sub == 6) & (lane % 8 == 2 * q + 1))
            total = total + jnp.where(chosen, v[4 * j + q], 0.0)
        rows.append(jnp.sum(total, axis=0, keepdims=True))
    return rows


def pack_sums3(v):
    even = is_even("group")
    tiles = v.shape[0]
    start = jnp.where(even, 8, 4)
    sub, lane = iota((24, NZ), 0), iota((24, NZ), 1)
    once = (sub >= start) & (sub < start + 8) & (sub % 2 == 0)
    total = jnp.zeros((24, NZ), F32)
    for q in range(tiles // 2):
        part = jnp.where(even, v[q], v[tiles // 2 + q])
        total = total + jnp.where(once & (lane % 8 == q), part, 0.0)
    return [jnp.sum(total, axis=0, keepdims=True)]


def descend_third(r2, s2, wx2, wy2, wz2, di2):
    first = r2 * di2
    second = first + di2 * (r2 - operate(first, s2, wx2, wy2, wz2, 1, 4))
    return second, restrict(r2 - operate(second, s2, wx2, wy2, wz2, 1, 4), 1, 4)


def sides_kernel(here, first_ref, second_ref):
    even = is_even("group", 2, 1)
    low, high = here[:, 0, 0:5], here[:, 1, 0:5]
    first_ref[:, 0:5] = jnp.where(even, high, low)
    second_ref[:, 0:5] = jnp.where(even, low, high)
    for core in range(2):
        rows = here[:, core, 5, 0:1, :]
        first_ref[:, 5, core : core + 1, :] = rows
        second_ref[:, 5, core : core + 1, :] = rows


def third_kernel(
    first, here, second,
    r2_ref, s2_ref, di2_ref, wx2_ref, wy2_ref, wz2_ref, e22_ref,
    s3_ref, di3_ref, wx3_ref, wy3_ref, wz3_ref, msg_ref,
):
    s3, wx3, wy3, wz3 = unpack_bands3(band_rows3(here, first, second))
    s3_ref[...], wx3_ref[...], wy3_ref[...], wz3_ref[...] = s3, wx3, wy3, wz3
    di3_ref[...] = relax_factor(s3, wx3, wy3, wz3, 2, 8)
    inner = s3 + wx3 + x_high(wx3) + wz3 + turn(wz3, -8, 2)
    low, own, high = pair_rows(here, first, second)
    r2, s2, wx2, wy2, wz2 = (unpack_level2(f, own, low, high) for f in range(5))
    di2 = relax_factor(s2, wx2, wy2, wz2, 1, 4)
    r2_ref[...], s2_ref[...], di2_ref[...] = r2, s2, di2
    wx2_ref[...], wy2_ref[...], wz2_ref[...] = wx2, wy2, wz2
    e22, r3 = descend_third(r2, s2, wx2, wy2, wz2, di2)
    e22_ref[...] = e22
    send(msg_ref, pack_level3(r3) + pack_sums3(inner))


def third_again_kernel(
    own, first, second, s2_ref, di2_ref, wx2_ref, wy2_ref, wz2_ref, r2_ref, e22_ref, msg_ref
):
    r2 = unpack_level2(0, message_rows(own), *both_sides(first, second, 1, 0))
    r2_ref[...] = r2
    e22, r3 = descend_third(
        r2, s2_ref[...], wx2_ref[...], wy2_ref[...], wz2_ref[...], di2_ref[...]
    )
    e22_ref[...] = e22
    send(msg_ref, pack_level3(r3))


def third_masks(shape):
    sub, lane = iota(shape, 1), iota(shape, 2)
    return sub // 4, (sub % 4) // 2, lane % 8


def octuple(v):
    v = pair_sum(v, 1, 2)
    v = v + turn(v, 2, 2)
    return v + turn(v, 4, 2)


def shifted(v, lanes):
    return turn(v, -lanes, 2) if lanes else v


def unpack_bands3(sources):
    shape = (sources[0].shape[0], 24, NZ)
    dev, half, slot = third_masks(shape)
    rows = jnp.broadcast_to(sources[0], shape)
    for d in range(1, 5):
        rows = jnp.where(dev == d, jnp.broadcast_to(sources[d], shape), rows)
    rows = jnp.where(dev < 5, rows, 0.0)
    return [octuple(jnp.where(slot == half, shifted(rows, 2 * f), 0.0)) for f in range(4)]


def unpack_r3(v):
    group = lax.axis_index("group")
    at = iota(v.shape, 1)
    shape = (v.shape[0], 24, NZ)
    dev, half, slot = third_masks(shape)
    rows = jnp.zeros(shape, F32)
    for d in range(5):
        near = jnp.sum(jnp.where(at == group + (d - 2), v, 0.0), axis=1, keepdims=True)
        rows = jnp.where(dev == d, jnp.broadcast_to(near, shape), rows)
    parts = [jnp.where(slot == half, shifted(rows, 2 * q), 0.0) for q in range(4)]
    return octuple(jnp.stack(parts, axis=1).reshape((4 * v.shape[0], 24, NZ)))


def line_sums(v, held):
    total = jnp.sum(v, axis=1, keepdims=True)
    lane = iota(total.shape, 2) % 8
    width = 8 // held
    parts = [jnp.where(lane < width, shifted(total, width * q), 0.0) for q in range(held)]
    wide = jnp.stack(parts, axis=1).reshape((held * v.shape[0], 1, NZ))
    return octuple(wide)


def solve_third(r3, line, s3, di3, wx3, wy3, wz3):
    v = jnp.broadcast_to(line, r3.shape)
    for _ in range(COARSE_SWEEPS):
        v = v + di3 * (r3 - operate(v, s3, wx3, wy3, wz3, 2, 8))
    return turn(v, -4, 1)[:, 0:16]


def widen_y(v):
    shape = (v.shape[0], 8, NZ)
    sub = iota(shape, 1)
    parts = []
    for at in (2, 4, 6, 8):
        first = jnp.broadcast_to(v[:, at : at + 1], shape)
        second = jnp.broadcast_to(v[:, at + 1 : at + 2], shape)
        parts.append(jnp.where(sub < 4, first, second))
    return jnp.concatenate(parts, axis=1)


def climb_to_second(
    corr3, r2_ref, s2_ref, di2_ref, wx2_ref, wy2_ref, wz2_ref, e22_ref, corr3_ref, corr2_ref
):
    tile, tiles = lax.axis_index("tile"), lax.axis_size("tile")
    start = jnp.clip(tile - 2, 0, tiles - 4)
    corr3_ref[...] = corr3
    rows = pl.ds(2 * start, 8)
    v = e22_ref[rows] + x_repeat(corr3_ref[pl.ds(start, 4)])
    v = v + di2_ref[rows] * (
        r2_ref[rows]
        - operate(v, s2_ref[rows], wx2_ref[rows], wy2_ref[rows], wz2_ref[rows], 1, 4)
    )
    corr2_ref[0:4] = jnp.zeros((4, 16, NZ), F32)
    corr2_ref[4:12] = v
    corr2_ref[12:16] = jnp.zeros((4, 16, NZ), F32)
    near = corr2_ref[pl.ds(2 * (tile - start) + 2, 6)]
    return x_repeat(widen_y(near))


def climb_to_first(v, r1_ref, s1_ref, di1_ref, wx1_ref, wy1_ref, wz1_ref):
    rows = slice(2, 10)
    v = v[rows]
    return v + di1_ref[rows] * (
        r1_ref[rows]
        - operate(v, s1_ref[rows], wx1_ref[rows], wy1_ref[rows], wz1_ref[rows], 2, 2)
    )


def strided(ref, first, thirds, groups, rows):
    parts = [ref[pl.ds(first + j, groups, stride=rows), :] for j in range(thirds)]
    return jnp.stack(parts, axis=0)


def climb_kernel(
    third_ref, s3_ref, di3_ref, wx3_ref, wy3_ref, wz3_ref,
    r2_ref, s2_ref, di2_ref, wx2_ref, wy2_ref, wz2_ref, e22_ref,
    r1_ref, s1_ref, di1_ref, wx1_ref, wy1_ref, wz1_ref, e21_ref, e2_ref,
    pre_ref, below_ref, corr3_ref, corr2_ref, rows_ref,
    *, groups, thirds, rows,
):
    rows_ref[0 : groups * rows] = third_ref[...]
    r3 = strided(rows_ref, 0, thirds, groups, rows)
    tiles = lax.axis_size("tile")
    sums = strided(rows_ref, thirds, 1, groups, rows)
    odd = iota(sums.shape, 1) % 2
    below = jnp.concatenate(
        [line_sums(jnp.where(odd == half, sums, 0.0), 8)[: tiles // 2] for half in range(2)], axis=0
    )
    below_ref[...] = below
    corr3 = solve_third(
        unpack_r3(r3), line_sums(r3, 4) / below,
        s3_ref[...], di3_ref[...], wx3_ref[...], wy3_ref[...], wz3_ref[...],
    )
    corr2 = climb_to_second(
        corr3, r2_ref, s2_ref, di2_ref, wx2_ref, wy2_ref, wz2_ref, e22_ref, corr3_ref, corr2_ref
    )
    v = climb_to_first(
        e21_ref[...] + corr2, r1_ref, s1_ref, di1_ref, wx1_ref, wy1_ref, wz1_ref
    )
    own1 = x_repeat(v[2:6])
    pre_ref[...] = e2_ref[9:17, 8:24, :] + own1[:, 8:24, :]


def tile_rows(refs, even, off, at):
    tile = lax.axis_index("tile")
    total = jnp.zeros((2, NZ), F32)
    for t in range(lax.axis_size("tile")):
        rows = refs[0][t, at] if len(refs) == 1 else jnp.where(even, refs[0][t, at], refs[1][t, at])
        total = total + jnp.where(tile + off == t, rows, 0.0)
    return total


def ring_row(own, first, second, off):
    even = is_even("group")
    pairs = [tile_rows((own,), even, off, 1), tile_rows((own,), even, off, 2)]
    packed = [tile_rows((second, first), even, off, 2)[1:2]]
    packed += [pair[k : k + 1] for pair in pairs for k in range(2)]
    packed += [tile_rows((first, second), even, off, 1)[0:1]]
    return spread_pairs([row[None] for row in packed], 1)


def spread_pairs(packed, height):
    shape = (height, WY, NZ)
    sub, lane = iota(shape, 1), iota(shape, 2)
    rows = jnp.zeros(shape, F32)
    for k, row in enumerate(packed):
        rows = jnp.where(sub // 4 == k + 1, jnp.broadcast_to(row, shape), rows)
    return pair_sum(jnp.where(lane % 2 == (sub // 2) % 2, rows, 0.0), 1, 2)


def last_climb_kernel(
    third_ref, below_ref, s3_ref, di3_ref, wx3_ref, wy3_ref, wz3_ref,
    first, own, second,
    r2_ref, s2_ref, di2_ref, wx2_ref, wy2_ref, wz2_ref, e22_ref,
    r1_ref, s1_ref, di1_ref, wx1_ref, wy1_ref, wz1_ref, e21_ref,
    e2_ref, rhs_ref, s_ref, di_ref, wx_ref, wy_ref, wz_ref, u_ref, r_ref,
    out_ref, left_ref, pre_ref, v_ref, corr3_ref, corr2_ref, rows_ref,
    *, groups, thirds, rows,
):
    rows_ref[0 : groups * rows] = third_ref[...]
    r3 = strided(rows_ref, 0, thirds, groups, rows)
    corr3 = solve_third(
        unpack_r3(r3), line_sums(r3, 4) / below_ref[...],
        s3_ref[...], di3_ref[...], wx3_ref[...], wy3_ref[...], wz3_ref[...],
    )
    corr2 = climb_to_second(
        corr3, r2_ref, s2_ref, di2_ref, wx2_ref, wy2_ref, wz2_ref, e22_ref, corr3_ref, corr2_ref
    )
    tiles = lax.axis_size("tile")
    middle = e21_ref[3:9]
    sub = iota(middle.shape, 1)
    edge_first = jnp.concatenate([first[tiles, k] for k in range(3)], axis=0)[:, None]
    edge_second = jnp.concatenate([second[tiles, k] for k in range(3)], axis=0)[:, None]
    edge_low, edge_high = sides(edge_first, edge_second, "group")
    nothing = jnp.zeros_like(edge_low)
    edges = spread_pairs([edge_low] + [nothing] * 4 + [edge_high], 6)
    kept = (sub >= 6) & (sub < 26)
    middle = jnp.where(kept, middle, edges)
    blank = jnp.zeros((2, WY, NZ), F32)
    ends = [ring_row(own, first, second, off) for off in (-1, 1)]
    e21 = jnp.concatenate([blank, ends[0], middle, ends[1], blank], axis=0)
    v = climb_to_first(e21 + corr2, r1_ref, s1_ref, di1_ref, wx1_ref, wy1_ref, wz1_ref)
    pre_ref[7:19] = e2_ref[7:19] + x_repeat(v[1:7])

    def post(i, carry):
        at = 8 + 2 * i
        here = pl.ds(at, 2)
        v, av = operate_rows(pre_ref, s_ref, wx_ref, wy_ref, wz_ref, at, 2)
        v_ref[here] = u_ref[here] + v + di_ref[here] * (r_ref[here] - av)
        return carry

    lax.fori_loop(0, BX // 2 + 1, post, 0, unroll=True)

    def remain(i, carry):
        at = 9 + 2 * i
        v, av = operate_rows(v_ref, s_ref, wx_ref, wy_ref, wz_ref, at, 2)
        left = rhs_ref[pl.ds(at, 2)] - av
        out_ref[pl.ds(2 * i, 2)] = v[:, 8:24]
        left_ref[pl.ds(2 * i, 2)] = left[:, 8:24]
        return carry

    lax.fori_loop(0, BX // 2, remain, 0, unroll=True)


def call(body, outs, operands, scratch=()):
    cells = sum(math.prod(shape) for shape in outs)
    vmem = pl.BlockSpec(memory_space=pltpu.VMEM)
    return pl.pallas_call(
        body,
        out_shape=[jax.ShapeDtypeStruct(shape, F32) for shape in outs],
        in_specs=[vmem] * len(operands),
        out_specs=[vmem] * len(outs),
        scratch_shapes=[pltpu.VMEM(shape, F32) for shape in scratch],
        compiler_params=pltpu.CompilerParams(vmem_limit_bytes=16 * 1024 * 1024),
        cost_estimate=pl.CostEstimate(
            flops=20 * cells, bytes_accessed=8 * cells, transcendentals=0
        ),
    )(*operands)


def swaps(to_first, to_second, axis, step=1, lead=0):
    count = lax.axis_size(axis)

    def swap(cells, odd):
        ups = [
            (i, i + step) for i in range(count - step) if (i // step) % 2 == odd
        ]
        return lax.ppermute(cells, axis, ups + [(j, i) for i, j in ups])

    return swap(to_first, lead), swap(to_second, 1 - lead)


def surround(cells, dim):
    first, second = swaps(cells, cells, "tile")
    ydim = dim + 1
    even = is_even("group", 1, 1)

    def halves(v):
        low = lax.slice_in_dim(v, 0, 8, axis=ydim)
        high = lax.slice_in_dim(v, BY - 8, BY, axis=ydim)
        return jnp.where(even, high, low), jnp.where(even, low, high)

    parts = [halves(v) for v in (first, cells, second)]
    to_first, to_second = (jnp.concatenate(list(v), axis=dim) for v in zip(*parts, strict=True))
    return first, cells, second, *swaps(to_first, to_second, "group", 1, 1)


def everyone(blocks, axis):
    return lax.all_to_all(blocks, axis, 0, 0, tiled=True)


def pairs_of_tiles(block):
    tiles, groups = lax.axis_size("tile"), lax.axis_size("group")
    members = [
        [t * groups + 2 * pair + core for t in range(tiles) for core in range(2)]
        for pair in range(groups // 2)
    ]
    given = lax.all_to_all(
        block, ("tile", "group"), 0, 0, axis_index_groups=members, tiled=True
    )
    return given.reshape((tiles, 2) + block.shape[1:])


def shards(pressure_head, old_head, soil_type, conduct_sat, alpha_param, shape_param, water_span):
    tiles, groups = lax.axis_size("tile"), lax.axis_size("group")
    thirds = tiles // 4
    top, one, two = (PX, WY, NZ), (L1X, WY, NZ), (2 * tiles, 16, NZ)
    three, line = (tiles, 24, NZ), (tiles, 1, NZ)
    rows_once, rows_again = thirds + 1, thirds

    fields = pl.pallas_call(
        soil_kernel,
        out_shape=jax.ShapeDtypeStruct((4, BX, BY, NZ), F32),
        in_specs=[pl.BlockSpec(memory_space=pltpu.HBM)] * 7,
        out_specs=pl.BlockSpec(memory_space=pltpu.VMEM),
        scratch_shapes=[
            pltpu.VMEM((BX, BY, NZ), F32),
            pltpu.VMEM((BX, BY, NZ), F32),
            pltpu.VMEM((BX, BY, NZ), jnp.int32),
            *[pltpu.SMEM((SOILS,), F32) for _ in range(4)],
            pltpu.SemaphoreType.DMA((7,)),
        ],
    )(pressure_head, old_head, soil_type, conduct_sat, alpha_param, shape_param, water_span)
    around = surround(fields, 1)
    rhs, s0, di0, wx0, wy0, wz0, e2, r1, s1, di1, wx1, wy1, wz1, e21, msg = call(
        assemble_kernel,
        [top] * 7 + [one] * 7 + [(2 * tiles, 6, 2, NZ)],
        list(around),
        [top] * 4,
    )
    bands0 = [s0, di0, wx0, wy0, wz0]
    bands1 = [s1, di1, wx1, wy1, wz1]

    here = pairs_of_tiles(msg)
    to_first, to_second = call(sides_kernel, [(tiles, 6, 2, NZ)] * 2, [here])
    first, second = swaps(to_first, to_second, "group", 2, 1)
    r2, s2, di2, wx2, wy2, wz2, e22, *bands3, msg = call(
        third_kernel,
        [two] * 7 + [three] * 5 + [(groups, rows_once, 1, NZ)],
        [first, here, second],
    )
    bands2 = [s2, di2, wx2, wy2, wz2]
    third = everyone(msg, "group").reshape(groups * rows_once, NZ)
    pre, below = call(
        functools.partial(climb_kernel, groups=groups, thirds=thirds, rows=rows_once),
        [(BX, BY, NZ), line],
        [third, *bands3, r2, *bands2, e22, r1, *bands1, e21, e2],
        [(tiles, 16, NZ), (16, 16, NZ), (groups * rows_once + 8, NZ)],
    )

    around = surround(pre, 0)
    u, rem, e2, r1, e21, msg, edge = call(
        again_kernel,
        [top] * 3 + [one] * 2 + [(tiles, 3, 2, NZ), (1, 3, 2, NZ)],
        [*around, rhs, *bands0, *bands1],
        [top] * 2,
    )
    own = jnp.concatenate([everyone(msg, "tile"), edge], axis=0)
    first, second = swaps(own, own, "group")
    r2, e22, msg = call(
        third_again_kernel,
        [two] * 2 + [(groups, rows_again, 1, NZ)],
        [own, first, second, *bands2],
    )
    third = everyone(msg, "group").reshape(groups * rows_again, NZ)
    update, remainder = call(
        functools.partial(last_climb_kernel, groups=groups, thirds=thirds, rows=rows_again),
        [(BX, BY, NZ)] * 2,
        [third, below, *bands3, first, own, second, r2, *bands2, e22, r1, *bands1, e21]
        + [e2, rhs, *bands0, u, rem],
        [top] * 2 + [(tiles, 16, NZ), (16, 16, NZ), (groups * rows_again + 8, NZ)],
    )
    return update, remainder


def solution(mesh):
    spec = P("tile", "group", None)
    return jax.shard_map(
        shards,
        mesh=mesh,
        in_specs=(spec, spec, spec, P(), P(), P(), P()),
        out_specs=(spec, spec),
        check_vma=False,
    )
```

```python
import functools
import math

import jax
import jax.numpy as jnp
from jax import lax
from jax.experimental import pallas as pl
from jax.experimental.pallas import tpu as pltpu
from jax.sharding import PartitionSpec as P

OMEGA = 2.0 / 3.0
STORAGE = 0.01
COARSE_SWEEPS = 4
SOILS = 12

BX, BY, NZ = 8, 16, 128
WX, WY = 24, 32
PX = WX + 2
L1X = WX // 2
F32 = jnp.float32


def iota(shape, dim):
    return lax.broadcasted_iota(jnp.int32, shape, dim)


def turn(v, step, axis):
    size = v.shape[axis]
    return pltpu.roll(v, step % size, axis)


def bit_of(v, step, axis):
    return (iota(v.shape, axis) // step) % 2 == 0


def pair_sum(v, step, axis):
    return v + jnp.where(bit_of(v, step, axis), turn(v, -step, axis), turn(v, step, axis))


def pair_low(v, step, axis):
    return jnp.where(bit_of(v, step, axis), v, turn(v, step, axis))


def x_low(v):
    return jnp.concatenate([v[:1], v[:-1]], axis=0)


def x_high(v):
    return jnp.concatenate([v[1:], jnp.zeros_like(v[:1])], axis=0)


def x_pair(v):
    return jnp.sum(v.reshape((v.shape[0] // 2, 2) + v.shape[1:]), axis=1)


def x_even(v):
    return v.reshape((v.shape[0] // 2, 2) + v.shape[1:])[:, 0]


def x_repeat(v):
    size = v.shape[0]
    wide = jnp.broadcast_to(v[:, None], (size, 2) + v.shape[1:])
    return wide.reshape((2 * size,) + v.shape[1:])


def operate(v, storage, wx, wy, wz, sy, sz):
    fx = wx * (v - x_low(v))
    fy = wy * (v - turn(v, sy, 1))
    fz = wz * (v - turn(v, sz, 2))
    flux = (fx - x_high(fx)) + (fy - turn(fy, -sy, 1)) + (fz - turn(fz, -sz, 2))
    return storage * v + flux


def relax_factor(storage, wx, wy, wz, sy, sz):
    diagonal = storage + wx + x_high(wx) + wy + turn(wy, -sy, 1) + wz + turn(wz, -sz, 2)
    return jnp.where(diagonal > 0.0, OMEGA / diagonal, 0.0)


def restrict(v, sy, sz):
    return pair_sum(pair_sum(x_pair(v), sy, 1), sz, 2)


def coarsen(storage, wx, wy, wz, sy, sz):
    return (
        restrict(storage, sy, sz),
        pair_sum(pair_sum(x_even(wx), sy, 1), sz, 2),
        pair_low(pair_sum(x_pair(wy), sz, 2), sy, 1),
        pair_low(pair_sum(x_pair(wz), sy, 1), sz, 2),
    )


def operate_rows(v_ref, s_ref, wx_ref, wy_ref, wz_ref, at, size):
    v = v_ref[pl.ds(at, size)]
    wx = wx_ref[pl.ds(at, size)]
    fy = wy_ref[pl.ds(at, size)] * (v - turn(v, 1, 1))
    fz = wz_ref[pl.ds(at, size)] * (v - turn(v, 1, 2))
    flux = wx * (v - v_ref[pl.ds(at - 1, size)])
    flux = flux - wx_ref[pl.ds(at + 1, size)] * (v_ref[pl.ds(at + 1, size)] - v)
    flux = flux + (fy - turn(fy, -1, 1)) + (fz - turn(fz, -1, 2))
    return v, s_ref[pl.ds(at, size)] * v + flux


def blank_ends(ref):
    ref[0] = jnp.zeros((WY, NZ), F32)
    ref[PX - 1] = jnp.zeros((WY, NZ), F32)


def blank_level1(ref, size):
    ref[0:size] = jnp.zeros((size, WY, NZ), F32)
    ref[L1X - size :] = jnp.zeros((size, WY, NZ), F32)


def pack_level2(v):
    sub, lane = iota(v.shape, 1), iota(v.shape, 2)
    chosen = (sub >= 8) & (sub < 24) & (sub % 4 == 0) & ((sub - 8) // 4 == lane % 4)
    return jnp.sum(jnp.where(chosen, v, 0.0), axis=1)


def send(msg_ref, rows):
    rows = list(rows)
    parts, height = msg_ref.shape[1:3]
    spare = parts * height - sum(row.shape[0] for row in rows)
    if spare:
        rows.append(jnp.zeros((spare, NZ), F32))
    whole = jnp.concatenate(rows, axis=0)
    for part in range(parts):
        piece = whole[part * height : (part + 1) * height]
        for peer in range(msg_ref.shape[0]):
            msg_ref[peer, part] = piece


def pack_bands3(fields):
    sub, lane = iota((1, WY, NZ), 1), iota((1, WY, NZ), 2)
    total = jnp.zeros((1, WY, NZ), F32)
    for f, v in enumerate(fields):
        chosen = ((sub == 8) & (lane % 8 == 2 * f)) | ((sub == 16) & (lane % 8 == 2 * f + 1))
        total = total + jnp.where(chosen, v, 0.0)
    return jnp.sum(total, axis=1)


def pack_ring1(v):
    sub, lane = iota((2, WY, NZ), 1), iota((2, WY, NZ), 2)
    rows = v[5:7]
    parts = []
    for k in range(4):
        chosen = ((sub == 8 + 4 * k) & (lane % 2 == 0)) | ((sub == 10 + 4 * k) & (lane % 2 == 1))
        parts.append(jnp.sum(jnp.where(chosen, rows, 0.0), axis=1, keepdims=True))
    return [jnp.concatenate([part[x] for part in parts], axis=0) for x in range(2)]


def pack_edge1(v):
    sub, lane = iota((6, WY, NZ), 1), iota((6, WY, NZ), 2)
    chosen = ((sub == 20) & (lane % 2 == 0)) | ((sub == 10) & (lane % 2 == 1))
    return jnp.sum(jnp.where(chosen, v[3:9], 0.0), axis=1)


def descend_top(r_ref, e1_ref, e2_ref, s_ref, wx_ref, wy_ref, wz_ref, di_ref, r1_ref):
    def second(i, carry):
        at = 1 + 2 * i
        v, av = operate_rows(e1_ref, s_ref, wx_ref, wy_ref, wz_ref, at, 2)
        e2_ref[pl.ds(at, 2)] = v + di_ref[pl.ds(at, 2)] * (r_ref[pl.ds(at, 2)] - av)
        return carry

    lax.fori_loop(1, WX // 2 - 1, second, 0, unroll=True)

    def third(i, carry):
        at = 1 + 2 * i
        _, av = operate_rows(e2_ref, s_ref, wx_ref, wy_ref, wz_ref, at, 2)
        r1_ref[pl.ds(i, 1)] = restrict(r_ref[pl.ds(at, 2)] - av, 1, 1)
        return carry

    lax.fori_loop(2, WX // 2 - 2, third, 0, unroll=True)


def descend_second(r1, s1, wx1, wy1, wz1, di1):
    first = r1 * di1
    second = first + di1 * (r1 - operate(first, s1, wx1, wy1, wz1, 2, 2))
    defect = r1 - operate(second, s1, wx1, wy1, wz1, 2, 2)
    return second, restrict(defect, 2, 2)


def soil_kernel(
    head_in, old_in, soil_in, ks_in, alpha_in, shape_in, span_in, out_ref,
    head_ref, old_ref, soil_ref, ks_ref, alpha_ref, shape_ref, span_ref, sems,
):
    given = (head_in, old_in, soil_in, ks_in, alpha_in, shape_in, span_in)
    held = (head_ref, old_ref, soil_ref, ks_ref, alpha_ref, shape_ref, span_ref)
    copies = [
        pltpu.make_async_copy(src, dst, sems.at[i])
        for i, (src, dst) in enumerate(zip(given, held, strict=True))
    ]
    for copy in copies:
        copy.start()
    for copy in copies:
        copy.wait()

    def cells(i, carry):
        row = pl.ds(i, 1)
        head, old, soil = head_ref[row], old_ref[row], soil_ref[row]
        ks = jnp.full(soil.shape, ks_ref[0])
        alpha = jnp.full(soil.shape, alpha_ref[0])
        shape_n = jnp.full(soil.shape, shape_ref[0])
        span = jnp.full(soil.shape, span_ref[0])
        for kind in range(1, SOILS):
            hit = soil == kind
            ks = jnp.where(hit, ks_ref[kind], ks)
            alpha = jnp.where(hit, alpha_ref[kind], alpha)
            shape_n = jnp.where(hit, shape_ref[kind], shape_n)
            span = jnp.where(hit, span_ref[kind], span)
        shape_m = 1.0 - 1.0 / shape_n
        power = jnp.exp(shape_n * jnp.log(alpha * -head))
        old_power = jnp.exp(shape_n * jnp.log(alpha * -old))
        saturation = jnp.exp(-shape_m * jnp.log1p(power))
        old_saturation = jnp.exp(-shape_m * jnp.log1p(old_power))
        portion = 1.0 / (1.0 + power)
        factor = 1.0 - jnp.exp(shape_m * jnp.log(power / (1.0 + power)))
        capacity = span * shape_m * shape_n * power / -head * saturation * portion
        out_ref[0, row] = head
        out_ref[1, row] = ks * jnp.sqrt(saturation) * factor * factor
        out_ref[2, row] = capacity + STORAGE
        out_ref[3, row] = span * (saturation - old_saturation) + STORAGE * (head - old)
        return carry

    lax.fori_loop(0, BX, cells, 0, unroll=True)


def is_even(axis, step=1, lead=0):
    return (lax.axis_index(axis) // step) % 2 == lead


def sides(first, second, axis, lead=0):
    even = is_even(axis, 1, lead)
    return jnp.where(even, second, first), jnp.where(even, first, second)


def fill_window(ref, xfirst, own, xsecond, yfirst, ysecond):
    ref[1 : 1 + BX, 8:24, :], ref[1 + 2 * BX : 1 + 3 * BX, 8:24, :] = sides(xfirst, xsecond, "tile")
    ref[1 + BX : 1 + 2 * BX, 8:24, :] = own
    ylow, yhigh = sides(yfirst, ysecond, "group", 1)
    for y, part in ((0, ylow), (24, yhigh)):
        low, high = sides(part[:BX], part[2 * BX :], "tile")
        ref[1 : 1 + BX, y : y + 8, :] = low
        ref[1 + BX : 1 + 2 * BX, y : y + 8, :] = part[BX : 2 * BX]
        ref[1 + 2 * BX : 1 + 3 * BX, y : y + 8, :] = high


def assemble_kernel(
    xfirst, own, xsecond, yfirst, ysecond,
    r_ref, s_ref, di_ref, wx_ref, wy_ref, wz_ref, e2_ref,
    r1_ref, s1_ref, di1_ref, wx1_ref, wy1_ref, wz1_ref, e21_ref, msg_ref,
    h_ref, k_ref, m_ref, e1_ref,
):
    for ref in (h_ref, k_ref, s_ref, wx_ref, wy_ref, wz_ref, di_ref, r_ref, e1_ref, e2_ref):
        blank_ends(ref)
    for f, ref in enumerate((h_ref, k_ref, s_ref, m_ref)):
        fill_window(ref, xfirst[f], own[f], xsecond[f], yfirst[f], ysecond[f])

    def harmonic(a, b):
        total = a + b
        return jnp.where(total > 0.0, 2.0 * a * b / total, 0.0)

    def faces(i, carry):
        at = 1 + 2 * i
        k = k_ref[pl.ds(at, 2)]
        wx_ref[pl.ds(at, 2)] = harmonic(k, k_ref[pl.ds(at - 1, 2)])
        wy_ref[pl.ds(at, 2)] = harmonic(k, turn(k, 1, 1))
        wz = harmonic(k, turn(k, 1, 2))
        wz_ref[pl.ds(at, 2)] = jnp.where(iota(wz.shape, 2) == 0, 0.0, wz)
        return carry

    lax.fori_loop(0, WX // 2, faces, 0, unroll=True)

    def right_side(i, carry):
        at = 1 + 2 * i
        rows = pl.ds(at, 2)
        h, wx, wy, wz = h_ref[rows], wx_ref[rows], wy_ref[rows], wz_ref[rows]
        wx_up = wx_ref[pl.ds(at + 1, 2)]
        fy = wy * (h - turn(h, 1, 1))
        fz = wz * (h - turn(h, 1, 2) + 1.0)
        flux = wx * (h - h_ref[pl.ds(at - 1, 2)]) - wx_up * (h_ref[pl.ds(at + 1, 2)] - h)
        flux = flux + (fy - turn(fy, -1, 1)) + (fz - turn(fz, -1, 2))
        rhs = -(m_ref[rows] + flux)
        diagonal = s_ref[rows] + wx + wx_up + wy + turn(wy, -1, 1) + wz + turn(wz, -1, 2)
        di = jnp.where(diagonal > 0.0, OMEGA / diagonal, 0.0)
        r_ref[rows] = rhs
        di_ref[rows] = di
        e1_ref[rows] = rhs * di
        return carry

    lax.fori_loop(0, WX // 2, right_side, 0, unroll=True)

    def bands(i, carry):
        rows = pl.ds(1 + 2 * i, 2)
        s1, wx1, wy1, wz1 = coarsen(s_ref[rows], wx_ref[rows], wy_ref[rows], wz_ref[rows], 1, 1)
        row = pl.ds(i, 1)
        s1_ref[row], wx1_ref[row], wy1_ref[row], wz1_ref[row] = s1, wx1, wy1, wz1
        return carry

    lax.fori_loop(1, WX // 2 - 1, bands, 0, unroll=True)
    for ref in (s1_ref, wx1_ref, wy1_ref, wz1_ref):
        blank_level1(ref, 1)
    blank_level1(r1_ref, 2)
    descend_top(r_ref, e1_ref, e2_ref, s_ref, wx_ref, wy_ref, wz_ref, di_ref, r1_ref)

    s1, wx1, wy1, wz1 = s1_ref[...], wx1_ref[...], wy1_ref[...], wz1_ref[...]
    di1 = relax_factor(s1, wx1, wy1, wz1, 2, 2)
    di1_ref[...] = di1
    e21, r2 = descend_second(r1_ref[...], s1, wx1, wy1, wz1, di1)
    e21_ref[...] = e21
    bands2 = coarsen(s1, wx1, wy1, wz1, 2, 2)
    bands3 = coarsen(*(v[2:4] for v in bands2), 4, 4)
    rows = [pack_level2(v[2:4]) for v in (r2,) + bands2]
    send(msg_ref, rows + [pack_bands3(bands3)])


def again_kernel(
    xfirst, own, xsecond, yfirst, ysecond, rhs_ref, s_ref, di_ref, wx_ref, wy_ref, wz_ref,
    s1_ref, di1_ref, wx1_ref, wy1_ref, wz1_ref,
    u_ref, r_ref, e2_ref, r1_ref, e21_ref, msg_ref, edge_ref, pre_ref, e1_ref,
):
    for ref in (pre_ref, u_ref, r_ref, e1_ref, e2_ref):
        blank_ends(ref)
    fill_window(pre_ref, xfirst[...], own[...], xsecond[...], yfirst[...], ysecond[...])

    def post(i, carry):
        at = 1 + 2 * i
        rows = pl.ds(at, 2)
        v, av = operate_rows(pre_ref, s_ref, wx_ref, wy_ref, wz_ref, at, 2)
        u_ref[rows] = v + di_ref[rows] * (rhs_ref[rows] - av)
        return carry

    lax.fori_loop(0, WX // 2, post, 0, unroll=True)

    def remain(i, carry):
        at = 1 + 2 * i
        rows = pl.ds(at, 2)
        _, av = operate_rows(u_ref, s_ref, wx_ref, wy_ref, wz_ref, at, 2)
        left = rhs_ref[rows] - av
        r_ref[rows] = left
        e1_ref[rows] = left * di_ref[rows]
        return carry

    lax.fori_loop(1, WX // 2 - 1, remain, 0, unroll=True)
    descend_top(r_ref, e1_ref, e2_ref, s_ref, wx_ref, wy_ref, wz_ref, di_ref, r1_ref)
    blank_level1(r1_ref, 2)
    e21, r2 = descend_second(
        r1_ref[...], s1_ref[...], wx1_ref[...], wy1_ref[...], wz1_ref[...], di1_ref[...]
    )
    e21_ref[...] = e21
    tile = lax.axis_index("tile")
    to_low, to_high = pack_ring1(e21)
    for peer in range(msg_ref.shape[0]):
        ring = jnp.where(tile > peer, to_low, to_high)
        msg_ref[peer, 0] = pack_level2(r2[2:4])
        msg_ref[peer, 1], msg_ref[peer, 2] = ring[0:2], ring[2:4]
    send(edge_ref, [pack_edge1(e21)])


def message_rows(ref):
    tiles = lax.axis_size("tile")
    return lambda field, half: ref[0:tiles, field, half : half + 1, :]


def choose(which, one, two):
    return lambda field, half: jnp.where(which, one(field, half), two(field, half))


def both_sides(first, second, step, lead):
    even = is_even("group", step, lead)
    one, two = message_rows(first), message_rows(second)
    return choose(even, two, one), choose(even, one, two)


def pair_rows(here, first, second):
    before, after = both_sides(first, second, 2, 1)
    even = is_even("group")
    one, two = message_rows(here.at[:, 0]), message_rows(here.at[:, 1])
    return choose(even, before, one), choose(even, one, two), choose(even, two, after)


def band_rows3(here, first, second):
    before, after = both_sides(first, second, 2, 1)
    even = is_even("group")
    six = [before(5, half) for half in range(2)]
    six += [here[:, core, 5, 0:1, :] for core in range(2)]
    six += [after(5, half) for half in range(2)]
    return [jnp.where(even, six[i], six[i + 1]) for i in range(5)]


def unpack_level2(field, own, low, high):
    tiles = lax.axis_size("tile")
    shape = (tiles, 16, NZ)
    sub, lane = iota(shape, 1), iota(shape, 2)
    halves = []
    for half in range(2):

        def spread(pick, half=half):
            return jnp.broadcast_to(pick(field, half), shape)

        v = jnp.where(sub < 4, spread(low), jnp.where(sub < 8, spread(own), spread(high)))
        v = jnp.where((lane % 4 == sub % 4) & (sub < 12), v, 0.0)
        halves.append(pair_sum(pair_sum(v, 1, 2), 2, 2))
    return jnp.stack(halves, axis=1).reshape((2 * tiles, 16, NZ))


def pack_level3(v):
    sub, lane = iota((16, NZ), 0), iota((16, NZ), 1)
    rows = []
    for j in range(v.shape[0] // 4):
        total = jnp.zeros((16, NZ), F32)
        for q in range(4):
            chosen = ((sub == 4) & (lane % 8 == 2 * q)) | ((sub == 6) & (lane % 8 == 2 * q + 1))
            total = total + jnp.where(chosen, v[4 * j + q], 0.0)
        rows.append(jnp.sum(total, axis=0, keepdims=True))
    return rows


def pack_sums3(v):
    even = is_even("group")
    tiles = v.shape[0]
    start = jnp.where(even, 8, 4)
    sub, lane = iota((24, NZ), 0), iota((24, NZ), 1)
    once = (sub >= start) & (sub < start + 8) & (sub % 2 == 0)
    total = jnp.zeros((24, NZ), F32)
    for q in range(tiles // 2):
        part = jnp.where(even, v[q], v[tiles // 2 + q])
        total = total + jnp.where(once & (lane % 8 == q), part, 0.0)
    return [jnp.sum(total, axis=0, keepdims=True)]


def descend_third(r2, s2, wx2, wy2, wz2, di2):
    first = r2 * di2
    second = first + di2 * (r2 - operate(first, s2, wx2, wy2, wz2, 1, 4))
    return second, restrict(r2 - operate(second, s2, wx2, wy2, wz2, 1, 4), 1, 4)


def sides_kernel(here, first_ref, second_ref):
    even = is_even("group", 2, 1)
    low, high = here[:, 0, 0:5], here[:, 1, 0:5]
    first_ref[:, 0:5] = jnp.where(even, high, low)
    second_ref[:, 0:5] = jnp.where(even, low, high)
    for core in range(2):
        rows = here[:, core, 5, 0:1, :]
        first_ref[:, 5, core : core + 1, :] = rows
        second_ref[:, 5, core : core + 1, :] = rows


def third_kernel(
    first, here, second,
    r2_ref, s2_ref, di2_ref, wx2_ref, wy2_ref, wz2_ref, e22_ref,
    s3_ref, di3_ref, wx3_ref, wy3_ref, wz3_ref, msg_ref,
):
    s3, wx3, wy3, wz3 = unpack_bands3(band_rows3(here, first, second))
    s3_ref[...], wx3_ref[...], wy3_ref[...], wz3_ref[...] = s3, wx3, wy3, wz3
    di3_ref[...] = relax_factor(s3, wx3, wy3, wz3, 2, 8)
    inner = s3 + wx3 + x_high(wx3) + wz3 + turn(wz3, -8, 2)
    low, own, high = pair_rows(here, first, second)
    r2, s2, wx2, wy2, wz2 = (unpack_level2(f, own, low, high) for f in range(5))
    di2 = relax_factor(s2, wx2, wy2, wz2, 1, 4)
    r2_ref[...], s2_ref[...], di2_ref[...] = r2, s2, di2
    wx2_ref[...], wy2_ref[...], wz2_ref[...] = wx2, wy2, wz2
    e22, r3 = descend_third(r2, s2, wx2, wy2, wz2, di2)
    e22_ref[...] = e22
    send(msg_ref, pack_level3(r3) + pack_sums3(inner))


def third_again_kernel(
    own, first, second, s2_ref, di2_ref, wx2_ref, wy2_ref, wz2_ref, r2_ref, e22_ref, msg_ref
):
    r2 = unpack_level2(0, message_rows(own), *both_sides(first, second, 1, 0))
    r2_ref[...] = r2
    e22, r3 = descend_third(
        r2, s2_ref[...], wx2_ref[...], wy2_ref[...], wz2_ref[...], di2_ref[...]
    )
    e22_ref[...] = e22
    send(msg_ref, pack_level3(r3))


def third_masks(shape):
    sub, lane = iota(shape, 1), iota(shape, 2)
    return sub // 4, (sub % 4) // 2, lane % 8


def octuple(v):
    v = pair_sum(v, 1, 2)
    v = v + turn(v, 2, 2)
    return v + turn(v, 4, 2)


def shifted(v, lanes):
    return turn(v, -lanes, 2) if lanes else v


def unpack_bands3(sources):
    shape = (sources[0].shape[0], 24, NZ)
    dev, half, slot = third_masks(shape)
    rows = jnp.broadcast_to(sources[0], shape)
    for d in range(1, 5):
        rows = jnp.where(dev == d, jnp.broadcast_to(sources[d], shape), rows)
    rows = jnp.where(dev < 5, rows, 0.0)
    return [octuple(jnp.where(slot == half, shifted(rows, 2 * f), 0.0)) for f in range(4)]


def unpack_r3(v):
    group = lax.axis_index("group")
    at = iota(v.shape, 1)
    shape = (v.shape[0], 24, NZ)
    dev, half, slot = third_masks(shape)
    rows = jnp.zeros(shape, F32)
    for d in range(5):
        near = jnp.sum(jnp.where(at == group + (d - 2), v, 0.0), axis=1, keepdims=True)
        rows = jnp.where(dev == d, jnp.broadcast_to(near, shape), rows)
    parts = [jnp.where(slot == half, shifted(rows, 2 * q), 0.0) for q in range(4)]
    return octuple(jnp.stack(parts, axis=1).reshape((4 * v.shape[0], 24, NZ)))


def line_sums(v, held):
    total = jnp.sum(v, axis=1, keepdims=True)
    lane = iota(total.shape, 2) % 8
    width = 8 // held
    parts = [jnp.where(lane < width, shifted(total, width * q), 0.0) for q in range(held)]
    wide = jnp.stack(parts, axis=1).reshape((held * v.shape[0], 1, NZ))
    return octuple(wide)


def solve_third(r3, line, s3, di3, wx3, wy3, wz3):
    v = jnp.broadcast_to(line, r3.shape)
    for _ in range(COARSE_SWEEPS):
        v = v + di3 * (r3 - operate(v, s3, wx3, wy3, wz3, 2, 8))
    return turn(v, -4, 1)[:, 0:16]


def widen_y(v):
    shape = (v.shape[0], 8, NZ)
    sub = iota(shape, 1)
    parts = []
    for at in (2, 4, 6, 8):
        first = jnp.broadcast_to(v[:, at : at + 1], shape)
        second = jnp.broadcast_to(v[:, at + 1 : at + 2], shape)
        parts.append(jnp.where(sub < 4, first, second))
    return jnp.concatenate(parts, axis=1)


def climb_to_second(
    corr3, r2_ref, s2_ref, di2_ref, wx2_ref, wy2_ref, wz2_ref, e22_ref, corr3_ref, corr2_ref
):
    tile, tiles = lax.axis_index("tile"), lax.axis_size("tile")
    start = jnp.clip(tile - 2, 0, tiles - 4)
    corr3_ref[...] = corr3
    rows = pl.ds(2 * start, 8)
    v = e22_ref[rows] + x_repeat(corr3_ref[pl.ds(start, 4)])
    v = v + di2_ref[rows] * (
        r2_ref[rows]
        - operate(v, s2_ref[rows], wx2_ref[rows], wy2_ref[rows], wz2_ref[rows], 1, 4)
    )
    corr2_ref[0:4] = jnp.zeros((4, 16, NZ), F32)
    corr2_ref[4:12] = v
    corr2_ref[12:16] = jnp.zeros((4, 16, NZ), F32)
    near = corr2_ref[pl.ds(2 * (tile - start) + 2, 6)]
    return x_repeat(widen_y(near))


def climb_to_first(v, r1_ref, s1_ref, di1_ref, wx1_ref, wy1_ref, wz1_ref):
    rows = slice(2, 10)
    v = v[rows]
    return v + di1_ref[rows] * (
        r1_ref[rows]
        - operate(v, s1_ref[rows], wx1_ref[rows], wy1_ref[rows], wz1_ref[rows], 2, 2)
    )


def strided(ref, first, thirds, groups, rows):
    parts = [ref[pl.ds(first + j, groups, stride=rows), :] for j in range(thirds)]
    return jnp.stack(parts, axis=0)


def climb_kernel(
    third_ref, s3_ref, di3_ref, wx3_ref, wy3_ref, wz3_ref,
    r2_ref, s2_ref, di2_ref, wx2_ref, wy2_ref, wz2_ref, e22_ref,
    r1_ref, s1_ref, di1_ref, wx1_ref, wy1_ref, wz1_ref, e21_ref, e2_ref,
    pre_ref, below_ref, corr3_ref, corr2_ref, rows_ref,
    *, groups, thirds, rows,
):
    rows_ref[0 : groups * rows] = third_ref[...]
    r3 = strided(rows_ref, 0, thirds, groups, rows)
    tiles = lax.axis_size("tile")
    sums = strided(rows_ref, thirds, 1, groups, rows)
    odd = iota(sums.shape, 1) % 2
    below = jnp.concatenate(
        [line_sums(jnp.where(odd == half, sums, 0.0), 8)[: tiles // 2] for half in range(2)], axis=0
    )
    below_ref[...] = below
    corr3 = solve_third(
        unpack_r3(r3), line_sums(r3, 4) / below,
        s3_ref[...], di3_ref[...], wx3_ref[...], wy3_ref[...], wz3_ref[...],
    )
    corr2 = climb_to_second(
        corr3, r2_ref, s2_ref, di2_ref, wx2_ref, wy2_ref, wz2_ref, e22_ref, corr3_ref, corr2_ref
    )
    v = climb_to_first(
        e21_ref[...] + corr2, r1_ref, s1_ref, di1_ref, wx1_ref, wy1_ref, wz1_ref
    )
    own1 = x_repeat(v[2:6])
    pre_ref[...] = e2_ref[9:17, 8:24, :] + own1[:, 8:24, :]


def tile_rows(refs, even, off, at):
    tile = lax.axis_index("tile")
    total = jnp.zeros((2, NZ), F32)
    for t in range(lax.axis_size("tile")):
        rows = refs[0][t, at] if len(refs) == 1 else jnp.where(even, refs[0][t, at], refs[1][t, at])
        total = total + jnp.where(tile + off == t, rows, 0.0)
    return total


def ring_row(own, first, second, off):
    even = is_even("group")
    pairs = [tile_rows((own,), even, off, 1), tile_rows((own,), even, off, 2)]
    packed = [tile_rows((second, first), even, off, 2)[1:2]]
    packed += [pair[k : k + 1] for pair in pairs for k in range(2)]
    packed += [tile_rows((first, second), even, off, 1)[0:1]]
    return spread_pairs([row[None] for row in packed], 1)


def spread_pairs(packed, height):
    shape = (height, WY, NZ)
    sub, lane = iota(shape, 1), iota(shape, 2)
    rows = jnp.zeros(shape, F32)
    for k, row in enumerate(packed):
        rows = jnp.where(sub // 4 == k + 1, jnp.broadcast_to(row, shape), rows)
    return pair_sum(jnp.where(lane % 2 == (sub // 2) % 2, rows, 0.0), 1, 2)


def last_climb_kernel(
    third_ref, below_ref, s3_ref, di3_ref, wx3_ref, wy3_ref, wz3_ref,
    first, own, second,
    r2_ref, s2_ref, di2_ref, wx2_ref, wy2_ref, wz2_ref, e22_ref,
    r1_ref, s1_ref, di1_ref, wx1_ref, wy1_ref, wz1_ref, e21_ref,
    e2_ref, rhs_ref, s_ref, di_ref, wx_ref, wy_ref, wz_ref, u_ref, r_ref,
    out_ref, left_ref, pre_ref, v_ref, corr3_ref, corr2_ref, rows_ref,
    *, groups, thirds, rows,
):
    rows_ref[0 : groups * rows] = third_ref[...]
    r3 = strided(rows_ref, 0, thirds, groups, rows)
    corr3 = solve_third(
        unpack_r3(r3), line_sums(r3, 4) / below_ref[...],
        s3_ref[...], di3_ref[...], wx3_ref[...], wy3_ref[...], wz3_ref[...],
    )
    corr2 = climb_to_second(
        corr3, r2_ref, s2_ref, di2_ref, wx2_ref, wy2_ref, wz2_ref, e22_ref, corr3_ref, corr2_ref
    )
    tiles = lax.axis_size("tile")
    middle = e21_ref[3:9]
    sub = iota(middle.shape, 1)
    edge_first = jnp.concatenate([first[tiles, k] for k in range(3)], axis=0)[:, None]
    edge_second = jnp.concatenate([second[tiles, k] for k in range(3)], axis=0)[:, None]
    edge_low, edge_high = sides(edge_first, edge_second, "group")
    nothing = jnp.zeros_like(edge_low)
    edges = spread_pairs([edge_low] + [nothing] * 4 + [edge_high], 6)
    kept = (sub >= 6) & (sub < 26)
    middle = jnp.where(kept, middle, edges)
    blank = jnp.zeros((2, WY, NZ), F32)
    ends = [ring_row(own, first, second, off) for off in (-1, 1)]
    e21 = jnp.concatenate([blank, ends[0], middle, ends[1], blank], axis=0)
    v = climb_to_first(e21 + corr2, r1_ref, s1_ref, di1_ref, wx1_ref, wy1_ref, wz1_ref)
    pre_ref[7:19] = e2_ref[7:19] + x_repeat(v[1:7])

    def post(i, carry):
        at = 8 + 2 * i
        here = pl.ds(at, 2)
        v, av = operate_rows(pre_ref, s_ref, wx_ref, wy_ref, wz_ref, at, 2)
        v_ref[here] = u_ref[here] + v + di_ref[here] * (r_ref[here] - av)
        return carry

    lax.fori_loop(0, BX // 2 + 1, post, 0, unroll=True)

    def remain(i, carry):
        at = 9 + 2 * i
        v, av = operate_rows(v_ref, s_ref, wx_ref, wy_ref, wz_ref, at, 2)
        left = rhs_ref[pl.ds(at, 2)] - av
        out_ref[pl.ds(2 * i, 2)] = v[:, 8:24]
        left_ref[pl.ds(2 * i, 2)] = left[:, 8:24]
        return carry

    lax.fori_loop(0, BX // 2, remain, 0, unroll=True)


def call(body, outs, operands, scratch=()):
    cells = sum(math.prod(shape) for shape in outs)
    vmem = pl.BlockSpec(memory_space=pltpu.VMEM)
    return pl.pallas_call(
        body,
        out_shape=[jax.ShapeDtypeStruct(shape, F32) for shape in outs],
        in_specs=[vmem] * len(operands),
        out_specs=[vmem] * len(outs),
        scratch_shapes=[pltpu.VMEM(shape, F32) for shape in scratch],
        compiler_params=pltpu.CompilerParams(vmem_limit_bytes=16 * 1024 * 1024),
        cost_estimate=pl.CostEstimate(
            flops=20 * cells, bytes_accessed=8 * cells, transcendentals=0
        ),
    )(*operands)


def swaps(to_first, to_second, axis, step=1, lead=0):
    count = lax.axis_size(axis)

    def swap(cells, odd):
        ups = [
            (i, i + step) for i in range(count - step) if (i // step) % 2 == odd
        ]
        return lax.ppermute(cells, axis, ups + [(j, i) for i, j in ups])

    return swap(to_first, lead), swap(to_second, 1 - lead)


def surround(cells, dim):
    first, second = swaps(cells, cells, "tile")
    ydim = dim + 1
    even = is_even("group", 1, 1)

    def halves(v):
        low = lax.slice_in_dim(v, 0, 8, axis=ydim)
        high = lax.slice_in_dim(v, BY - 8, BY, axis=ydim)
        return jnp.where(even, high, low), jnp.where(even, low, high)

    parts = [halves(v) for v in (first, cells, second)]
    to_first, to_second = (jnp.concatenate(list(v), axis=dim) for v in zip(*parts, strict=True))
    return first, cells, second, *swaps(to_first, to_second, "group", 1, 1)


def everyone(blocks, axis):
    return lax.all_to_all(blocks, axis, 0, 0, tiled=True)


def pairs_of_tiles(block):
    tiles, groups = lax.axis_size("tile"), lax.axis_size("group")
    members = [
        [t * groups + 2 * pair + core for t in range(tiles) for core in range(2)]
        for pair in range(groups // 2)
    ]
    given = lax.all_to_all(
        block, ("tile", "group"), 0, 0, axis_index_groups=members, tiled=True
    )
    return given.reshape((tiles, 2) + block.shape[1:])


def shards(pressure_head, old_head, soil_type, conduct_sat, alpha_param, shape_param, water_span):
    tiles, groups = lax.axis_size("tile"), lax.axis_size("group")
    thirds = tiles // 4
    top, one, two = (PX, WY, NZ), (L1X, WY, NZ), (2 * tiles, 16, NZ)
    three, line = (tiles, 24, NZ), (tiles, 1, NZ)
    rows_once, rows_again = thirds + 1, thirds

    fields = pl.pallas_call(
        soil_kernel,
        out_shape=jax.ShapeDtypeStruct((4, BX, BY, NZ), F32),
        in_specs=[pl.BlockSpec(memory_space=pltpu.HBM)] * 7,
        out_specs=pl.BlockSpec(memory_space=pltpu.VMEM),
        scratch_shapes=[
            pltpu.VMEM((BX, BY, NZ), F32),
            pltpu.VMEM((BX, BY, NZ), F32),
            pltpu.VMEM((BX, BY, NZ), jnp.int32),
            *[pltpu.SMEM((SOILS,), F32) for _ in range(4)],
            pltpu.SemaphoreType.DMA((7,)),
        ],
    )(pressure_head, old_head, soil_type, conduct_sat, alpha_param, shape_param, water_span)
    around = surround(fields, 1)
    rhs, s0, di0, wx0, wy0, wz0, e2, r1, s1, di1, wx1, wy1, wz1, e21, msg = call(
        assemble_kernel,
        [top] * 7 + [one] * 7 + [(2 * tiles, 6, 2, NZ)],
        list(around),
        [top] * 4,
    )
    bands0 = [s0, di0, wx0, wy0, wz0]
    bands1 = [s1, di1, wx1, wy1, wz1]

    here = pairs_of_tiles(msg)
    to_first, to_second = call(sides_kernel, [(tiles, 6, 2, NZ)] * 2, [here])
    first, second = swaps(to_first, to_second, "group", 2, 1)
    r2, s2, di2, wx2, wy2, wz2, e22, *bands3, msg = call(
        third_kernel,
        [two] * 7 + [three] * 5 + [(groups, rows_once, 1, NZ)],
        [first, here, second],
    )
    bands2 = [s2, di2, wx2, wy2, wz2]
    third = everyone(msg, "group").reshape(groups * rows_once, NZ)
    pre, below = call(
        functools.partial(climb_kernel, groups=groups, thirds=thirds, rows=rows_once),
        [(BX, BY, NZ), line],
        [third, *bands3, r2, *bands2, e22, r1, *bands1, e21, e2],
        [(tiles, 16, NZ), (16, 16, NZ), (groups * rows_once + 8, NZ)],
    )

    around = surround(pre, 0)
    u, rem, e2, r1, e21, msg, edge = call(
        again_kernel,
        [top] * 3 + [one] * 2 + [(tiles, 3, 2, NZ), (1, 3, 2, NZ)],
        [*around, rhs, *bands0, *bands1],
        [top] * 2,
    )
    own = jnp.concatenate([everyone(msg, "tile"), edge], axis=0)
    first, second = swaps(own, own, "group")
    r2, e22, msg = call(
        third_again_kernel,
        [two] * 2 + [(groups, rows_again, 1, NZ)],
        [own, first, second, *bands2],
    )
    third = everyone(msg, "group").reshape(groups * rows_again, NZ)
    update, remainder = call(
        functools.partial(last_climb_kernel, groups=groups, thirds=thirds, rows=rows_again),
        [(BX, BY, NZ)] * 2,
        [third, below, *bands3, first, own, second, r2, *bands2, e22, r1, *bands1, e21]
        + [e2, rhs, *bands0, u, rem],
        [top] * 2 + [(tiles, 16, NZ), (16, 16, NZ), (groups * rows_again + 8, NZ)],
    )
    return update, remainder


def solution(mesh):
    spec = P("tile", "group", None)
    return jax.shard_map(
        shards,
        mesh=mesh,
        in_specs=(spec, spec, spec, P(), P(), P(), P()),
        out_specs=(spec, spec),
        check_vma=False,
    )
```
